32 devices in a mesh: dp: 32 (over z, y, x, core).
Axes of the slice: x: 2, y: 2, z: 4, core: 2. Of those that a mesh axis runs over, the one named last changes fastest.
Arguments:
- images: bfloat16 [32, 3, 384, 384], P('dp'), may hold values from -6 to 6
- res_ids: int32 [32], P('dp'), may hold values 0 or 1
- labels: int32 [32], P('dp'), may hold values from 0 to 999
- rel_index: int32 [576, 576], replicated, may hold values from 0 to 2208, as said below
- master: float32 [2334720], P('dp'), as said below
- first_moment: float32 [2334720], P('dp')
- second_moment: float32 [2334720], P('dp'), as said below
- ema_weights: float32 [2334720], P('dp')
Outputs:
- loss_sum: float32 [], replicated
- grad_norm: float32 [], replicated
- new_weights: float32 [2334720], P('dp')
- new_first: float32 [2334720], P('dp')
- new_second: float32 [2334720], P('dp')
- new_ema: float32 [2334720], P('dp')
- weights_low: bfloat16 [2334720], P('dp')
The draws below stay inside these ranges and needn't reach their ends.
Inputs may be any that keep to these rules, and one draw needn't show every extreme that they name: `rel_index`: entry (i, j) names the table slot of the 2-D offset between token positions i and j on a grid of side 384/16; equal offsets share a slot and different offsets have different slots. `master`: the zero tail beyond 2333028 entries is zero. `second_moment`: positive.
All inputs are finite; a program needn't handle non-finite values. No bound on the sum of `res_ids` on one device may be relied on, other than what follows from the above.
Results may differ from the reference program's by a relative error of at most 0.0052.
The reference program's roundings to bfloat16 on the way (of `params`, `base`, `project` and `blended`) count: a program that leaves them out, or rounds other values in their place, can miss the bound.
Values may be sent and summed in bfloat16 or wider, within the bound.
No kernel may reach another device: no remote copies, remote signals or barrier semaphores. Data moves between devices by JAX's collectives and lax.ppermute only.
A program may use at most 640 MiB of HBM per device.

```python
import math
import jax
import jax.numpy as jnp
from jax import lax

STEM_CH = 64
MB_CH = 192
EXPAND = 768
SQUEEZE = 48
DIM = 384
HEADS = 12
HEAD_DIM = 32
MLP = 1536
CLASSES = 1000
CANVAS = 384
SMALL_RES = 224
STEP = 10
IMAGES = 32
PARAMS = 2333028
PFLAT = 2334720


NORM_NAMES = ('stem_norm', 'mid_norm', 'dw_norm', 'pre_norm', 'mlp_norm', 'head_norm')


BIAS_NAMES = ('se_down_bias', 'se_up_bias', 'out_bias', 'mlp_in_bias', 'mlp_out_bias', 'head_bias')


def layout_drawn():
    table_slots = (2 * (CANVAS // 16) - 1) ** 2
    return [('stem_w', (3, 3, 3, STEM_CH)), ('stem_norm', (2, STEM_CH)), ('mb_short', (STEM_CH, MB_CH)), ('mb_expand', (STEM_CH, EXPAND)), ('mid_norm', (2, EXPAND)), ('mb_depth', (9, EXPAND)), ('dw_norm', (2, EXPAND)), ('se_down', (EXPAND, SQUEEZE)), ('se_down_bias', (SQUEEZE,)), ('se_up', (SQUEEZE, EXPAND)), ('se_up_bias', (EXPAND,)), ('mb_proj', (EXPAND, MB_CH)), ('at_short', (MB_CH, DIM)), ('pre_norm', (2, MB_CH)), ('qkv', (MB_CH, 3 * DIM)), ('attn_out', (DIM, DIM)), ('out_bias', (DIM,)), ('rel_table', (HEADS, table_slots)), ('mlp_norm', (2, DIM)), ('mlp_in', (DIM, MLP)), ('mlp_in_bias', (MLP,)), ('mlp_out', (MLP, DIM)), ('mlp_out_bias', (DIM,)), ('head_norm', (2, DIM)), ('head_w', (DIM, CLASSES)), ('head_bias', (CLASSES,))]


def base_weights(key):
    pieces = []
    spreads = []
    for position, (entry_name, entry_shape) in enumerate(layout_drawn()):
        entry_size = math.prod(entry_shape)
        piece_key = jax.random.fold_in(key, 100 + position)
        normal = jax.random.normal(piece_key, (entry_size,), jnp.float32)
        if entry_name in NORM_NAMES:
            half_size = entry_size // 2
            gain_part = 1.0 + 0.3 * jax.random.uniform(jax.random.fold_in(piece_key, 1), (half_size,), jnp.float32, -1.0, 1.0)
            values = jnp.concatenate([gain_part, 0.2 * normal[half_size:]])
            spread_now = 0.2
        elif entry_name in BIAS_NAMES:
            spread_now = 0.2
            values = spread_now * normal
        elif entry_name == 'rel_table':
            spread_now = 0.5
            values = spread_now * normal
        elif entry_name == 'attn_out':
            spread_now = 4.0 / math.sqrt(DIM)
            values = spread_now * normal
        else:
            spread_now = (entry_size // entry_shape[-1]) ** (-0.5)
            values = spread_now * normal
        pieces.append(values)
        spreads.append(jnp.full((entry_size,), spread_now, jnp.float32))
    padding = jnp.zeros((PFLAT - PARAMS,), jnp.float32)
    return (jnp.concatenate(pieces + [padding]), jnp.concatenate(spreads + [padding]))


def draw_master(key, part):
    return base_weights(key)[0]


def draw_ema_weights(key, part):
    values, spreads = base_weights(key)
    key = jax.random.fold_in(key, 21)
    return values + 0.3 * spreads * jax.random.normal(key, (PFLAT,), jnp.float32)


def draw_first_moment(key, part):
    key = jax.random.fold_in(key, 31)
    return 0.05 / math.sqrt(PARAMS) * jax.random.normal(key, (PFLAT,), jnp.float32)


def draw_second_moment(key, part):
    key = jax.random.fold_in(key, 41)
    factor = jnp.exp(jax.random.uniform(key, (PFLAT,), jnp.float32, 0.0, math.log(4.0)))
    return (0.05 / math.sqrt(PARAMS)) ** 2 * factor


def draw_rel_index(key, part):
    key = jax.random.fold_in(key, 5)
    grid_side = CANVAS // 16
    span_side = 2 * grid_side - 1
    places = jnp.arange(grid_side * grid_side)
    row_of = places // grid_side
    col_of = places % grid_side
    canonical = (row_of[:, None] - row_of[None, :] + grid_side - 1) * span_side + (col_of[:, None] - col_of[None, :] + grid_side - 1)
    shuffled = jax.random.permutation(key, span_side * span_side)
    return shuffled[canonical].astype(jnp.int32)


def touch_ends(values, key, smallest, high):
    shape = values.shape
    index_at = [jax.random.randint(jax.random.fold_in(key, axis), (), 0, shape[axis]) for axis in range(len(shape))]
    values = values.at[tuple(index_at)].set(smallest)
    longest = shape.index(max(shape))
    index_at[longest] = (index_at[longest] + 1) % shape[longest]
    return values.at[tuple(index_at)].set(high)


def steps_of(rng, shape, shards, low, high):
    gain, own = 1.0, jax.random.fold_in(rng, 6)
    for dim, shards_of in shards:
        draws = jnp.exp(jax.random.uniform(jax.random.fold_in(own, dim), (shards_of,), jnp.float32, low / len(shards), high / len(shards)))
        gain = gain * jnp.repeat(draws, shape[dim] // shards_of).reshape([-1 if axis == dim else 1 for axis in range(len(shape))])
    return gain


def noise(own_key, shape, scale, bound, cuts=(), dtype=jnp.bfloat16):
    loudness = steps_of(own_key, shape, cuts, -0.22, 0.18) if cuts else 1.0
    entries = jax.random.normal(own_key, shape, jnp.float32) * scale * loudness
    return jnp.minimum(jnp.maximum(entries, -bound), bound).astype(dtype)


def setup_inputs(seed: int = 0) -> dict:
    keys = jax.random.split(jax.random.key(seed), 9)
    return {
        "images": noise(keys[0], (IMAGES, 3, CANVAS, CANVAS), 1.0, 6.0, ((0, 32),)),
        "res_ids": touch_ends((jax.random.randint(keys[1], (IMAGES,), 0, 10) < 3).astype(jnp.int32), jax.random.fold_in(keys[1], 1), 0, 1),
        "labels": touch_ends(jax.random.randint(keys[2], (IMAGES,), 0, CLASSES), jax.random.fold_in(keys[2], 1), 0, CLASSES - 1).astype(jnp.int32),
        "rel_index": draw_rel_index(jax.random.fold_in(keys[8], 71), 0),
        "master": draw_master(jax.random.fold_in(keys[8], 71), 0),
        "first_moment": draw_first_moment(jax.random.fold_in(keys[8], 71), 0),
        "second_moment": draw_second_moment(jax.random.fold_in(keys[8], 71), 0),
        "ema_weights": draw_ema_weights(jax.random.fold_in(keys[8], 71), 0),
    }


PREC = lax.Precision.HIGHEST
EPS = 1e-05
CLIP = 0.05
BETA_ONE = 0.5
BETA_TWO = 0.5
ADAM_EPS = 1e-08
RATE = 0.05
DECAY = 0.05
EMA_DECAY = 0.9
SMOOTH = 0.1

@jax.custom_vjp
def low(v):
    return lax.optimization_barrier(v.astype(jnp.bfloat16)).astype(jnp.float32)

@jax.custom_vjp
def low_back(v):
    return v

def low_keep(v):
    return (low(v), None)

def low_pass(kept, grad):
    return (grad,)

def back_keep(v):
    return (v, None)

def back_low(kept, grad):
    return (low(grad),)
low.defvjp(low_keep, low_pass)
low_back.defvjp(back_keep, back_low)

def layout():
    table_slots = (2 * (CANVAS // 16) - 1) ** 2
    return [('stem_w', (3, 3, 3, STEM_CH)), ('stem_norm', (2, STEM_CH)), ('mb_short', (STEM_CH, MB_CH)), ('mb_expand', (STEM_CH, EXPAND)), ('mid_norm', (2, EXPAND)), ('mb_depth', (9, EXPAND)), ('dw_norm', (2, EXPAND)), ('se_down', (EXPAND, SQUEEZE)), ('se_down_bias', (SQUEEZE,)), ('se_up', (SQUEEZE, EXPAND)), ('se_up_bias', (EXPAND,)), ('mb_proj', (EXPAND, MB_CH)), ('at_short', (MB_CH, DIM)), ('pre_norm', (2, MB_CH)), ('qkv', (MB_CH, 3 * DIM)), ('attn_out', (DIM, DIM)), ('out_bias', (DIM,)), ('rel_table', (HEADS, table_slots)), ('mlp_norm', (2, DIM)), ('mlp_in', (DIM, MLP)), ('mlp_in_bias', (MLP,)), ('mlp_out', (MLP, DIM)), ('mlp_out_bias', (DIM,)), ('head_norm', (2, DIM)), ('head_w', (DIM, CLASSES)), ('head_bias', (CLASSES,))]

def unpack(flat):
    params = {}
    offset = 0
    for entry_name, entry_shape in layout():
        entry_size = math.prod(entry_shape)
        params[entry_name] = flat[offset:offset + entry_size].reshape(entry_shape)
        offset += entry_size
    return params

def side_mask(res_ids, full_side, small_side):
    extent = jnp.where(res_ids == 1, full_side, small_side)
    inside = jnp.arange(full_side)[None, :] < extent[:, None]
    return (inside[:, :, None] & inside[:, None, :]).astype(jnp.float32)

def pool_by(inputs, factor):
    batch_size, height, across, channels = inputs.shape
    blocks = inputs.reshape(batch_size, height // factor, factor, across // factor, factor, channels)
    return lax.optimization_barrier(jnp.mean(blocks, axis=(2, 4)))

def moments(inputs, inside):
    weighted = inputs * inside[..., None]
    return (lax.optimization_barrier(jnp.sum(weighted, axis=(0, 1, 2))), lax.optimization_barrier(jnp.sum(weighted * inputs, axis=(0, 1, 2))))

def batch_norm(inputs, first, second, counted, gain_bias):
    center = first / counted
    spread = second / counted - center * center
    return (inputs - center) * lax.rsqrt(spread + EPS) * gain_bias[0] + gain_bias[1]

def layer_norm(inputs, gain_bias):
    centered = inputs - lax.optimization_barrier(jnp.mean(inputs, axis=-1, keepdims=True))
    inverse = lax.rsqrt(lax.optimization_barrier(jnp.mean(centered * centered, axis=-1, keepdims=True)) + EPS)
    return centered * inverse * gain_bias[0] + gain_bias[1]

def stem_part(params, images, res_ids):
    pixels = images.astype(jnp.float32) * side_mask(res_ids, CANVAS, SMALL_RES)[:, None]
    output = lax.conv_general_dilated(pixels, params['stem_w'], (2, 2), ((1, 1), (1, 1)), dimension_numbers=('NCHW', 'HWIO', 'NHWC'), precision=PREC)
    return low_back(output)

def block_entry(params, stem_out, stem_pair, counted):
    active = jax.nn.gelu(batch_norm(stem_out, stem_pair[0], stem_pair[1], counted, params['stem_norm']))
    base = low(pool_by(active, 4))
    expanded = low_back(jnp.matmul(base, params['mb_expand'], precision=PREC))
    return (expanded, base)

def block_depth(params, expanded, mid_pair, counted, inside):
    active = jax.nn.gelu(batch_norm(expanded, mid_pair[0], mid_pair[1], counted, params['mid_norm'])) * inside[..., None]
    extent = active.shape[1]
    padded = jnp.pad(active, ((0, 0), (1, 1), (1, 1), (0, 0)))
    summed = jnp.zeros_like(active)
    for offset_y in range(3):
        for offset_x in range(3):
            summed = summed + padded[:, offset_y:offset_y + extent, offset_x:offset_x + extent] * params['mb_depth'][3 * offset_y + offset_x]
    return summed

def attend(project, key_valid, table, rel_index):
    reshaped = project.reshape(project.shape[0], 3, HEADS, HEAD_DIM)
    queries, keys_in, values = (reshaped[:, 0], reshaped[:, 1], reshaped[:, 2])
    logits = low_back(jnp.einsum('qhd,khd->hqk', queries, keys_in, precision=PREC)) * HEAD_DIM ** (-0.5) + table[:, rel_index]
    logits = jnp.where(key_valid[None, None, :] > 0, logits, -1e+30)
    attention = low(jax.nn.softmax(logits, axis=-1))
    blended = low(low_back(jnp.einsum('hqk,khd->qhd', attention, values, precision=PREC)))
    return blended.reshape(blended.shape[0], HEADS * HEAD_DIM)

def block_tail(params, depth_out, depth_pair, counted, base, inside, res_ids, labels, rel_index):
    active = jax.nn.gelu(batch_norm(depth_out, depth_pair[0], depth_pair[1], counted, params['dw_norm'])) * inside[..., None]
    pooled = lax.optimization_barrier(jnp.sum(active, axis=(1, 2))) / lax.optimization_barrier(jnp.sum(inside, axis=(1, 2)))[:, None]
    squeeze = jax.nn.silu(jnp.matmul(pooled, params['se_down'], precision=PREC) + params['se_down_bias'])
    excite = jax.nn.sigmoid(jnp.matmul(squeeze, params['se_up'], precision=PREC) + params['se_up_bias'])
    scaled = low(active * excite[:, None, None, :])
    block_out = low_back(jnp.matmul(scaled, params['mb_proj'], precision=PREC)) + low_back(jnp.matmul(base, params['mb_short'], precision=PREC))
    batch_size = block_out.shape[0]
    normed = pool_by(layer_norm(block_out, params['pre_norm']), 2).reshape(batch_size, -1, MB_CH)
    skipped = low(pool_by(block_out, 2).reshape(batch_size, -1, MB_CH))
    project = low(low_back(jnp.matmul(low(normed), params['qkv'], precision=PREC)))
    token_valid = side_mask(res_ids, CANVAS // 16, SMALL_RES // 16).reshape(batch_size, -1)
    checked = jax.checkpoint(attend)
    attended = lax.map(lambda item_pair: checked(item_pair[0], item_pair[1], params['rel_table'], rel_index), (project, token_valid))
    section = low_back(jnp.matmul(skipped, params['at_short'], precision=PREC)) + low_back(jnp.matmul(attended, params['attn_out'], precision=PREC)) + params['out_bias']
    hidden = low(jax.nn.gelu(low_back(jnp.matmul(low(layer_norm(section, params['mlp_norm'])), params['mlp_in'], precision=PREC)) + params['mlp_in_bias']))
    section = section + low_back(jnp.matmul(hidden, params['mlp_out'], precision=PREC)) + params['mlp_out_bias']
    feature = lax.optimization_barrier(jnp.sum(section * token_valid[..., None], axis=1)) / lax.optimization_barrier(jnp.sum(token_valid, axis=1))[:, None]
    logits = low_back(jnp.matmul(low(layer_norm(feature, params['head_norm'])), params['head_w'], precision=PREC)) + params['head_bias']
    log_probs = jax.nn.log_softmax(logits, axis=-1)
    picked = jnp.take_along_axis(log_probs, labels[:, None], axis=1)[:, 0]
    return -jnp.sum((1.0 - SMOOTH) * picked + SMOOTH * lax.optimization_barrier(jnp.mean(log_probs, axis=-1)))

def forward(master, images, res_ids, labels, rel_index):
    params = unpack(low(master))
    stem_valid = side_mask(res_ids, CANVAS // 2, SMALL_RES // 2)
    mid_valid = side_mask(res_ids, CANVAS // 8, SMALL_RES // 8)
    stem_out = jax.checkpoint(stem_part)(params, images, res_ids)
    expanded, base = jax.checkpoint(block_entry)(params, stem_out, moments(stem_out, stem_valid), jnp.sum(stem_valid))
    mid_count = jnp.sum(mid_valid)
    depth_out = jax.checkpoint(block_depth)(params, expanded, moments(expanded, mid_valid), mid_count, mid_valid)
    return block_tail(params, depth_out, moments(depth_out, mid_valid), mid_count, base, mid_valid, res_ids, labels, rel_index)

def reference(images, res_ids, labels, rel_index, master, first_moment, second_moment, ema_weights):
    loss_sum, pullback = jax.vjp(lambda flat: forward(flat, images, res_ids, labels, rel_index), master)
    gradient, = pullback(jnp.ones_like(loss_sum) / IMAGES)
    grad_norm = jnp.sqrt(jnp.sum(gradient * gradient))
    clipped = gradient * (CLIP / jnp.maximum(grad_norm, CLIP))
    moment_one = BETA_ONE * first_moment + (1.0 - BETA_ONE) * clipped
    moment_two = BETA_TWO * second_moment + (1.0 - BETA_TWO) * clipped * clipped
    update = moment_one / (1.0 - BETA_ONE ** STEP) / (jnp.sqrt(moment_two / (1.0 - BETA_TWO ** STEP)) + ADAM_EPS)
    weights = master - RATE * (update + DECAY * master)
    averaged = EMA_DECAY * ema_weights + (1.0 - EMA_DECAY) * weights
    return (loss_sum, grad_norm, weights, moment_one, moment_two, averaged, weights.astype(jnp.bfloat16))
```

```python
import functools
import math

import jax
import jax.numpy as jnp
import numpy as np
from jax import lax
from jax.experimental import pallas as pl
from jax.experimental.pallas import tpu as pltpu
from jax.sharding import PartitionSpec as P

STEM_CH = 64
MB_CH = 192
EXPAND = 768
SQUEEZE = 48
DIM = 384
HEADS = 12
HEAD_DIM = 32
MLP = 1536
CLASSES = 1000
CANVAS = 384
SMALL_RES = 224
STEP = 10

EPS = 1e-05
CLIP = 0.05
BETA_ONE = 0.5
BETA_TWO = 0.5
ADAM_EPS = 1e-08
RATE = 0.05
DECAY = 0.05
EMA_DECAY = 0.9
SMOOTH = 0.1

SIDE = CANVAS // 8
SMALL_SIDE = SMALL_RES // 8
HALF = SIDE // 2
QUAD = HALF * HALF
PLACES = SIDE * SIDE
TAPS = 288
BLOCK = 128
CHUNKS = EXPAND // BLOCK

F32 = jnp.float32
BF16 = jnp.bfloat16
HIGH = lax.Precision.HIGHEST
VMEM_MAX = 56 * 1024 * 1024
GELU_A = math.sqrt(2.0 / math.pi)
GELU_B = 0.044715


def layout():
    table_slots = (2 * (CANVAS // 16) - 1) ** 2
    return [
        ("stem_w", (3, 3, 3, STEM_CH)),
        ("stem_norm", (2, STEM_CH)),
        ("mb_short", (STEM_CH, MB_CH)),
        ("mb_expand", (STEM_CH, EXPAND)),
        ("mid_norm", (2, EXPAND)),
        ("mb_depth", (9, EXPAND)),
        ("dw_norm", (2, EXPAND)),
        ("se_down", (EXPAND, SQUEEZE)),
        ("se_down_bias", (SQUEEZE,)),
        ("se_up", (SQUEEZE, EXPAND)),
        ("se_up_bias", (EXPAND,)),
        ("mb_proj", (EXPAND, MB_CH)),
        ("at_short", (MB_CH, DIM)),
        ("pre_norm", (2, MB_CH)),
        ("qkv", (MB_CH, 3 * DIM)),
        ("attn_out", (DIM, DIM)),
        ("out_bias", (DIM,)),
        ("rel_table", (HEADS, table_slots)),
        ("mlp_norm", (2, DIM)),
        ("mlp_in", (DIM, MLP)),
        ("mlp_in_bias", (MLP,)),
        ("mlp_out", (MLP, DIM)),
        ("mlp_out_bias", (DIM,)),
        ("head_norm", (2, DIM)),
        ("head_w", (DIM, CLASSES)),
        ("head_bias", (CLASSES,)),
    ]


def offsets():
    table = {}
    offset = 0
    for name, shape in layout():
        table[name] = (offset, shape)
        offset += math.prod(shape)
    return table


OFFSETS = offsets()
STEM_END = OFFSETS["mb_short"][0]
EARLY_END = OFFSETS["se_down"][0]


def dot(a, b, dims=((1,), (0,)), precision=None):
    return lax.dot_general(a, b, (dims, ((), ())), precision=precision, preferred_element_type=F32)


NT = ((1,), (1,))
TN = ((0,), (0,))


def gelu_pair(u):
    sq = u * u
    t = jnp.tanh(u * (GELU_A + (GELU_A * GELU_B) * sq))
    half = 0.5 + 0.5 * t
    slope = half + (0.5 * u) * (1.0 - t * t) * (GELU_A + (3.0 * GELU_A * GELU_B) * sq)
    return u * half, slope


def gelu(u):
    sq = u * u
    t = jnp.tanh(u * (GELU_A + (GELU_A * GELU_B) * sq))
    return u * (0.5 + 0.5 * t)


def limit_of(res_ref):
    return jnp.where(res_ref[0] == 1, SIDE, SMALL_SIDE)


def group_mask(group, limit, first_row, rows, lanes):
    place = lax.broadcasted_iota(jnp.int32, (rows, lanes), 0) + first_row
    up = place // HALF
    across = place - up * HALF
    y = 2 * up + group // 2
    x = 2 * across + group % 2
    return jnp.where((y < limit) & (x < limit), 1.0, 0.0)


def params_of(limit=VMEM_MAX):
    return pltpu.CompilerParams(vmem_limit_bytes=limit)


SMEM_SPEC = pl.BlockSpec(memory_space=pltpu.SMEM)
VMEM_SPEC = pl.BlockSpec(memory_space=pltpu.VMEM)


def patch_kernel(res_ref, img_ref, patch_ref, gram_ref):
    limit = limit_of(res_ref)
    lane = lax.broadcasted_iota(jnp.int32, (32, CANVAS), 1)
    rem = lane % 8
    row = lax.broadcasted_iota(jnp.int32, (SIDE, CANVAS), 0)
    col = lax.broadcasted_iota(jnp.int32, (SIDE, CANVAS), 1)
    wanted = jnp.where(row < HALF, 2 * row, 2 * (row - HALF) + 1)
    pick = jnp.where(col // 8 == wanted, 1.0, 0.0).astype(BF16)
    sub = lax.broadcasted_iota(jnp.int32, (8, CANVAS), 0)
    tap = lax.broadcasted_iota(jnp.int32, (2 * HALF, TAPS), 1)
    ones_at = (tap % 64 == 27) & (tap < 256)

    def step(i, _):
        bands = [[], [], [], []]
        above = []
        for c in range(3):
            before = img_ref[0, c, pl.ds(pl.multiple_of(jnp.maximum(32 * i - 16, 0), 16), 16), :]
            above.append(jnp.where(i > 0, before.astype(F32)[8:16], 0.0))
            for q in range(2):
                band = img_ref[0, c, pl.ds(pl.multiple_of(32 * i + 16 * q, 16), 16), :].astype(F32)
                bands[2 * q].append(band[0:8])
                bands[2 * q + 1].append(band[8:16])
        made = []
        for q in range(4):
            prev = above if q == 0 else bands[q - 1]
            edge = jnp.zeros((8, CANVAS), F32)
            for c in range(3):
                edge = jnp.where(sub == c, prev[c][7:8], edge)
            rows = jnp.concatenate(bands[q] + [edge], axis=0)
            rolled = pltpu.roll(rows, 8, 1)
            pieces = [jnp.where((rem == 7) & (lane >= 8), rolled, 0.0)]
            pieces += [jnp.where(rem == r, rows, 0.0) for r in range(8)]
            wide = jnp.concatenate(pieces, axis=0).astype(BF16)
            made.append(dot(pick, wide, NT))
        for py in range(2):
            for px in range(2):
                group = 2 * py + px
                two = jnp.concatenate(
                    [made[py][HALF * px : HALF * px + HALF], made[2 + py][HALF * px : HALF * px + HALF]],
                    axis=0,
                )
                inside = group_mask(group, limit, 2 * HALF * i, 2 * HALF, TAPS)
                two = jnp.where(ones_at, 1.0, two) * inside
                patch_ref[pl.ds(pl.multiple_of(group * QUAD + 2 * HALF * i, 16), 2 * HALF), :] = (
                    two.astype(BF16)
                )
        return 0

    lax.fori_loop(0, HALF // 2, step, 0)
    patches = patch_ref[...]
    gram = dot(patches, patches, TN)
    total = gram[0:96, 0:96]
    for px in range(1, 4):
        total = total + gram[64 * px : 64 * px + 96, 64 * px : 64 * px + 96]
    gram_ref[...] = jnp.concatenate([total, jnp.zeros((96, 32), F32)], axis=1)


def make_patches(res_ids, images):
    return pl.pallas_call(
        patch_kernel,
        out_shape=(
            jax.ShapeDtypeStruct((PLACES, TAPS), BF16),
            jax.ShapeDtypeStruct((96, 128), F32),
        ),
        in_specs=[SMEM_SPEC, VMEM_SPEC],
        out_specs=(VMEM_SPEC, VMEM_SPEC),
        compiler_params=params_of(),
        cost_estimate=pl.CostEstimate(flops=2 * 10**9, bytes_accessed=4 * 10**6, transcendentals=0),
        name="patches",
    )(res_ids, images)


def spread_taps():
    table = np.zeros((8, TAPS, 64), np.float32)
    for px in range(4):
        for py in range(4):
            pair, half = px * 2 + py // 2, py % 2
            for dy in range(3):
                for dx in range(3):
                    for c in range(3):
                        ry = 2 * py + dy - 1
                        r = 24 + c if ry < 0 else 8 * c + ry
                        k = (2 * px + dx) * 32 + r
                        table[pair, k, half * 32 + (dy * 3 + dx) * 3 + c] = 1.0
    return table


def spread_weights(spread_ref, stem_w, out_ref, pairs=8):
    zero = jnp.zeros((32, STEM_CH), F32)
    double = jnp.concatenate(
        [jnp.concatenate([stem_w, zero], axis=1), jnp.concatenate([zero, stem_w], axis=1)], axis=0
    ).astype(BF16)
    for pair in range(pairs):
        out_ref[:, 128 * pair : 128 * pair + 128] = dot(spread_ref[pair], double).astype(BF16)


def stem_stats(gram, first_phases):
    weights = first_phases.astype(F32)
    product = dot(gram[:, :96], weights, precision=HIGH)
    second = jnp.sum(weights * product, axis=0, keepdims=True)
    first = product[27:28]
    count = 4.0 * gram[27:28, 27:28]
    both = jnp.concatenate([first, second, jnp.zeros((6, 256), F32)], axis=0)
    folded = both[:, 0:64] + both[:, 64:128] + both[:, 128:192] + both[:, 192:256]
    return folded[0:1] / count, folded[1:2] / count


def stem_kernel(patch_ref, gram_ref, stem_w_ref, norm_ref, spread_ref, base_ref, slope_ref, bgram_ref, big):
    spread_weights(spread_ref, stem_w_ref[...], big)
    mean, square = stem_stats(gram_ref[...], big[0:96, 0:256])
    inverse = lax.rsqrt(square - mean * mean + EPS)
    gain = norm_ref[0:1] * inverse
    shift = norm_ref[1:2] - mean * gain
    gain = jnp.concatenate([gain] * 4, axis=1)
    shift = jnp.concatenate([shift] * 4, axis=1)
    rows = 256
    lane = lax.broadcasted_iota(jnp.int32, (rows, 128), 1)

    def step(i, _):
        at = pl.ds(pl.multiple_of(i * rows, rows), rows)
        block = patch_ref[at, :]
        pooled = jnp.zeros((rows, 128), F32)
        for j in range(4):
            u = dot(block, big[:, 256 * j : 256 * j + 256]) * gain + shift
            value, slope = gelu_pair(u)
            slope_ref[at, 256 * j : 256 * j + 256] = slope.astype(BF16)
            pooled = pooled + value[:, 0:128] + value[:, 128:256]
        pooled = (pooled + pltpu.roll(pooled, 64, 1)) * (1.0 / 16.0)
        ones = block[:, 0:128].astype(F32)
        ones = pltpu.roll(ones, 64 - 27, 1)
        pooled = jnp.where(lane < 64, pooled, jnp.where(lane == 64, ones, 0.0))
        base_ref[at, :] = pooled.astype(BF16)
        return 0

    lax.fori_loop(0, PLACES // rows, step, 0)
    base = base_ref[...]
    masked = (base.astype(F32) * base[:, 64:65].astype(F32)).astype(BF16)
    bgram_ref[...] = dot(masked, base, TN)[0:72]


def stem_forward(patches, gram, stem_w, norm, spread):
    return pl.pallas_call(
        stem_kernel,
        out_shape=(
            jax.ShapeDtypeStruct((PLACES, 128), BF16),
            jax.ShapeDtypeStruct((PLACES, 1024), BF16),
            jax.ShapeDtypeStruct((72, 128), F32),
        ),
        in_specs=[VMEM_SPEC] * 5,
        out_specs=(VMEM_SPEC,) * 3,
        scratch_shapes=[pltpu.VMEM((TAPS, 1024), BF16)],
        compiler_params=params_of(),
        cost_estimate=pl.CostEstimate(flops=3 * 10**9, bytes_accessed=8 * 10**6, transcendentals=2 * 10**6),
        name="stem_forward",
    )(patches, gram, stem_w, norm, spread)


def taps_row(load, weight, py):
    sources = [(1, -1), (0, 0), (1, 0)] if py == 0 else [(0, 0), (1, 0), (0, 1)]
    rows = [[load(2 * gy + px, off) for px in range(2)] for gy, off in sources]

    def column(px, dx):
        total = rows[0][px] * weight(0, dx)
        total = total + rows[1][px] * weight(1, dx)
        return total + rows[2][px] * weight(2, dx)

    even = column(0, 1) + column(1, 2) + shift_down(column(1, 0))
    odd = column(1, 1) + column(0, 0) + shift_up(column(0, 2))
    return even, odd


def shift_down(v):
    at = lax.broadcasted_iota(jnp.int32, v.shape, 0)
    return jnp.where(at == 0, 0.0, pltpu.roll(v, 1, 0))


def shift_up(v):
    at = lax.broadcasted_iota(jnp.int32, v.shape, 0)
    return jnp.where(at == HALF - 1, 0.0, pltpu.roll(v, HALF - 1, 0))


def bn_stats(bgram, expand_w, count):
    weights = expand_w.astype(F32)
    square_of = jnp.concatenate([bgram, jnp.zeros((56, 128), F32)], axis=0)
    product = dot(square_of, weights, precision=HIGH)
    mean = product[64:65] / count
    second = jnp.sum(weights * product, axis=0, keepdims=True) / count
    return mean, lax.rsqrt(second - mean * mean + EPS)


def depth_kernel(res_ref, base_ref, expand_ref, bgram_ref, norm_ref, depth_ref, out_ref, h_ref, hx_ref, act_ref, slope_ref, stat_ref, pad_a, pad_b, pad_c):
    limit = limit_of(res_ref)
    count = bgram_ref[64:65, 64:65]
    mean, inverse = bn_stats(bgram_ref[...], expand_ref[...], count)
    zero = jnp.zeros((4, 1, HALF, BLOCK), F32)
    for pad in (pad_a, pad_b, pad_c):
        pad[:, 0:1] = zero
        pad[:, HALF + 1 : HALF + 2] = zero
    rows = 2 * HALF
    for group in range(4):

        def fill(i, _, group=group):
            first = pl.multiple_of(group * QUAD + rows * i, 16)
            at = pl.ds(first, rows)
            x = dot(base_ref[at, :], expand_ref[...])
            hat = (x - mean) * inverse
            inside = group_mask(group, limit, rows * i, rows, BLOCK)
            value, slope = gelu_pair(hat * norm_ref[0:1] + norm_ref[1:2])
            value = value * inside
            slope = slope * inside
            act_ref[at, :] = value.astype(BF16)
            slope_ref[at, :] = slope.astype(BF16)
            hat = hat * slope
            for half in range(2):
                cut = slice(HALF * half, HALF * half + HALF)
                pad_a[group, 2 * i + half + 1] = value[cut]
                pad_b[group, 2 * i + half + 1] = slope[cut]
                pad_c[group, 2 * i + half + 1] = hat[cut]
            return 0

        lax.fori_loop(0, HALF // 2, fill, 0)

    def weight(dy, dx):
        return depth_ref[3 * dy + dx : 3 * dy + dx + 1]

    def fold(v):
        return v[0:8] + v[8:16] + v[16:24]

    def step(up, sums):
        sums = list(sums)
        for py in range(2):
            made = []
            for pad in (pad_a, pad_b, pad_c):
                made.append(taps_row(lambda g, off, pad=pad: pad[g, up + 1 + off], weight, py))
            for px in range(2):
                group = 2 * py + px
                inside = group_mask(group, limit, HALF * up, HALF, BLOCK)
                x, h, hx = (m[px] for m in made)
                x = x * inside
                at = pl.ds(pl.multiple_of(group * QUAD + HALF * up, 8), HALF)
                out_ref[at, :] = x
                h_ref[at, :] = h
                hx_ref[at, :] = hx
                for k, term in enumerate((x, x * x, h * inside, h * x, hx * inside, hx * x)):
                    sums[k] = sums[k] + fold(term)
        return tuple(sums)

    sums = lax.fori_loop(0, HALF, step, (jnp.zeros((8, BLOCK), F32),) * 6)
    rows_out = [jnp.sum(s, axis=0, keepdims=True) for s in sums]
    stat_ref[...] = jnp.concatenate(rows_out + [jnp.zeros((2, BLOCK), F32)], axis=0)


def depth_forward(res_ids, base, expand_w, bgram, mid_norm, mb_depth):
    col = lambda rows: pl.BlockSpec((rows, BLOCK), lambda j: (0, j))
    whole = lambda rows: pl.BlockSpec((rows, BLOCK), lambda j: (0, 0))
    pad = pltpu.VMEM((4, HALF + 2, HALF, BLOCK), F32)
    return pl.pallas_call(
        depth_kernel,
        grid=(CHUNKS,),
        out_shape=(
            jax.ShapeDtypeStruct((PLACES, EXPAND), F32),
            jax.ShapeDtypeStruct((PLACES, EXPAND), F32),
            jax.ShapeDtypeStruct((PLACES, EXPAND), F32),
            jax.ShapeDtypeStruct((PLACES, EXPAND), BF16),
            jax.ShapeDtypeStruct((PLACES, EXPAND), BF16),
            jax.ShapeDtypeStruct((8, EXPAND), F32),
        ),
        in_specs=[SMEM_SPEC, whole(PLACES), col(128), whole(72), col(2), col(9)],
        out_specs=(col(PLACES),) * 5 + (col(8),),
        scratch_shapes=[pad, pad, pad],
        compiler_params=params_of(),
        cost_estimate=pl.CostEstimate(flops=3 * 10**8, bytes_accessed=30 * 10**6, transcendentals=2 * 10**6),
        name="depth_forward",
    )(res_ids, base, expand_w, bgram, mid_norm, mb_depth)


SPAN = 2 * HALF - 1
WIDE = 2 * HALF * HALF
TOKENS = QUAD


def squeeze_lanes():
    table = np.zeros((16 * 48, 16 * 24), np.float32)
    for e in range(16):
        for x in range(24):
            table[e * 48 + x, e * 24 + x] = 1.0
    return table


def slots_of(rel_index):
    last = TOKENS - 1
    corner = lambda i: rel_index[i].reshape(HALF, HALF)
    low_row = jnp.concatenate([corner(last), corner(last - HALF + 1)[:, 1:]], axis=1)
    high_row = jnp.concatenate([corner(HALF - 1), corner(0)[:, 1:]], axis=1)
    return jnp.concatenate([low_row, high_row[1:]], axis=0)


def bias_kernel(f_ref, pick_ref, out_ref):
    f = f_ref[...]
    for x in range(HALF):
        turned = pltpu.roll(f, (WIDE * 2 - (HALF - 1 - x)) % (WIDE * 2), 1) if x != HALF - 1 else f
        turned = turned.astype(BF16)
        for part in range(3):
            piece = dot(turned[:, 768 * part : 768 * part + 768], pick_ref[...])
            for head in range(HEADS):
                out_ref[head, x : x + 1, 384 * part : 384 * part + 384] = piece[head : head + 1]


def build_bias(f, pick):
    return pl.pallas_call(
        bias_kernel,
        out_shape=jax.ShapeDtypeStruct((HEADS, HALF, WIDE), F32),
        in_specs=[VMEM_SPEC] * 2,
        out_specs=VMEM_SPEC,
        compiler_params=params_of(),
        cost_estimate=pl.CostEstimate(flops=10**8, bytes_accessed=2 * 10**6, transcendentals=0),
        name="bias_build",
    )(f, pick)


def bias_back_kernel(grad_ref, pick_ref, out_ref):
    total = jnp.zeros((16, 2 * WIDE), F32)
    for x in range(HALF):
        rows = jnp.concatenate(
            [grad_ref[head, x : x + 1, :] for head in range(HEADS)] + [jnp.zeros((4, WIDE), F32)], axis=0
        )
        high = rows.astype(BF16)
        rest = (rows - high.astype(F32)).astype(BF16)
        wide = jnp.concatenate(
            [
                dot(high[:, 384 * part : 384 * part + 384], pick_ref[...], NT)
                + dot(rest[:, 384 * part : 384 * part + 384], pick_ref[...], NT)
                for part in range(3)
            ],
            axis=1,
        )
        total = total + (pltpu.roll(wide, HALF - 1 - x, 1) if x != HALF - 1 else wide)
    out_ref[...] = total


def bias_back(grad, pick):
    return pl.pallas_call(
        bias_back_kernel,
        out_shape=jax.ShapeDtypeStruct((16, 2 * WIDE), F32),
        in_specs=[VMEM_SPEC] * 2,
        out_specs=VMEM_SPEC,
        compiler_params=params_of(),
        cost_estimate=pl.CostEstimate(flops=10**8, bytes_accessed=2 * 10**6, transcendentals=0),
        name="bias_back",
    )(grad, pick)


def sigmoid(v):
    return 1.0 / (1.0 + jnp.exp(-v))


def row8(rows):
    width = rows[0].shape[1]
    return jnp.concatenate(rows + [jnp.zeros((8 - len(rows), width), F32)], axis=0)


def dw_stats(stat, count):
    mean = stat[0:1] / count
    return mean, lax.rsqrt(stat[1:2] / count - mean * mean + EPS)


def valid_places(limit):
    return (limit * limit).astype(F32)


def excite_kernel(
    res_ref, depth_ref, stat_ref, bgram_ref, norm_ref, down_ref, down_b_ref, up_ref, up_b_ref,
    proj_ref, base_ref, short_ref, pre_ref, qkv_ref,
    act_ref, slope_ref, block_ref, skip_ref, normed_ref, project_ref, vec_ref, small_ref, held,
):
    limit = limit_of(res_ref)
    count = bgram_ref[64:65, 64:65]
    mean, inverse = dw_stats(stat_ref[...], count)
    gain = norm_ref[0:1] * inverse
    shift = norm_ref[1:2] - mean * gain
    rows = 2 * HALF
    total = jnp.zeros((8, EXPAND), F32)
    for group in range(4):

        def fill(i, total, group=group):
            at = pl.ds(pl.multiple_of(group * QUAD + rows * i, 16), rows)
            value, slope = gelu_pair(depth_ref[at, :] * gain + shift)
            inside = group_mask(group, limit, rows * i, rows, BLOCK)
            inside = jnp.concatenate([inside] * CHUNKS, axis=1)
            value = value * inside
            held[at, :] = value
            act_ref[at, :] = value.astype(BF16)
            slope_ref[at, :] = (slope * inside).astype(BF16)
            for k in range(rows // 8):
                total = total + value[8 * k : 8 * k + 8]
            return total

        total = lax.fori_loop(0, QUAD // rows, fill, total)
    pooled = jnp.sum(total, axis=0, keepdims=True) / valid_places(limit)
    before = dot(row8([pooled]), down_ref[...].astype(F32), precision=HIGH)[0:1] + down_b_ref[...]
    gate = sigmoid(before)
    squeeze = before * gate
    excite = sigmoid(
        dot(row8([squeeze]), up_ref[...].astype(F32), precision=HIGH)[0:1] + up_b_ref[...]
    )
    vec_ref[...] = row8([pooled, excite, mean, inverse])
    small_ref[...] = row8([squeeze, gate * (1.0 + before * (1.0 - gate))])

    big = 192
    def section(i, _):
        at = pl.ds(pl.multiple_of(big * i, 16), big)
        scaled = (held[at, :] * excite).astype(BF16)
        block_ref[at, :] = dot(scaled, proj_ref[...]) + dot(base_ref[at, :], short_ref[...])
        return 0

    lax.fori_loop(0, PLACES // big, section, 0)
    part = 96

    def tokens(i, _):
        skipped = jnp.zeros((part, MB_CH), F32)
        normed = jnp.zeros((part, MB_CH), F32)
        for group in range(4):
            block = block_ref[pl.ds(pl.multiple_of(group * QUAD + part * i, 16), part), :]
            skipped = skipped + block
            hat, _ = normalise(block)
            normed = normed + hat
        at = pl.ds(pl.multiple_of(part * i, 16), part)
        skip_ref[at, :] = (0.25 * skipped).astype(BF16)
        low = (0.25 * normed * pre_ref[0:1] + pre_ref[1:2]).astype(BF16)
        normed_ref[at, :] = low
        project_ref[at, :] = dot(low, qkv_ref[...]).astype(BF16)
        return 0

    lax.fori_loop(0, TOKENS // part, tokens, 0)


def normalise(v):
    centered = v - jnp.mean(v, axis=-1, keepdims=True)
    inverse = lax.rsqrt(jnp.mean(centered * centered, axis=-1, keepdims=True) + EPS)
    return centered * inverse, inverse


def normalise_back(grad_hat, hat, inverse):
    first = jnp.mean(grad_hat, axis=-1, keepdims=True)
    second = jnp.mean(grad_hat * hat, axis=-1, keepdims=True)
    return inverse * (grad_hat - first - hat * second)


def excite_forward(res_ids, depth, stat, bgram, base, p):
    return pl.pallas_call(
        excite_kernel,
        out_shape=(
            jax.ShapeDtypeStruct((PLACES, EXPAND), BF16),
            jax.ShapeDtypeStruct((PLACES, EXPAND), BF16),
            jax.ShapeDtypeStruct((PLACES, MB_CH), F32),
            jax.ShapeDtypeStruct((TOKENS, MB_CH), BF16),
            jax.ShapeDtypeStruct((TOKENS, MB_CH), BF16),
            jax.ShapeDtypeStruct((TOKENS, 3 * DIM), BF16),
            jax.ShapeDtypeStruct((8, EXPAND), F32),
            jax.ShapeDtypeStruct((8, SQUEEZE), F32),
        ),
        in_specs=[SMEM_SPEC] + [VMEM_SPEC] * 13,
        out_specs=(VMEM_SPEC,) * 8,
        scratch_shapes=[pltpu.VMEM((PLACES, EXPAND), F32)],
        compiler_params=params_of(),
        cost_estimate=pl.CostEstimate(flops=10**9, bytes_accessed=18 * 10**6, transcendentals=2 * 10**6),
        name="excite_forward",
    )(
        res_ids, depth, stat, bgram, p["dw_norm"], p["se_down"], p["se_down_bias"], p["se_up"], p["se_up_bias"],
        p["mb_proj"], base, p["mb_short"], p["pre_norm"], p["qkv"],
    )


SCALE = HEAD_DIM ** (-0.5)
PER = BLOCK // HEAD_DIM
ATT_ROWS = 2 * HALF


def token_valid(limit, shape, axis):
    at = lax.broadcasted_iota(jnp.int32, shape, axis)
    y = at // HALF
    x = at - y * HALF
    return (2 * y < limit) & (2 * x < limit)


def head_lanes(h):
    lane = lax.broadcasted_iota(jnp.int32, (TOKENS, BLOCK), 1)
    return lane // HEAD_DIM == h


def attend_kernel(res_ref, q_ref, k_ref, v_ref, bias_ref, out_ref, p_ref, scores):
    limit = limit_of(res_ref)
    usable = token_valid(limit, (1, TOKENS), 1)

    def head(h, total):
        mine = head_lanes(h)
        q = jnp.where(mine, q_ref[...], jnp.zeros((), BF16))
        scores[...] = dot(q, k_ref[...], NT)
        bias = bias_ref[h]

        def rows(i, _):
            at = pl.ds(pl.multiple_of(ATT_ROWS * i, 16), ATT_ROWS)
            shifted = [
                pltpu.roll(bias, lax.rem(WIDE - (HALF - 1 - (2 * i + k)) * HALF, WIDE), 1)[:, :TOKENS]
                for k in range(2)
            ]
            s = scores[at, :] * SCALE + jnp.concatenate(shifted, axis=0)
            s = jnp.where(usable, s, -1e30)
            e = jnp.exp(s - jnp.max(s, axis=-1, keepdims=True))
            weights = e * (1.0 / jnp.sum(e, axis=-1, keepdims=True))
            p_ref[h, at, :] = weights.astype(BF16)
            return 0

        lax.fori_loop(0, TOKENS // ATT_ROWS, rows, 0)
        return jnp.where(mine, dot(p_ref[h], v_ref[...]), total)

    total = lax.fori_loop(0, PER, head, jnp.zeros((TOKENS, BLOCK), F32))
    out_ref[...] = total.astype(BF16)


def attend_forward(res_ids, project, bias):
    part = lambda k: pl.BlockSpec((TOKENS, BLOCK), lambda j: (0, 3 * k + j))
    return pl.pallas_call(
        attend_kernel,
        grid=(HEADS // PER,),
        out_shape=(
            jax.ShapeDtypeStruct((TOKENS, DIM), BF16),
            jax.ShapeDtypeStruct((HEADS, TOKENS, TOKENS), BF16),
        ),
        in_specs=[SMEM_SPEC, part(0), part(1), part(2), pl.BlockSpec((PER, HALF, WIDE), lambda j: (j, 0, 0))],
        out_specs=(
            pl.BlockSpec((TOKENS, BLOCK), lambda j: (0, j)),
            pl.BlockSpec((PER, TOKENS, TOKENS), lambda j: (j, 0, 0)),
        ),
        scratch_shapes=[pltpu.VMEM((TOKENS, TOKENS), F32)],
        compiler_params=params_of(),
        cost_estimate=pl.CostEstimate(flops=3 * 10**9, bytes_accessed=11 * 10**6, transcendentals=4 * 10**6),
        name="attend_forward",
    )(res_ids, project, project, project, bias)


def attend_back_kernel(q_ref, k_ref, v_ref, o_ref, do_ref, p_ref, dq_ref, dk_ref, dv_ref, dbias_ref, scores, low):
    def head(h, carry):
        dq, dk, dv = carry
        mine = head_lanes(h)
        grad = jnp.where(mine, do_ref[...], jnp.zeros((), BF16))
        scores[...] = dot(grad, v_ref[...], NT)
        dbias_ref[h] = jnp.zeros((HALF, WIDE), F32)

        def rows(i, _):
            at = pl.ds(pl.multiple_of(ATT_ROWS * i, 16), ATT_ROWS)
            lane = lax.broadcasted_iota(jnp.int32, (ATT_ROWS, BLOCK), 1)
            both = do_ref[at, :].astype(F32) * o_ref[at, :].astype(F32)
            both = jnp.where(lane // HEAD_DIM == h, both, 0.0)
            delta = jnp.sum(both, axis=-1, keepdims=True)
            ds = p_ref[h, at, :].astype(F32) * (scores[at, :] - delta)
            low[at, :] = (ds * SCALE).astype(BF16)
            wide = jnp.concatenate([ds, jnp.zeros((ATT_ROWS, WIDE - TOKENS), F32)], axis=1)
            total = dbias_ref[h]
            for k in range(2):
                total = total + pltpu.roll(
                    wide[HALF * k : HALF * k + HALF], (HALF - 1 - (2 * i + k)) * HALF, 1
                )
            dbias_ref[h] = total
            return 0

        lax.fori_loop(0, TOKENS // ATT_ROWS, rows, 0)
        dq = jnp.where(mine, dot(low[...], k_ref[...]), dq)
        dk = jnp.where(mine, dot(low[...], q_ref[...], TN), dk)
        dv = jnp.where(mine, dot(p_ref[h], do_ref[...], TN), dv)
        return dq, dk, dv

    zero = jnp.zeros((TOKENS, BLOCK), F32)
    dq, dk, dv = lax.fori_loop(0, PER, head, (zero, zero, zero))
    dq_ref[...] = dq.astype(BF16)
    dk_ref[...] = dk.astype(BF16)
    dv_ref[...] = dv.astype(BF16)


def attend_backward(project, blended, grad, weights):
    part = lambda k: pl.BlockSpec((TOKENS, BLOCK), lambda j: (0, 3 * k + j))
    return pl.pallas_call(
        attend_back_kernel,
        grid=(HEADS // PER,),
        out_shape=(jax.ShapeDtypeStruct((TOKENS, DIM), BF16),) * 3
        + (jax.ShapeDtypeStruct((HEADS, HALF, WIDE), F32),),
        in_specs=[
            part(0), part(1), part(2), part(0), part(0),
            pl.BlockSpec((PER, TOKENS, TOKENS), lambda j: (j, 0, 0)),
        ],
        out_specs=(part(0), part(0), part(0), pl.BlockSpec((PER, HALF, WIDE), lambda j: (j, 0, 0))),
        scratch_shapes=[pltpu.VMEM((TOKENS, TOKENS), F32), pltpu.VMEM((TOKENS, TOKENS), BF16)],
        compiler_params=params_of(),
        cost_estimate=pl.CostEstimate(flops=6 * 10**9, bytes_accessed=13 * 10**6, transcendentals=0),
        name="attend_backward",
    )(project, project, project, blended, grad, weights)


MLP_ROWS = 96


def mlp_kernel(
    share, res_ref, label_ref, skip_ref, blend_ref, short_ref, out_ref, out_b_ref, norm_ref, in_ref, in_b_ref,
    back_ref, back_b_ref, hnorm_ref, head_ref, head_b_ref,
    loss_ref, dblend_ref, dskip_ref, dshort_ref, dout_ref, dout_b_ref, dnorm_ref, din_ref, din_b_ref,
    dback_ref, dback_b_ref, dhnorm_ref, dhead_ref, dhead_b_ref,
    section, low, slopes, dpres, grads,
):
    limit = limit_of(res_ref)
    n_valid = (limit // 2 * (limit // 2)).astype(F32)
    steps = TOKENS // MLP_ROWS
    cut = 384

    def valid_rows(i):
        at = lax.broadcasted_iota(jnp.int32, (MLP_ROWS, 1), 0) + MLP_ROWS * i
        y = at // HALF
        x = at - y * HALF
        return jnp.where((2 * y < limit) & (2 * x < limit), 1.0, 0.0)

    def forward(i, carry):
        feature, used = carry
        at = pl.ds(pl.multiple_of(MLP_ROWS * i, 16), MLP_ROWS)
        first = dot(skip_ref[at, :], short_ref[...]) + dot(blend_ref[at, :], out_ref[...]) + out_b_ref[...]
        section[at, :] = first
        hat, _ = normalise(first)
        normed = (hat * norm_ref[0:1] + norm_ref[1:2]).astype(BF16)
        low[at, :] = normed
        inside = valid_rows(i)
        second = first + back_b_ref[...]
        parts = []
        for j in range(MLP // cut):
            cols = slice(cut * j, cut * j + cut)
            value, slope = gelu_pair(dot(normed, in_ref[:, cols]) + in_b_ref[:, cols])
            slopes[at, cols] = slope * inside
            value = value.astype(BF16)
            parts.append(jnp.sum(value.astype(F32) * inside, axis=0, keepdims=True))
            second = second + dot(value, back_ref[cols, :])
        feature = feature + jnp.sum(second * inside, axis=0, keepdims=True)
        return feature, used + jnp.concatenate(parts, axis=1)

    feature, used = lax.fori_loop(
        0, steps, forward, (jnp.zeros((1, DIM), F32), jnp.zeros((1, MLP), F32))
    )
    feature = feature / n_valid
    hat, inverse = normalise(feature)
    normed = (hat * hnorm_ref[0:1] + hnorm_ref[1:2]).astype(BF16)
    normed8 = jnp.concatenate([normed.astype(F32), jnp.zeros((15, DIM), F32)], axis=0).astype(BF16)
    logits = dot(normed8, head_ref[...])[0:1] + head_b_ref[...]
    peak = jnp.max(logits, axis=-1, keepdims=True)
    exps = jnp.exp(logits - peak)
    total = jnp.sum(exps, axis=-1, keepdims=True)
    log_probs = logits - peak - jnp.log(total)
    at_class = lax.broadcasted_iota(jnp.int32, (1, CLASSES), 1)
    goal = jnp.where(at_class == label_ref[0], 1.0 - SMOOTH, 0.0) + SMOOTH / CLASSES
    loss = -jnp.sum(goal * log_probs, axis=-1, keepdims=True)
    loss_ref[...] = jnp.broadcast_to(loss, (8, 128))
    grad = (exps / total - goal) * share
    dhead_b_ref[...] = grad
    grad16 = jnp.concatenate([grad, jnp.zeros((15, CLASSES), F32)], axis=0).astype(BF16)
    dhead_ref[...] = dot(normed8, grad16, TN)
    grad = dot(grad16, head_ref[...], NT)[0:1]
    dhnorm_ref[...] = jnp.concatenate([grad * hat, grad], axis=0)
    grad = normalise_back(grad * hnorm_ref[0:1], hat, inverse) / n_valid
    low_grad = jnp.concatenate([grad, jnp.zeros((15, DIM), F32)], axis=0).astype(BF16)
    used16 = jnp.concatenate([used, jnp.zeros((7, MLP), F32)], axis=0)
    dback_ref[...] = dot(used16, low_grad[0:16].astype(F32)[0:8], TN, precision=HIGH)
    dback_b_ref[...] = grad * n_valid
    dhidden = dot(low_grad, back_ref[...], NT)[0:1]

    def backward(i, carry):
        dnorm0, dnorm1, dbias, dout_b = carry
        at = pl.ds(pl.multiple_of(MLP_ROWS * i, 16), MLP_ROWS)
        dnormed = jnp.zeros((MLP_ROWS, DIM), F32)
        parts = []
        for j in range(MLP // cut):
            cols = slice(cut * j, cut * j + cut)
            dpre = slopes[at, cols] * dhidden[:, cols]
            parts.append(jnp.sum(dpre, axis=0, keepdims=True))
            dpre = dpre.astype(BF16)
            dpres[at, cols] = dpre
            dnormed = dnormed + dot(dpre, in_ref[:, cols], NT)
        hat, inverse = normalise(section[at, :])
        dnorm0 = dnorm0 + jnp.sum(dnormed * hat, axis=0, keepdims=True)
        dnorm1 = dnorm1 + jnp.sum(dnormed, axis=0, keepdims=True)
        dsection = normalise_back(dnormed * norm_ref[0:1], hat, inverse) + valid_rows(i) * grad
        grads[at, :] = dsection.astype(BF16)
        dout_b = dout_b + jnp.sum(dsection, axis=0, keepdims=True)
        dblend_ref[at, :] = dot(grads[at, :], out_ref[...], NT).astype(BF16)
        dskip_ref[at, :] = dot(grads[at, :], short_ref[...], NT)
        return dnorm0, dnorm1, dbias + jnp.concatenate(parts, axis=1), dout_b

    row = jnp.zeros((1, DIM), F32)
    dnorm0, dnorm1, dbias, dout_b = lax.fori_loop(0, steps, backward, (row, row, jnp.zeros((1, MLP), F32), row))
    dnorm_ref[...] = jnp.concatenate([dnorm0, dnorm1], axis=0)
    din_b_ref[...] = dbias
    dout_b_ref[...] = dout_b
    din_ref[...] = dot(low[...], dpres[...], TN)
    dout_ref[...] = dot(blend_ref[...], grads[...], TN)
    dshort_ref[...] = dot(skip_ref[...], grads[...], TN)


def mlp_both(share, res_ids, labels, skipped, blended, p):
    s = jax.ShapeDtypeStruct
    return pl.pallas_call(
        functools.partial(mlp_kernel, share),
        out_shape=(
            s((8, 128), F32), s((TOKENS, DIM), BF16), s((TOKENS, MB_CH), F32), s((MB_CH, DIM), F32),
            s((DIM, DIM), F32), s((1, DIM), F32), s((2, DIM), F32), s((DIM, MLP), F32), s((1, MLP), F32),
            s((MLP, DIM), F32), s((1, DIM), F32), s((2, DIM), F32), s((DIM, CLASSES), F32), s((1, CLASSES), F32),
        ),
        in_specs=[SMEM_SPEC] * 2 + [VMEM_SPEC] * 13,
        out_specs=(VMEM_SPEC,) * 14,
        scratch_shapes=[
            pltpu.VMEM((TOKENS, DIM), F32),
            pltpu.VMEM((TOKENS, DIM), BF16),
            pltpu.VMEM((TOKENS, MLP), F32),
            pltpu.VMEM((TOKENS, MLP), BF16),
            pltpu.VMEM((TOKENS, DIM), BF16),
        ],
        compiler_params=params_of(),
        cost_estimate=pl.CostEstimate(flops=5 * 10**9, bytes_accessed=14 * 10**6, transcendentals=10**6),
        name="mlp_both",
    )(
        res_ids, labels, skipped, blended, p["at_short"], p["attn_out"], p["out_bias"], p["mlp_norm"], p["mlp_in"],
        p["mlp_in_bias"], p["mlp_out"], p["mlp_out_bias"], p["head_norm"], p["head_w"], p["head_bias"],
    )


def proj_back_kernel(
    res_ref, dq_ref, dk_ref, dv_ref, normed_ref, qkv_ref, dskip_ref, block_ref, pre_ref, act_ref, vec_ref,
    small_ref, proj_ref, short_ref, base_ref, down_ref, up_ref,
    dqkv_ref, dpre_ref, dblock_ref, dproj_ref, dshort_ref, dbase_ref, ddown_ref, ddown_b_ref, dup_ref, dup_b_ref,
    dpool_ref,
):
    limit = limit_of(res_ref)
    part = 96

    def tokens(i, carry):
        dpre0, dpre1 = carry
        at = pl.ds(pl.multiple_of(part * i, 16), part)
        grad = dot(dq_ref[at, :], qkv_ref[:, 0:DIM], NT)
        grad = grad + dot(dk_ref[at, :], qkv_ref[:, DIM : 2 * DIM], NT)
        grad = grad + dot(dv_ref[at, :], qkv_ref[:, 2 * DIM :], NT)
        dskip = 0.25 * dskip_ref[at, :]
        dpre1 = dpre1 + jnp.sum(grad, axis=0, keepdims=True)
        grad = 0.25 * grad
        dhat = grad * pre_ref[0:1]
        for group in range(4):
            places = pl.ds(pl.multiple_of(group * QUAD + part * i, 16), part)
            hat, inverse = normalise(block_ref[places, :])
            dpre0 = dpre0 + jnp.sum(grad * hat, axis=0, keepdims=True)
            dblock = normalise_back(dhat, hat, inverse) + dskip
            dblock_ref[places, :] = dblock.astype(BF16)
        return dpre0, dpre1

    row = jnp.zeros((1, MB_CH), F32)
    dpre0, dpre1 = lax.fori_loop(0, TOKENS // part, tokens, (row, row))
    dpre_ref[...] = jnp.concatenate([dpre0, dpre1], axis=0)
    for k, grad_ref in enumerate((dq_ref, dk_ref, dv_ref)):
        dqkv_ref[:, DIM * k : DIM * k + DIM] = dot(normed_ref[...], grad_ref[...], TN)
    dshort_ref[...] = dot(base_ref[...], dblock_ref[...], TN)[0:STEM_CH]
    dbase_ref[...] = dot(dblock_ref[...], short_ref[...], NT)
    excite = vec_ref[1:2]
    parts = []
    for j in range(CHUNKS):
        cols = slice(BLOCK * j, BLOCK * j + BLOCK)
        act = act_ref[:, cols].astype(F32)
        scaled = (act * excite[:, cols]).astype(BF16)
        dproj_ref[cols, :] = dot(scaled, dblock_ref[...], TN)
        dscaled = dot(dblock_ref[...], proj_ref[cols, :], NT)
        parts.append(jnp.sum(dscaled * act, axis=0, keepdims=True))
    dexcite = jnp.concatenate(parts, axis=1)
    dafter = dexcite * excite * (1.0 - excite)
    dup_b_ref[...] = dafter
    dup_ref[...] = dot(row8([small_ref[0:1]]), row8([dafter]), TN, precision=HIGH)
    dsqueeze = dot(row8([dafter]), up_ref[...].astype(F32), NT, precision=HIGH)[0:1]
    dbefore = dsqueeze * small_ref[1:2]
    ddown_b_ref[...] = dbefore
    ddown_ref[...] = dot(row8([vec_ref[0:1]]), row8([dbefore]), TN, precision=HIGH)
    dpool = dot(row8([dbefore]), down_ref[...].astype(F32), NT, precision=HIGH)
    dpool_ref[...] = dpool / valid_places(limit)


def proj_backward(res_ids, dq, dk, dv, normed, dskip, block, act, vec, small, base, p):
    s = jax.ShapeDtypeStruct
    return pl.pallas_call(
        proj_back_kernel,
        out_shape=(
            s((MB_CH, 3 * DIM), F32), s((2, MB_CH), F32), s((PLACES, MB_CH), BF16), s((EXPAND, MB_CH), F32),
            s((STEM_CH, MB_CH), F32), s((PLACES, 128), F32), s((EXPAND, SQUEEZE), F32), s((1, SQUEEZE), F32),
            s((SQUEEZE, EXPAND), F32), s((1, EXPAND), F32), s((8, EXPAND), F32),
        ),
        in_specs=[SMEM_SPEC] + [VMEM_SPEC] * 16,
        out_specs=(VMEM_SPEC,) * 11,
        compiler_params=params_of(),
        cost_estimate=pl.CostEstimate(flops=3 * 10**9, bytes_accessed=13 * 10**6, transcendentals=0),
        name="proj_backward",
    )(
        res_ids, dq, dk, dv, normed, p["qkv"], dskip, block, p["pre_norm"], act, vec, small, p["mb_proj"],
        p["mb_short"], base, p["se_down"], p["se_up"],
    )


def excite_back_kernel(res_ref, dblock_ref, proj_ref, vec_ref, dpool_ref, slope_ref, x_ref, h_ref, hx_ref, out_ref, sum_ref):
    excite, mean, inverse = vec_ref[1:2], vec_ref[2:3], vec_ref[3:4]
    dpool = dpool_ref[0:1]
    rows = 96

    def fold(v):
        total = v[0:8]
        for k in range(1, rows // 8):
            total = total + v[8 * k : 8 * k + 8]
        return total

    def step(i, sums):
        at = pl.ds(pl.multiple_of(rows * i, 16), rows)
        grad = dot(dblock_ref[at, :], proj_ref[...], NT) * excite + dpool
        grad = grad * slope_ref[at, :].astype(F32)
        out_ref[at, :] = grad
        hat = (x_ref[at, :] - mean) * inverse
        terms = (grad, grad * hat, grad * h_ref[at, :], grad * hx_ref[at, :])
        return tuple(s + fold(t) for s, t in zip(sums, terms))

    sums = lax.fori_loop(0, PLACES // rows, step, (jnp.zeros((8, BLOCK), F32),) * 4)
    sum_ref[...] = row8([jnp.sum(s, axis=0, keepdims=True) for s in sums])


def excite_backward(res_ids, dblock, proj, vec, dpool, slope, depth, h, hx):
    col = lambda rows: pl.BlockSpec((rows, BLOCK), lambda j: (0, j))
    return pl.pallas_call(
        excite_back_kernel,
        grid=(CHUNKS,),
        out_shape=(jax.ShapeDtypeStruct((PLACES, EXPAND), F32), jax.ShapeDtypeStruct((8, EXPAND), F32)),
        in_specs=[
            SMEM_SPEC,
            pl.BlockSpec((PLACES, MB_CH), lambda j: (0, 0)),
            pl.BlockSpec((BLOCK, MB_CH), lambda j: (j, 0)),
            col(8), col(8), col(PLACES), col(PLACES), col(PLACES), col(PLACES),
        ],
        out_specs=(col(PLACES), col(8)),
        compiler_params=params_of(),
        cost_estimate=pl.CostEstimate(flops=10**9, bytes_accessed=32 * 10**6, transcendentals=0),
        name="excite_backward",
    )(res_ids, dblock, proj, vec, dpool, slope, depth, h, hx)


def depth_back_kernel(
    res_ref, du_ref, x_ref, vec_ref, sum_ref, stat_ref, bgram_ref, base_ref, expand_ref, mid_ref, dwn_ref, depth_ref,
    act_ref, slope_ref, dbase_in_ref,
    dbase_ref, dexpand_ref, ddepth_ref, norms_ref, pad, hold,
):
    limit = limit_of(res_ref)
    count = bgram_ref[64:65, 64:65]
    mean1, inverse1 = bn_stats(bgram_ref[...], expand_ref[...], count)
    mean2, inverse2 = vec_ref[2:3], vec_ref[3:4]
    p1, q2, p3, p4 = (sum_ref[k : k + 1] for k in range(4))
    mh, xh, mhx, xhx = (stat_ref[k : k + 1] for k in range(2, 6))
    c1 = p1 / count
    c2 = q2 / count
    scale2 = dwn_ref[0:1] * inverse2
    s1 = scale2 * (p3 - c1 * mh - c2 * (xh - mean2 * mh) * inverse2)
    s2 = scale2 * (p4 - c1 * mhx - c2 * (xhx - mean2 * mhx) * inverse2)
    norms_ref[...] = row8([s2, s1, q2, p1])
    zero = jnp.zeros((4, 1, HALF, BLOCK), F32)
    pad[:, 0:1] = zero
    pad[:, HALF + 1 : HALF + 2] = zero

    def fill(up, _):
        for group in range(4):
            at = pl.ds(pl.multiple_of(group * QUAD + HALF * up, 8), HALF)
            inside = group_mask(group, limit, HALF * up, HALF, BLOCK)
            hat = (x_ref[at, :] - mean2) * inverse2
            pad[group, up + 1] = scale2 * (du_ref[at, :] - inside * (c1 + hat * c2))
        return 0

    lax.fori_loop(0, HALF, fill, 0)

    def weight(dy, dx):
        return depth_ref[8 - 3 * dy - dx : 9 - 3 * dy - dx]

    def fold(v):
        return v[0:8] + v[8:16] + v[16:24]

    def step(k, sums):
        sums = list(sums)
        ups = [2 * k, 2 * k + 1]
        slopes = [None] * 4
        acts = [None] * 4
        for group in range(4):
            at = pl.ds(pl.multiple_of(group * QUAD + 2 * HALF * k, 16), 2 * HALF)
            slopes[group] = slope_ref[at, :].astype(F32)
            acts[group] = act_ref[at, :].astype(F32)
        for half, up in enumerate(ups):
            cut = slice(HALF * half, HALF * half + HALF)
            for py in range(2):
                sources = [(1, -1), (0, 0), (1, 0)] if py == 0 else [(0, 0), (1, 0), (0, 1)]
                rows = [[pad[2 * gy + px, up + 1 + off] for px in range(2)] for gy, off in sources]
                low_act, high_act = acts[2 * py][cut], acts[2 * py + 1][cut]
                even = jnp.zeros((HALF, BLOCK), F32)
                odd = jnp.zeros((HALF, BLOCK), F32)
                for t in range(3):
                    left, right = rows[t]
                    before, after = shift_down(right), shift_up(left)
                    even = even + before * weight(t, 0) + left * weight(t, 1) + right * weight(t, 2)
                    odd = odd + left * weight(t, 0) + right * weight(t, 1) + after * weight(t, 2)
                    for s, (a, b) in enumerate(((before, left), (left, right), (right, after))):
                        tap = 3 * (2 - t) + 2 - s
                        sums[tap] = sums[tap] + fold(low_act * a + high_act * b)
                for px, grad in enumerate((even, odd)):
                    hold[2 * py + px, up] = grad * slopes[2 * py + px][cut]
        return tuple(sums)

    sums = lax.fori_loop(0, HALF // 2, step, (jnp.zeros((8, BLOCK), F32),) * 9)
    ddepth_ref[...] = jnp.concatenate([jnp.sum(s, axis=0, keepdims=True) for s in sums], axis=0)
    scale1 = mid_ref[0:1] * inverse1
    d1 = s1 / count
    d2 = s2 / count

    @pl.when(pl.program_id(0) == 0)
    def _():
        dbase_ref[...] = dbase_in_ref[...]

    rows = 4 * HALF
    total = jnp.zeros((128, BLOCK), F32)
    for group in range(4):

        def finish(i, total, group=group):
            at = pl.ds(pl.multiple_of(group * QUAD + rows * i, 16), rows)
            base = base_ref[at, :]
            hat = (dot(base, expand_ref[...]) - mean1) * inverse1
            inside = group_mask(group, limit, rows * i, rows, BLOCK)
            grad = jnp.concatenate([hold[group, 4 * i + k] for k in range(4)], axis=0)
            grad = (scale1 * (grad - inside * (d1 + hat * d2))).astype(BF16)
            dbase_ref[at, :] = dbase_ref[at, :] + dot(grad, expand_ref[...], NT)
            return total + dot(base, grad, TN)

        total = lax.fori_loop(0, QUAD // rows, finish, total)
    dexpand_ref[...] = total[0:STEM_CH]


def depth_backward(res_ids, du, depth, vec, sums, stat, bgram, base, expand_w, mid_norm, dw_norm, mb_depth, act, slope, dbase):
    col = lambda rows: pl.BlockSpec((rows, BLOCK), lambda j: (0, j))
    whole = lambda rows: pl.BlockSpec((rows, BLOCK), lambda j: (0, 0))
    s = jax.ShapeDtypeStruct
    return pl.pallas_call(
        depth_back_kernel,
        grid=(CHUNKS,),
        out_shape=(
            s((PLACES, 128), F32), s((STEM_CH, EXPAND), F32), s((9, EXPAND), F32), s((8, EXPAND), F32),
        ),
        in_specs=[
            SMEM_SPEC, col(PLACES), col(PLACES), col(8), col(8), col(8), whole(72), whole(PLACES), col(128), col(2),
            col(2), col(9), col(PLACES), col(PLACES), whole(PLACES),
        ],
        out_specs=(whole(PLACES), col(STEM_CH), col(9), col(8)),
        scratch_shapes=[
            pltpu.VMEM((4, HALF + 2, HALF, BLOCK), F32),
            pltpu.VMEM((4, HALF, HALF, BLOCK), F32),
        ],
        compiler_params=params_of(),
        cost_estimate=pl.CostEstimate(flops=5 * 10**8, bytes_accessed=22 * 10**6, transcendentals=0),
        name="depth_backward",
    )(res_ids, du, depth, vec, sums, stat, bgram, base, expand_w, mid_norm, dw_norm, mb_depth, act, slope, dbase)


def stem_back_kernel(patch_ref, slope_ref, dbase_ref, spread_ref, out_ref, total):
    total[...] = jnp.zeros_like(total)
    rows = 256

    def step(i, _):
        at = pl.ds(pl.multiple_of(i * rows, rows), rows)
        grad = dbase_ref[at, 0:64] * (1.0 / 16.0)
        grad = jnp.concatenate([grad, grad], axis=1)
        grad = jnp.concatenate([grad, grad], axis=1)
        block = patch_ref[at, :]
        for j in range(4):
            cols = slice(256 * j, 256 * j + 256)
            wide = (slope_ref[at, cols].astype(F32) * grad).astype(BF16)
            total[:, cols] = total[:, cols] + dot(block, wide, TN)
        return 0

    lax.fori_loop(0, PLACES // rows, step, 0)
    merged = total[0:96, 0:256]
    for px in range(1, 4):
        merged = merged + total[64 * px : 64 * px + 96, 256 * px : 256 * px + 256]
    result = jnp.zeros((32, STEM_CH), F32)
    for pair in range(2):
        wide = dot(spread_ref[pair][0:96].astype(F32), merged[:, 128 * pair : 128 * pair + 128], TN, precision=HIGH)
        result = result + wide[0:32, 0:64] + wide[32:64, 64:128]
    ones = merged[27:28]
    ones = ones[:, 0:64] + ones[:, 64:128] + ones[:, 128:192] + ones[:, 192:256]
    at = lax.broadcasted_iota(jnp.int32, (32, STEM_CH), 0)
    out_ref[...] = jnp.where(at == 27, ones, result)


def stem_backward(patches, slope, dbase, spread):
    return pl.pallas_call(
        stem_back_kernel,
        out_shape=jax.ShapeDtypeStruct((32, STEM_CH), F32),
        in_specs=[VMEM_SPEC] * 4,
        out_specs=VMEM_SPEC,
        scratch_shapes=[pltpu.VMEM((TAPS, 1024), F32)],
        compiler_params=params_of(),
        cost_estimate=pl.CostEstimate(flops=2 * 10**9, bytes_accessed=8 * 10**6, transcendentals=0),
        name="stem_backward",
    )(patches, slope, dbase, spread)


def stem_finish_kernel(grad_ref, gram_ref, stem_w_ref, norm_ref, spread_ref, out_ref, norm_out_ref, big):
    spread_weights(spread_ref, stem_w_ref[...], big, 2)
    weights = stem_w_ref[...]
    gram = gram_ref[...][:, :96]
    mean, square = stem_stats(gram_ref[...], big[0:96, 0:256])
    inverse = lax.rsqrt(square - mean * mean + EPS)
    count = 4.0 * gram_ref[27:28, 27:28]
    product = dot(gram, big[0:96, 0:256].astype(F32), precision=HIGH)
    cross = jnp.zeros((32, STEM_CH), F32)
    plain = jnp.zeros((32, STEM_CH), F32)
    sums = jnp.broadcast_to(gram[:, 27:28], (96, 128))
    for pair in range(2):
        spread = spread_ref[pair][0:96].astype(F32)
        wide = dot(spread, product[:, 128 * pair : 128 * pair + 128], TN, precision=HIGH)
        cross = cross + wide[0:32, 0:64] + wide[32:64, 64:128]
        wide = dot(spread, sums, TN, precision=HIGH)
        plain = plain + wide[0:32, 0:64] + wide[32:64, 0:64]
    at = lax.broadcasted_iota(jnp.int32, (32, STEM_CH), 0)
    taps = at < 27
    grad = jnp.where(taps, grad_ref[...], 0.0)
    first = grad_ref[27:28]
    second = (jnp.sum(grad * weights, axis=0, keepdims=True) - mean * first) * inverse
    hat = (cross - mean * plain) * inverse
    result = norm_ref[0:1] * inverse * (grad - (plain * first + hat * second) / count)
    out_ref[...] = jnp.where(taps, result, 0.0)
    norm_out_ref[...] = jnp.concatenate([second, first], axis=0)


def stem_finish(grad, gram, stem_w, norm, spread):
    return pl.pallas_call(
        stem_finish_kernel,
        out_shape=(jax.ShapeDtypeStruct((32, STEM_CH), F32), jax.ShapeDtypeStruct((2, STEM_CH), F32)),
        in_specs=[VMEM_SPEC] * 5,
        out_specs=(VMEM_SPEC,) * 2,
        scratch_shapes=[pltpu.VMEM((TAPS, 256), BF16)],
        compiler_params=params_of(),
        cost_estimate=pl.CostEstimate(flops=10**7, bytes_accessed=10**6, transcendentals=0),
        name="stem_finish",
    )(grad, gram, stem_w, norm, spread)


def levels_of(devices):
    levels = []
    stride = 1
    while stride < devices:
        radix = 2 if stride == 1 or devices // stride == 2 else 4
        levels.append((stride, radix))
        stride *= radix
    return levels


def pairs_of(devices, mask):
    return [(i, i ^ mask) for i in range(devices)]


def exchange(v, devices, wide=True):
    if devices & (devices - 1):
        return lax.psum(v, "dp")
    levels = levels_of(devices)
    if not wide:
        levels = [(1 << k, 2) for k in range(devices.bit_length() - 1)]
    for stride, radix in levels:
        moved = [lax.ppermute(v, "dp", pairs_of(devices, stride * j)) for j in range(1, radix)]
        if radix == 2:
            v = v + moved[0]
        else:
            v = (v + moved[0]) + (moved[1] + moved[2])
    return v


def piece(flat, name, begin=0):
    offset, shape = OFFSETS[name]
    size = math.prod(shape)
    return flat[offset - begin : offset - begin + size].reshape(shape)


ROW_NAMES = ("se_down_bias", "se_up_bias", "out_bias", "mlp_in_bias", "mlp_out_bias", "head_bias")
NORM_NAMES = ("pre_norm", "mlp_norm", "head_norm")


def on_device(images, res_ids, labels, rel_index, master, first_moment, second_moment, ema_weights):
    devices = lax.axis_size("dp")
    me = lax.axis_index("dp")
    length = master.shape[0]
    total_length = length * devices
    images_total = res_ids.shape[0] * devices

    low_master = lax.optimization_barrier(master.astype(BF16))
    gathered = lax.all_gather(low_master, "dp", axis=0, tiled=True)
    early = lax.dynamic_update_slice(
        jnp.zeros((EARLY_END + length,), F32), low_master.astype(F32), (jnp.minimum(me * length, EARLY_END),)
    )[:EARLY_END]

    patches, gram = make_patches(res_ids, images)
    stem_rows = -(-STEM_END // 128)
    stem_flat = jnp.pad(early[:STEM_END], (0, stem_rows * 128 - STEM_END)).reshape(stem_rows, 128)
    packet = exchange(jnp.concatenate([gram, stem_flat], axis=0), devices)
    gram = packet[:96]
    stem_flat = packet[96:].reshape(-1)
    rest = exchange(early[STEM_END:].astype(BF16), devices, wide=False)

    spread = jnp.asarray(spread_taps(), BF16)
    stem_w = jnp.pad(piece(stem_flat, "stem_w").reshape(27, STEM_CH), ((0, 5), (0, 0)))
    stem_norm = piece(stem_flat, "stem_norm")
    base, stem_slope, bgram = stem_forward(patches, gram, stem_w, stem_norm, spread)
    bgram = exchange(bgram, devices)

    expand_w = jnp.pad(piece(rest, "mb_expand", STEM_END), ((0, 64), (0, 0)))
    mid_norm = piece(rest, "mid_norm", STEM_END).astype(F32)
    mb_depth = piece(rest, "mb_depth", STEM_END).astype(F32)
    depth, h, hx, act1, slope1, stat = depth_forward(res_ids, base, expand_w, bgram, mid_norm, mb_depth)
    stat = exchange(stat, devices)

    p = {}
    for name in ("se_down", "se_up", "mb_proj", "at_short", "qkv", "attn_out", "mlp_in", "mlp_out", "head_w"):
        p[name] = piece(gathered, name)
    for name in ROW_NAMES:
        p[name] = piece(gathered, name).astype(F32).reshape(1, -1)
    for name in NORM_NAMES:
        p[name] = piece(gathered, name).astype(F32)
    p["dw_norm"] = piece(rest, "dw_norm", STEM_END).astype(F32)
    p["mb_short"] = jnp.pad(piece(rest, "mb_short", STEM_END), ((0, 64), (0, 0)))

    slots = slots_of(rel_index).reshape(-1)
    where_from = jnp.zeros((SPAN * SPAN,), jnp.int32).at[slots].set(jnp.arange(SPAN * SPAN, dtype=jnp.int32))
    table = piece(gathered, "rel_table").astype(F32)
    ordered = jnp.take(table, slots, axis=1).reshape(HEADS, SPAN, SPAN)
    ordered = jnp.pad(ordered, ((0, 4), (0, 1), (0, 1))).reshape(16, 2 * WIDE)
    pick = jnp.asarray(squeeze_lanes(), BF16)
    bias = build_bias(ordered, pick)

    act2, slope2, block, skipped, normed, project, vec, small = excite_forward(res_ids, depth, stat, bgram, base, p)
    blended, weights = attend_forward(res_ids, project, bias)
    (
        loss, dblend, dskip, g_short, g_out, g_out_b, g_mnorm, g_in, g_in_b, g_back, g_back_b, g_hnorm, g_head, g_head_b,
    ) = mlp_both(1.0 / images_total, res_ids, labels, skipped, blended, p)
    dq, dk, dv, dbias = attend_backward(project, blended, dblend, weights)
    g_qkv, g_pre, dblock, g_proj, g_mbshort, dbase, g_down, g_down_b, g_up, g_up_b, dpool = proj_backward(
        res_ids, dq, dk, dv, normed, dskip, block, act2, vec, small, base, p
    )
    dtable = bias_back(dbias, pick)
    dtable = dtable[:HEADS].reshape(HEADS, SPAN + 1, SPAN + 1)[:, :SPAN, :SPAN].reshape(HEADS, SPAN * SPAN)
    g_table = jnp.take(dtable, where_from, axis=1)
    du, sums = excite_backward(res_ids, dblock, p["mb_proj"], vec, dpool, slope2, depth, h, hx)
    sums = exchange(sums, devices)
    dbase, g_expand, g_depth, g_norms = depth_backward(
        res_ids, du, depth, vec, sums, stat, bgram, base, expand_w, mid_norm, p["dw_norm"], mb_depth, act1, slope1, dbase
    )

    grads = {
        "mb_short": g_mbshort, "se_down": g_down, "se_down_bias": g_down_b, "se_up": g_up, "se_up_bias": g_up_b,
        "mb_proj": g_proj, "at_short": g_short, "pre_norm": g_pre, "qkv": g_qkv, "attn_out": g_out,
        "out_bias": g_out_b, "rel_table": g_table, "mlp_norm": g_mnorm, "mlp_in": g_in, "mlp_in_bias": g_in_b,
        "mlp_out": g_back, "mlp_out_bias": g_back_b, "head_norm": g_hnorm, "head_w": g_head, "head_bias": g_head_b,
    }
    flat = []
    for name, shape in layout():
        flat.append(grads[name].reshape(-1) if name in grads else jnp.zeros((math.prod(shape),), F32))
    used = sum(f.shape[0] for f in flat)
    flat.append(jnp.zeros((total_length - used,), F32))
    flat = jnp.concatenate(flat).reshape(total_length // 128, 128)
    late = lax.psum_scatter(flat, "dp", scatter_dimension=0, tiled=True).reshape(-1)

    mids = jnp.concatenate([g_expand.reshape(-1, 128), g_depth.reshape(-1, 128)], axis=0)
    mids = exchange(mids, devices, wide=False).reshape(-1)
    g_expand = mids[: STEM_CH * EXPAND]
    g_depth = mids[STEM_CH * EXPAND :]

    stem = stem_backward(patches, stem_slope, dbase, spread)
    square = jnp.sum(late * late).reshape(1, 1)
    lane = lax.broadcasted_iota(jnp.int32, (8, 128), 1)
    scalars = jnp.where(lane == 0, loss, jnp.where(lane == 1, square, 0.0))
    packet = exchange(jnp.concatenate([stem.reshape(16, 128), scalars], axis=0), devices)
    loss_sum = packet[16, 0]
    square = packet[16, 1]
    g_stem, g_stem_norm = stem_finish(packet[:16].reshape(32, STEM_CH), gram, stem_w, stem_norm, spread)
    early_grad = jnp.concatenate(
        [
            g_stem[:27].reshape(-1), g_stem_norm.reshape(-1), jnp.zeros((STEM_CH * MB_CH,), F32), g_expand,
            g_norms[0:2].reshape(-1), g_depth, g_norms[2:4].reshape(-1),
        ]
    )
    grad_norm = jnp.sqrt(square + jnp.sum(early_grad * early_grad))
    mine = lax.dynamic_slice(
        jnp.pad(early_grad, (0, length)), (jnp.minimum(me * length, EARLY_END),), (length,)
    )
    shard = late + mine
    clipped = shard * (CLIP / jnp.maximum(grad_norm, CLIP))
    moment_one = BETA_ONE * first_moment + (1.0 - BETA_ONE) * clipped
    moment_two = BETA_TWO * second_moment + (1.0 - BETA_TWO) * clipped * clipped
    update = (
        moment_one
        / (1.0 - BETA_ONE**STEP)
        / (jnp.sqrt(moment_two / (1.0 - BETA_TWO**STEP)) + ADAM_EPS)
    )
    weights_out = master - RATE * (update + DECAY * master)
    averaged = EMA_DECAY * ema_weights + (1.0 - EMA_DECAY) * weights_out
    return (
        loss_sum,
        grad_norm,
        weights_out,
        moment_one,
        moment_two,
        averaged,
        weights_out.astype(BF16),
    )


def solution(mesh):
    in_specs = (
        P("dp", None, None, None),
        P("dp"),
        P("dp"),
        P(),
        P("dp"),
        P("dp"),
        P("dp"),
        P("dp"),
    )
    out_specs = (P(), P(), P("dp"), P("dp"), P("dp"), P("dp"), P("dp"))
    return jax.shard_map(
        on_device, mesh=mesh, in_specs=in_specs, out_specs=out_specs, check_vma=False
    )
```

```python
import functools
import math

import jax
import jax.numpy as jnp
import numpy as np
from jax import lax
from jax.experimental import pallas as pl
from jax.experimental.pallas import tpu as pltpu
from jax.sharding import PartitionSpec as P

STEM_CH = 64
MB_CH = 192
EXPAND = 768
SQUEEZE = 48
DIM = 384
HEADS = 12
HEAD_DIM = 32
MLP = 1536
CLASSES = 1000
CANVAS = 384
SMALL_RES = 224
STEP = 10

EPS = 1e-05
CLIP = 0.05
BETA_ONE = 0.5
BETA_TWO = 0.5
ADAM_EPS = 1e-08
RATE = 0.05
DECAY = 0.05
EMA_DECAY = 0.9
SMOOTH = 0.1

SIDE = CANVAS // 8
SMALL_SIDE = SMALL_RES // 8
HALF = SIDE // 2
QUAD = HALF * HALF
PLACES = SIDE * SIDE
TAPS = 288
BLOCK = 128
CHUNKS = EXPAND // BLOCK
WIDE = 2 * HALF * HALF
TOKENS = QUAD

F32 = jnp.float32
BF16 = jnp.bfloat16
HIGH = lax.Precision.HIGHEST
VMEM_MAX = 56 * 1024 * 1024
GELU_A = math.sqrt(2.0 / math.pi)
GELU_B = 0.044715


def layout():
    table_slots = (2 * (CANVAS // 16) - 1) ** 2
    return [
        ("stem_w", (3, 3, 3, STEM_CH)),
        ("stem_norm", (2, STEM_CH)),
        ("mb_short", (STEM_CH, MB_CH)),
        ("mb_expand", (STEM_CH, EXPAND)),
        ("mid_norm", (2, EXPAND)),
        ("mb_depth", (9, EXPAND)),
        ("dw_norm", (2, EXPAND)),
        ("se_down", (EXPAND, SQUEEZE)),
        ("se_down_bias", (SQUEEZE,)),
        ("se_up", (SQUEEZE, EXPAND)),
        ("se_up_bias", (EXPAND,)),
        ("mb_proj", (EXPAND, MB_CH)),
        ("at_short", (MB_CH, DIM)),
        ("pre_norm", (2, MB_CH)),
        ("qkv", (MB_CH, 3 * DIM)),
        ("attn_out", (DIM, DIM)),
        ("out_bias", (DIM,)),
        ("rel_table", (HEADS, table_slots)),
        ("mlp_norm", (2, DIM)),
        ("mlp_in", (DIM, MLP)),
        ("mlp_in_bias", (MLP,)),
        ("mlp_out", (MLP, DIM)),
        ("mlp_out_bias", (DIM,)),
        ("head_norm", (2, DIM)),
        ("head_w", (DIM, CLASSES)),
        ("head_bias", (CLASSES,)),
    ]


def offsets():
    table = {}
    offset = 0
    for name, shape in layout():
        table[name] = (offset, shape)
        offset += math.prod(shape)
    return table


OFFSETS = offsets()
STEM_END = OFFSETS["mb_short"][0]
EARLY_END = OFFSETS["se_down"][0]


def dot(a, b, dims=((1,), (0,)), precision=None):
    return lax.dot_general(a, b, (dims, ((), ())), precision=precision, preferred_element_type=F32)


NT = ((1,), (1,))
TN = ((0,), (0,))


def gelu_pair(u):
    sq = u * u
    t = jnp.tanh(u * (GELU_A + (GELU_A * GELU_B) * sq))
    half = 0.5 + 0.5 * t
    slope = half + (0.5 * u) * (1.0 - t * t) * (GELU_A + (3.0 * GELU_A * GELU_B) * sq)
    return u * half, slope


def gelu(u):
    sq = u * u
    t = jnp.tanh(u * (GELU_A + (GELU_A * GELU_B) * sq))
    return u * (0.5 + 0.5 * t)


def limit_of(res_ref):
    return jnp.where(res_ref[0] == 1, SIDE, SMALL_SIDE)


def group_mask(group, limit, first_row, rows, lanes):
    place = lax.broadcasted_iota(jnp.int32, (rows, lanes), 0) + first_row
    up = place // HALF
    across = place - up * HALF
    y = 2 * up + group // 2
    x = 2 * across + group % 2
    return jnp.where((y < limit) & (x < limit), 1.0, 0.0)


def cost(us):
    return pl.CostEstimate(flops=int(us * 1.0e9), bytes_accessed=1000, transcendentals=0)


def params_of(limit=VMEM_MAX):
    return pltpu.CompilerParams(vmem_limit_bytes=limit)


SMEM_SPEC = pl.BlockSpec(memory_space=pltpu.SMEM)
VMEM_SPEC = pl.BlockSpec(memory_space=pltpu.VMEM)


def patch_kernel(res_ref, img_ref, patch_ref, gram_ref, mask_ref):
    limit = limit_of(res_ref)
    lane = lax.broadcasted_iota(jnp.int32, (32, CANVAS), 1)
    rem = lane % 8
    row = lax.broadcasted_iota(jnp.int32, (SIDE, CANVAS), 0)
    col = lax.broadcasted_iota(jnp.int32, (SIDE, CANVAS), 1)
    wanted = jnp.where(row < HALF, 2 * row, 2 * (row - HALF) + 1)
    pick = jnp.where(col // 8 == wanted, 1.0, 0.0).astype(BF16)
    sub = lax.broadcasted_iota(jnp.int32, (8, CANVAS), 0)
    tap = lax.broadcasted_iota(jnp.int32, (2 * HALF, TAPS), 1)
    ones_at = (tap % 64 == 27) & (tap < 256)

    def step(i, _):
        bands = [[], [], [], []]
        above = []
        for c in range(3):
            before = img_ref[0, c, pl.ds(pl.multiple_of(jnp.maximum(32 * i - 16, 0), 16), 16), :]
            above.append(jnp.where(i > 0, before.astype(F32)[8:16], 0.0))
            for q in range(2):
                band = img_ref[0, c, pl.ds(pl.multiple_of(32 * i + 16 * q, 16), 16), :].astype(F32)
                bands[2 * q].append(band[0:8])
                bands[2 * q + 1].append(band[8:16])
        made = []
        for q in range(4):
            prev = above if q == 0 else bands[q - 1]
            edge = jnp.zeros((8, CANVAS), F32)
            for c in range(3):
                edge = jnp.where(sub == c, prev[c][7:8], edge)
            rows = jnp.concatenate(bands[q] + [edge], axis=0)
            rolled = pltpu.roll(rows, 8, 1)
            pieces = [jnp.where((rem == 7) & (lane >= 8), rolled, 0.0)]
            pieces += [jnp.where(rem == r, rows, 0.0) for r in range(8)]
            wide = jnp.concatenate(pieces, axis=0).astype(BF16)
            made.append(dot(pick, wide, NT))
        for py in range(2):
            for px in range(2):
                group = 2 * py + px
                two = jnp.concatenate(
                    [made[py][HALF * px : HALF * px + HALF], made[2 + py][HALF * px : HALF * px + HALF]],
                    axis=0,
                )
                inside = group_mask(group, limit, 2 * HALF * i, 2 * HALF, 128)
                mask_ref[pl.ds(pl.multiple_of(group * QUAD + 2 * HALF * i, 16), 2 * HALF), :] = inside
                two = jnp.where(ones_at, 1.0, two) * inside[:, 0:1]
                patch_ref[pl.ds(pl.multiple_of(group * QUAD + 2 * HALF * i, 16), 2 * HALF), :] = (
                    two.astype(BF16)
                )
        return 0

    lax.fori_loop(0, HALF // 2, step, 0)
    patches = patch_ref[...]
    gram = dot(patches, patches, TN)
    total = gram[0:96, 0:96]
    for px in range(1, 4):
        total = total + gram[64 * px : 64 * px + 96, 64 * px : 64 * px + 96]
    gram_ref[...] = jnp.concatenate([total, jnp.zeros((96, 32), F32)], axis=1)


def make_patches(res_ids, images):
    return pl.pallas_call(
        patch_kernel,
        out_shape=(
            jax.ShapeDtypeStruct((PLACES, TAPS), BF16),
            jax.ShapeDtypeStruct((96, 128), F32),
            jax.ShapeDtypeStruct((PLACES, 128), F32),
        ),
        in_specs=[SMEM_SPEC, VMEM_SPEC],
        out_specs=(VMEM_SPEC,) * 3,
        compiler_params=params_of(),
        cost_estimate=cost(8),
        name="patches",
    )(res_ids, images)


def spread_taps():
    table = np.zeros((8, TAPS, 64), np.float32)
    for px in range(4):
        for py in range(4):
            pair, half = px * 2 + py // 2, py % 2
            for dy in range(3):
                for dx in range(3):
                    for c in range(3):
                        ry = 2 * py + dy - 1
                        r = 24 + c if ry < 0 else 8 * c + ry
                        k = (2 * px + dx) * 32 + r
                        table[pair, k, half * 32 + (dy * 3 + dx) * 3 + c] = 1.0
    return table


def spread_weights(spread_ref, stem_w, out_ref, pairs=8):
    zero = jnp.zeros((32, STEM_CH), F32)
    double = jnp.concatenate(
        [jnp.concatenate([stem_w, zero], axis=1), jnp.concatenate([zero, stem_w], axis=1)], axis=0
    ).astype(BF16)
    for pair in range(pairs):
        out_ref[:, 128 * pair : 128 * pair + 128] = dot(spread_ref[pair], double).astype(BF16)


def stem_stats(gram, first_phases):
    weights = first_phases.astype(F32)
    product = dot(gram[:, :96], weights, precision=HIGH)
    second = jnp.sum(weights * product, axis=0, keepdims=True)
    first = product[27:28]
    count = 4.0 * gram[27:28, 27:28]
    both = jnp.concatenate([first, second, jnp.zeros((6, 256), F32)], axis=0)
    folded = both[:, 0:64] + both[:, 64:128] + both[:, 128:192] + both[:, 192:256]
    return folded[0:1] / count, folded[1:2] / count


def stem_kernel(patch_ref, gram_ref, stem_w_ref, norm_ref, spread_ref, base_ref, slope_ref, bgram_ref, big):
    spread_weights(spread_ref, stem_w_ref[...], big)
    mean, square = stem_stats(gram_ref[...], big[0:96, 0:256])
    inverse = lax.rsqrt(square - mean * mean + EPS)
    gain = norm_ref[0:1] * inverse
    shift = norm_ref[1:2] - mean * gain
    gain = jnp.concatenate([gain] * 4, axis=1)
    shift = jnp.concatenate([shift] * 4, axis=1)
    rows = 256
    lane = lax.broadcasted_iota(jnp.int32, (rows, 128), 1)

    def step(i, _):
        at = pl.ds(pl.multiple_of(i * rows, rows), rows)
        block = patch_ref[at, :]
        pooled = jnp.zeros((rows, 128), F32)
        for j in range(4):
            u = dot(block, big[:, 256 * j : 256 * j + 256]) * gain + shift
            value, slope = gelu_pair(u)
            slope_ref[at, 256 * j : 256 * j + 256] = slope.astype(BF16)
            pooled = pooled + value[:, 0:128] + value[:, 128:256]
        pooled = (pooled + pltpu.roll(pooled, 64, 1)) * (1.0 / 16.0)
        ones = block[:, 0:128].astype(F32)
        ones = pltpu.roll(ones, 64 - 27, 1)
        pooled = jnp.where(lane < 64, pooled, jnp.where(lane == 64, ones, 0.0))
        base_ref[at, :] = pooled.astype(BF16)
        return 0

    lax.fori_loop(0, PLACES // rows, step, 0)
    base = base_ref[...]
    masked = (base.astype(F32) * base[:, 64:65].astype(F32)).astype(BF16)
    bgram_ref[...] = dot(masked, base, TN)[0:72]


def stem_forward(patches, gram, stem_w, norm, spread):
    return pl.pallas_call(
        stem_kernel,
        out_shape=(
            jax.ShapeDtypeStruct((PLACES, 128), BF16),
            jax.ShapeDtypeStruct((PLACES, 1024), BF16),
            jax.ShapeDtypeStruct((72, 128), F32),
        ),
        in_specs=[VMEM_SPEC] * 5,
        out_specs=(VMEM_SPEC,) * 3,
        scratch_shapes=[pltpu.VMEM((TAPS, 1024), BF16)],
        compiler_params=params_of(),
        cost_estimate=cost(13),
        name="stem_forward",
    )(patches, gram, stem_w, norm, spread)


def taps_row(load, weight, py):
    sources = [(1, -1), (0, 0), (1, 0)] if py == 0 else [(0, 0), (1, 0), (0, 1)]
    rows = [[load(2 * gy + px, off) for px in range(2)] for gy, off in sources]

    def column(px, dx):
        total = rows[0][px] * weight(0, dx)
        total = total + rows[1][px] * weight(1, dx)
        return total + rows[2][px] * weight(2, dx)

    even = column(0, 1) + column(1, 2) + shift_down(column(1, 0))
    odd = column(1, 1) + column(0, 0) + shift_up(column(0, 2))
    return even, odd


def shift_down(v):
    at = lax.broadcasted_iota(jnp.int32, v.shape, 0)
    return jnp.where(at == 0, 0.0, pltpu.roll(v, 1, 0))


def shift_up(v):
    at = lax.broadcasted_iota(jnp.int32, v.shape, 0)
    return jnp.where(at == HALF - 1, 0.0, pltpu.roll(v, HALF - 1, 0))


def bn_stats(bgram, expand_w, count):
    weights = expand_w.astype(F32)
    square_of = jnp.concatenate([bgram, jnp.zeros((56, 128), F32)], axis=0)
    product = dot(square_of, weights, precision=HIGH)
    mean = product[64:65] / count
    second = jnp.sum(weights * product, axis=0, keepdims=True) / count
    return mean, lax.rsqrt(second - mean * mean + EPS)


def depth_kernel(mask_ref, base_ref, expand_ref, bgram_ref, norm_ref, depth_ref, out_ref, act_ref, slope_ref, stat_ref, pad):
    count = bgram_ref[64:65, 64:65]
    mean, inverse = bn_stats(bgram_ref[...], expand_ref[...], count)
    gain = norm_ref[0:1] * inverse
    shift = norm_ref[1:2] - mean * gain
    zero = jnp.zeros((4, 1, HALF, BLOCK), F32)
    pad[:, 0:1] = zero
    pad[:, HALF + 1 : HALF + 2] = zero
    rows = 4 * HALF
    for group in range(4):

        def fill(i, _, group=group):
            first = pl.multiple_of(group * QUAD + rows * i, 16)
            at = pl.ds(first, rows)
            x = dot(base_ref[at, :], expand_ref[...])
            inside = mask_ref[at, :]
            value, slope = gelu_pair(x * gain + shift)
            value = value * inside
            act_ref[at, :] = value.astype(BF16)
            slope_ref[at, :] = (slope * inside).astype(BF16)
            for k in range(4):
                pad[group, 4 * i + k + 1] = value[HALF * k : HALF * k + HALF]
            return 0

        lax.fori_loop(0, QUAD // rows, fill, 0)

    def weight(dy, dx):
        return depth_ref[3 * dy + dx : 3 * dy + dx + 1]

    def fold(v):
        return v[0:8] + v[8:16] + v[16:24]

    def step(up, sums):
        first, second = sums
        for py in range(2):
            made = taps_row(lambda g, off: pad[g, up + 1 + off], weight, py)
            for px in range(2):
                at = pl.ds(pl.multiple_of((2 * py + px) * QUAD + HALF * up, 8), HALF)
                x = made[px] * mask_ref[at, :]
                out_ref[at, :] = x
                first = first + fold(x)
                second = second + fold(x * x)
        return first, second

    sums = lax.fori_loop(0, HALF, step, (jnp.zeros((8, BLOCK), F32),) * 2)
    rows_out = [jnp.sum(s, axis=0, keepdims=True) for s in sums]
    stat_ref[...] = jnp.concatenate(rows_out + [jnp.zeros((6, BLOCK), F32)], axis=0)


def depth_forward(mask, base, expand_w, bgram, mid_norm, mb_depth):
    col = lambda rows: pl.BlockSpec((rows, BLOCK), lambda j: (0, j))
    whole = lambda rows: pl.BlockSpec((rows, BLOCK), lambda j: (0, 0))
    return pl.pallas_call(
        depth_kernel,
        grid=(CHUNKS,),
        out_shape=(
            jax.ShapeDtypeStruct((PLACES, EXPAND), F32),
            jax.ShapeDtypeStruct((PLACES, EXPAND), BF16),
            jax.ShapeDtypeStruct((PLACES, EXPAND), BF16),
            jax.ShapeDtypeStruct((8, EXPAND), F32),
        ),
        in_specs=[whole(PLACES), whole(PLACES), col(128), whole(72), col(2), col(9)],
        out_specs=(col(PLACES),) * 3 + (col(8),),
        scratch_shapes=[pltpu.VMEM((4, HALF + 2, HALF, BLOCK), F32)],
        compiler_params=params_of(),
        cost_estimate=cost(25),
        name="depth_forward",
    )(mask, base, expand_w, bgram, mid_norm, mb_depth)


EARLY_ROWS = 576
STEM_ROWS = 15


def runs_of(offset, rows, width):
    period = min(128 // math.gcd(width, 128), rows)
    stride = period * width // 128 if rows > period else 1
    for j in range(period):
        start = offset + j * width
        yield j, period, start // 128, start % 128, -(-(rows - j) // period), stride


def rows_at(first, count, stride):
    return pl.ds(first, count) if stride == 1 or count == 1 else pl.ds(first, count, stride=stride)


def chunks_of(count, size=128):
    for begin in range(0, count, size):
        yield begin, min(size, count - begin)


def take_matrix(flat, out_ref, hold, offset, rows, width):
    direct = True
    for j, period, first, shift, count, stride in runs_of(offset, rows, width):
        direct = period == 1
        for t in range(-(-width // 128)):
            wide = min(128, width - 128 * t)
            for begin, size in chunks_of(count):
                at = first + t + begin * stride
                value = flat[rows_at(at, size, stride), :]
                if shift:
                    if shift + wide > 128:
                        lane = lax.broadcasted_iota(jnp.int32, (size, 128), 1)
                        value = jnp.where(lane >= shift, value, flat[rows_at(at + 1, size, stride), :])
                    value = pltpu.roll(value, 128 - shift, 1)
                if direct:
                    out_ref[begin : begin + size, 128 * t : 128 * t + wide] = value[:, :wide].astype(out_ref.dtype)
                elif count == 1:
                    out_ref[j : j + 1, 128 * t : 128 * t + wide] = value[:, :wide].astype(out_ref.dtype)
                else:
                    hold[t, rows_at(j + begin * period, size, period), :] = value
    if not direct and count > 1:
        for t in range(-(-width // 128)):
            wide = min(128, width - 128 * t)
            out_ref[0:rows, 128 * t : 128 * t + wide] = hold[t, 0:rows, 0:wide].astype(out_ref.dtype)


def put_matrix(flat, value_of, base, offset, rows, width):
    for j, period, first, shift, count, stride in runs_of(offset, rows, width):
        tiles = -(-width // 128)
        for begin, size in chunks_of(count):
            before = None
            lane = lax.broadcasted_iota(jnp.int32, (size, 128), 1)
            picked = rows_at(j + begin * period, size, period)
            at = first - base + begin * stride
            for t in range(tiles):
                value = value_of(picked, t)
                if shift:
                    value = pltpu.roll(value, shift, 1)
                    mixed = jnp.where(lane >= shift, value, 0.0 if before is None else before)
                else:
                    mixed = value
                before = value
                where = rows_at(at + t, size, stride)
                full = 0 < t < tiles - 1 or (shift == 0 and width % 128 == 0)
                flat[where, :] = mixed if full else flat[where, :] + mixed
            if shift:
                where = rows_at(at + tiles, size, stride)
                flat[where, :] = flat[where, :] + jnp.where(lane < shift, before, 0.0)


def unpack_kernel(names, shapes, shards, shard_rows, held_rows, flat_ref, *refs):
    outs, (flat, hold) = refs[: len(names)], refs[len(names) :]
    for d in range(shards):
        flat[d * shard_rows : (d + 1) * shard_rows, :] = flat_ref[d * held_rows : (d + 1) * held_rows, :].astype(F32)[
            :shard_rows
        ]
    for name, shape, out in zip(names, shapes, outs):
        offset, own = OFFSETS[name]
        width = own[-1]
        rows = math.prod(own) // width
        if shape[0][0] > rows or shape[0][1] > width:
            out[...] = jnp.zeros_like(out)
        take_matrix(flat, out, hold, offset, rows, width)


def unpack(flat, shards, shard_rows, shapes):
    names = tuple(shapes)
    kinds = tuple(shapes[n] for n in names)
    total = max(shards * shard_rows, flat.shape[0]) + 8
    kernel = functools.partial(unpack_kernel, names, kinds, shards, shard_rows, flat.shape[0] // shards)
    made = pl.pallas_call(
        kernel,
        out_shape=tuple(jax.ShapeDtypeStruct(*k) for k in kinds),
        in_specs=[VMEM_SPEC],
        out_specs=(VMEM_SPEC,) * len(names),
        scratch_shapes=[pltpu.VMEM((total, 128), F32), pltpu.VMEM((8, EXPAND, 128), F32)],
        compiler_params=params_of(),
        cost_estimate=cost(6),
        name="unpack",
    )(flat)
    return dict(zip(names, made))


EARLY_SHAPES = {
    "mb_short": ((128, MB_CH), BF16), "mb_expand": ((128, EXPAND), BF16), "mid_norm": ((2, EXPAND), F32),
    "mb_depth": ((9, EXPAND), F32), "dw_norm": ((2, EXPAND), F32),
}
LATE_SHAPES = {
    "se_down": ((EXPAND, SQUEEZE), BF16), "se_down_bias": ((1, SQUEEZE), F32), "se_up": ((SQUEEZE, EXPAND), BF16),
    "se_up_bias": ((1, EXPAND), F32), "mb_proj": ((EXPAND, MB_CH), BF16), "at_short": ((MB_CH, DIM), BF16),
    "pre_norm": ((2, MB_CH), F32), "qkv": ((MB_CH, 3 * DIM), BF16), "attn_out": ((DIM, DIM), BF16),
    "out_bias": ((1, DIM), F32), "rel_table": ((16, 2 * WIDE), F32), "mlp_norm": ((2, DIM), F32),
    "mlp_in": ((DIM, MLP), BF16), "mlp_in_bias": ((1, MLP), F32), "mlp_out": ((MLP, DIM), BF16),
    "mlp_out_bias": ((1, DIM), F32), "head_norm": ((2, DIM), F32), "head_w": ((DIM, CLASSES), BF16),
    "head_bias": ((1, CLASSES), F32),
}


def pack_kernel(names, base, shards, shard_rows, core_ref, *refs):
    grads, (keep_ref, send_ref), (flat, hold) = refs[: len(names)], refs[len(names) : -2], refs[-2:]
    rows_all = flat.shape[0]
    step = 384

    def clear(i, _):
        flat[pl.ds(pl.multiple_of(i * step, 8), step), :] = jnp.zeros((step, 128), F32)
        return 0

    lax.fori_loop(0, rows_all // step, clear, 0)
    for name, grad in zip(names, grads):
        offset, own = OFFSETS[name]
        width = own[-1]
        rows = math.prod(own) // width
        tiles = -(-width // 128)
        read = lambda r, t: grad[r, 128 * t : 128 * t + 128]
        if grad.shape[1] < 128 * tiles:
            hold[tiles - 1, 0:rows, :] = jnp.zeros((rows, 128), F32)
            for t in range(tiles):
                wide = min(128, width - 128 * t)
                hold[t, 0:rows, 0:wide] = grad[0:rows, 128 * t : 128 * t + wide]
            read = lambda r, t: hold[t, r, :]
        put_matrix(flat, read, base, offset, rows, width)

    def share(k, _):
        block = flat[pl.ds(k * shard_rows, shard_rows), :]
        ours = k % 2 == core_ref[0]

        @pl.when(ours)
        def _():
            keep_ref[k // 2, 0:shard_rows] = block

        @pl.when(jnp.logical_not(ours))
        def _():
            send_ref[k // 2, 0:shard_rows] = block

        return 0

    lax.fori_loop(0, shards, share, 0)


def pack(core, grads, base, shards, shard_rows, held_rows):
    names = tuple(grads)
    total = -(-(shards * shard_rows + 8) // 384) * 384
    out = jax.ShapeDtypeStruct((shards // 2, held_rows, 128), F32)
    return pl.pallas_call(
        functools.partial(pack_kernel, names, base, shards, shard_rows),
        out_shape=(out, out),
        in_specs=[SMEM_SPEC] + [VMEM_SPEC] * len(names),
        out_specs=(VMEM_SPEC,) * 2,
        scratch_shapes=[pltpu.VMEM((total, 128), F32), pltpu.VMEM((2, EXPAND, 128), F32)],
        compiler_params=params_of(),
        cost_estimate=cost(6),
        name="pack",
    )(core, *grads.values())


def shard_kernel(
    length, first_ref, late_ref, mid_ref, small_ref, used_ref, back_ref, normed_ref, head_ref, norms_ref,
    out_ref, square_ref, flat, hold,
):
    rows = length // 128
    lead = 16
    flat[...] = jnp.zeros_like(flat)
    start = first_ref[0] * length
    lane = lax.broadcasted_iota(jnp.int32, (8, 128), 1)

    def add_rows(first, value):
        flat[pl.ds(first, value.shape[0]), :] = flat[pl.ds(first, value.shape[0]), :] + value

    def place(name, left_ref, right, tall):
        offset, (count, width) = OFFSETS[name]
        first = (start - offset + 2**20 * width) // width - 2**20
        inside = (first > -tall) & (first < count)
        held = jnp.where(inside, first, -tall)
        part = left_ref.shape[2]
        made = dot(left_ref[0, pl.ds(held + tall, tall), :], right[:part], precision=HIGH)
        for g in range(1, left_ref.shape[0]):
            made = made + dot(
                left_ref[g, pl.ds(held + tall, tall), :], right[g * part : (g + 1) * part], precision=HIGH
            )
        tiles = -(-width // 128)
        for t in range(tiles):
            wide = min(128, made.shape[1] - 128 * t)
            hold[t, 0:tall, 0:wide] = made[:, 128 * t : 128 * t + wide]
        period = 128 // math.gcd(width, 128)
        stride = period * width // 128

        @pl.when(inside)
        def _():
            for j in range(period):
                begin = offset + (first + j) * width - start + 128 * lead
                row = begin // 128
                shift = begin - row * 128
                size = tall // period
                at_lane = lax.broadcasted_iota(jnp.int32, (size, 128), 1)
                for t in range(tiles):
                    value = hold[t, rows_at(j, size, period), :]
                    value = pltpu.roll(value, shift, 1)
                    where = rows_at(row + t, size, stride)
                    flat[where, :] = flat[where, :] + jnp.where(at_lane >= shift, value, 0.0)
                    where = rows_at(row + t + 1, size, stride)
                    flat[where, :] = flat[where, :] + jnp.where(at_lane < shift, value, 0.0)

    def place_row(offset, value):
        width = value.shape[1]
        begin = offset - start

        @pl.when((begin > -width) & (begin < length))
        def _():
            at = begin + 128 * lead
            row = at // 128
            shift = at - row * 128
            one = lane[0:1]
            for t in range(width // 128):
                tile = pltpu.roll(value[:, 128 * t : 128 * t + 128], shift, 1)
                add_rows(row + t, jnp.where(one >= shift, tile, 0.0))
                add_rows(row + t + 1, jnp.where(one < shift, tile, 0.0))

    place("mlp_out", used_ref, back_ref[...], used_ref.shape[1] - MLP >> 1)
    place("head_w", normed_ref, head_ref[...], normed_ref.shape[1] - DIM >> 1)
    place_row(OFFSETS["mlp_out_bias"][0], small_ref[0:1, 0:DIM])
    place_row(OFFSETS["head_norm"][0], small_ref[1:2, 0:DIM])
    place_row(OFFSETS["head_norm"][0] + DIM, small_ref[2:3, 0:DIM])
    place_row(OFFSETS["head_bias"][0], small_ref[3:4, 0:1024])
    for k, name in enumerate(("mid_norm", "mid_norm", "dw_norm", "dw_norm")):
        place_row(OFFSETS[name][0] + (k % 2) * EXPAND, norms_ref[k : k + 1])
    total = flat[lead : lead + rows, :] + late_ref[0:rows] + mid_ref[0:rows]
    out_ref[...] = total
    square_ref[...] = jnp.broadcast_to(jnp.sum(total * total).reshape(1, 1), (8, 128))


def shard_parts(me, length, late, mid, small, used, back, normed, head, norms):
    rows = length // 128
    return pl.pallas_call(
        functools.partial(shard_kernel, length),
        out_shape=(jax.ShapeDtypeStruct((rows, 128), F32), jax.ShapeDtypeStruct((8, 128), F32)),
        in_specs=[SMEM_SPEC] + [VMEM_SPEC] * 8,
        out_specs=(VMEM_SPEC,) * 2,
        scratch_shapes=[
            pltpu.VMEM((rows + 1024, 128), F32),
            pltpu.VMEM((8, max(used.shape[1] - MLP, normed.shape[1] - DIM) // 2, 128), F32),
        ],
        compiler_params=params_of(),
        cost_estimate=cost(4),
        name="shard_parts",
    )(me, late, mid, small, used, back, normed, head, norms)


def squeeze_lanes():
    table = np.zeros((16 * 48, 16 * 24), np.float32)
    for e in range(16):
        for x in range(24):
            table[e * 48 + x, e * 24 + x] = 1.0
    return table


def slots_of(rel_index):
    last = TOKENS - 1
    corner = lambda i: rel_index[i].reshape(HALF, HALF)
    low_row = jnp.concatenate([corner(last), corner(last - HALF + 1)[:, 1:]], axis=1)
    high_row = jnp.concatenate([corner(HALF - 1), corner(0)[:, 1:]], axis=1)
    return jnp.concatenate([low_row, high_row[1:]], axis=0)


def one_hot(slot_ref, c):
    at = lax.broadcasted_iota(jnp.int32, (256, 2 * WIDE), 1)
    return jnp.where(slot_ref[256 * c : 256 * c + 256, :] == at, 1.0, 0.0).astype(BF16)


def bias_kernel(table_ref, slot_ref, pick_ref, out_ref, held):
    table = table_ref[...].astype(BF16)
    f = jnp.concatenate([dot(table, one_hot(slot_ref, c), NT) for c in range(2 * WIDE // 256)], axis=1)
    for x in range(HALF):
        turned = pltpu.roll(f, (WIDE * 2 - (HALF - 1 - x)) % (WIDE * 2), 1) if x != HALF - 1 else f
        held[16 * x : 16 * x + 16, :] = turned.astype(BF16)
    for part in range(3):
        made = dot(held[:, 768 * part : 768 * part + 768], pick_ref[...])
        for t in range(3):
            for x in range(HALF):
                out_ref[3 * part + t, pl.ds(x, HEADS, stride=HALF), :] = made[
                    16 * x : 16 * x + HEADS, 128 * t : 128 * t + 128
                ]


def build_bias(table, slots, pick):
    return pl.pallas_call(
        bias_kernel,
        out_shape=jax.ShapeDtypeStruct((9, HEADS * HALF, 128), F32),
        in_specs=[VMEM_SPEC] * 3,
        out_specs=VMEM_SPEC,
        scratch_shapes=[pltpu.VMEM((16 * HALF, 2 * WIDE), BF16)],
        compiler_params=params_of(),
        cost_estimate=cost(8),
        name="bias_build",
    )(table, slots, pick)


def halves_of(v):
    high = v.astype(BF16)
    return high, (v - high.astype(F32)).astype(BF16)


def bias_back_kernel(grad_ref, slot_ref, pick_ref, out_ref, held):
    for part in range(3):
        rows = jnp.concatenate([grad_ref[3 * part + t] for t in range(3)], axis=1)
        high, rest = halves_of(rows)
        wide = dot(high, pick_ref[...]) + dot(rest, pick_ref[...])
        for t in range(6):
            held[6 * part + t] = wide[:, 128 * t : 128 * t + 128]
    total = jnp.zeros((16, 2 * WIDE), F32)
    for x in range(HALF):
        wide = jnp.concatenate([held[t, pl.ds(x, HEADS, stride=HALF), :] for t in range(18)], axis=1)
        wide = jnp.concatenate([wide, jnp.zeros((4, 2 * WIDE), F32)], axis=0)
        total = total + (pltpu.roll(wide, HALF - 1 - x, 1) if x != HALF - 1 else wide)
    high, rest = halves_of(total)
    result = jnp.zeros((16, 2 * WIDE), F32)
    for c in range(2 * WIDE // 256):
        hot = one_hot(slot_ref, c)
        cols = slice(256 * c, 256 * c + 256)
        result = result + dot(high[:, cols], hot) + dot(rest[:, cols], hot)
    out_ref[...] = result


def bias_back(grad, slots, pick):
    return pl.pallas_call(
        bias_back_kernel,
        out_shape=jax.ShapeDtypeStruct((16, 2 * WIDE), F32),
        in_specs=[VMEM_SPEC] * 3,
        out_specs=VMEM_SPEC,
        scratch_shapes=[pltpu.VMEM((18, HEADS * HALF, 128), F32)],
        compiler_params=params_of(),
        cost_estimate=cost(10),
        name="bias_back",
    )(grad, slots, pick)


def sigmoid(v):
    return 1.0 / (1.0 + jnp.exp(-v))


def row8(rows):
    width = rows[0].shape[1]
    return jnp.concatenate(rows + [jnp.zeros((8 - len(rows), width), F32)], axis=0)


def dw_stats(stat, count):
    mean = stat[0:1] / count
    return mean, lax.rsqrt(stat[1:2] / count - mean * mean + EPS)


def valid_places(limit):
    return (limit * limit).astype(F32)


def excite_kernel(
    res_ref, mask_ref, depth_ref, stat_ref, bgram_ref, norm_ref, down_ref, down_b_ref, up_ref, up_b_ref,
    proj_ref, base_ref, short_ref, pre_ref, qkv_ref,
    act_ref, slope_ref, block_ref, skip_ref, normed_ref, project_ref, vec_ref, small_ref, held,
):
    limit = limit_of(res_ref)
    count = bgram_ref[64:65, 64:65]
    mean, inverse = dw_stats(stat_ref[...], count)
    gain = norm_ref[0:1] * inverse
    shift = norm_ref[1:2] - mean * gain
    rows = 2 * HALF
    total = jnp.zeros((8, EXPAND), F32)
    for group in range(4):

        def fill(i, total, group=group):
            at = pl.ds(pl.multiple_of(group * QUAD + rows * i, 16), rows)
            value, slope = gelu_pair(depth_ref[at, :] * gain + shift)
            inside = mask_ref[at, :]
            inside = jnp.concatenate([inside] * CHUNKS, axis=1)
            value = value * inside
            held[at, :] = value
            act_ref[at, :] = value.astype(BF16)
            slope_ref[at, :] = (slope * inside).astype(BF16)
            for k in range(rows // 8):
                total = total + value[8 * k : 8 * k + 8]
            return total

        total = lax.fori_loop(0, QUAD // rows, fill, total)
    pooled = jnp.sum(total, axis=0, keepdims=True) / valid_places(limit)
    before = dot(row8([pooled]), down_ref[...].astype(F32), precision=HIGH)[0:1] + down_b_ref[...]
    gate = sigmoid(before)
    squeeze = before * gate
    excite = sigmoid(
        dot(row8([squeeze]), up_ref[...].astype(F32), precision=HIGH)[0:1] + up_b_ref[...]
    )
    vec_ref[...] = row8([pooled, excite, mean, inverse])
    small_ref[...] = row8([squeeze, gate * (1.0 + before * (1.0 - gate))])

    big = 192
    def section(i, _):
        at = pl.ds(pl.multiple_of(big * i, 16), big)
        scaled = (held[at, :] * excite).astype(BF16)
        block_ref[at, :] = dot(scaled, proj_ref[...]) + dot(base_ref[at, :], short_ref[...])
        return 0

    lax.fori_loop(0, PLACES // big, section, 0)
    part = 96

    def tokens(i, _):
        skipped = jnp.zeros((part, MB_CH), F32)
        normed = jnp.zeros((part, MB_CH), F32)
        for group in range(4):
            block = block_ref[pl.ds(pl.multiple_of(group * QUAD + part * i, 16), part), :]
            skipped = skipped + block
            hat, _ = normalise(block)
            normed = normed + hat
        at = pl.ds(pl.multiple_of(part * i, 16), part)
        skip_ref[at, :] = (0.25 * skipped).astype(BF16)
        low = (0.25 * normed * pre_ref[0:1] + pre_ref[1:2]).astype(BF16)
        normed_ref[at, :] = low
        project_ref[at, :] = dot(low, qkv_ref[...]).astype(BF16)
        return 0

    lax.fori_loop(0, TOKENS // part, tokens, 0)


def normalise(v):
    centered = v - jnp.mean(v, axis=-1, keepdims=True)
    inverse = lax.rsqrt(jnp.mean(centered * centered, axis=-1, keepdims=True) + EPS)
    return centered * inverse, inverse


def normalise_back(grad_hat, hat, inverse):
    first = jnp.mean(grad_hat, axis=-1, keepdims=True)
    second = jnp.mean(grad_hat * hat, axis=-1, keepdims=True)
    return inverse * (grad_hat - first - hat * second)


def excite_forward(res_ids, mask, depth, stat, bgram, base, p):
    return pl.pallas_call(
        excite_kernel,
        out_shape=(
            jax.ShapeDtypeStruct((PLACES, EXPAND), BF16),
            jax.ShapeDtypeStruct((PLACES, EXPAND), BF16),
            jax.ShapeDtypeStruct((PLACES, MB_CH), F32),
            jax.ShapeDtypeStruct((TOKENS, MB_CH), BF16),
            jax.ShapeDtypeStruct((TOKENS, MB_CH), BF16),
            jax.ShapeDtypeStruct((TOKENS, 3 * DIM), BF16),
            jax.ShapeDtypeStruct((8, EXPAND), F32),
            jax.ShapeDtypeStruct((8, SQUEEZE), F32),
        ),
        in_specs=[SMEM_SPEC] + [VMEM_SPEC] * 14,
        out_specs=(VMEM_SPEC,) * 8,
        scratch_shapes=[pltpu.VMEM((PLACES, EXPAND), F32)],
        compiler_params=params_of(),
        cost_estimate=cost(18),
        name="excite_forward",
    )(
        res_ids, mask, depth, stat, bgram, p["dw_norm"], p["se_down"], p["se_down_bias"], p["se_up"], p["se_up_bias"],
        p["mb_proj"], base, p["mb_short"], p["pre_norm"], p["qkv"],
    )


SCALE = HEAD_DIM ** (-0.5)
PER = BLOCK // HEAD_DIM
ATT_ROWS = 2 * HALF


def token_valid(limit, shape, axis):
    at = lax.broadcasted_iota(jnp.int32, shape, axis)
    y = at // HALF
    x = at - y * HALF
    return (2 * y < limit) & (2 * x < limit)


def head_lanes(h):
    lane = lax.broadcasted_iota(jnp.int32, (TOKENS, BLOCK), 1)
    return lane // HEAD_DIM == h


def bias_cut(up):
    offset = (HALF - 1 - up) * HALF
    lead = offset % 128
    return offset // 128, (5 if lead <= 64 else 6), lead


def attend_kernel(res_ref, q_ref, k_ref, v_ref, bias_ref, out_ref, p_ref, scores):
    limit = limit_of(res_ref)
    usable = token_valid(limit, (1, TOKENS), 1)

    def head(h, total):
        mine = head_lanes(h)
        q = jnp.where(mine, q_ref[...], jnp.zeros((), BF16))
        scores[...] = dot(q, k_ref[...], NT)
        bias_rows = pl.ds(pl.multiple_of(h * HALF, 8), HALF)
        for i in range(TOKENS // ATT_ROWS):
            at = slice(ATT_ROWS * i, ATT_ROWS * i + ATT_ROWS)
            shifted = []
            for k in range(2):
                tile, tiles, lead = bias_cut(2 * i + k)
                bias = jnp.concatenate([bias_ref[tile + t, bias_rows, :] for t in range(tiles)], axis=1)
                if lead:
                    bias = pltpu.roll(bias, 128 * tiles - lead, 1)
                shifted.append(bias[:, :TOKENS])
            s = scores[at, :] * SCALE + jnp.concatenate(shifted, axis=0)
            s = jnp.where(usable, s, -1e30)
            e = jnp.exp(s - jnp.max(s, axis=-1, keepdims=True))
            weights = e * (1.0 / jnp.sum(e, axis=-1, keepdims=True))
            p_ref[h, at, :] = weights.astype(BF16)
        return jnp.where(mine, dot(p_ref[h], v_ref[...]), total)

    total = lax.fori_loop(0, PER, head, jnp.zeros((TOKENS, BLOCK), F32))
    out_ref[...] = total.astype(BF16)


def attend_forward(res_ids, project, bias):
    part = lambda k: pl.BlockSpec((TOKENS, BLOCK), lambda j: (0, 3 * k + j))
    return pl.pallas_call(
        attend_kernel,
        grid=(HEADS // PER,),
        out_shape=(
            jax.ShapeDtypeStruct((TOKENS, DIM), BF16),
            jax.ShapeDtypeStruct((HEADS, TOKENS, TOKENS), BF16),
        ),
        in_specs=[SMEM_SPEC, part(0), part(1), part(2), pl.BlockSpec((9, PER * HALF, 128), lambda j: (0, j, 0))],
        out_specs=(
            pl.BlockSpec((TOKENS, BLOCK), lambda j: (0, j)),
            pl.BlockSpec((PER, TOKENS, TOKENS), lambda j: (j, 0, 0)),
        ),
        scratch_shapes=[pltpu.VMEM((TOKENS, TOKENS), F32)],
        compiler_params=params_of(),
        cost_estimate=cost(35),
        name="attend_forward",
    )(res_ids, project, project, project, bias)


def attend_back_kernel(q_ref, k_ref, v_ref, o_ref, do_ref, p_ref, dq_ref, dk_ref, dv_ref, dbias_ref, scores, low, bias):
    def head(h, carry):
        dq, dk, dv = carry
        mine = head_lanes(h)
        grad = jnp.where(mine, do_ref[...], jnp.zeros((), BF16))
        scores[...] = dot(grad, v_ref[...], NT)
        bias[...] = jnp.zeros((HALF, WIDE), F32)
        lane = lax.broadcasted_iota(jnp.int32, (ATT_ROWS, BLOCK), 1)
        for i in range(TOKENS // ATT_ROWS):
            at = slice(ATT_ROWS * i, ATT_ROWS * i + ATT_ROWS)
            both = do_ref[at, :].astype(F32) * o_ref[at, :].astype(F32)
            both = jnp.where(lane // HEAD_DIM == h, both, 0.0)
            delta = jnp.sum(both, axis=-1, keepdims=True)
            ds = p_ref[h, at, :].astype(F32) * (scores[at, :] - delta)
            low[at, :] = (ds * SCALE).astype(BF16)
            for k in range(2):
                tile, tiles, lead = bias_cut(2 * i + k)
                wide = jnp.concatenate(
                    [ds[HALF * k : HALF * k + HALF], jnp.zeros((HALF, 128 * tiles - TOKENS), F32)], axis=1
                )
                if lead:
                    wide = pltpu.roll(wide, lead, 1)
                cols = slice(128 * tile, 128 * (tile + tiles))
                bias[:, cols] = bias[:, cols] + wide
        for t in range(9):
            dbias_ref[t, pl.ds(pl.multiple_of(h * HALF, 8), HALF), :] = bias[:, 128 * t : 128 * t + 128]
        dq = jnp.where(mine, dot(low[...], k_ref[...]), dq)
        dk = jnp.where(mine, dot(low[...], q_ref[...], TN), dk)
        dv = jnp.where(mine, dot(p_ref[h], do_ref[...], TN), dv)
        return dq, dk, dv

    zero = jnp.zeros((TOKENS, BLOCK), F32)
    dq, dk, dv = lax.fori_loop(0, PER, head, (zero, zero, zero))
    dq_ref[...] = dq.astype(BF16)
    dk_ref[...] = dk.astype(BF16)
    dv_ref[...] = dv.astype(BF16)


def attend_backward(project, blended, grad, weights):
    part = lambda k: pl.BlockSpec((TOKENS, BLOCK), lambda j: (0, 3 * k + j))
    bias = pl.BlockSpec((9, PER * HALF, 128), lambda j: (0, j, 0))
    return pl.pallas_call(
        attend_back_kernel,
        grid=(HEADS // PER,),
        out_shape=(jax.ShapeDtypeStruct((TOKENS, DIM), BF16),) * 3
        + (jax.ShapeDtypeStruct((9, HEADS * HALF, 128), F32),),
        in_specs=[
            part(0), part(1), part(2), part(0), part(0),
            pl.BlockSpec((PER, TOKENS, TOKENS), lambda j: (j, 0, 0)),
        ],
        out_specs=(part(0), part(0), part(0), bias),
        scratch_shapes=[
            pltpu.VMEM((TOKENS, TOKENS), F32), pltpu.VMEM((TOKENS, TOKENS), BF16), pltpu.VMEM((HALF, WIDE), F32),
        ],
        compiler_params=params_of(),
        cost_estimate=cost(40),
        name="attend_backward",
    )(project, project, project, blended, grad, weights)


MLP_ROWS = 96


def mlp_kernel(
    share, res_ref, label_ref, skip_ref, blend_ref, short_ref, out_ref, out_b_ref, norm_ref, in_ref, in_b_ref,
    back_ref, back_b_ref, hnorm_ref, head_ref, head_b_ref,
    loss_ref, dblend_ref, dskip_ref, dshort_ref, dout_ref, dout_b_ref, dnorm_ref, din_ref, din_b_ref,
    vec_ref, few_ref,
    section, low, slopes, dpres, grads,
):
    limit = limit_of(res_ref)
    n_valid = (limit // 2 * (limit // 2)).astype(F32)
    steps = TOKENS // MLP_ROWS
    cut = 384

    def valid_rows(i):
        at = lax.broadcasted_iota(jnp.int32, (MLP_ROWS, 1), 0) + MLP_ROWS * i
        y = at // HALF
        x = at - y * HALF
        return jnp.where((2 * y < limit) & (2 * x < limit), 1.0, 0.0)

    def forward(i, carry):
        feature, used = carry
        at = pl.ds(pl.multiple_of(MLP_ROWS * i, 16), MLP_ROWS)
        first = dot(skip_ref[at, :], short_ref[...]) + dot(blend_ref[at, :], out_ref[...]) + out_b_ref[...]
        section[at, :] = first
        hat, _ = normalise(first)
        normed = (hat * norm_ref[0:1] + norm_ref[1:2]).astype(BF16)
        low[at, :] = normed
        inside = valid_rows(i)
        second = first + back_b_ref[...]
        parts = []
        for j in range(MLP // cut):
            cols = slice(cut * j, cut * j + cut)
            value, slope = gelu_pair(dot(normed, in_ref[:, cols]) + in_b_ref[:, cols])
            slopes[at, cols] = slope * inside
            value = value.astype(BF16)
            parts.append(jnp.sum(value.astype(F32) * inside, axis=0, keepdims=True))
            second = second + dot(value, back_ref[cols, :])
        feature = feature + jnp.sum(second * inside, axis=0, keepdims=True)
        return feature, used + jnp.concatenate(parts, axis=1)

    feature, used = lax.fori_loop(
        0, steps, forward, (jnp.zeros((1, DIM), F32), jnp.zeros((1, MLP), F32))
    )
    feature = feature / n_valid
    hat, inverse = normalise(feature)
    normed = (hat * hnorm_ref[0:1] + hnorm_ref[1:2]).astype(BF16)
    normed8 = jnp.concatenate([normed.astype(F32), jnp.zeros((15, DIM), F32)], axis=0).astype(BF16)
    logits = dot(normed8, head_ref[...])[0:1] + head_b_ref[...]
    peak = jnp.max(logits, axis=-1, keepdims=True)
    exps = jnp.exp(logits - peak)
    total = jnp.sum(exps, axis=-1, keepdims=True)
    log_probs = logits - peak - jnp.log(total)
    at_class = lax.broadcasted_iota(jnp.int32, (1, CLASSES), 1)
    goal = jnp.where(at_class == label_ref[0], 1.0 - SMOOTH, 0.0) + SMOOTH / CLASSES
    loss = -jnp.sum(goal * log_probs, axis=-1, keepdims=True)
    loss_ref[...] = jnp.broadcast_to(loss, (8, 128))
    grad = (exps / total - goal) * share
    few_ref[...] = jnp.zeros_like(few_ref)
    few_ref[3:4, 0:CLASSES] = grad
    grad16 = jnp.concatenate([grad, jnp.zeros((15, CLASSES), F32)], axis=0).astype(BF16)
    vec_ref[...] = jnp.zeros_like(vec_ref)
    vec_ref[2:3, 0:DIM] = normed8.astype(F32)[0:1]
    vec_ref[3:4, 0:CLASSES] = grad16.astype(F32)[0:1]
    grad = dot(grad16, head_ref[...], NT)[0:1]
    few_ref[1:3, 0:DIM] = jnp.concatenate([grad * hat, grad], axis=0)
    grad = normalise_back(grad * hnorm_ref[0:1], hat, inverse) / n_valid
    low_grad = jnp.concatenate([grad, jnp.zeros((15, DIM), F32)], axis=0).astype(BF16)
    vec_ref[0:1, :] = used
    vec_ref[1:2, 0:DIM] = low_grad.astype(F32)[0:1]
    few_ref[0:1, 0:DIM] = grad * n_valid
    dhidden = dot(low_grad, back_ref[...], NT)[0:1]

    def backward(i, carry):
        dnorm0, dnorm1, dbias, dout_b = carry
        at = pl.ds(pl.multiple_of(MLP_ROWS * i, 16), MLP_ROWS)
        dnormed = jnp.zeros((MLP_ROWS, DIM), F32)
        parts = []
        for j in range(MLP // cut):
            cols = slice(cut * j, cut * j + cut)
            dpre = slopes[at, cols] * dhidden[:, cols]
            parts.append(jnp.sum(dpre, axis=0, keepdims=True))
            dpre = dpre.astype(BF16)
            dpres[at, cols] = dpre
            dnormed = dnormed + dot(dpre, in_ref[:, cols], NT)
        hat, inverse = normalise(section[at, :])
        dnorm0 = dnorm0 + jnp.sum(dnormed * hat, axis=0, keepdims=True)
        dnorm1 = dnorm1 + jnp.sum(dnormed, axis=0, keepdims=True)
        dsection = normalise_back(dnormed * norm_ref[0:1], hat, inverse) + valid_rows(i) * grad
        grads[at, :] = dsection.astype(BF16)
        dout_b = dout_b + jnp.sum(dsection, axis=0, keepdims=True)
        dblend_ref[at, :] = dot(grads[at, :], out_ref[...], NT).astype(BF16)
        dskip_ref[at, :] = dot(grads[at, :], short_ref[...], NT)
        return dnorm0, dnorm1, dbias + jnp.concatenate(parts, axis=1), dout_b

    row = jnp.zeros((1, DIM), F32)
    dnorm0, dnorm1, dbias, dout_b = lax.fori_loop(0, steps, backward, (row, row, jnp.zeros((1, MLP), F32), row))
    dnorm_ref[...] = jnp.concatenate([dnorm0, dnorm1], axis=0)
    din_b_ref[...] = dbias
    dout_b_ref[...] = dout_b
    din_ref[...] = dot(low[...], dpres[...], TN)
    dout_ref[...] = dot(blend_ref[...], grads[...], TN)
    dshort_ref[...] = dot(skip_ref[...], grads[...], TN)


def mlp_both(share, res_ids, labels, skipped, blended, p):
    s = jax.ShapeDtypeStruct
    return pl.pallas_call(
        functools.partial(mlp_kernel, share),
        out_shape=(
            s((8, 128), F32), s((TOKENS, DIM), BF16), s((TOKENS, MB_CH), F32), s((MB_CH, DIM), F32),
            s((DIM, DIM), F32), s((1, DIM), F32), s((2, DIM), F32), s((DIM, MLP), F32), s((1, MLP), F32),
            s((8, MLP), F32), s((8, 1024), F32),
        ),
        in_specs=[SMEM_SPEC] * 2 + [VMEM_SPEC] * 13,
        out_specs=(VMEM_SPEC,) * 11,
        scratch_shapes=[
            pltpu.VMEM((TOKENS, DIM), F32),
            pltpu.VMEM((TOKENS, DIM), BF16),
            pltpu.VMEM((TOKENS, MLP), F32),
            pltpu.VMEM((TOKENS, MLP), BF16),
            pltpu.VMEM((TOKENS, DIM), BF16),
        ],
        compiler_params=params_of(),
        cost_estimate=cost(23),
        name="mlp_both",
    )(
        res_ids, labels, skipped, blended, p["at_short"], p["attn_out"], p["out_bias"], p["mlp_norm"], p["mlp_in"],
        p["mlp_in_bias"], p["mlp_out"], p["mlp_out_bias"], p["head_norm"], p["head_w"], p["head_bias"],
    )


def proj_back_kernel(
    res_ref, dq_ref, dk_ref, dv_ref, normed_ref, qkv_ref, dskip_ref, block_ref, pre_ref, act_ref, vec_ref,
    small_ref, proj_ref, short_ref, base_ref, down_ref, up_ref,
    dqkv_ref, dpre_ref, dblock_ref, dproj_ref, dshort_ref, dbase_ref, ddown_ref, ddown_b_ref, dup_ref, dup_b_ref,
    dpool_ref,
):
    limit = limit_of(res_ref)
    part = 96

    def tokens(i, carry):
        dpre0, dpre1 = carry
        at = pl.ds(pl.multiple_of(part * i, 16), part)
        grad = dot(dq_ref[at, :], qkv_ref[:, 0:DIM], NT)
        grad = grad + dot(dk_ref[at, :], qkv_ref[:, DIM : 2 * DIM], NT)
        grad = grad + dot(dv_ref[at, :], qkv_ref[:, 2 * DIM :], NT)
        dskip = 0.25 * dskip_ref[at, :]
        dpre1 = dpre1 + jnp.sum(grad, axis=0, keepdims=True)
        grad = 0.25 * grad
        dhat = grad * pre_ref[0:1]
        for group in range(4):
            places = pl.ds(pl.multiple_of(group * QUAD + part * i, 16), part)
            hat, inverse = normalise(block_ref[places, :])
            dpre0 = dpre0 + jnp.sum(grad * hat, axis=0, keepdims=True)
            dblock = normalise_back(dhat, hat, inverse) + dskip
            dblock_ref[places, :] = dblock.astype(BF16)
        return dpre0, dpre1

    row = jnp.zeros((1, MB_CH), F32)
    dpre0, dpre1 = lax.fori_loop(0, TOKENS // part, tokens, (row, row))
    dpre_ref[...] = jnp.concatenate([dpre0, dpre1], axis=0)
    for k, grad_ref in enumerate((dq_ref, dk_ref, dv_ref)):
        dqkv_ref[:, DIM * k : DIM * k + DIM] = dot(normed_ref[...], grad_ref[...], TN)
    dshort_ref[...] = dot(base_ref[...], dblock_ref[...], TN)[0:STEM_CH]
    dbase_ref[...] = dot(dblock_ref[...], short_ref[...], NT)
    excite = vec_ref[1:2]
    parts = []
    for j in range(CHUNKS):
        cols = slice(BLOCK * j, BLOCK * j + BLOCK)
        act = act_ref[:, cols].astype(F32)
        scaled = (act * excite[:, cols]).astype(BF16)
        dproj_ref[cols, :] = dot(scaled, dblock_ref[...], TN)
        dscaled = dot(dblock_ref[...], proj_ref[cols, :], NT)
        parts.append(jnp.sum(dscaled * act, axis=0, keepdims=True))
    dexcite = jnp.concatenate(parts, axis=1)
    dafter = dexcite * excite * (1.0 - excite)
    dup_b_ref[...] = dafter
    dup_ref[...] = dot(row8([small_ref[0:1]]), row8([dafter]), TN, precision=HIGH)
    dsqueeze = dot(row8([dafter]), up_ref[...].astype(F32), NT, precision=HIGH)[0:1]
    dbefore = dsqueeze * small_ref[1:2]
    ddown_b_ref[...] = dbefore
    ddown_ref[...] = dot(row8([vec_ref[0:1]]), row8([dbefore]), TN, precision=HIGH)
    dpool = dot(row8([dbefore]), down_ref[...].astype(F32), NT, precision=HIGH)
    dpool_ref[...] = dpool / valid_places(limit)


def proj_backward(res_ids, dq, dk, dv, normed, dskip, block, act, vec, small, base, p):
    s = jax.ShapeDtypeStruct
    return pl.pallas_call(
        proj_back_kernel,
        out_shape=(
            s((MB_CH, 3 * DIM), F32), s((2, MB_CH), F32), s((PLACES, MB_CH), BF16), s((EXPAND, MB_CH), F32),
            s((STEM_CH, MB_CH), F32), s((PLACES, 128), F32), s((EXPAND, SQUEEZE), F32), s((1, SQUEEZE), F32),
            s((SQUEEZE, EXPAND), F32), s((1, EXPAND), F32), s((8, EXPAND), F32),
        ),
        in_specs=[SMEM_SPEC] + [VMEM_SPEC] * 16,
        out_specs=(VMEM_SPEC,) * 11,
        compiler_params=params_of(),
        cost_estimate=cost(13),
        name="proj_backward",
    )(
        res_ids, dq, dk, dv, normed, p["qkv"], dskip, block, p["pre_norm"], act, vec, small, p["mb_proj"],
        p["mb_short"], base, p["se_down"], p["se_up"],
    )


def excite_back_kernel(dblock_ref, proj_ref, vec_ref, dpool_ref, slope_ref, x_ref, out_ref, sum_ref):
    excite, mean, inverse = vec_ref[1:2], vec_ref[2:3], vec_ref[3:4]
    dpool = dpool_ref[0:1]
    rows = 192

    def fold(v):
        total = v[0:8]
        for k in range(1, rows // 8):
            total = total + v[8 * k : 8 * k + 8]
        return total

    def step(i, sums):
        at = pl.ds(pl.multiple_of(rows * i, 16), rows)
        grad = dot(dblock_ref[at, :], proj_ref[...], NT) * excite + dpool
        grad = grad * slope_ref[at, :].astype(F32)
        out_ref[at, :] = grad.astype(BF16)
        hat = (x_ref[at, :] - mean) * inverse
        return sums[0] + fold(grad), sums[1] + fold(grad * hat)

    sums = lax.fori_loop(0, PLACES // rows, step, (jnp.zeros((8, BLOCK), F32),) * 2)
    sum_ref[...] = row8([jnp.sum(s, axis=0, keepdims=True) for s in sums])


def excite_backward(dblock, proj, vec, dpool, slope, depth):
    col = lambda rows: pl.BlockSpec((rows, BLOCK), lambda j: (0, j))
    return pl.pallas_call(
        excite_back_kernel,
        grid=(CHUNKS,),
        out_shape=(jax.ShapeDtypeStruct((PLACES, EXPAND), BF16), jax.ShapeDtypeStruct((8, EXPAND), F32)),
        in_specs=[
            pl.BlockSpec((PLACES, MB_CH), lambda j: (0, 0)),
            pl.BlockSpec((BLOCK, MB_CH), lambda j: (j, 0)),
            col(8), col(8), col(PLACES), col(PLACES),
        ],
        out_specs=(col(PLACES), col(8)),
        compiler_params=params_of(),
        cost_estimate=cost(12),
        name="excite_backward",
    )(dblock, proj, vec, dpool, slope, depth)


def depth_back_kernel(
    mask_ref, du_ref, x_ref, vec_ref, sum_ref, bgram_ref, base_ref, expand_ref, dwn_ref, depth_ref, act_ref, slope_ref,
    out_ref, cross_ref, ddepth_ref, sums_ref, pad,
):
    count = bgram_ref[64:65, 64:65]
    mean1, inverse1 = bn_stats(bgram_ref[...], expand_ref[...], count)
    mean2, inverse2 = vec_ref[2:3], vec_ref[3:4]
    c1 = sum_ref[0:1] / count
    c2 = sum_ref[1:2] / count
    scale2 = dwn_ref[0:1] * inverse2
    slant = scale2 * inverse2 * c2
    level = scale2 * c1 - slant * mean2
    zero = jnp.zeros((4, 1, HALF, BLOCK), F32)
    pad[:, 0:1] = zero
    pad[:, HALF + 1 : HALF + 2] = zero
    rows = 2 * HALF

    def fill(i, _):
        for group in range(4):
            at = pl.ds(pl.multiple_of(group * QUAD + rows * i, 16), rows)
            grad = scale2 * du_ref[at, :].astype(F32) - mask_ref[at, :] * (level + x_ref[at, :] * slant)
            for k in range(2):
                pad[group, 2 * i + k + 1] = grad[HALF * k : HALF * k + HALF]
        return 0

    lax.fori_loop(0, HALF // 2, fill, 0)

    def weight(dy, dx):
        return depth_ref[8 - 3 * dy - dx : 9 - 3 * dy - dx]

    def fold(v):
        return v[0:8] + v[8:16] + v[16:24]

    def step(k, sums):
        sums = list(sums)
        for py in range(2):
            places = [
                pl.ds(pl.multiple_of((2 * py + px) * QUAD + 2 * HALF * k, 16), 2 * HALF) for px in range(2)
            ]
            low_both, high_both = (act_ref[at, :].astype(F32) for at in places)
            made = [[], []]
            for half in range(2):
                up = 2 * k + half
                cut = slice(HALF * half, HALF * half + HALF)
                sources = [(1, -1), (0, 0), (1, 0)] if py == 0 else [(0, 0), (1, 0), (0, 1)]
                low_act, high_act = low_both[cut], high_both[cut]
                even = odd = None
                for t, (gy, off) in enumerate(sources):
                    left, right = pad[2 * gy, up + 1 + off], pad[2 * gy + 1, up + 1 + off]
                    before, after = shift_down(right), shift_up(left)
                    a = before * weight(t, 0) + left * weight(t, 1) + right * weight(t, 2)
                    b = left * weight(t, 0) + right * weight(t, 1) + after * weight(t, 2)
                    even = a if even is None else even + a
                    odd = b if odd is None else odd + b
                    for s, (a, b) in enumerate(((before, left), (left, right), (right, after))):
                        tap = 3 * (2 - t) + 2 - s
                        sums[tap] = sums[tap] + fold(low_act * a + high_act * b)
                made[0].append(even)
                made[1].append(odd)
            for px in range(2):
                grad = jnp.concatenate(made[px], axis=0) * slope_ref[places[px], :].astype(F32)
                out_ref[places[px], :] = grad.astype(BF16)
        return tuple(sums)

    sums = lax.fori_loop(0, HALF // 2, step, (jnp.zeros((8, BLOCK), F32),) * 9)
    ddepth_ref[...] = jnp.concatenate(
        [jnp.sum(s, axis=0, keepdims=True) for s in sums] + [jnp.zeros((7, BLOCK), F32)], axis=0
    )
    cross = dot(base_ref[...], out_ref[...], TN)
    cross_ref[...] = cross[0:72]
    first = cross[64:65]
    second = (jnp.sum(cross[0:64] * expand_ref[0:64, :].astype(F32), axis=0, keepdims=True) - mean1 * first) * inverse1
    sums_ref[...] = row8([second, first])


def depth_backward(mask, du, depth, vec, sums, bgram, base, expand_w, dw_norm, mb_depth, act, slope):
    col = lambda rows: pl.BlockSpec((rows, BLOCK), lambda j: (0, j))
    whole = lambda rows: pl.BlockSpec((rows, BLOCK), lambda j: (0, 0))
    s = jax.ShapeDtypeStruct
    return pl.pallas_call(
        depth_back_kernel,
        grid=(CHUNKS,),
        out_shape=(s((PLACES, EXPAND), BF16), s((72, EXPAND), F32), s((16, EXPAND), F32), s((8, EXPAND), F32)),
        in_specs=[
            whole(PLACES), col(PLACES), col(PLACES), col(8), col(8), whole(72), whole(PLACES), col(128), col(2),
            col(9), col(PLACES), col(PLACES),
        ],
        out_specs=(col(PLACES), col(72), col(16), col(8)),
        scratch_shapes=[pltpu.VMEM((4, HALF + 2, HALF, BLOCK), F32)],
        compiler_params=params_of(),
        cost_estimate=cost(35),
        name="depth_backward",
    )(mask, du, depth, vec, sums, bgram, base, expand_w, dw_norm, mb_depth, act, slope)


def stem_back_kernel(
    mask_ref, patch_ref, slope_ref, dbase_ref, du_ref, sum_ref, bgram_ref, base_ref, expand_ref, mid_ref, spread_ref,
    out_ref, total,
):
    count = bgram_ref[64:65, 64:65]
    mean, inverse = bn_stats(bgram_ref[...], expand_ref[...], count)
    second, first = sum_ref[0:1] / count, sum_ref[1:2] / count
    scale = mid_ref[0:1] * inverse
    slant = scale * inverse * second
    level = scale * first - slant * mean
    total[...] = jnp.zeros_like(total)
    rows = 256

    def step(i, _):
        at = pl.ds(pl.multiple_of(i * rows, rows), rows)
        x = dot(base_ref[at, :], expand_ref[...])
        inside = jnp.concatenate([mask_ref[at, :]] * CHUNKS, axis=1)
        grad = (scale * du_ref[at, :].astype(F32) - inside * (level + x * slant)).astype(BF16)
        grad = dot(grad, expand_ref[...], NT) + dbase_ref[at, :]
        grad = grad[:, 0:64] * (1.0 / 16.0)
        grad = jnp.concatenate([grad, grad], axis=1)
        grad = jnp.concatenate([grad, grad], axis=1)
        block = patch_ref[at, :]
        for j in range(4):
            cols = slice(256 * j, 256 * j + 256)
            wide = (slope_ref[at, cols].astype(F32) * grad).astype(BF16)
            total[:, cols] = total[:, cols] + dot(block, wide, TN)
        return 0

    lax.fori_loop(0, PLACES // rows, step, 0)
    merged = total[0:96, 0:256]
    for px in range(1, 4):
        merged = merged + total[64 * px : 64 * px + 96, 256 * px : 256 * px + 256]
    result = jnp.zeros((32, STEM_CH), F32)
    for pair in range(2):
        wide = dot(spread_ref[pair][0:96].astype(F32), merged[:, 128 * pair : 128 * pair + 128], TN, precision=HIGH)
        result = result + wide[0:32, 0:64] + wide[32:64, 64:128]
    ones = merged[27:28]
    ones = ones[:, 0:64] + ones[:, 64:128] + ones[:, 128:192] + ones[:, 192:256]
    at = lax.broadcasted_iota(jnp.int32, (32, STEM_CH), 0)
    out_ref[...] = jnp.where(at == 27, ones, result)


def stem_backward(mask, patches, slope, dbase, du, sums, bgram, base, expand_w, mid_norm, spread):
    return pl.pallas_call(
        stem_back_kernel,
        out_shape=jax.ShapeDtypeStruct((32, STEM_CH), F32),
        in_specs=[VMEM_SPEC] * 11,
        out_specs=VMEM_SPEC,
        scratch_shapes=[pltpu.VMEM((TAPS, 1024), F32)],
        compiler_params=params_of(),
        cost_estimate=cost(15),
        name="stem_backward",
    )(mask, patches, slope, dbase, du, sums, bgram, base, expand_w, mid_norm, spread)


def expand_finish_kernel(cross_ref, ddepth_ref, sum_ref, bgram_ref, expand_ref, mid_ref, out_ref, square_ref, flat, hold):
    count = bgram_ref[64:65, 64:65]
    square_of = jnp.concatenate([bgram_ref[...], jnp.zeros((56, 128), F32)], axis=0)
    weights = expand_ref[...].astype(F32)
    product = dot(square_of, weights, precision=HIGH)
    mean = product[64:65] / count
    variance = jnp.sum(weights * product, axis=0, keepdims=True) / count - mean * mean
    inverse = lax.rsqrt(variance + EPS)
    second, first = sum_ref[0:1] / count, sum_ref[1:2] / count
    plain = bgram_ref[0:64, 64:65]
    hat = (product[0:64] - mean * plain) * inverse
    hold[...] = mid_ref[0:1] * inverse * (cross_ref[0:64, :] - first * plain - second * hat)
    flat[...] = jnp.zeros_like(flat)
    for name, source in (("mb_expand", hold), ("mb_depth", ddepth_ref)):
        offset, (rows, width) = OFFSETS[name]
        put_matrix(flat, lambda r, t: source[r, 128 * t : 128 * t + 128], 0, offset, rows, width)
    out_ref[...] = flat[0:EARLY_ROWS, :]
    total = flat[0:EARLY_ROWS, :]
    square_ref[...] = jnp.broadcast_to(jnp.sum(total * total).reshape(1, 1), (8, 128))


def expand_finish(cross, ddepth, sums, bgram, expand_w, mid_norm):
    return pl.pallas_call(
        expand_finish_kernel,
        out_shape=(jax.ShapeDtypeStruct((EARLY_ROWS, 128), F32), jax.ShapeDtypeStruct((8, 128), F32)),
        in_specs=[VMEM_SPEC] * 6,
        out_specs=(VMEM_SPEC,) * 2,
        scratch_shapes=[pltpu.VMEM((EARLY_ROWS + 8, 128), F32), pltpu.VMEM((STEM_CH, EXPAND), F32)],
        compiler_params=params_of(),
        cost_estimate=cost(3),
        name="expand_finish",
    )(cross, ddepth, sums, bgram, expand_w, mid_norm)


def stem_finish_kernel(grad_ref, gram_ref, stem_w_ref, norm_ref, spread_ref, out_ref, norm_out_ref, big):
    spread_weights(spread_ref, stem_w_ref[...], big, 2)
    weights = stem_w_ref[...]
    gram = gram_ref[...][:, :96]
    mean, square = stem_stats(gram_ref[...], big[0:96, 0:256])
    inverse = lax.rsqrt(square - mean * mean + EPS)
    count = 4.0 * gram_ref[27:28, 27:28]
    product = dot(gram, big[0:96, 0:256].astype(F32), precision=HIGH)
    cross = jnp.zeros((32, STEM_CH), F32)
    plain = jnp.zeros((32, STEM_CH), F32)
    sums = jnp.broadcast_to(gram[:, 27:28], (96, 128))
    for pair in range(2):
        spread = spread_ref[pair][0:96].astype(F32)
        wide = dot(spread, product[:, 128 * pair : 128 * pair + 128], TN, precision=HIGH)
        cross = cross + wide[0:32, 0:64] + wide[32:64, 64:128]
        wide = dot(spread, sums, TN, precision=HIGH)
        plain = plain + wide[0:32, 0:64] + wide[32:64, 0:64]
    at = lax.broadcasted_iota(jnp.int32, (32, STEM_CH), 0)
    taps = at < 27
    grad = jnp.where(taps, grad_ref[...], 0.0)
    first = grad_ref[27:28]
    second = (jnp.sum(grad * weights, axis=0, keepdims=True) - mean * first) * inverse
    hat = (cross - mean * plain) * inverse
    result = norm_ref[0:1] * inverse * (grad - (plain * first + hat * second) / count)
    out_ref[...] = jnp.where(taps, result, 0.0)
    norm_out_ref[...] = jnp.concatenate([second, first], axis=0)


def stem_finish(grad, gram, stem_w, norm, spread):
    return pl.pallas_call(
        stem_finish_kernel,
        out_shape=(jax.ShapeDtypeStruct((32, STEM_CH), F32), jax.ShapeDtypeStruct((2, STEM_CH), F32)),
        in_specs=[VMEM_SPEC] * 5,
        out_specs=(VMEM_SPEC,) * 2,
        scratch_shapes=[pltpu.VMEM((TAPS, 256), BF16)],
        compiler_params=params_of(),
        cost_estimate=cost(3),
        name="stem_finish",
    )(grad, gram, stem_w, norm, spread)


def levels_of(devices):
    levels = []
    stride = 1
    while stride < devices:
        radix = 2 if stride == 1 or devices // stride == 2 else 4
        levels.append((stride, radix))
        stride *= radix
    return levels


def pairs_of(devices, mask):
    return [(i, i ^ mask) for i in range(devices)]


def exchange(v, devices, wide=True):
    if devices & (devices - 1):
        return lax.psum(v, "dp")
    levels = levels_of(devices)
    if not wide:
        levels = [(1 << k, 2) for k in range(devices.bit_length() - 1)]
    for stride, radix in levels:
        moved = [lax.ppermute(v, "dp", pairs_of(devices, stride * j)) for j in range(1, radix)]
        if radix == 2:
            v = v + moved[0]
        else:
            v = (v + moved[0]) + (moved[1] + moved[2])
    return v


def take(blocks, digit, axis):
    return lax.dynamic_index_in_dim(blocks, digit, axis, keepdims=False)


def scatter_sum(keep, send, devices, me, low, high):
    levels = levels_of(devices)
    terms = [keep, lax.ppermute(send, "dp", pairs_of(devices, 1))]
    for stride, radix in levels[1:]:
        digit = (me // stride) % radix
        top = stride * radix == devices
        if top:
            blocks = [t.reshape((high - low,) + t.shape[-2:]) for t in terms]
            part = lambda d: sum(take(b, jnp.clip(d - low, 0, high - low - 1), 0) for b in blocks)
        else:
            blocks = [t.reshape((-1, radix) + t.shape[-2:]) for t in terms]
            part = lambda d: sum(take(b, d, 1) for b in blocks)
        moved = []
        for j in range(1, radix):
            pairs = pairs_of(devices, stride * j)
            if top:
                pairs = [(a, b) for a, b in pairs if low <= b // stride < high]
            moved.append(lax.ppermute(part(digit ^ j), "dp", pairs))
        mine = part(digit)
        if top:
            mine = jnp.where((digit >= low) & (digit < high), mine, 0.0)
        total = mine
        for m in moved:
            total = total + m
        terms = [total]
    return terms[0].reshape(terms[0].shape[-2:])


def round_up(n, m):
    return -(-n // m) * m


def on_device(images, res_ids, labels, rel_index, master, first_moment, second_moment, ema_weights):
    devices = lax.axis_size("dp")
    me = lax.axis_index("dp").astype(jnp.int32)
    length = master.shape[0]
    rows = length // 128
    held = round_up(rows, 16)
    images_total = res_ids.shape[0] * devices

    low_master = lax.optimization_barrier(master.astype(BF16).reshape(rows, 128))
    gathered = lax.all_gather(jnp.pad(low_master, ((0, held - rows), (0, 0))), "dp", axis=0, tiled=True)
    early = lax.dynamic_update_slice(
        jnp.zeros((EARLY_ROWS + rows, 128), BF16), low_master, (jnp.minimum(me * rows, EARLY_ROWS), 0)
    )[:EARLY_ROWS]

    patches, gram, mask = make_patches(res_ids, images)
    packet = exchange(jnp.concatenate([gram, early[:16].astype(F32)], axis=0), devices)
    gram = packet[:96]
    stem_flat = packet[96 : 96 + STEM_ROWS].reshape(-1)
    e = unpack(exchange(early, devices, wide=False), 1, EARLY_ROWS, EARLY_SHAPES)

    spread = jnp.asarray(spread_taps(), BF16)
    stem_w = jnp.pad(stem_flat[: 27 * STEM_CH].reshape(27, STEM_CH), ((0, 5), (0, 0)))
    stem_norm = stem_flat[27 * STEM_CH : STEM_END].reshape(2, STEM_CH)
    base, stem_slope, bgram = stem_forward(patches, gram, stem_w, stem_norm, spread)
    bgram = exchange(bgram, devices)
    depth, act1, slope1, stat = depth_forward(
        mask, base, e["mb_expand"], bgram, e["mid_norm"], e["mb_depth"]
    )
    stat = exchange(stat[:2].reshape(12, 128), devices).reshape(2, EXPAND)

    p = unpack(gathered, devices, rows, LATE_SHAPES)
    p["dw_norm"] = e["dw_norm"]
    p["mb_short"] = e["mb_short"]
    slots = slots_of(rel_index)
    slots = jnp.pad(slots, ((0, 1), (0, 1)), constant_values=2 * WIDE - 1).reshape(2 * WIDE, 1)
    pick = squeeze_lanes()
    pick, pick_back = jnp.asarray(pick, BF16), jnp.asarray(pick.T, BF16)
    bias = build_bias(p["rel_table"], slots, pick)

    act2, slope2, block, skipped, normed, project, vec, small = excite_forward(res_ids, mask, depth, stat, bgram, base, p)
    blended, weights = attend_forward(res_ids, project, bias)
    loss, dblend, dskip, g_short, g_out, g_out_b, g_mnorm, g_in, g_in_b, vectors, few = mlp_both(
        1.0 / images_total, res_ids, labels, skipped, blended, p
    )

    core = (me % 2).reshape(1)
    top_radix = levels_of(devices)[-1][1]

    def scattered(grads, begin, end):
        span = devices // top_radix
        low = begin // length // span
        high = (end - 1) // length // span + 1
        keep, send = pack(core, grads, low * span * rows, (high - low) * span, rows, held)
        return scatter_sum(keep, send, devices, me, low, high)

    middle = scattered(
        {"mlp_norm": g_mnorm, "mlp_in": g_in, "mlp_in_bias": g_in_b},
        OFFSETS["mlp_norm"][0], OFFSETS["mlp_out"][0],
    )
    vectors = lax.all_gather(vectors, "dp", axis=0, tiled=False)

    dq, dk, dv, dbias = attend_backward(project, blended, dblend, weights)
    g_qkv, g_pre, dblock, g_proj, g_mbshort, dbase, g_down, g_down_b, g_up, g_up_b, dpool = proj_backward(
        res_ids, dq, dk, dv, normed, dskip, block, act2, vec, small, base, p
    )
    du, sums = excite_backward(dblock, p["mb_proj"], vec, dpool, slope2, depth)
    sums = exchange(jnp.concatenate([sums[:2].reshape(12, 128), few[:4].reshape(32, 128)], axis=0), devices)
    few = sums[12:].reshape(4, 1024)
    dw_sums = sums[:12].reshape(2, EXPAND)
    g_table = bias_back(dbias, slots, pick_back)
    late = scattered(
        {
            "mb_short": g_mbshort, "se_down": g_down, "se_down_bias": g_down_b, "se_up": g_up, "se_up_bias": g_up_b,
            "mb_proj": g_proj, "at_short": g_short, "pre_norm": g_pre, "qkv": g_qkv, "attn_out": g_out,
            "out_bias": g_out_b, "rel_table": g_table,
        },
        OFFSETS["mb_short"][0], OFFSETS["mlp_norm"][0],
    )
    du, cross, g_depth, sums = depth_backward(
        mask, du, depth, vec, dw_sums, bgram, base, e["mb_expand"], e["dw_norm"], e["mb_depth"], act1, slope1
    )
    mid_sums = exchange(sums[:2].reshape(12, 128), devices).reshape(2, EXPAND)
    early_grad = exchange(jnp.concatenate([cross, g_depth], axis=0), devices, wide=False)
    g_norms = jnp.concatenate([mid_sums, dw_sums[1:2], dw_sums[0:1]], axis=0)

    def tall(name, unit):
        return round_up(round_up(length, OFFSETS[name][1][1]) // OFFSETS[name][1][1] + 1, unit)

    def padded(v, name, unit):
        edge = tall(name, unit)
        group = min(devices, 128)
        v = v.reshape(devices // group, group, v.shape[1]).transpose(0, 2, 1)
        return jnp.pad(v, ((0, 0), (edge, edge), (0, 0)))

    shard, square = shard_parts(
        me.reshape(1), length, late, middle, few,
        padded(vectors[:, 0, :], "mlp_out", 8), vectors[:, 1, :DIM],
        padded(vectors[:, 2, :DIM], "head_w", 16), vectors[:, 3, :1024], g_norms,
    )

    stem = stem_backward(
        mask, patches, stem_slope, dbase, du, mid_sums, bgram, base, e["mb_expand"], e["mid_norm"], spread
    )
    early_grad, early_square = expand_finish(
        early_grad[:72], early_grad[72:], mid_sums, bgram, e["mb_expand"], e["mid_norm"]
    )
    square = square[0, 0]
    lane = lax.broadcasted_iota(jnp.int32, (8, 128), 1)
    scalars = jnp.where(lane == 0, loss, jnp.where(lane == 1, square, 0.0))
    packet = exchange(jnp.concatenate([stem.reshape(16, 128), scalars], axis=0), devices)
    loss_sum = packet[16, 0]
    square = packet[16, 1]
    g_stem, g_stem_norm = stem_finish(packet[:16].reshape(32, STEM_CH), gram, stem_w, stem_norm, spread)
    grad_norm = jnp.sqrt(square + early_square[0, 0] + jnp.sum(g_stem * g_stem) + jnp.sum(g_stem_norm * g_stem_norm))
    stem_grad = jnp.concatenate([g_stem[:27], g_stem_norm, jnp.zeros((1, STEM_CH), F32)], axis=0).reshape(15, 128)
    early_grad = jnp.pad(early_grad, ((0, rows), (0, 0))) + jnp.pad(stem_grad, ((0, EARLY_ROWS + rows - 15), (0, 0)))
    shard = shard + lax.dynamic_slice(early_grad, (jnp.minimum(me * rows, EARLY_ROWS), 0), (rows, 128))
    shard = shard.reshape(length)
    clipped = shard * (CLIP / jnp.maximum(grad_norm, CLIP))
    moment_one = BETA_ONE * first_moment + (1.0 - BETA_ONE) * clipped
    moment_two = BETA_TWO * second_moment + (1.0 - BETA_TWO) * clipped * clipped
    update = (
        moment_one
        / (1.0 - BETA_ONE**STEP)
        / (jnp.sqrt(moment_two / (1.0 - BETA_TWO**STEP)) + ADAM_EPS)
    )
    weights_out = master - RATE * (update + DECAY * master)
    averaged = EMA_DECAY * ema_weights + (1.0 - EMA_DECAY) * weights_out
    return (
        loss_sum,
        grad_norm,
        weights_out,
        moment_one,
        moment_two,
        averaged,
        weights_out.astype(BF16),
    )


def solution(mesh):
    in_specs = (
        P("dp", None, None, None),
        P("dp"),
        P("dp"),
        P(),
        P("dp"),
        P("dp"),
        P("dp"),
        P("dp"),
    )
    out_specs = (P(), P(), P("dp"), P("dp"), P("dp"), P("dp"), P("dp"))
    return jax.shard_map(
        on_device, mesh=mesh, in_specs=in_specs, out_specs=out_specs, check_vma=False
    )
```

```python
import functools
import math

import jax
import jax.numpy as jnp
import numpy as np
from jax import lax
from jax.experimental import pallas as pl
from jax.experimental.pallas import tpu as pltpu
from jax.sharding import PartitionSpec as P

STEM_CH = 64
MB_CH = 192
EXPAND = 768
SQUEEZE = 48
DIM = 384
HEADS = 12
HEAD_DIM = 32
MLP = 1536
CLASSES = 1000
CANVAS = 384
SMALL_RES = 224
STEP = 10

EPS = 1e-05
CLIP = 0.05
BETA_ONE = 0.5
BETA_TWO = 0.5
ADAM_EPS = 1e-08
RATE = 0.05
DECAY = 0.05
EMA_DECAY = 0.9
SMOOTH = 0.1

SIDE = CANVAS // 8
SMALL_SIDE = SMALL_RES // 8
HALF = SIDE // 2
QUAD = HALF * HALF
PLACES = SIDE * SIDE
TAPS = 288
BLOCK = 128
CHUNKS = EXPAND // BLOCK
WIDE = 2 * HALF * HALF
TOKENS = QUAD

F32 = jnp.float32
BF16 = jnp.bfloat16
HIGH = lax.Precision.HIGHEST
VMEM_MAX = 56 * 1024 * 1024
GELU_A = math.sqrt(2.0 / math.pi)
GELU_B = 0.044715


def layout():
    table_slots = (2 * (CANVAS // 16) - 1) ** 2
    return [
        ("stem_w", (3, 3, 3, STEM_CH)),
        ("stem_norm", (2, STEM_CH)),
        ("mb_short", (STEM_CH, MB_CH)),
        ("mb_expand", (STEM_CH, EXPAND)),
        ("mid_norm", (2, EXPAND)),
        ("mb_depth", (9, EXPAND)),
        ("dw_norm", (2, EXPAND)),
        ("se_down", (EXPAND, SQUEEZE)),
        ("se_down_bias", (SQUEEZE,)),
        ("se_up", (SQUEEZE, EXPAND)),
        ("se_up_bias", (EXPAND,)),
        ("mb_proj", (EXPAND, MB_CH)),
        ("at_short", (MB_CH, DIM)),
        ("pre_norm", (2, MB_CH)),
        ("qkv", (MB_CH, 3 * DIM)),
        ("attn_out", (DIM, DIM)),
        ("out_bias", (DIM,)),
        ("rel_table", (HEADS, table_slots)),
        ("mlp_norm", (2, DIM)),
        ("mlp_in", (DIM, MLP)),
        ("mlp_in_bias", (MLP,)),
        ("mlp_out", (MLP, DIM)),
        ("mlp_out_bias", (DIM,)),
        ("head_norm", (2, DIM)),
        ("head_w", (DIM, CLASSES)),
        ("head_bias", (CLASSES,)),
    ]


def offsets():
    table = {}
    offset = 0
    for name, shape in layout():
        table[name] = (offset, shape)
        offset += math.prod(shape)
    return table


OFFSETS = offsets()
STEM_END = OFFSETS["mb_short"][0]
EARLY_END = OFFSETS["se_down"][0]


def dot(a, b, dims=((1,), (0,)), precision=None):
    return lax.dot_general(a, b, (dims, ((), ())), precision=precision, preferred_element_type=F32)


NT = ((1,), (1,))
TN = ((0,), (0,))


def gelu_pair(u):
    sq = u * u
    t = jnp.tanh(u * (GELU_A + (GELU_A * GELU_B) * sq))
    half = 0.5 + 0.5 * t
    slope = half + (0.5 * u) * (1.0 - t * t) * (GELU_A + (3.0 * GELU_A * GELU_B) * sq)
    return u * half, slope


def gelu(u):
    sq = u * u
    t = jnp.tanh(u * (GELU_A + (GELU_A * GELU_B) * sq))
    return u * (0.5 + 0.5 * t)


def limit_of(res_ref):
    return jnp.where(res_ref[0] == 1, SIDE, SMALL_SIDE)


def group_mask(group, limit, first_row, rows, lanes):
    place = lax.broadcasted_iota(jnp.int32, (rows, lanes), 0) + first_row
    up = place // HALF
    across = place - up * HALF
    y = 2 * up + group // 2
    x = 2 * across + group % 2
    return jnp.where((y < limit) & (x < limit), 1.0, 0.0)


def cost(us):
    return pl.CostEstimate(flops=int(us * 0.005e9), bytes_accessed=1000, transcendentals=0)


def params_of(limit=VMEM_MAX):
    return pltpu.CompilerParams(vmem_limit_bytes=limit)


SMEM_SPEC = pl.BlockSpec(memory_space=pltpu.SMEM)
VMEM_SPEC = pl.BlockSpec(memory_space=pltpu.VMEM)


def patch_kernel(res_ref, img_ref, patch_ref, gram_ref, mask_ref):
    limit = limit_of(res_ref)
    lane = lax.broadcasted_iota(jnp.int32, (32, CANVAS), 1)
    rem = lane % 8
    row = lax.broadcasted_iota(jnp.int32, (SIDE, CANVAS), 0)
    col = lax.broadcasted_iota(jnp.int32, (SIDE, CANVAS), 1)
    wanted = jnp.where(row < HALF, 2 * row, 2 * (row - HALF) + 1)
    pick = jnp.where(col // 8 == wanted, 1.0, 0.0).astype(BF16)
    sub = lax.broadcasted_iota(jnp.int32, (8, CANVAS), 0)
    tap = lax.broadcasted_iota(jnp.int32, (2 * HALF, TAPS), 1)
    ones_at = (tap % 64 == 27) & (tap < 256)

    def step(i, _):
        bands = [[], [], [], []]
        above = []
        for c in range(3):
            before = img_ref[0, c, pl.ds(pl.multiple_of(jnp.maximum(32 * i - 16, 0), 16), 16), :]
            above.append(jnp.where(i > 0, before.astype(F32)[8:16], 0.0))
            for q in range(2):
                band = img_ref[0, c, pl.ds(pl.multiple_of(32 * i + 16 * q, 16), 16), :].astype(F32)
                bands[2 * q].append(band[0:8])
                bands[2 * q + 1].append(band[8:16])
        made = []
        for q in range(4):
            prev = above if q == 0 else bands[q - 1]
            edge = jnp.zeros((8, CANVAS), F32)
            for c in range(3):
                edge = jnp.where(sub == c, prev[c][7:8], edge)
            rows = jnp.concatenate(bands[q] + [edge], axis=0)
            rolled = pltpu.roll(rows, 8, 1)
            pieces = [jnp.where((rem == 7) & (lane >= 8), rolled, 0.0)]
            pieces += [jnp.where(rem == r, rows, 0.0) for r in range(8)]
            wide = jnp.concatenate(pieces, axis=0).astype(BF16)
            made.append(dot(pick, wide, NT))
        for py in range(2):
            for px in range(2):
                group = 2 * py + px
                two = jnp.concatenate(
                    [made[py][HALF * px : HALF * px + HALF], made[2 + py][HALF * px : HALF * px + HALF]],
                    axis=0,
                )
                inside = group_mask(group, limit, 2 * HALF * i, 2 * HALF, 128)
                mask_ref[pl.ds(pl.multiple_of(group * QUAD + 2 * HALF * i, 16), 2 * HALF), :] = inside
                two = jnp.where(ones_at, 1.0, two) * inside[:, 0:1]
                patch_ref[pl.ds(pl.multiple_of(group * QUAD + 2 * HALF * i, 16), 2 * HALF), :] = (
                    two.astype(BF16)
                )
        return 0

    lax.fori_loop(0, HALF // 2, step, 0)
    patches = patch_ref[...]
    gram = dot(patches, patches, TN)
    total = gram[0:96, 0:96]
    for px in range(1, 4):
        total = total + gram[64 * px : 64 * px + 96, 64 * px : 64 * px + 96]
    gram_ref[...] = jnp.concatenate([total, jnp.zeros((96, 32), F32)], axis=1)


def make_patches(res_ids, images):
    return pl.pallas_call(
        patch_kernel,
        out_shape=(
            jax.ShapeDtypeStruct((PLACES, TAPS), BF16),
            jax.ShapeDtypeStruct((96, 128), F32),
            jax.ShapeDtypeStruct((PLACES, 128), F32),
        ),
        in_specs=[SMEM_SPEC, VMEM_SPEC],
        out_specs=(VMEM_SPEC,) * 3,
        compiler_params=params_of(),
        cost_estimate=cost(8),
        name="patches",
    )(res_ids, images)


def spread_taps():
    table = np.zeros((8, TAPS, 64), np.float32)
    for px in range(4):
        for py in range(4):
            pair, half = px * 2 + py // 2, py % 2
            for dy in range(3):
                for dx in range(3):
                    for c in range(3):
                        ry = 2 * py + dy - 1
                        r = 24 + c if ry < 0 else 8 * c + ry
                        k = (2 * px + dx) * 32 + r
                        table[pair, k, half * 32 + (dy * 3 + dx) * 3 + c] = 1.0
    return table


def spread_weights(spread_ref, stem_w, out_ref, pairs=8):
    zero = jnp.zeros((32, STEM_CH), F32)
    double = jnp.concatenate(
        [jnp.concatenate([stem_w, zero], axis=1), jnp.concatenate([zero, stem_w], axis=1)], axis=0
    ).astype(BF16)
    for pair in range(pairs):
        out_ref[:, 128 * pair : 128 * pair + 128] = dot(spread_ref[pair], double).astype(BF16)


def stem_stats(gram, first_phases):
    weights = first_phases.astype(F32)
    product = dot(gram[:, :96], weights, precision=HIGH)
    second = jnp.sum(weights * product, axis=0, keepdims=True)
    first = product[27:28]
    count = 4.0 * gram[27:28, 27:28]
    both = jnp.concatenate([first, second, jnp.zeros((6, 256), F32)], axis=0)
    folded = both[:, 0:64] + both[:, 64:128] + both[:, 128:192] + both[:, 192:256]
    return folded[0:1] / count, folded[1:2] / count


def stem_kernel(patch_ref, gram_ref, stem_w_ref, norm_ref, spread_ref, base_ref, slope_ref, bgram_ref, big):
    spread_weights(spread_ref, stem_w_ref[...], big)
    mean, square = stem_stats(gram_ref[...], big[0:96, 0:256])
    inverse = lax.rsqrt(square - mean * mean + EPS)
    gain = norm_ref[0:1] * inverse
    shift = norm_ref[1:2] - mean * gain
    gain = jnp.concatenate([gain] * 4, axis=1)
    shift = jnp.concatenate([shift] * 4, axis=1)
    rows = 768
    lane = lax.broadcasted_iota(jnp.int32, (rows, 128), 1)

    def step(i, _):
        at = pl.ds(pl.multiple_of(i * rows, rows), rows)
        block = patch_ref[at, :]
        pooled = jnp.zeros((rows, 128), F32)
        for j in range(4):
            u = dot(block, big[:, 256 * j : 256 * j + 256]) * gain + shift
            value, slope = gelu_pair(u)
            slope_ref[at, 256 * j : 256 * j + 256] = slope.astype(BF16)
            pooled = pooled + value[:, 0:128] + value[:, 128:256]
        pooled = (pooled + pltpu.roll(pooled, 64, 1)) * (1.0 / 16.0)
        ones = block[:, 0:128].astype(F32)
        ones = pltpu.roll(ones, 64 - 27, 1)
        pooled = jnp.where(lane < 64, pooled, jnp.where(lane == 64, ones, 0.0))
        base_ref[at, :] = pooled.astype(BF16)
        return 0

    lax.fori_loop(0, PLACES // rows, step, 0)
    base = base_ref[...]
    masked = (base.astype(F32) * base[:, 64:65].astype(F32)).astype(BF16)
    bgram_ref[...] = dot(masked, base, TN)[0:72]


def stem_forward(patches, gram, stem_w, norm, spread):
    return pl.pallas_call(
        stem_kernel,
        out_shape=(
            jax.ShapeDtypeStruct((PLACES, 128), BF16),
            jax.ShapeDtypeStruct((PLACES, 1024), BF16),
            jax.ShapeDtypeStruct((72, 128), F32),
        ),
        in_specs=[VMEM_SPEC] * 5,
        out_specs=(VMEM_SPEC,) * 3,
        scratch_shapes=[pltpu.VMEM((TAPS, 1024), BF16)],
        compiler_params=params_of(),
        cost_estimate=cost(10),
        name="stem_forward",
    )(patches, gram, stem_w, norm, spread)


def taps_row(load, weight, py):
    sources = [(1, -1), (0, 0), (1, 0)] if py == 0 else [(0, 0), (1, 0), (0, 1)]
    rows = [[load(2 * gy + px, off) for px in range(2)] for gy, off in sources]

    def column(px, dx):
        total = rows[0][px] * weight(0, dx)
        total = total + rows[1][px] * weight(1, dx)
        return total + rows[2][px] * weight(2, dx)

    even = column(0, 1) + column(1, 2) + shift_down(column(1, 0))
    odd = column(1, 1) + column(0, 0) + shift_up(column(0, 2))
    return even, odd


def shift_down(v):
    at = lax.broadcasted_iota(jnp.int32, v.shape, 0)
    return jnp.where(at == 0, 0.0, pltpu.roll(v, 1, 0))


def shift_up(v):
    at = lax.broadcasted_iota(jnp.int32, v.shape, 0)
    return jnp.where(at == HALF - 1, 0.0, pltpu.roll(v, HALF - 1, 0))


def bn_stats(bgram, expand_w, count):
    weights = expand_w.astype(F32)
    square_of = jnp.concatenate([bgram, jnp.zeros((56, 128), F32)], axis=0)
    product = dot(square_of, weights, precision=HIGH)
    mean = product[64:65] / count
    second = jnp.sum(weights * product, axis=0, keepdims=True) / count
    return mean, lax.rsqrt(second - mean * mean + EPS)


def depth_kernel(mask_ref, base_ref, expand_ref, bgram_ref, norm_ref, depth_ref, out_ref, act_ref, slope_ref, stat_ref, pad, wide):
    count = bgram_ref[64:65, 64:65]
    mean, inverse = bn_stats(bgram_ref[...], expand_ref[...], count)
    gain = norm_ref[0:1] * inverse
    shift = norm_ref[1:2] - mean * gain
    zero = jnp.zeros((4, 1, HALF, BLOCK), F32)
    pad[:, 0:1] = zero
    pad[:, HALF + 1 : HALF + 2] = zero
    wide[...] = dot(base_ref[...], expand_ref[...])
    rows = 8 * HALF
    for group in range(4):

        def fill(i, _, group=group):
            first = pl.multiple_of(group * QUAD + rows * i, 16)
            at = pl.ds(first, rows)
            x = wide[at, :]
            inside = mask_ref[at, :]
            value, slope = gelu_pair(x * gain + shift)
            value = value * inside
            act_ref[at, :] = value.astype(BF16)
            slope_ref[at, :] = (slope * inside).astype(BF16)
            for k in range(8):
                pad[group, 8 * i + k + 1] = value[HALF * k : HALF * k + HALF]
            return 0

        lax.fori_loop(0, QUAD // rows, fill, 0)

    def weight(dy, dx):
        return depth_ref[3 * dy + dx : 3 * dy + dx + 1]

    def fold(v):
        return v[0:8] + v[8:16] + v[16:24]

    def step(up, sums):
        first, second = sums
        for py in range(2):
            made = taps_row(lambda g, off: pad[g, up + 1 + off], weight, py)
            for px in range(2):
                at = pl.ds(pl.multiple_of((2 * py + px) * QUAD + HALF * up, 8), HALF)
                x = made[px] * mask_ref[at, :]
                out_ref[at, :] = x
                first = first + fold(x)
                second = second + fold(x * x)
        return first, second

    sums = lax.fori_loop(0, HALF, step, (jnp.zeros((8, BLOCK), F32),) * 2)
    rows_out = [jnp.sum(s, axis=0, keepdims=True) for s in sums]
    stat_ref[...] = jnp.concatenate(rows_out + [jnp.zeros((6, BLOCK), F32)], axis=0)


def depth_forward(mask, base, expand_w, bgram, mid_norm, mb_depth):
    col = lambda rows: pl.BlockSpec((rows, BLOCK), lambda j: (0, j))
    whole = lambda rows: pl.BlockSpec((rows, BLOCK), lambda j: (0, 0))
    return pl.pallas_call(
        depth_kernel,
        grid=(CHUNKS,),
        out_shape=(
            jax.ShapeDtypeStruct((PLACES, EXPAND), F32),
            jax.ShapeDtypeStruct((PLACES, EXPAND), BF16),
            jax.ShapeDtypeStruct((PLACES, EXPAND), BF16),
            jax.ShapeDtypeStruct((8, EXPAND), F32),
        ),
        in_specs=[whole(PLACES), whole(PLACES), col(128), whole(72), col(2), col(9)],
        out_specs=(col(PLACES),) * 3 + (col(8),),
        scratch_shapes=[pltpu.VMEM((4, HALF + 2, HALF, BLOCK), F32), pltpu.VMEM((PLACES, BLOCK), F32)],
        compiler_params=params_of(),
        cost_estimate=cost(25),
        name="depth_forward",
    )(mask, base, expand_w, bgram, mid_norm, mb_depth)


EARLY_ROWS = 576
STEM_ROWS = 15


def runs_of(offset, rows, width):
    period = min(128 // math.gcd(width, 128), rows)
    stride = period * width // 128 if rows > period else 1
    for j in range(period):
        start = offset + j * width
        yield j, period, start // 128, start % 128, -(-(rows - j) // period), stride


def rows_at(first, count, stride):
    return pl.ds(first, count) if stride == 1 or count == 1 else pl.ds(first, count, stride=stride)


def chunks_of(count, size=128):
    for begin in range(0, count, size):
        yield begin, min(size, count - begin)


def round_up(n, m):
    return -(-n // m) * m


def take_matrix(flat, out_ref, hold, offset, rows, width):
    direct = True
    for j, period, first, shift, count, stride in runs_of(offset, rows, width):
        direct = period == 1
        for t in range(-(-width // 128)):
            wide = min(128, width - 128 * t)
            for begin, size in chunks_of(count):
                at = first + t + begin * stride
                value = flat[rows_at(at, size, stride), :]
                if shift:
                    if shift + wide > 128:
                        lane = lax.broadcasted_iota(jnp.int32, (size, 128), 1)
                        value = jnp.where(lane >= shift, value, flat[rows_at(at + 1, size, stride), :])
                    value = pltpu.roll(value, 128 - shift, 1)
                if direct:
                    out_ref[begin : begin + size, 128 * t : 128 * t + wide] = value[:, :wide].astype(out_ref.dtype)
                elif count == 1:
                    out_ref[j : j + 1, 128 * t : 128 * t + wide] = value[:, :wide].astype(out_ref.dtype)
                else:
                    hold[t, rows_at(j + begin * period, size, period), :] = value
    if not direct and count > 1:
        for t in range(-(-width // 128)):
            wide = min(128, width - 128 * t)
            out_ref[0:rows, 128 * t : 128 * t + wide] = hold[t, 0:rows, 0:wide].astype(out_ref.dtype)


def put_matrix(flat, value_of, base, offset, rows, width):
    for j, period, first, shift, count, stride in runs_of(offset, rows, width):
        tiles = -(-width // 128)
        for begin, size in chunks_of(count):
            before = None
            lane = lax.broadcasted_iota(jnp.int32, (size, 128), 1)
            picked = rows_at(j + begin * period, size, period)
            at = first - base + begin * stride
            for t in range(tiles):
                value = value_of(picked, t)
                if shift:
                    value = pltpu.roll(value, shift, 1)
                    mixed = jnp.where(lane >= shift, value, 0.0 if before is None else before)
                else:
                    mixed = value
                before = value
                where = rows_at(at + t, size, stride)
                full = 0 < t < tiles - 1 or (shift == 0 and width % 128 == 0)
                flat[where, :] = mixed if full else flat[where, :] + mixed
            if shift:
                where = rows_at(at + tiles, size, stride)
                flat[where, :] = flat[where, :] + jnp.where(lane < shift, before, 0.0)


def unpack_kernel(names, shapes, pieces, shard_rows, ids_ref, *refs):
    blocks, outs, (flat, hold) = refs[:pieces], refs[pieces:-2], refs[-2:]
    base = 0
    for block in blocks:

        def place(k, _, block=block, base=base):
            where = pl.ds(ids_ref[base + k] * shard_rows, shard_rows)
            flat[where, :] = block[k].astype(F32)[:shard_rows]
            return 0

        lax.fori_loop(0, block.shape[0], place, 0)
        base += block.shape[0]
    for name, shape, out in zip(names, shapes, outs):
        offset, own = OFFSETS[name]
        width = own[-1]
        rows = math.prod(own) // width
        if shape[0][0] > rows or shape[0][1] > width:
            out[...] = jnp.zeros_like(out)
        take_matrix(flat, out, hold, offset, rows, width)


def unpack(blocks, ids, shard_rows, shapes):
    names = tuple(shapes)
    kinds = tuple(shapes[n] for n in names)
    total = sum(b.shape[0] for b in blocks) * shard_rows + 8
    made = pl.pallas_call(
        functools.partial(unpack_kernel, names, kinds, len(blocks), shard_rows),
        out_shape=tuple(jax.ShapeDtypeStruct(*k) for k in kinds),
        in_specs=[SMEM_SPEC] + [VMEM_SPEC] * len(blocks),
        out_specs=(VMEM_SPEC,) * len(names),
        scratch_shapes=[pltpu.VMEM((total, 128), F32), pltpu.VMEM((8, EXPAND, 128), F32)],
        compiler_params=params_of(),
        cost_estimate=cost(6),
        name="unpack",
    )(ids, *blocks)
    return dict(zip(names, made))


EARLY_SHAPES = {
    "mb_short": ((128, MB_CH), BF16), "mb_expand": ((128, EXPAND), BF16), "mid_norm": ((2, EXPAND), F32),
    "mb_depth": ((9, EXPAND), F32), "dw_norm": ((2, EXPAND), F32),
}
LATE_SHAPES = {
    "se_down": ((EXPAND, SQUEEZE), BF16), "se_down_bias": ((1, SQUEEZE), F32), "se_up": ((SQUEEZE, EXPAND), BF16),
    "se_up_bias": ((1, EXPAND), F32), "mb_proj": ((EXPAND, MB_CH), BF16), "at_short": ((MB_CH, DIM), BF16),
    "pre_norm": ((2, MB_CH), F32), "qkv": ((MB_CH, 3 * DIM), BF16), "attn_out": ((DIM, DIM), BF16),
    "out_bias": ((1, DIM), F32), "rel_table": ((16, 2 * WIDE), F32), "mlp_norm": ((2, DIM), F32),
    "mlp_in": ((DIM, MLP), BF16), "mlp_in_bias": ((1, MLP), F32), "mlp_out": ((MLP, DIM), BF16),
    "mlp_out_bias": ((1, DIM), F32), "head_norm": ((2, DIM), F32), "head_w": ((DIM, CLASSES), BF16),
    "head_bias": ((1, CLASSES), F32),
}


ALL_SHAPES = EARLY_SHAPES | LATE_SHAPES


def pack_kernel(names, base, shards, shard_rows, core_ref, *refs):
    grads, (keep_ref, send_ref), (flat, hold) = refs[: len(names)], refs[len(names) : -2], refs[-2:]
    rows_all = flat.shape[0]
    step = 384

    def clear(i, _):
        flat[pl.ds(pl.multiple_of(i * step, 8), step), :] = jnp.zeros((step, 128), F32)
        return 0

    lax.fori_loop(0, rows_all // step, clear, 0)
    for name, grad in zip(names, grads):
        offset, own = OFFSETS[name]
        width = own[-1]
        rows = math.prod(own) // width
        tiles = -(-width // 128)
        read = lambda r, t: grad[r, 128 * t : 128 * t + 128]
        if grad.shape[1] < 128 * tiles:
            hold[tiles - 1, 0:rows, :] = jnp.zeros((rows, 128), F32)
            for t in range(tiles):
                wide = min(128, width - 128 * t)
                hold[t, 0:rows, 0:wide] = grad[0:rows, 128 * t : 128 * t + wide]
            read = lambda r, t: hold[t, r, :]
        put_matrix(flat, read, base, offset, rows, width)

    def share(k, _):
        block = flat[pl.ds(k * shard_rows, shard_rows), :]
        ours = k % 2 == core_ref[0]

        @pl.when(ours)
        def _():
            keep_ref[k // 2, 0:shard_rows] = block

        @pl.when(jnp.logical_not(ours))
        def _():
            send_ref[k // 2, 0:shard_rows] = block

        return 0

    lax.fori_loop(0, shards, share, 0)


def pack(core, grads, base, shards, shard_rows, held_rows):
    names = tuple(grads)
    total = -(-(shards * shard_rows + 8) // 384) * 384
    out = jax.ShapeDtypeStruct((shards // 2, held_rows, 128), F32)
    return pl.pallas_call(
        functools.partial(pack_kernel, names, base, shards, shard_rows),
        out_shape=(out, out),
        in_specs=[SMEM_SPEC] + [VMEM_SPEC] * len(names),
        out_specs=(VMEM_SPEC,) * 2,
        scratch_shapes=[pltpu.VMEM((total, 128), F32), pltpu.VMEM((2, EXPAND, 128), F32)],
        compiler_params=params_of(),
        cost_estimate=cost(6),
        name="pack",
    )(core, *grads.values())


def shard_kernel(
    length, tall_out, tall_head, first_ref, late_ref, mid_ref, small_ref, vector_ref, norms_ref,
    out_ref, square_ref, flat, hold, left_out, left_head,
):
    rows = length // 128
    lead = 16
    flat[...] = jnp.zeros_like(flat)
    start = first_ref[0] * length
    lane = lax.broadcasted_iota(jnp.int32, (8, 128), 1)

    def add_rows(first, value):
        flat[pl.ds(first, value.shape[0]), :] = flat[pl.ds(first, value.shape[0]), :] + value

    devices = vector_ref.shape[0]
    part = min(devices, 128)

    def place(name, left_ref, at_left, at_right, tall):
        offset, (count, width) = OFFSETS[name]
        first = (start - offset + 2**20 * width) // width - 2**20
        inside = (first > -tall) & (first < count)
        held = jnp.where(inside, first, -tall)
        made = jnp.zeros((tall, 128 * -(-width // 128)), F32)
        for g in range(devices // part):
            group = slice(g * part, g * part + part)
            left_ref[g] = jnp.zeros_like(left_ref[g])
            left_ref[g, tall : tall + count, :] = vector_ref[group, at_left, 0:count].T
            right = vector_ref[group, at_right, 0 : hold.shape[2] * -(-width // 128)]
            made = made + dot(left_ref[g, pl.ds(held + tall, tall), :], right, precision=HIGH)
        tiles = -(-width // 128)
        for t in range(tiles):
            wide = min(128, made.shape[1] - 128 * t)
            hold[t, 0:tall, 0:wide] = made[:, 128 * t : 128 * t + wide]
        period = 128 // math.gcd(width, 128)
        stride = period * width // 128

        @pl.when(inside)
        def _():
            for j in range(period):
                begin = offset + (first + j) * width - start + 128 * lead
                row = begin // 128
                shift = begin - row * 128
                size = tall // period
                at_lane = lax.broadcasted_iota(jnp.int32, (size, 128), 1)
                for t in range(tiles):
                    value = hold[t, rows_at(j, size, period), :]
                    value = pltpu.roll(value, shift, 1)
                    where = rows_at(row + t, size, stride)
                    flat[where, :] = flat[where, :] + jnp.where(at_lane >= shift, value, 0.0)
                    where = rows_at(row + t + 1, size, stride)
                    flat[where, :] = flat[where, :] + jnp.where(at_lane < shift, value, 0.0)

    def place_row(offset, value):
        width = value.shape[1]
        begin = offset - start

        @pl.when((begin > -width) & (begin < length))
        def _():
            at = begin + 128 * lead
            row = at // 128
            shift = at - row * 128
            one = lane[0:1]
            for t in range(width // 128):
                tile = pltpu.roll(value[:, 128 * t : 128 * t + 128], shift, 1)
                add_rows(row + t, jnp.where(one >= shift, tile, 0.0))
                add_rows(row + t + 1, jnp.where(one < shift, tile, 0.0))

    place("mlp_out", left_out, 0, 1, tall_out)
    place("head_w", left_head, 2, 3, tall_head)
    place_row(OFFSETS["mlp_out_bias"][0], small_ref[0:1, 0:DIM])
    place_row(OFFSETS["head_norm"][0], small_ref[1:2, 0:DIM])
    place_row(OFFSETS["head_norm"][0] + DIM, small_ref[2:3, 0:DIM])
    place_row(OFFSETS["head_bias"][0], small_ref[3:4, 0:1024])
    for k, name in enumerate(("mid_norm", "mid_norm", "dw_norm", "dw_norm")):
        place_row(OFFSETS[name][0] + (k % 2) * EXPAND, norms_ref[k : k + 1])
    total = flat[lead : lead + rows, :] + late_ref[0:rows] + mid_ref[0:rows]
    out_ref[...] = total
    square_ref[...] = jnp.broadcast_to(jnp.sum(total * total).reshape(1, 1), (8, 128))


def shard_parts(me, length, late, mid, small, vectors, norms):
    rows = length // 128
    devices = vectors.shape[0]
    part = min(devices, 128)

    def tall(name, unit):
        width = OFFSETS[name][1][1]
        return round_up(-(-length // width) + 1, unit)

    tall_out, tall_head = tall("mlp_out", 8), tall("head_w", 16)
    return pl.pallas_call(
        functools.partial(shard_kernel, length, tall_out, tall_head),
        out_shape=(jax.ShapeDtypeStruct((rows, 128), F32), jax.ShapeDtypeStruct((8, 128), F32)),
        in_specs=[SMEM_SPEC] + [VMEM_SPEC] * 5,
        out_specs=(VMEM_SPEC,) * 2,
        scratch_shapes=[
            pltpu.VMEM((rows + 1024, 128), F32),
            pltpu.VMEM((8, max(tall_out, tall_head), 128), F32),
            pltpu.VMEM((devices // part, MLP + 2 * tall_out, part), F32),
            pltpu.VMEM((devices // part, DIM + 2 * tall_head, part), F32),
        ],
        compiler_params=params_of(),
        cost_estimate=cost(4),
        name="shard_parts",
    )(me, late, mid, small, vectors, norms)


def squeeze_lanes():
    table = np.zeros((16 * 48, 16 * 24), np.float32)
    for e in range(16):
        for x in range(24):
            table[e * 48 + x, e * 24 + x] = 1.0
    return table


def slots_of(rel_index):
    last = TOKENS - 1
    corner = lambda i: rel_index[i].reshape(HALF, HALF)
    low_row = jnp.concatenate([corner(last), corner(last - HALF + 1)[:, 1:]], axis=1)
    high_row = jnp.concatenate([corner(HALF - 1), corner(0)[:, 1:]], axis=1)
    return jnp.concatenate([low_row, high_row[1:]], axis=0)


def one_hot(slot_ref, c):
    at = lax.broadcasted_iota(jnp.int32, (256, 2 * WIDE), 1)
    return jnp.where(slot_ref[256 * c : 256 * c + 256, :] == at, 1.0, 0.0).astype(BF16)


def bias_kernel(table_ref, slot_ref, pick_ref, out_ref, held):
    table = table_ref[...].astype(BF16)
    f = jnp.concatenate([dot(table, one_hot(slot_ref, c), NT) for c in range(2 * WIDE // 256)], axis=1)
    for x in range(HALF):
        turned = pltpu.roll(f, (WIDE * 2 - (HALF - 1 - x)) % (WIDE * 2), 1) if x != HALF - 1 else f
        held[16 * x : 16 * x + 16, :] = turned.astype(BF16)
    for part in range(3):
        made = dot(held[:, 768 * part : 768 * part + 768], pick_ref[...])
        for t in range(3):
            for x in range(HALF):
                out_ref[3 * part + t, pl.ds(x, HEADS, stride=HALF), :] = made[
                    16 * x : 16 * x + HEADS, 128 * t : 128 * t + 128
                ]


def build_bias(table, slots, pick):
    return pl.pallas_call(
        bias_kernel,
        out_shape=jax.ShapeDtypeStruct((9, HEADS * HALF, 128), F32),
        in_specs=[VMEM_SPEC] * 3,
        out_specs=VMEM_SPEC,
        scratch_shapes=[pltpu.VMEM((16 * HALF, 2 * WIDE), BF16)],
        compiler_params=params_of(),
        cost_estimate=cost(8),
        name="bias_build",
    )(table, slots, pick)


def halves_of(v):
    high = v.astype(BF16)
    return high, (v - high.astype(F32)).astype(BF16)


def bias_back_kernel(grad_ref, slot_ref, pick_ref, out_ref, held):
    for part in range(3):
        rows = jnp.concatenate([grad_ref[3 * part + t] for t in range(3)], axis=1)
        high, rest = halves_of(rows)
        wide = dot(high, pick_ref[...]) + dot(rest, pick_ref[...])
        for t in range(6):
            held[6 * part + t] = wide[:, 128 * t : 128 * t + 128]
    total = jnp.zeros((16, 2 * WIDE), F32)
    for x in range(HALF):
        wide = jnp.concatenate([held[t, pl.ds(x, HEADS, stride=HALF), :] for t in range(18)], axis=1)
        wide = jnp.concatenate([wide, jnp.zeros((4, 2 * WIDE), F32)], axis=0)
        total = total + (pltpu.roll(wide, HALF - 1 - x, 1) if x != HALF - 1 else wide)
    high, rest = halves_of(total)
    result = jnp.zeros((16, 2 * WIDE), F32)
    for c in range(2 * WIDE // 256):
        hot = one_hot(slot_ref, c)
        cols = slice(256 * c, 256 * c + 256)
        result = result + dot(high[:, cols], hot) + dot(rest[:, cols], hot)
    out_ref[...] = result


def bias_back(grad, slots, pick):
    return pl.pallas_call(
        bias_back_kernel,
        out_shape=jax.ShapeDtypeStruct((16, 2 * WIDE), F32),
        in_specs=[VMEM_SPEC] * 3,
        out_specs=VMEM_SPEC,
        scratch_shapes=[pltpu.VMEM((18, HEADS * HALF, 128), F32)],
        compiler_params=params_of(),
        cost_estimate=cost(10),
        name="bias_back",
    )(grad, slots, pick)


def sigmoid(v):
    return 1.0 / (1.0 + jnp.exp(-v))


def row8(rows):
    width = rows[0].shape[1]
    return jnp.concatenate(rows + [jnp.zeros((8 - len(rows), width), F32)], axis=0)


def dw_stats(stat, count):
    mean = stat[0:1] / count
    return mean, lax.rsqrt(stat[1:2] / count - mean * mean + EPS)


def valid_places(limit):
    return (limit * limit).astype(F32)


def excite_kernel(
    res_ref, mask_ref, depth_ref, stat_ref, bgram_ref, norm_ref, down_ref, down_b_ref, up_ref, up_b_ref,
    proj_ref, base_ref, short_ref, pre_ref, qkv_ref,
    act_ref, slope_ref, block_ref, skip_ref, normed_ref, project_ref, vec_ref, small_ref, held,
):
    limit = limit_of(res_ref)
    count = bgram_ref[64:65, 64:65]
    mean, inverse = dw_stats(stat_ref[...], count)
    gain = norm_ref[0:1] * inverse
    shift = norm_ref[1:2] - mean * gain
    rows = 2 * HALF
    total = jnp.zeros((8, EXPAND), F32)
    for group in range(4):

        def fill(i, total, group=group):
            at = pl.ds(pl.multiple_of(group * QUAD + rows * i, 16), rows)
            value, slope = gelu_pair(depth_ref[at, :] * gain + shift)
            inside = mask_ref[at, :]
            inside = jnp.concatenate([inside] * CHUNKS, axis=1)
            value = value * inside
            held[at, :] = value
            act_ref[at, :] = value.astype(BF16)
            slope_ref[at, :] = (slope * inside).astype(BF16)
            for k in range(rows // 8):
                total = total + value[8 * k : 8 * k + 8]
            return total

        total = lax.fori_loop(0, QUAD // rows, fill, total)
    pooled = jnp.sum(total, axis=0, keepdims=True) / valid_places(limit)
    before = dot(row8([pooled]), down_ref[...].astype(F32), precision=HIGH)[0:1] + down_b_ref[...]
    gate = sigmoid(before)
    squeeze = before * gate
    excite = sigmoid(
        dot(row8([squeeze]), up_ref[...].astype(F32), precision=HIGH)[0:1] + up_b_ref[...]
    )
    vec_ref[...] = row8([pooled, excite, mean, inverse])
    small_ref[...] = row8([squeeze, gate * (1.0 + before * (1.0 - gate))])

    big = 576
    def section(i, _):
        at = pl.ds(pl.multiple_of(big * i, 16), big)
        scaled = (held[at, :] * excite).astype(BF16)
        block_ref[at, :] = dot(scaled, proj_ref[...]) + dot(base_ref[at, :], short_ref[...])
        return 0

    lax.fori_loop(0, PLACES // big, section, 0)
    part = 96

    def tokens(i, _):
        skipped = jnp.zeros((part, MB_CH), F32)
        normed = jnp.zeros((part, MB_CH), F32)
        for group in range(4):
            block = block_ref[pl.ds(pl.multiple_of(group * QUAD + part * i, 16), part), :]
            skipped = skipped + block
            hat, _ = normalise(block)
            normed = normed + hat
        at = pl.ds(pl.multiple_of(part * i, 16), part)
        skip_ref[at, :] = (0.25 * skipped).astype(BF16)
        low = (0.25 * normed * pre_ref[0:1] + pre_ref[1:2]).astype(BF16)
        normed_ref[at, :] = low
        return 0

    lax.fori_loop(0, TOKENS // part, tokens, 0)
    project_ref[...] = dot(normed_ref[...], qkv_ref[...]).astype(BF16)


def normalise(v):
    centered = v - jnp.mean(v, axis=-1, keepdims=True)
    inverse = lax.rsqrt(jnp.mean(centered * centered, axis=-1, keepdims=True) + EPS)
    return centered * inverse, inverse


def normalise_back(grad_hat, hat, inverse):
    first = jnp.mean(grad_hat, axis=-1, keepdims=True)
    second = jnp.mean(grad_hat * hat, axis=-1, keepdims=True)
    return inverse * (grad_hat - first - hat * second)


def excite_forward(res_ids, mask, depth, stat, bgram, base, p):
    return pl.pallas_call(
        excite_kernel,
        out_shape=(
            jax.ShapeDtypeStruct((PLACES, EXPAND), BF16),
            jax.ShapeDtypeStruct((PLACES, EXPAND), BF16),
            jax.ShapeDtypeStruct((PLACES, MB_CH), F32),
            jax.ShapeDtypeStruct((TOKENS, MB_CH), BF16),
            jax.ShapeDtypeStruct((TOKENS, MB_CH), BF16),
            jax.ShapeDtypeStruct((TOKENS, 3 * DIM), BF16),
            jax.ShapeDtypeStruct((8, EXPAND), F32),
            jax.ShapeDtypeStruct((8, SQUEEZE), F32),
        ),
        in_specs=[SMEM_SPEC] + [VMEM_SPEC] * 14,
        out_specs=(VMEM_SPEC,) * 8,
        scratch_shapes=[pltpu.VMEM((PLACES, EXPAND), F32)],
        compiler_params=params_of(),
        cost_estimate=cost(18),
        name="excite_forward",
    )(
        res_ids, mask, depth, stat, bgram, p["dw_norm"], p["se_down"], p["se_down_bias"], p["se_up"], p["se_up_bias"],
        p["mb_proj"], base, p["mb_short"], p["pre_norm"], p["qkv"],
    )


SCALE = HEAD_DIM ** (-0.5)
PER = BLOCK // HEAD_DIM
ATT_ROWS = 2 * HALF


def token_valid(limit, shape, axis):
    at = lax.broadcasted_iota(jnp.int32, shape, axis)
    y = at // HALF
    x = at - y * HALF
    return (2 * y < limit) & (2 * x < limit)


def head_lanes(h):
    lane = lax.broadcasted_iota(jnp.int32, (TOKENS, BLOCK), 1)
    return lane // HEAD_DIM == h


def bias_cut(up):
    offset = (HALF - 1 - up) * HALF
    lead = offset % 128
    return offset // 128, (5 if lead <= 64 else 6), lead


def attend_kernel(res_ref, q_ref, k_ref, v_ref, bias_ref, out_ref, p_ref, scores):
    limit = limit_of(res_ref)
    usable = token_valid(limit, (1, TOKENS), 1)

    def head(h, total):
        mine = head_lanes(h)
        q = jnp.where(mine, q_ref[...], jnp.zeros((), BF16))
        scores[...] = dot(q, k_ref[...], NT)
        bias_rows = pl.ds(pl.multiple_of(h * HALF, 8), HALF)
        for i in range(TOKENS // ATT_ROWS):
            at = slice(ATT_ROWS * i, ATT_ROWS * i + ATT_ROWS)
            shifted = []
            for k in range(2):
                tile, tiles, lead = bias_cut(2 * i + k)
                bias = jnp.concatenate([bias_ref[tile + t, bias_rows, :] for t in range(tiles)], axis=1)
                if lead:
                    bias = pltpu.roll(bias, 128 * tiles - lead, 1)
                shifted.append(bias[:, :TOKENS])
            s = scores[at, :] * SCALE + jnp.concatenate(shifted, axis=0)
            s = jnp.where(usable, s, -1e30)
            e = jnp.exp(s - jnp.max(s, axis=-1, keepdims=True))
            weights = e * (1.0 / jnp.sum(e, axis=-1, keepdims=True))
            p_ref[h, at, :] = weights.astype(BF16)
        return jnp.where(mine, dot(p_ref[h], v_ref[...]), total)

    total = lax.fori_loop(0, PER, head, jnp.zeros((TOKENS, BLOCK), F32))
    out_ref[...] = total.astype(BF16)


def attend_forward(res_ids, project, bias):
    part = lambda k: pl.BlockSpec((TOKENS, BLOCK), lambda j: (0, 3 * k + j))
    return pl.pallas_call(
        attend_kernel,
        grid=(HEADS // PER,),
        out_shape=(
            jax.ShapeDtypeStruct((TOKENS, DIM), BF16),
            jax.ShapeDtypeStruct((HEADS, TOKENS, TOKENS), BF16),
        ),
        in_specs=[SMEM_SPEC, part(0), part(1), part(2), pl.BlockSpec((9, PER * HALF, 128), lambda j: (0, j, 0))],
        out_specs=(
            pl.BlockSpec((TOKENS, BLOCK), lambda j: (0, j)),
            pl.BlockSpec((PER, TOKENS, TOKENS), lambda j: (j, 0, 0)),
        ),
        scratch_shapes=[pltpu.VMEM((TOKENS, TOKENS), F32)],
        compiler_params=params_of(),
        cost_estimate=cost(35),
        name="attend_forward",
    )(res_ids, project, project, project, bias)


def attend_back_kernel(q_ref, k_ref, v_ref, o_ref, do_ref, p_ref, dq_ref, dk_ref, dv_ref, dbias_ref, scores, low, bias):
    def head(h, carry):
        dq, dk, dv = carry
        mine = head_lanes(h)
        grad = jnp.where(mine, do_ref[...], jnp.zeros((), BF16))
        scores[...] = dot(grad, v_ref[...], NT)
        bias[...] = jnp.zeros((HALF, WIDE), F32)
        lane = lax.broadcasted_iota(jnp.int32, (ATT_ROWS, BLOCK), 1)
        for i in range(TOKENS // ATT_ROWS):
            at = slice(ATT_ROWS * i, ATT_ROWS * i + ATT_ROWS)
            both = do_ref[at, :].astype(F32) * o_ref[at, :].astype(F32)
            both = jnp.where(lane // HEAD_DIM == h, both, 0.0)
            delta = jnp.sum(both, axis=-1, keepdims=True)
            ds = p_ref[h, at, :].astype(F32) * (scores[at, :] - delta)
            low[at, :] = (ds * SCALE).astype(BF16)
            for k in range(2):
                tile, tiles, lead = bias_cut(2 * i + k)
                wide = jnp.concatenate(
                    [ds[HALF * k : HALF * k + HALF], jnp.zeros((HALF, 128 * tiles - TOKENS), F32)], axis=1
                )
                if lead:
                    wide = pltpu.roll(wide, lead, 1)
                cols = slice(128 * tile, 128 * (tile + tiles))
                bias[:, cols] = bias[:, cols] + wide
        for t in range(9):
            dbias_ref[t, pl.ds(pl.multiple_of(h * HALF, 8), HALF), :] = bias[:, 128 * t : 128 * t + 128]
        dq = jnp.where(mine, dot(low[...], k_ref[...]), dq)
        dk = jnp.where(mine, dot(low[...], q_ref[...], TN), dk)
        dv = jnp.where(mine, dot(p_ref[h], do_ref[...], TN), dv)
        return dq, dk, dv

    zero = jnp.zeros((TOKENS, BLOCK), F32)
    dq, dk, dv = lax.fori_loop(0, PER, head, (zero, zero, zero))
    dq_ref[...] = dq.astype(BF16)
    dk_ref[...] = dk.astype(BF16)
    dv_ref[...] = dv.astype(BF16)


def attend_backward(project, blended, grad, weights):
    part = lambda k: pl.BlockSpec((TOKENS, BLOCK), lambda j: (0, 3 * k + j))
    bias = pl.BlockSpec((9, PER * HALF, 128), lambda j: (0, j, 0))
    return pl.pallas_call(
        attend_back_kernel,
        grid=(HEADS // PER,),
        out_shape=(jax.ShapeDtypeStruct((TOKENS, DIM), BF16),) * 3
        + (jax.ShapeDtypeStruct((9, HEADS * HALF, 128), F32),),
        in_specs=[
            part(0), part(1), part(2), part(0), part(0),
            pl.BlockSpec((PER, TOKENS, TOKENS), lambda j: (j, 0, 0)),
        ],
        out_specs=(part(0), part(0), part(0), bias),
        scratch_shapes=[
            pltpu.VMEM((TOKENS, TOKENS), F32), pltpu.VMEM((TOKENS, TOKENS), BF16), pltpu.VMEM((HALF, WIDE), F32),
        ],
        compiler_params=params_of(),
        cost_estimate=cost(40),
        name="attend_backward",
    )(project, project, project, blended, grad, weights)


MLP_ROWS = 192


def mlp_kernel(
    share, res_ref, label_ref, skip_ref, blend_ref, short_ref, out_ref, out_b_ref, norm_ref, in_ref, in_b_ref,
    back_ref, back_b_ref, hnorm_ref, head_ref, head_b_ref,
    loss_ref, dblend_ref, dskip_ref, dshort_ref, dout_ref, dout_b_ref, dnorm_ref, din_ref, din_b_ref,
    vec_ref, few_ref,
    section, low, slopes, dpres, grads,
):
    limit = limit_of(res_ref)
    n_valid = (limit // 2 * (limit // 2)).astype(F32)
    steps = TOKENS // MLP_ROWS
    cut = 384

    def valid_rows(i):
        at = lax.broadcasted_iota(jnp.int32, (MLP_ROWS, 1), 0) + MLP_ROWS * i
        y = at // HALF
        x = at - y * HALF
        return jnp.where((2 * y < limit) & (2 * x < limit), 1.0, 0.0)

    def forward(i, carry):
        feature, used = carry
        at = pl.ds(pl.multiple_of(MLP_ROWS * i, 16), MLP_ROWS)
        first = dot(skip_ref[at, :], short_ref[...]) + dot(blend_ref[at, :], out_ref[...]) + out_b_ref[...]
        section[at, :] = first
        hat, _ = normalise(first)
        normed = (hat * norm_ref[0:1] + norm_ref[1:2]).astype(BF16)
        low[at, :] = normed
        inside = valid_rows(i)
        second = first + back_b_ref[...]
        parts = []
        for j in range(MLP // cut):
            cols = slice(cut * j, cut * j + cut)
            value, slope = gelu_pair(dot(normed, in_ref[:, cols]) + in_b_ref[:, cols])
            slopes[at, cols] = slope * inside
            value = value.astype(BF16)
            parts.append(jnp.sum(value.astype(F32) * inside, axis=0, keepdims=True))
            second = second + dot(value, back_ref[cols, :])
        feature = feature + jnp.sum(second * inside, axis=0, keepdims=True)
        return feature, used + jnp.concatenate(parts, axis=1)

    feature, used = lax.fori_loop(
        0, steps, forward, (jnp.zeros((1, DIM), F32), jnp.zeros((1, MLP), F32))
    )
    feature = feature / n_valid
    hat, inverse = normalise(feature)
    normed = (hat * hnorm_ref[0:1] + hnorm_ref[1:2]).astype(BF16)
    normed8 = jnp.concatenate([normed.astype(F32), jnp.zeros((15, DIM), F32)], axis=0).astype(BF16)
    logits = dot(normed8, head_ref[...])[0:1] + head_b_ref[...]
    peak = jnp.max(logits, axis=-1, keepdims=True)
    exps = jnp.exp(logits - peak)
    total = jnp.sum(exps, axis=-1, keepdims=True)
    log_probs = logits - peak - jnp.log(total)
    at_class = lax.broadcasted_iota(jnp.int32, (1, CLASSES), 1)
    goal = jnp.where(at_class == label_ref[0], 1.0 - SMOOTH, 0.0) + SMOOTH / CLASSES
    loss = -jnp.sum(goal * log_probs, axis=-1, keepdims=True)
    loss_ref[...] = jnp.broadcast_to(loss, (8, 128))
    grad = (exps / total - goal) * share
    few_ref[...] = jnp.zeros_like(few_ref)
    few_ref[3:4, 0:CLASSES] = grad
    grad16 = jnp.concatenate([grad, jnp.zeros((15, CLASSES), F32)], axis=0).astype(BF16)
    vec_ref[...] = jnp.zeros_like(vec_ref)
    vec_ref[2:3, 0:DIM] = normed8.astype(F32)[0:1]
    vec_ref[3:4, 0:CLASSES] = grad16.astype(F32)[0:1]
    grad = dot(grad16, head_ref[...], NT)[0:1]
    few_ref[1:3, 0:DIM] = jnp.concatenate([grad * hat, grad], axis=0)
    grad = normalise_back(grad * hnorm_ref[0:1], hat, inverse) / n_valid
    low_grad = jnp.concatenate([grad, jnp.zeros((15, DIM), F32)], axis=0).astype(BF16)
    vec_ref[0:1, :] = used
    vec_ref[1:2, 0:DIM] = low_grad.astype(F32)[0:1]
    few_ref[0:1, 0:DIM] = grad * n_valid
    dhidden = dot(low_grad, back_ref[...], NT)[0:1]

    def backward(i, carry):
        dnorm0, dnorm1, dbias, dout_b = carry
        at = pl.ds(pl.multiple_of(MLP_ROWS * i, 16), MLP_ROWS)
        dnormed = jnp.zeros((MLP_ROWS, DIM), F32)
        parts = []
        for j in range(MLP // cut):
            cols = slice(cut * j, cut * j + cut)
            dpre = slopes[at, cols] * dhidden[:, cols]
            parts.append(jnp.sum(dpre, axis=0, keepdims=True))
            dpre = dpre.astype(BF16)
            dpres[at, cols] = dpre
            dnormed = dnormed + dot(dpre, in_ref[:, cols], NT)
        hat, inverse = normalise(section[at, :])
        dnorm0 = dnorm0 + jnp.sum(dnormed * hat, axis=0, keepdims=True)
        dnorm1 = dnorm1 + jnp.sum(dnormed, axis=0, keepdims=True)
        dsection = normalise_back(dnormed * norm_ref[0:1], hat, inverse) + valid_rows(i) * grad
        grads[at, :] = dsection.astype(BF16)
        dout_b = dout_b + jnp.sum(dsection, axis=0, keepdims=True)
        dblend_ref[at, :] = dot(grads[at, :], out_ref[...], NT).astype(BF16)
        dskip_ref[at, :] = dot(grads[at, :], short_ref[...], NT)
        return dnorm0, dnorm1, dbias + jnp.concatenate(parts, axis=1), dout_b

    row = jnp.zeros((1, DIM), F32)
    dnorm0, dnorm1, dbias, dout_b = lax.fori_loop(0, steps, backward, (row, row, jnp.zeros((1, MLP), F32), row))
    dnorm_ref[...] = jnp.concatenate([dnorm0, dnorm1], axis=0)
    din_b_ref[...] = dbias
    dout_b_ref[...] = dout_b
    din_ref[...] = dot(low[...], dpres[...], TN)
    dout_ref[...] = dot(blend_ref[...], grads[...], TN)
    dshort_ref[...] = dot(skip_ref[...], grads[...], TN)


def mlp_both(share, res_ids, labels, skipped, blended, p):
    s = jax.ShapeDtypeStruct
    return pl.pallas_call(
        functools.partial(mlp_kernel, share),
        out_shape=(
            s((8, 128), F32), s((TOKENS, DIM), BF16), s((TOKENS, MB_CH), F32), s((MB_CH, DIM), F32),
            s((DIM, DIM), F32), s((1, DIM), F32), s((2, DIM), F32), s((DIM, MLP), F32), s((1, MLP), F32),
            s((8, MLP), F32), s((8, 1024), F32),
        ),
        in_specs=[SMEM_SPEC] * 2 + [VMEM_SPEC] * 13,
        out_specs=(VMEM_SPEC,) * 11,
        scratch_shapes=[
            pltpu.VMEM((TOKENS, DIM), F32),
            pltpu.VMEM((TOKENS, DIM), BF16),
            pltpu.VMEM((TOKENS, MLP), F32),
            pltpu.VMEM((TOKENS, MLP), BF16),
            pltpu.VMEM((TOKENS, DIM), BF16),
        ],
        compiler_params=params_of(),
        cost_estimate=cost(23),
        name="mlp_both",
    )(
        res_ids, labels, skipped, blended, p["at_short"], p["attn_out"], p["out_bias"], p["mlp_norm"], p["mlp_in"],
        p["mlp_in_bias"], p["mlp_out"], p["mlp_out_bias"], p["head_norm"], p["head_w"], p["head_bias"],
    )


def proj_back_kernel(
    res_ref, dq_ref, dk_ref, dv_ref, normed_ref, qkv_ref, dskip_ref, block_ref, pre_ref, act_ref, vec_ref,
    small_ref, proj_ref, short_ref, base_ref, down_ref, up_ref,
    dqkv_ref, dpre_ref, dblock_ref, dproj_ref, dshort_ref, dbase_ref, ddown_ref, ddown_b_ref, dup_ref, dup_b_ref,
    dpool_ref, back,
):
    limit = limit_of(res_ref)
    part = 96
    grad = dot(dq_ref[...], qkv_ref[:, 0:DIM], NT)
    grad = grad + dot(dk_ref[...], qkv_ref[:, DIM : 2 * DIM], NT)
    back[...] = grad + dot(dv_ref[...], qkv_ref[:, 2 * DIM :], NT)

    def tokens(i, carry):
        dpre0, dpre1 = carry
        at = pl.ds(pl.multiple_of(part * i, 16), part)
        grad = back[at, :]
        dskip = 0.25 * dskip_ref[at, :]
        dpre1 = dpre1 + jnp.sum(grad, axis=0, keepdims=True)
        grad = 0.25 * grad
        dhat = grad * pre_ref[0:1]
        for group in range(4):
            places = pl.ds(pl.multiple_of(group * QUAD + part * i, 16), part)
            hat, inverse = normalise(block_ref[places, :])
            dpre0 = dpre0 + jnp.sum(grad * hat, axis=0, keepdims=True)
            dblock = normalise_back(dhat, hat, inverse) + dskip
            dblock_ref[places, :] = dblock.astype(BF16)
        return dpre0, dpre1

    row = jnp.zeros((1, MB_CH), F32)
    dpre0, dpre1 = lax.fori_loop(0, TOKENS // part, tokens, (row, row))
    dpre_ref[...] = jnp.concatenate([dpre0, dpre1], axis=0)
    for k, grad_ref in enumerate((dq_ref, dk_ref, dv_ref)):
        dqkv_ref[:, DIM * k : DIM * k + DIM] = dot(normed_ref[...], grad_ref[...], TN)
    dshort_ref[...] = dot(base_ref[...], dblock_ref[...], TN)[0:STEM_CH]
    dbase_ref[...] = dot(dblock_ref[...], short_ref[...], NT)
    excite = vec_ref[1:2]
    parts = []
    for j in range(CHUNKS):
        cols = slice(BLOCK * j, BLOCK * j + BLOCK)
        act = act_ref[:, cols].astype(F32)
        scaled = (act * excite[:, cols]).astype(BF16)
        dproj_ref[cols, :] = dot(scaled, dblock_ref[...], TN)
        dscaled = dot(dblock_ref[...], proj_ref[cols, :], NT)
        parts.append(jnp.sum(dscaled * act, axis=0, keepdims=True))
    dexcite = jnp.concatenate(parts, axis=1)
    dafter = dexcite * excite * (1.0 - excite)
    dup_b_ref[...] = dafter
    dup_ref[...] = dot(row8([small_ref[0:1]]), row8([dafter]), TN, precision=HIGH)
    dsqueeze = dot(row8([dafter]), up_ref[...].astype(F32), NT, precision=HIGH)[0:1]
    dbefore = dsqueeze * small_ref[1:2]
    ddown_b_ref[...] = dbefore
    ddown_ref[...] = dot(row8([vec_ref[0:1]]), row8([dbefore]), TN, precision=HIGH)
    dpool = dot(row8([dbefore]), down_ref[...].astype(F32), NT, precision=HIGH)
    dpool_ref[...] = dpool / valid_places(limit)


def proj_backward(res_ids, dq, dk, dv, normed, dskip, block, act, vec, small, base, p):
    s = jax.ShapeDtypeStruct
    return pl.pallas_call(
        proj_back_kernel,
        out_shape=(
            s((MB_CH, 3 * DIM), F32), s((2, MB_CH), F32), s((PLACES, MB_CH), BF16), s((EXPAND, MB_CH), F32),
            s((STEM_CH, MB_CH), F32), s((PLACES, 128), F32), s((EXPAND, SQUEEZE), F32), s((1, SQUEEZE), F32),
            s((SQUEEZE, EXPAND), F32), s((1, EXPAND), F32), s((8, EXPAND), F32),
        ),
        in_specs=[SMEM_SPEC] + [VMEM_SPEC] * 16,
        out_specs=(VMEM_SPEC,) * 11,
        scratch_shapes=[pltpu.VMEM((TOKENS, MB_CH), F32)],
        compiler_params=params_of(),
        cost_estimate=cost(13),
        name="proj_backward",
    )(
        res_ids, dq, dk, dv, normed, p["qkv"], dskip, block, p["pre_norm"], act, vec, small, p["mb_proj"],
        p["mb_short"], base, p["se_down"], p["se_up"],
    )


def excite_back_kernel(dblock_ref, proj_ref, vec_ref, dpool_ref, slope_ref, x_ref, out_ref, sum_ref, wide):
    excite, mean, inverse = vec_ref[1:2], vec_ref[2:3], vec_ref[3:4]
    dpool = dpool_ref[0:1]
    rows = 288
    wide[...] = dot(dblock_ref[...], proj_ref[...], NT)

    def fold(v):
        total = v[0:8]
        for k in range(1, rows // 8):
            total = total + v[8 * k : 8 * k + 8]
        return total

    def step(i, sums):
        at = pl.ds(pl.multiple_of(rows * i, 16), rows)
        grad = wide[at, :] * excite + dpool
        grad = grad * slope_ref[at, :].astype(F32)
        out_ref[at, :] = grad.astype(BF16)
        hat = (x_ref[at, :] - mean) * inverse
        return sums[0] + fold(grad), sums[1] + fold(grad * hat)

    sums = lax.fori_loop(0, PLACES // rows, step, (jnp.zeros((8, BLOCK), F32),) * 2)
    sum_ref[...] = row8([jnp.sum(s, axis=0, keepdims=True) for s in sums])


def excite_backward(dblock, proj, vec, dpool, slope, depth):
    col = lambda rows: pl.BlockSpec((rows, BLOCK), lambda j: (0, j))
    return pl.pallas_call(
        excite_back_kernel,
        grid=(CHUNKS,),
        out_shape=(jax.ShapeDtypeStruct((PLACES, EXPAND), BF16), jax.ShapeDtypeStruct((8, EXPAND), F32)),
        in_specs=[
            pl.BlockSpec((PLACES, MB_CH), lambda j: (0, 0)),
            pl.BlockSpec((BLOCK, MB_CH), lambda j: (j, 0)),
            col(8), col(8), col(PLACES), col(PLACES),
        ],
        out_specs=(col(PLACES), col(8)),
        scratch_shapes=[pltpu.VMEM((PLACES, BLOCK), F32)],
        compiler_params=params_of(),
        cost_estimate=cost(12),
        name="excite_backward",
    )(dblock, proj, vec, dpool, slope, depth)


def depth_back_kernel(
    mask_ref, du_ref, x_ref, vec_ref, sum_ref, bgram_ref, base_ref, expand_ref, dwn_ref, depth_ref, act_ref, slope_ref,
    out_ref, cross_ref, ddepth_ref, sums_ref, pad,
):
    count = bgram_ref[64:65, 64:65]
    mean1, inverse1 = bn_stats(bgram_ref[...], expand_ref[...], count)
    mean2, inverse2 = vec_ref[2:3], vec_ref[3:4]
    c1 = sum_ref[0:1] / count
    c2 = sum_ref[1:2] / count
    scale2 = dwn_ref[0:1] * inverse2
    slant = scale2 * inverse2 * c2
    level = scale2 * c1 - slant * mean2
    zero = jnp.zeros((4, 1, HALF, BLOCK), F32)
    pad[:, 0:1] = zero
    pad[:, HALF + 1 : HALF + 2] = zero
    rows = 2 * HALF

    def fill(i, _):
        for group in range(4):
            at = pl.ds(pl.multiple_of(group * QUAD + rows * i, 16), rows)
            grad = scale2 * du_ref[at, :].astype(F32) - mask_ref[at, :] * (level + x_ref[at, :] * slant)
            for k in range(2):
                pad[group, 2 * i + k + 1] = grad[HALF * k : HALF * k + HALF]
        return 0

    lax.fori_loop(0, HALF // 2, fill, 0)

    def weight(dy, dx):
        return depth_ref[8 - 3 * dy - dx : 9 - 3 * dy - dx]

    def fold(v):
        return v[0:8] + v[8:16] + v[16:24]

    def step(k, sums):
        sums = list(sums)
        for py in range(2):
            places = [
                pl.ds(pl.multiple_of((2 * py + px) * QUAD + 2 * HALF * k, 16), 2 * HALF) for px in range(2)
            ]
            low_both, high_both = (act_ref[at, :].astype(F32) for at in places)
            made = [[], []]
            for half in range(2):
                up = 2 * k + half
                cut = slice(HALF * half, HALF * half + HALF)
                sources = [(1, -1), (0, 0), (1, 0)] if py == 0 else [(0, 0), (1, 0), (0, 1)]
                low_act, high_act = low_both[cut], high_both[cut]
                even = odd = None
                for t, (gy, off) in enumerate(sources):
                    left, right = pad[2 * gy, up + 1 + off], pad[2 * gy + 1, up + 1 + off]
                    before, after = shift_down(right), shift_up(left)
                    a = before * weight(t, 0) + left * weight(t, 1) + right * weight(t, 2)
                    b = left * weight(t, 0) + right * weight(t, 1) + after * weight(t, 2)
                    even = a if even is None else even + a
                    odd = b if odd is None else odd + b
                    for s, (a, b) in enumerate(((before, left), (left, right), (right, after))):
                        tap = 3 * (2 - t) + 2 - s
                        sums[tap] = sums[tap] + fold(low_act * a + high_act * b)
                made[0].append(even)
                made[1].append(odd)
            for px in range(2):
                grad = jnp.concatenate(made[px], axis=0) * slope_ref[places[px], :].astype(F32)
                out_ref[places[px], :] = grad.astype(BF16)
        return tuple(sums)

    sums = lax.fori_loop(0, HALF // 2, step, (jnp.zeros((8, BLOCK), F32),) * 9)
    ddepth_ref[...] = jnp.concatenate(
        [jnp.sum(s, axis=0, keepdims=True) for s in sums] + [jnp.zeros((7, BLOCK), F32)], axis=0
    )
    cross = dot(base_ref[...], out_ref[...], TN)
    cross_ref[...] = cross[0:72]
    first = cross[64:65]
    second = (jnp.sum(cross[0:64] * expand_ref[0:64, :].astype(F32), axis=0, keepdims=True) - mean1 * first) * inverse1
    sums_ref[...] = row8([second, first])


def depth_backward(mask, du, depth, vec, sums, bgram, base, expand_w, dw_norm, mb_depth, act, slope):
    col = lambda rows: pl.BlockSpec((rows, BLOCK), lambda j: (0, j))
    whole = lambda rows: pl.BlockSpec((rows, BLOCK), lambda j: (0, 0))
    s = jax.ShapeDtypeStruct
    return pl.pallas_call(
        depth_back_kernel,
        grid=(CHUNKS,),
        out_shape=(s((PLACES, EXPAND), BF16), s((72, EXPAND), F32), s((16, EXPAND), F32), s((8, EXPAND), F32)),
        in_specs=[
            whole(PLACES), col(PLACES), col(PLACES), col(8), col(8), whole(72), whole(PLACES), col(128), col(2),
            col(9), col(PLACES), col(PLACES),
        ],
        out_specs=(col(PLACES), col(72), col(16), col(8)),
        scratch_shapes=[pltpu.VMEM((4, HALF + 2, HALF, BLOCK), F32)],
        compiler_params=params_of(),
        cost_estimate=cost(35),
        name="depth_backward",
    )(mask, du, depth, vec, sums, bgram, base, expand_w, dw_norm, mb_depth, act, slope)


def stem_back_kernel(
    mask_ref, patch_ref, slope_ref, dbase_ref, du_ref, sum_ref, bgram_ref, base_ref, expand_ref, mid_ref, spread_ref,
    out_ref, total,
):
    count = bgram_ref[64:65, 64:65]
    mean, inverse = bn_stats(bgram_ref[...], expand_ref[...], count)
    second, first = sum_ref[0:1] / count, sum_ref[1:2] / count
    scale = mid_ref[0:1] * inverse
    slant = scale * inverse * second
    level = scale * first - slant * mean
    total[...] = jnp.zeros_like(total)
    rows = 768

    def step(i, _):
        at = pl.ds(pl.multiple_of(i * rows, rows), rows)
        x = dot(base_ref[at, :], expand_ref[...])
        inside = jnp.concatenate([mask_ref[at, :]] * CHUNKS, axis=1)
        grad = (scale * du_ref[at, :].astype(F32) - inside * (level + x * slant)).astype(BF16)
        grad = dot(grad, expand_ref[...], NT) + dbase_ref[at, :]
        grad = grad[:, 0:64] * (1.0 / 16.0)
        grad = jnp.concatenate([grad, grad], axis=1)
        grad = jnp.concatenate([grad, grad], axis=1)
        block = patch_ref[at, :]
        for j in range(4):
            cols = slice(256 * j, 256 * j + 256)
            wide = (slope_ref[at, cols].astype(F32) * grad).astype(BF16)
            total[:, cols] = total[:, cols] + dot(block, wide, TN)
        return 0

    lax.fori_loop(0, PLACES // rows, step, 0)
    merged = total[0:96, 0:256]
    for px in range(1, 4):
        merged = merged + total[64 * px : 64 * px + 96, 256 * px : 256 * px + 256]
    result = jnp.zeros((32, STEM_CH), F32)
    for pair in range(2):
        wide = dot(spread_ref[pair][0:96].astype(F32), merged[:, 128 * pair : 128 * pair + 128], TN, precision=HIGH)
        result = result + wide[0:32, 0:64] + wide[32:64, 64:128]
    ones = merged[27:28]
    ones = ones[:, 0:64] + ones[:, 64:128] + ones[:, 128:192] + ones[:, 192:256]
    at = lax.broadcasted_iota(jnp.int32, (32, STEM_CH), 0)
    out_ref[...] = jnp.where(at == 27, ones, result)


def stem_backward(mask, patches, slope, dbase, du, sums, bgram, base, expand_w, mid_norm, spread):
    return pl.pallas_call(
        stem_back_kernel,
        out_shape=jax.ShapeDtypeStruct((32, STEM_CH), F32),
        in_specs=[VMEM_SPEC] * 11,
        out_specs=VMEM_SPEC,
        scratch_shapes=[pltpu.VMEM((TAPS, 1024), F32)],
        compiler_params=params_of(),
        cost_estimate=cost(15),
        name="stem_backward",
    )(mask, patches, slope, dbase, du, sums, bgram, base, expand_w, mid_norm, spread)


def expand_finish_kernel(cross_ref, ddepth_ref, sum_ref, bgram_ref, expand_ref, mid_ref, out_ref, square_ref, flat, hold):
    count = bgram_ref[64:65, 64:65]
    square_of = jnp.concatenate([bgram_ref[...], jnp.zeros((56, 128), F32)], axis=0)
    weights = expand_ref[...].astype(F32)
    product = dot(square_of, weights, precision=HIGH)
    mean = product[64:65] / count
    variance = jnp.sum(weights * product, axis=0, keepdims=True) / count - mean * mean
    inverse = lax.rsqrt(variance + EPS)
    second, first = sum_ref[0:1] / count, sum_ref[1:2] / count
    plain = bgram_ref[0:64, 64:65]
    hat = (product[0:64] - mean * plain) * inverse
    hold[...] = mid_ref[0:1] * inverse * (cross_ref[0:64, :] - first * plain - second * hat)
    flat[...] = jnp.zeros_like(flat)
    for name, source in (("mb_expand", hold), ("mb_depth", ddepth_ref)):
        offset, (rows, width) = OFFSETS[name]
        put_matrix(flat, lambda r, t: source[r, 128 * t : 128 * t + 128], 0, offset, rows, width)
    out_ref[...] = flat[0:EARLY_ROWS, :]
    total = flat[0:EARLY_ROWS, :]
    square_ref[...] = jnp.broadcast_to(jnp.sum(total * total).reshape(1, 1), (8, 128))


def expand_finish(cross, ddepth, sums, bgram, expand_w, mid_norm):
    return pl.pallas_call(
        expand_finish_kernel,
        out_shape=(jax.ShapeDtypeStruct((EARLY_ROWS, 128), F32), jax.ShapeDtypeStruct((8, 128), F32)),
        in_specs=[VMEM_SPEC] * 6,
        out_specs=(VMEM_SPEC,) * 2,
        scratch_shapes=[pltpu.VMEM((EARLY_ROWS + 8, 128), F32), pltpu.VMEM((STEM_CH, EXPAND), F32)],
        compiler_params=params_of(),
        cost_estimate=cost(3),
        name="expand_finish",
    )(cross, ddepth, sums, bgram, expand_w, mid_norm)


def finish_kernel(
    first_ref, packet_ref, gram_ref, stem_w_ref, norm_ref, spread_ref, early_ref, early_square_ref, shard_ref,
    out_ref, scalar_ref, big, grad_ref, flat,
):
    both = packet_ref[0:16]
    grad_ref[pl.ds(0, 16, stride=2), :] = both
    grad_ref[pl.ds(1, 16, stride=2), :] = pltpu.roll(both, 64, 1)
    spread_weights(spread_ref, stem_w_ref[...], big, 2)
    weights = stem_w_ref[...]
    gram = gram_ref[...][:, :96]
    mean, square = stem_stats(gram_ref[...], big[0:96, 0:256])
    inverse = lax.rsqrt(square - mean * mean + EPS)
    count = 4.0 * gram_ref[27:28, 27:28]
    product = dot(gram, big[0:96, 0:256].astype(F32), precision=HIGH)
    cross = jnp.zeros((32, STEM_CH), F32)
    plain = jnp.zeros((32, STEM_CH), F32)
    sums = jnp.broadcast_to(gram[:, 27:28], (96, 128))
    for pair in range(2):
        spread = spread_ref[pair][0:96].astype(F32)
        wide = dot(spread, product[:, 128 * pair : 128 * pair + 128], TN, precision=HIGH)
        cross = cross + wide[0:32, 0:64] + wide[32:64, 64:128]
        wide = dot(spread, sums, TN, precision=HIGH)
        plain = plain + wide[0:32, 0:64] + wide[32:64, 0:64]
    at = lax.broadcasted_iota(jnp.int32, (32, STEM_CH), 0)
    taps = at < 27
    grad = jnp.where(taps, grad_ref[:, 0:64], 0.0)
    first = grad_ref[27:28, 0:64]
    second = (jnp.sum(grad * weights, axis=0, keepdims=True) - mean * first) * inverse
    hat = (cross - mean * plain) * inverse
    result = norm_ref[0:1] * inverse * (grad - (plain * first + hat * second) / count)
    result = jnp.where(taps, result, jnp.where(at == 27, second, jnp.where(at == 28, first, 0.0)))
    square = packet_ref[16:17, 1:2] + early_square_ref[0:1, 0:1] + jnp.sum(result * result).reshape(1, 1)
    norm = jnp.sqrt(square)
    lane = lax.broadcasted_iota(jnp.int32, (8, 128), 1)
    scale = CLIP / jnp.maximum(norm, CLIP)
    scalar_ref[...] = jnp.where(lane == 0, packet_ref[16:17, 0:1], jnp.where(lane == 1, norm, scale))
    grad_ref[:, 0:64] = result
    lane = lax.broadcasted_iota(jnp.int32, (16, 128), 1)
    both = jnp.where(
        lane < 64, grad_ref[pl.ds(0, 16, stride=2), :], pltpu.roll(grad_ref[pl.ds(1, 16, stride=2), :], 64, 1)
    )
    rows = shard_ref.shape[0]
    flat[0:16, :] = early_ref[0:16] + both
    flat[16:EARLY_ROWS, :] = early_ref[16:EARLY_ROWS]
    flat[EARLY_ROWS:, :] = jnp.zeros((flat.shape[0] - EARLY_ROWS, 128), F32)
    begin = jnp.minimum(first_ref[0] * rows, EARLY_ROWS)
    out_ref[...] = shard_ref[...] + flat[pl.ds(begin, rows), :]


def finish(me, packet, gram, stem_w, norm, spread, early, early_square, shard):
    rows = shard.shape[0]
    return pl.pallas_call(
        finish_kernel,
        out_shape=(jax.ShapeDtypeStruct((rows, 128), F32), jax.ShapeDtypeStruct((8, 128), F32)),
        in_specs=[SMEM_SPEC] + [VMEM_SPEC] * 8,
        out_specs=(VMEM_SPEC,) * 2,
        scratch_shapes=[
            pltpu.VMEM((TAPS, 256), BF16), pltpu.VMEM((32, 128), F32),
            pltpu.VMEM((round_up(EARLY_ROWS + rows, 8), 128), F32),
        ],
        compiler_params=params_of(),
        cost_estimate=cost(4),
        name="finish",
    )(me, packet, gram, stem_w, norm, spread, early, early_square, shard)


def levels_of(devices):
    levels = []
    stride = 1
    while stride < devices:
        radix = 2 if stride == 1 or devices // stride == 2 else 4
        levels.append((stride, radix))
        stride *= radix
    return levels


def pairs_of(devices, mask):
    return [(i, i ^ mask) for i in range(devices)]


def add_level(v, moved):
    return v + moved[0] if len(moved) == 1 else (v + moved[0]) + (moved[1] + moved[2])


def send_level(v, devices, level):
    stride, radix = level
    return [lax.ppermute(v, "dp", pairs_of(devices, stride * j)) for j in range(1, radix)]


def exchange(v, devices, levels):
    for level in levels:
        v = add_level(v, send_level(v, devices, level))
    return v


def spread_blocks(blocks, ids, devices, level):
    stride, radix = level
    moved = send_level(blocks, devices, level)
    return jnp.concatenate([blocks] + moved), jnp.concatenate([ids ^ (stride * j) for j in range(radix)])


def take(blocks, digit, axis):
    return lax.dynamic_index_in_dim(blocks, digit, axis, keepdims=False)


class Scatter:
    def __init__(self, keep, send, devices, me, low, high):
        self.devices, self.me, self.low, self.high = devices, me, low, high
        self.levels = levels_of(devices)
        self.at = 0
        self.mine, self.parts = [keep], [send]
        self.moved = []

    def launch(self):
        stride, radix = self.levels[self.at]
        top = stride * radix == self.devices
        self.moved = []
        for j, part in zip(range(1, radix), self.parts):
            pairs = pairs_of(self.devices, stride * j)
            if top:
                pairs = [(a, b) for a, b in pairs if self.low <= b // stride < self.high]
            self.moved.append(lax.ppermute(part, "dp", pairs))

    def land(self):
        terms = self.mine + self.moved
        self.at += 1
        if self.at == len(self.levels):
            total = sum(terms[1:], terms[0])
            self.result = total.reshape(total.shape[-2:])
            return
        if len(terms) > 2:
            terms = [sum(terms[1:], terms[0])]
        stride, radix = self.levels[self.at]
        digit = (self.me // stride) % radix
        span = self.high - self.low
        if stride * radix == self.devices:
            blocks = [t.reshape((span,) + t.shape[-2:]) for t in terms]
            part = lambda d: sum(take(b, jnp.clip(d - self.low, 0, span - 1), 0) for b in blocks)
            mine = jnp.where((digit >= self.low) & (digit < self.high), part(digit), 0.0)
        else:
            blocks = [t.reshape((-1, radix) + t.shape[-2:]) for t in terms]
            part = lambda d: sum(take(b, d, 1) for b in blocks)
            mine = part(digit)
        self.mine = [mine]
        self.parts = [part(digit ^ j) for j in range(1, radix)]

    def finish(self):
        if not self.moved:
            self.launch()
        self.land()
        while self.at < len(self.levels):
            self.launch()
            self.land()
        return self.result


def tie(*values):
    return lax.optimization_barrier(values)


def on_device(images, res_ids, labels, rel_index, master, first_moment, second_moment, ema_weights):
    devices = lax.axis_size("dp")
    me = lax.axis_index("dp").astype(jnp.int32)
    length = master.shape[0]
    rows = length // 128
    held = round_up(rows, 16)
    images_total = res_ids.shape[0] * devices

    levels = levels_of(devices)
    low_master = lax.optimization_barrier(master.astype(BF16).reshape(rows, 128))
    blocks, ids = spread_blocks(
        jnp.pad(low_master, ((0, held - rows), (0, 0)))[None], me[None], devices, levels[-1]
    )
    stem_part = lax.dynamic_update_slice(
        jnp.zeros((16 + rows, 128), BF16), low_master, (jnp.minimum(me * rows, 16), 0)
    )[:16]
    patches, gram, mask = make_patches(res_ids, images)
    packet = jnp.concatenate([gram, stem_part.astype(F32)], axis=0)
    packet, blocks = tie(packet, blocks)
    packet = exchange(packet, devices, levels[:-1])
    packet, blocks = tie(packet, blocks)
    for level in levels[-2:0:-1]:
        blocks, ids = spread_blocks(blocks, ids, devices, level)
    packet = exchange(packet, devices, levels[-1:])
    gram = packet[:96]
    stem_flat = packet[96 : 96 + STEM_ROWS].reshape(-1)

    spread = jnp.asarray(spread_taps(), BF16)
    stem_w = jnp.pad(stem_flat[: 27 * STEM_CH].reshape(27, STEM_CH), ((0, 5), (0, 0)))
    stem_norm = stem_flat[27 * STEM_CH : STEM_END].reshape(2, STEM_CH)
    base, stem_slope, bgram = stem_forward(patches, gram, stem_w, stem_norm, spread)
    bgram, blocks = tie(bgram, blocks)
    others = lax.ppermute(blocks, "dp", pairs_of(devices, 1))
    bgram = exchange(bgram, devices, levels[:-1])
    bgram, others = tie(bgram, others)
    sent = send_level(bgram, devices, levels[-1])
    p = unpack([blocks, others], jnp.concatenate([ids, ids ^ 1]), rows, ALL_SHAPES)
    bgram = add_level(bgram, sent)
    depth, act1, slope1, stat = depth_forward(mask, base, p["mb_expand"], bgram, p["mid_norm"], p["mb_depth"])
    stat = exchange(stat[:2].reshape(12, 128), devices, levels).reshape(2, EXPAND)
    slots = slots_of(rel_index)
    slots = jnp.pad(slots, ((0, 1), (0, 1)), constant_values=2 * WIDE - 1).reshape(2 * WIDE, 1)
    pick = squeeze_lanes()
    pick, pick_back = jnp.asarray(pick, BF16), jnp.asarray(pick.T, BF16)
    bias = build_bias(p["rel_table"], slots, pick)

    act2, slope2, block, skipped, normed, project, vec, small = excite_forward(res_ids, mask, depth, stat, bgram, base, p)
    blended, weights = attend_forward(res_ids, project, bias)
    loss, dblend, dskip, g_short, g_out, g_out_b, g_mnorm, g_in, g_in_b, vectors, few = mlp_both(
        1.0 / images_total, res_ids, labels, skipped, blended, p
    )

    core = (me % 2).reshape(1)
    top_radix = levels_of(devices)[-1][1]

    def scattered(grads, begin, end):
        span = devices // top_radix
        low = begin // length // span
        high = (end - 1) // length // span + 1
        keep, send = pack(core, grads, low * span * rows, (high - low) * span, rows, held)
        return Scatter(keep, send, devices, me, low, high)

    middle = scattered(
        {
            "attn_out": g_out, "out_bias": g_out_b, "mlp_norm": g_mnorm, "mlp_in": g_in, "mlp_in_bias": g_in_b,
        },
        OFFSETS["attn_out"][0], OFFSETS["mlp_out"][0],
    )
    dblend, middle.parts = tie(dblend, middle.parts)
    middle.launch()
    vectors = lax.all_gather(vectors, "dp", axis=0, tiled=False)

    dq, dk, dv, dbias = attend_backward(project, blended, dblend, weights)
    dbias, middle.moved = tie(dbias, middle.moved)
    middle.land()
    dbias, middle.parts = tie(dbias, middle.parts)
    middle.launch()
    g_table = bias_back(dbias, slots, pick_back)
    dq, g_table = tie(dq, g_table)
    g_qkv, g_pre, dblock, g_proj, g_mbshort, dbase, g_down, g_down_b, g_up, g_up_b, dpool = proj_backward(
        res_ids, dq, dk, dv, normed, dskip, block, act2, vec, small, base, p
    )
    late = scattered(
        {
            "mb_short": g_mbshort, "se_down": g_down, "se_down_bias": g_down_b, "se_up": g_up, "se_up_bias": g_up_b,
            "mb_proj": g_proj, "at_short": g_short, "pre_norm": g_pre, "qkv": g_qkv, "rel_table": g_table,
        },
        OFFSETS["mb_short"][0], OFFSETS["mlp_norm"][0],
    )
    dblock, late.parts, middle.moved = tie(dblock, late.parts, middle.moved)
    late.launch()
    middle.land()
    dblock, middle.parts = tie(dblock, middle.parts)
    middle.launch()
    du, sums = excite_backward(dblock, p["mb_proj"], vec, dpool, slope2, depth)
    sums = exchange(jnp.concatenate([sums[:2].reshape(12, 128), few[:4].reshape(32, 128)], axis=0), devices, levels)
    sums, late.moved = tie(sums, late.moved)
    late.land()
    sums, late.parts = tie(sums, late.parts)
    late.launch()
    few = sums[12:].reshape(4, 1024)
    dw_sums = sums[:12].reshape(2, EXPAND)
    du, cross, g_depth, sums = depth_backward(
        mask, du, depth, vec, dw_sums, bgram, base, p["mb_expand"], p["dw_norm"], p["mb_depth"], act1, slope1
    )
    sums, late.moved = tie(sums, late.moved)
    late.land()
    mid_sums = sums[:2].reshape(12, 128)
    cross = jnp.concatenate([cross, g_depth], axis=0)
    steps = [(1 << k, 2) for k in range(devices.bit_length() - 1)]
    for k, level in enumerate(levels):
        sent = send_level(mid_sums, devices, level)
        other = send_level(cross, devices, steps[k])
        mid_sums, cross = tie(add_level(mid_sums, sent), add_level(cross, other))
        if k == 0:
            late.launch()
    mid_sums = mid_sums.reshape(2, EXPAND)
    sent = send_level(cross, devices, steps[len(levels)])
    g_norms = jnp.concatenate([mid_sums, dw_sums[1:2], dw_sums[0:1]], axis=0)

    stem = stem_backward(
        mask, patches, stem_slope, dbase, du, mid_sums, bgram, base, p["mb_expand"], p["mid_norm"], spread
    )
    stem, sent, late.moved = tie(stem, sent, late.moved)
    cross = add_level(cross, sent)
    shard, square = shard_parts(me.reshape(1), length, late.finish(), middle.finish(), few, vectors, g_norms)
    lane = lax.broadcasted_iota(jnp.int32, (8, 128), 1)
    scalars = jnp.where(lane == 0, loss, jnp.where(lane == 1, square, 0.0))
    packet = jnp.concatenate([stem.reshape(16, 128), scalars], axis=0)
    cross, packet = tie(cross, packet)
    cross = exchange(cross, devices, steps[len(levels) + 1 :])
    packet = exchange(packet, devices, levels)
    early_grad, early_square = expand_finish(cross[:72], cross[72:], mid_sums, bgram, p["mb_expand"], p["mid_norm"])
    shard, scalars = finish(
        me.reshape(1), packet, gram, stem_w, stem_norm, spread, early_grad, early_square, shard
    )
    loss_sum, grad_norm = scalars[0, 0], scalars[0, 1]
    shard = shard.reshape(length)
    clipped = shard * scalars[0, 2]
    moment_one = BETA_ONE * first_moment + (1.0 - BETA_ONE) * clipped
    moment_two = BETA_TWO * second_moment + (1.0 - BETA_TWO) * clipped * clipped
    update = (
        moment_one
        / (1.0 - BETA_ONE**STEP)
        / (jnp.sqrt(moment_two / (1.0 - BETA_TWO**STEP)) + ADAM_EPS)
    )
    weights_out = master - RATE * (update + DECAY * master)
    averaged = EMA_DECAY * ema_weights + (1.0 - EMA_DECAY) * weights_out
    return (
        loss_sum,
        grad_norm,
        weights_out,
        moment_one,
        moment_two,
        averaged,
        weights_out.astype(BF16),
    )


def solution(mesh):
    in_specs = (
        P("dp", None, None, None),
        P("dp"),
        P("dp"),
        P(),
        P("dp"),
        P("dp"),
        P("dp"),
        P("dp"),
    )
    out_specs = (P(), P(), P("dp"), P("dp"), P("dp"), P("dp"), P("dp"))
    return jax.shard_map(
        on_device, mesh=mesh, in_specs=in_specs, out_specs=out_specs, check_vma=False
    )
```

```python
import functools
import math

import jax
import jax.numpy as jnp
import numpy as np
from jax import lax
from jax.experimental import pallas as pl
from jax.experimental.pallas import tpu as pltpu
from jax.sharding import PartitionSpec as P

STEM_CH = 64
MB_CH = 192
EXPAND = 768
SQUEEZE = 48
DIM = 384
HEADS = 12
HEAD_DIM = 32
MLP = 1536
CLASSES = 1000
CANVAS = 384
SMALL_RES = 224
STEP = 10

EPS = 1e-05
CLIP = 0.05
BETA_ONE = 0.5
BETA_TWO = 0.5
ADAM_EPS = 1e-08
RATE = 0.05
DECAY = 0.05
EMA_DECAY = 0.9
SMOOTH = 0.1

SIDE = CANVAS // 8
SMALL_SIDE = SMALL_RES // 8
HALF = SIDE // 2
QUAD = HALF * HALF
PLACES = SIDE * SIDE
TAPS = 288
BLOCK = 128
CHUNKS = EXPAND // BLOCK
WIDE = 2 * HALF * HALF
TOKENS = QUAD

F32 = jnp.float32
BF16 = jnp.bfloat16
HIGH = lax.Precision.HIGHEST
GELU_A = math.sqrt(2.0 / math.pi)
GELU_B = 0.044715


def layout():
    table_slots = (2 * (CANVAS // 16) - 1) ** 2
    return [
        ("stem_w", (3, 3, 3, STEM_CH)),
        ("stem_norm", (2, STEM_CH)),
        ("mb_short", (STEM_CH, MB_CH)),
        ("mb_expand", (STEM_CH, EXPAND)),
        ("mid_norm", (2, EXPAND)),
        ("mb_depth", (9, EXPAND)),
        ("dw_norm", (2, EXPAND)),
        ("se_down", (EXPAND, SQUEEZE)),
        ("se_down_bias", (SQUEEZE,)),
        ("se_up", (SQUEEZE, EXPAND)),
        ("se_up_bias", (EXPAND,)),
        ("mb_proj", (EXPAND, MB_CH)),
        ("at_short", (MB_CH, DIM)),
        ("pre_norm", (2, MB_CH)),
        ("qkv", (MB_CH, 3 * DIM)),
        ("attn_out", (DIM, DIM)),
        ("out_bias", (DIM,)),
        ("rel_table", (HEADS, table_slots)),
        ("mlp_norm", (2, DIM)),
        ("mlp_in", (DIM, MLP)),
        ("mlp_in_bias", (MLP,)),
        ("mlp_out", (MLP, DIM)),
        ("mlp_out_bias", (DIM,)),
        ("head_norm", (2, DIM)),
        ("head_w", (DIM, CLASSES)),
        ("head_bias", (CLASSES,)),
    ]


def offsets():
    table = {}
    offset = 0
    for name, shape in layout():
        table[name] = (offset, shape)
        offset += math.prod(shape)
    return table


OFFSETS = offsets()
STEM_END = OFFSETS["mb_short"][0]
EARLY_END = OFFSETS["se_down"][0]


def dot(a, b, dims=((1,), (0,)), precision=None):
    return lax.dot_general(a, b, (dims, ((), ())), precision=precision, preferred_element_type=F32)


NT = ((1,), (1,))
TN = ((0,), (0,))


def gelu_pair(u):
    sq = u * u
    t = jnp.tanh(u * (GELU_A + (GELU_A * GELU_B) * sq))
    half = 0.5 + 0.5 * t
    slope = half + (0.5 * u) * (1.0 - t * t) * (GELU_A + (3.0 * GELU_A * GELU_B) * sq)
    return u * half, slope


def gelu(u):
    sq = u * u
    t = jnp.tanh(u * (GELU_A + (GELU_A * GELU_B) * sq))
    return u * (0.5 + 0.5 * t)


def limit_of(res_ref):
    return jnp.where(res_ref[0] == 1, SIDE, SMALL_SIDE)


def group_mask(group, limit, first_row, rows, lanes):
    place = lax.broadcasted_iota(jnp.int32, (rows, lanes), 0) + first_row
    up = place // HALF
    across = place - up * HALF
    y = 2 * up + group // 2
    x = 2 * across + group % 2
    return jnp.where((y < limit) & (x < limit), 1.0, 0.0)


def cost(us):
    return pl.CostEstimate(flops=int(us * 2.0e9), bytes_accessed=1000, transcendentals=0)


def params_of(megabytes):
    return pltpu.CompilerParams(vmem_limit_bytes=megabytes * 1024 * 1024)


SMEM_SPEC = pl.BlockSpec(memory_space=pltpu.SMEM)
VMEM_SPEC = pl.BlockSpec(memory_space=pltpu.VMEM)


def patch_kernel(res_ref, img_ref, stem_ref, patch_ref, packet_ref, mask_ref):
    limit = limit_of(res_ref)
    lane = lax.broadcasted_iota(jnp.int32, (32, CANVAS), 1)
    rem = lane % 8
    row = lax.broadcasted_iota(jnp.int32, (SIDE, CANVAS), 0)
    col = lax.broadcasted_iota(jnp.int32, (SIDE, CANVAS), 1)
    wanted = jnp.where(row < HALF, 2 * row, 2 * (row - HALF) + 1)
    pick = jnp.where(col // 8 == wanted, 1.0, 0.0).astype(BF16)
    sub = lax.broadcasted_iota(jnp.int32, (8, CANVAS), 0)
    tap = lax.broadcasted_iota(jnp.int32, (2 * HALF, TAPS), 1)
    ones_at = (tap % 64 == 27) & (tap < 256)

    def step(i, _):
        bands = [[], [], [], []]
        above = []
        for c in range(3):
            before = img_ref[0, c, pl.ds(pl.multiple_of(jnp.maximum(32 * i - 16, 0), 16), 16), :]
            above.append(jnp.where(i > 0, before.astype(F32)[8:16], 0.0))
            for q in range(2):
                band = img_ref[0, c, pl.ds(pl.multiple_of(32 * i + 16 * q, 16), 16), :].astype(F32)
                bands[2 * q].append(band[0:8])
                bands[2 * q + 1].append(band[8:16])
        made = []
        for q in range(4):
            prev = above if q == 0 else bands[q - 1]
            edge = jnp.zeros((8, CANVAS), F32)
            for c in range(3):
                edge = jnp.where(sub == c, prev[c][7:8], edge)
            rows = jnp.concatenate(bands[q] + [edge], axis=0)
            rolled = pltpu.roll(rows, 8, 1)
            pieces = [jnp.where((rem == 7) & (lane >= 8), rolled, 0.0)]
            pieces += [jnp.where(rem == r, rows, 0.0) for r in range(8)]
            wide = jnp.concatenate(pieces, axis=0).astype(BF16)
            made.append(dot(pick, wide, NT))
        for py in range(2):
            for px in range(2):
                group = 2 * py + px
                two = jnp.concatenate(
                    [made[py][HALF * px : HALF * px + HALF], made[2 + py][HALF * px : HALF * px + HALF]],
                    axis=0,
                )
                inside = group_mask(group, limit, 2 * HALF * i, 2 * HALF, 128)
                mask_ref[pl.ds(pl.multiple_of(group * QUAD + 2 * HALF * i, 16), 2 * HALF), :] = inside
                two = jnp.where(ones_at, 1.0, two) * inside[:, 0:1]
                patch_ref[pl.ds(pl.multiple_of(group * QUAD + 2 * HALF * i, 16), 2 * HALF), :] = (
                    two.astype(BF16)
                )
        return 0

    lax.fori_loop(0, HALF // 2, step, 0)
    patches = patch_ref[...]
    gram = dot(patches, patches, TN)
    total = gram[0:96, 0:96]
    for px in range(1, 4):
        total = total + gram[64 * px : 64 * px + 96, 64 * px : 64 * px + 96]
    packet_ref[0:96, :] = jnp.concatenate([total, jnp.zeros((96, 32), F32)], axis=1)
    packet_ref[96:112, :] = stem_ref[...].astype(F32)


def make_patches(res_ids, images, stem):
    return pl.pallas_call(
        patch_kernel,
        out_shape=(
            jax.ShapeDtypeStruct((PLACES, TAPS), BF16),
            jax.ShapeDtypeStruct((112, 128), F32),
            jax.ShapeDtypeStruct((PLACES, 128), F32),
        ),
        in_specs=[SMEM_SPEC, VMEM_SPEC, VMEM_SPEC],
        out_specs=(VMEM_SPEC,) * 3,
        compiler_params=params_of(16),
        cost_estimate=cost(8),
        name="patches",
    )(res_ids, images, stem)


def spread_taps():
    table = np.zeros((8, TAPS, 64), np.float32)
    for px in range(4):
        for py in range(4):
            pair, half = px * 2 + py // 2, py % 2
            for dy in range(3):
                for dx in range(3):
                    for c in range(3):
                        ry = 2 * py + dy - 1
                        r = 24 + c if ry < 0 else 8 * c + ry
                        k = (2 * px + dx) * 32 + r
                        table[pair, k, half * 32 + (dy * 3 + dx) * 3 + c] = 1.0
    return table


def spread_weights(spread_ref, stem_w, out_ref, pairs=8):
    zero = jnp.zeros((32, STEM_CH), F32)
    double = jnp.concatenate(
        [jnp.concatenate([stem_w, zero], axis=1), jnp.concatenate([zero, stem_w], axis=1)], axis=0
    ).astype(BF16)
    for pair in range(pairs):
        out_ref[:, 128 * pair : 128 * pair + 128] = dot(spread_ref[pair], double).astype(BF16)


def stem_stats(gram, first_phases):
    weights = first_phases.astype(F32)
    product = dot(gram[:, :96], weights, precision=HIGH)
    second = jnp.sum(weights * product, axis=0, keepdims=True)
    first = product[27:28]
    count = 4.0 * gram[27:28, 27:28]
    both = jnp.concatenate([first, second, jnp.zeros((6, 256), F32)], axis=0)
    folded = both[:, 0:64] + both[:, 64:128] + both[:, 128:192] + both[:, 192:256]
    return folded[0:1] / count, folded[1:2] / count


def pairs_apart(rows, hold):
    hold[pl.ds(0, 16, stride=2), :] = rows
    hold[pl.ds(1, 16, stride=2), :] = pltpu.roll(rows, 64, 1)
    return hold[:, 0:64]


def pairs_together(rows, hold):
    hold[:, 0:64] = rows
    lane = lax.broadcasted_iota(jnp.int32, (16, 128), 1)
    return jnp.where(
        lane < 64, hold[pl.ds(0, 16, stride=2), :], pltpu.roll(hold[pl.ds(1, 16, stride=2), :], 64, 1)
    )


def stem_params(packet_ref, hold):
    rows = pairs_apart(packet_ref[96:112, :], hold)
    at = lax.broadcasted_iota(jnp.int32, (32, STEM_CH), 0)
    return jnp.where(at < 27, rows, 0.0), rows[27:28], rows[28:29]


STEM_STEPS = 3
STEM_BLOCK = PLACES // STEM_STEPS


def stem_kernel(patch_ref, packet_ref, spread_ref, base_ref, slope_ref, bgram_ref, big, hold, norm):
    @pl.when(pl.program_id(0) == 0)
    def _():
        weights, gain, shift = stem_params(packet_ref, hold)
        spread_weights(spread_ref, weights, big)
        mean, square = stem_stats(packet_ref[0:96, :], big[0:96, 0:256])
        gain = gain * lax.rsqrt(square - mean * mean + EPS)
        shift = shift - mean * gain
        norm[0:1, :] = jnp.concatenate([gain] * 4, axis=1)
        norm[1:2, :] = jnp.concatenate([shift] * 4, axis=1)
        bgram_ref[...] = jnp.zeros_like(bgram_ref)

    gain, shift = norm[0:1, :], norm[1:2, :]
    lane = lax.broadcasted_iota(jnp.int32, (STEM_BLOCK, 128), 1)
    block = patch_ref[...]
    pooled = jnp.zeros((STEM_BLOCK, 128), F32)
    for j in range(4):
        u = dot(block, big[:, 256 * j : 256 * j + 256]) * gain + shift
        value, slope = gelu_pair(u)
        slope_ref[:, 256 * j : 256 * j + 256] = slope.astype(BF16)
        pooled = pooled + value[:, 0:128] + value[:, 128:256]
    pooled = (pooled + pltpu.roll(pooled, 64, 1)) * (1.0 / 16.0)
    ones = block[:, 0:128].astype(F32)
    ones = pltpu.roll(ones, 64 - 27, 1)
    pooled = jnp.where(lane < 64, pooled, jnp.where(lane == 64, ones, 0.0)).astype(BF16)
    base_ref[...] = pooled
    masked = (pooled.astype(F32) * pooled[:, 64:65].astype(F32)).astype(BF16)
    bgram_ref[...] = bgram_ref[...] + dot(masked, pooled, TN)[0:72]


def stem_forward(patches, packet, spread):
    part = lambda width: pl.BlockSpec((STEM_BLOCK, width), lambda i: (i, 0))
    whole = lambda shape: pl.BlockSpec(shape, lambda i: (0,) * len(shape))
    return pl.pallas_call(
        stem_kernel,
        grid=(STEM_STEPS,),
        out_shape=(
            jax.ShapeDtypeStruct((PLACES, 128), BF16),
            jax.ShapeDtypeStruct((PLACES, 1024), BF16),
            jax.ShapeDtypeStruct((72, 128), F32),
        ),
        in_specs=[part(TAPS), whole((112, 128)), whole((8, TAPS, 64))],
        out_specs=(part(128), part(1024), whole((72, 128))),
        scratch_shapes=[
            pltpu.VMEM((TAPS, 1024), BF16), pltpu.VMEM((32, 128), F32), pltpu.VMEM((8, 256), F32),
        ],
        compiler_params=params_of(28),
        cost_estimate=cost(10),
        name="stem_forward",
    )(patches, packet, spread)


def taps_row(load, weight, py):
    sources = [(1, -1), (0, 0), (1, 0)] if py == 0 else [(0, 0), (1, 0), (0, 1)]
    rows = [[load(2 * gy + px, off) for px in range(2)] for gy, off in sources]

    def column(px, dx):
        total = rows[0][px] * weight(0, dx)
        total = total + rows[1][px] * weight(1, dx)
        return total + rows[2][px] * weight(2, dx)

    even = column(0, 1) + column(1, 2) + shift_down(column(1, 0))
    odd = column(1, 1) + column(0, 0) + shift_up(column(0, 2))
    return even, odd


def shift_down(v):
    at = lax.broadcasted_iota(jnp.int32, v.shape, 0)
    return jnp.where(at == 0, 0.0, pltpu.roll(v, 1, 0))


def shift_up(v):
    at = lax.broadcasted_iota(jnp.int32, v.shape, 0)
    return jnp.where(at == HALF - 1, 0.0, pltpu.roll(v, HALF - 1, 0))


def bn_stats(bgram, expand_w, count):
    weights = expand_w.astype(F32)
    square_of = jnp.concatenate([bgram, jnp.zeros((56, 128), F32)], axis=0)
    product = dot(square_of, weights, precision=HIGH)
    mean = product[64:65] / count
    second = jnp.sum(weights * product, axis=0, keepdims=True) / count
    return mean, lax.rsqrt(second - mean * mean + EPS)


def depth_kernel(mask_ref, base_ref, expand_ref, bgram_ref, norm_ref, depth_ref, out_ref, act_ref, slope_ref, stat_ref, pad, wide):
    count = bgram_ref[64:65, 64:65]
    mean, inverse = bn_stats(bgram_ref[...], expand_ref[...], count)
    gain = norm_ref[0:1] * inverse
    shift = norm_ref[1:2] - mean * gain
    zero = jnp.zeros((4, 1, HALF, BLOCK), F32)
    pad[:, 0:1] = zero
    pad[:, HALF + 1 : HALF + 2] = zero
    wide[...] = dot(base_ref[...], expand_ref[...])
    rows = 8 * HALF
    for group in range(4):

        def fill(i, _, group=group):
            first = pl.multiple_of(group * QUAD + rows * i, 16)
            at = pl.ds(first, rows)
            x = wide[at, :]
            inside = mask_ref[at, :]
            value, slope = gelu_pair(x * gain + shift)
            value = value * inside
            act_ref[at, :] = value.astype(BF16)
            slope_ref[at, :] = (slope * inside).astype(BF16)
            for k in range(8):
                pad[group, 8 * i + k + 1] = value[HALF * k : HALF * k + HALF]
            return 0

        lax.fori_loop(0, QUAD // rows, fill, 0)

    def weight(dy, dx):
        return depth_ref[3 * dy + dx : 3 * dy + dx + 1]

    def fold(v):
        return v[0:8] + v[8:16] + v[16:24]

    def step(up, sums):
        first, second = sums
        for py in range(2):
            made = taps_row(lambda g, off: pad[g, up + 1 + off], weight, py)
            for px in range(2):
                at = pl.ds(pl.multiple_of((2 * py + px) * QUAD + HALF * up, 8), HALF)
                x = made[px] * mask_ref[at, :]
                out_ref[at, :] = x
                first = first + fold(x)
                second = second + fold(x * x)
        return first, second

    sums = lax.fori_loop(0, HALF, step, (jnp.zeros((8, BLOCK), F32),) * 2)
    rows_out = [jnp.sum(s, axis=0, keepdims=True) for s in sums]
    stat_ref[...] = jnp.concatenate(rows_out + [jnp.zeros((6, BLOCK), F32)], axis=0)


def depth_forward(mask, base, expand_w, bgram, mid_norm, mb_depth):
    col = lambda rows: pl.BlockSpec((rows, BLOCK), lambda j: (0, j))
    whole = lambda rows: pl.BlockSpec((rows, BLOCK), lambda j: (0, 0))
    return pl.pallas_call(
        depth_kernel,
        grid=(CHUNKS,),
        out_shape=(
            jax.ShapeDtypeStruct((PLACES, EXPAND), F32),
            jax.ShapeDtypeStruct((PLACES, EXPAND), BF16),
            jax.ShapeDtypeStruct((PLACES, EXPAND), BF16),
            jax.ShapeDtypeStruct((8, EXPAND), F32),
        ),
        in_specs=[whole(PLACES), whole(PLACES), col(128), whole(72), col(2), col(9)],
        out_specs=(col(PLACES),) * 3 + (col(8),),
        scratch_shapes=[pltpu.VMEM((4, HALF + 2, HALF, BLOCK), F32), pltpu.VMEM((PLACES, BLOCK), F32)],
        compiler_params=params_of(56),
        cost_estimate=cost(25),
        name="depth_forward",
    )(mask, base, expand_w, bgram, mid_norm, mb_depth)


EARLY_ROWS = 576
STEM_ROWS = 15


def runs_of(offset, rows, width):
    period = min(128 // math.gcd(width, 128), rows)
    stride = period * width // 128 if rows > period else 1
    for j in range(period):
        start = offset + j * width
        yield j, period, start // 128, start % 128, -(-(rows - j) // period), stride


def rows_at(first, count, stride):
    return pl.ds(first, count) if stride == 1 or count == 1 else pl.ds(first, count, stride=stride)


def chunks_of(count, size=128):
    for begin in range(0, count, size):
        yield begin, min(size, count - begin)


def round_up(n, m):
    return -(-n // m) * m


def take_matrix(flat, out_ref, hold, offset, rows, width):
    direct = True
    for j, period, first, shift, count, stride in runs_of(offset, rows, width):
        direct = period == 1
        for t in range(-(-width // 128)):
            wide = min(128, width - 128 * t)
            for begin, size in chunks_of(count):
                at = first + t + begin * stride
                value = flat[rows_at(at, size, stride), :]
                if shift:
                    if shift + wide > 128:
                        lane = lax.broadcasted_iota(jnp.int32, (size, 128), 1)
                        value = jnp.where(lane >= shift, value, flat[rows_at(at + 1, size, stride), :])
                    value = pltpu.roll(value, 128 - shift, 1)
                if direct:
                    out_ref[begin : begin + size, 128 * t : 128 * t + wide] = value[:, :wide].astype(out_ref.dtype)
                elif count == 1:
                    out_ref[j : j + 1, 128 * t : 128 * t + wide] = value[:, :wide].astype(out_ref.dtype)
                else:
                    hold[t, rows_at(j + begin * period, size, period), :] = value
    if not direct and count > 1:
        for t in range(-(-width // 128)):
            wide = min(128, width - 128 * t)
            out_ref[0:rows, 128 * t : 128 * t + wide] = hold[t, 0:rows, 0:wide].astype(out_ref.dtype)


def put_matrix(flat, value_of, base, offset, rows, width):
    for j, period, first, shift, count, stride in runs_of(offset, rows, width):
        tiles = -(-width // 128)
        for begin, size in chunks_of(count):
            before = None
            lane = lax.broadcasted_iota(jnp.int32, (size, 128), 1)
            picked = rows_at(j + begin * period, size, period)
            at = first - base + begin * stride
            for t in range(tiles):
                value = value_of(picked, t)
                if shift:
                    value = pltpu.roll(value, shift, 1)
                    mixed = jnp.where(lane >= shift, value, 0.0 if before is None else before)
                else:
                    mixed = value
                before = value
                where = rows_at(at + t, size, stride)
                full = 0 < t < tiles - 1 or (shift == 0 and width % 128 == 0)
                flat[where, :] = mixed if full else flat[where, :] + mixed
            if shift:
                where = rows_at(at + tiles, size, stride)
                flat[where, :] = flat[where, :] + jnp.where(lane < shift, before, 0.0)


def unpack_kernel(names, shapes, pieces, shard_rows, me_ref, masks_ref, *refs):
    blocks, outs, (flat, hold) = refs[:pieces], refs[pieces:-2], refs[-2:]
    base = 0
    for block in blocks:

        def place(k, _, block=block, base=base):
            where = pl.ds((masks_ref[base + k] ^ me_ref[0]) * shard_rows, shard_rows)
            flat[where, :] = block[k].astype(F32)[:shard_rows]
            return 0

        lax.fori_loop(0, block.shape[0], place, 0)
        base += block.shape[0]
    for name, shape, out in zip(names, shapes, outs):
        offset, own = OFFSETS[name]
        width = own[-1]
        rows = math.prod(own) // width
        if shape[0][0] > rows or shape[0][1] > width:
            out[...] = jnp.zeros_like(out)
        take_matrix(flat, out, hold, offset, rows, width)


def unpack(blocks, me, masks, shard_rows, shapes):
    names = tuple(shapes)
    kinds = tuple(shapes[n] for n in names)
    total = sum(b.shape[0] for b in blocks) * shard_rows + 8
    made = pl.pallas_call(
        functools.partial(unpack_kernel, names, kinds, len(blocks), shard_rows),
        out_shape=tuple(jax.ShapeDtypeStruct(*k) for k in kinds),
        in_specs=[SMEM_SPEC] * 2 + [VMEM_SPEC] * len(blocks),
        out_specs=(VMEM_SPEC,) * len(names),
        scratch_shapes=[pltpu.VMEM((total, 128), F32), pltpu.VMEM((8, EXPAND, 128), F32)],
        compiler_params=params_of(32),
        cost_estimate=cost(6),
        name="unpack",
    )(me, jnp.asarray(masks, jnp.int32), *blocks)
    return dict(zip(names, made))


EARLY_SHAPES = {
    "mb_short": ((128, MB_CH), BF16), "mb_expand": ((128, EXPAND), BF16), "mid_norm": ((2, EXPAND), F32),
    "mb_depth": ((9, EXPAND), F32), "dw_norm": ((2, EXPAND), F32),
}
LATE_SHAPES = {
    "se_down": ((EXPAND, SQUEEZE), BF16), "se_down_bias": ((1, SQUEEZE), F32), "se_up": ((SQUEEZE, EXPAND), BF16),
    "se_up_bias": ((1, EXPAND), F32), "mb_proj": ((EXPAND, MB_CH), BF16), "at_short": ((MB_CH, DIM), BF16),
    "pre_norm": ((2, MB_CH), F32), "qkv": ((MB_CH, 3 * DIM), BF16), "attn_out": ((DIM, DIM), BF16),
    "out_bias": ((1, DIM), F32), "rel_table": ((16, 2 * WIDE), F32), "mlp_norm": ((2, DIM), F32),
    "mlp_in": ((DIM, MLP), BF16), "mlp_in_bias": ((1, MLP), F32), "mlp_out": ((MLP, DIM), BF16),
    "mlp_out_bias": ((1, DIM), F32), "head_norm": ((2, DIM), F32), "head_w": ((DIM, CLASSES), BF16),
    "head_bias": ((1, CLASSES), F32),
}


ALL_SHAPES = EARLY_SHAPES | LATE_SHAPES


def pack_kernel(names, base, shards, shard_rows, core_ref, *refs):
    grads, (keep_ref, send_ref), (flat, hold) = refs[: len(names)], refs[len(names) : -2], refs[-2:]
    rows_all = flat.shape[0]
    step = 384

    def clear(i, _):
        flat[pl.ds(pl.multiple_of(i * step, 8), step), :] = jnp.zeros((step, 128), F32)
        return 0

    lax.fori_loop(0, rows_all // step, clear, 0)
    for name, grad in zip(names, grads):
        offset, own = OFFSETS[name]
        width = own[-1]
        rows = math.prod(own) // width
        tiles = -(-width // 128)
        read = lambda r, t: grad[r, 128 * t : 128 * t + 128]
        if grad.shape[1] < 128 * tiles:
            hold[tiles - 1, 0:rows, :] = jnp.zeros((rows, 128), F32)
            for t in range(tiles):
                wide = min(128, width - 128 * t)
                hold[t, 0:rows, 0:wide] = grad[0:rows, 128 * t : 128 * t + wide]
            read = lambda r, t: hold[t, r, :]
        put_matrix(flat, read, base, offset, rows, width)

    def share(k, _):
        block = flat[pl.ds(k * shard_rows, shard_rows), :]
        ours = k % 2 == core_ref[0]

        @pl.when(ours)
        def _():
            keep_ref[k // 2, 0:shard_rows] = block

        @pl.when(jnp.logical_not(ours))
        def _():
            send_ref[k // 2, 0:shard_rows] = block

        return 0

    lax.fori_loop(0, shards, share, 0)


def pack(core, grads, base, shards, shard_rows, held_rows):
    names = tuple(grads)
    total = -(-(shards * shard_rows + 8) // 384) * 384
    out = jax.ShapeDtypeStruct((shards // 2, held_rows, 128), F32)
    return pl.pallas_call(
        functools.partial(pack_kernel, names, base, shards, shard_rows),
        out_shape=(out, out),
        in_specs=[SMEM_SPEC] + [VMEM_SPEC] * len(names),
        out_specs=(VMEM_SPEC,) * 2,
        scratch_shapes=[pltpu.VMEM((total, 128), F32), pltpu.VMEM((2, EXPAND, 128), F32)],
        compiler_params=params_of(32),
        cost_estimate=cost(6),
        name="pack",
    )(core, *grads.values())


def shard_kernel(
    length, tall_out, tall_head, first_ref, late_ref, mid_ref, dw_ref, norm_ref, vector_ref, stem_ref, loss_ref,
    out_ref, packet_ref, flat, hold, left_out, left_head,
):
    rows = length // 128
    lead = 16
    flat[...] = jnp.zeros_like(flat)
    start = first_ref[0] * length
    lane = lax.broadcasted_iota(jnp.int32, (8, 128), 1)

    def add_rows(first, value):
        flat[pl.ds(first, value.shape[0]), :] = flat[pl.ds(first, value.shape[0]), :] + value

    devices = vector_ref.shape[0]
    part = min(devices, 128)

    def place(name, left_ref, at_left, at_right, tall):
        offset, (count, width) = OFFSETS[name]
        first = (start - offset + 2**20 * width) // width - 2**20
        inside = (first > -tall) & (first < count)
        held = jnp.where(inside, first, -tall)
        made = jnp.zeros((tall, 128 * -(-width // 128)), F32)
        for g in range(devices // part):
            group = slice(g * part, g * part + part)
            left_ref[g] = jnp.zeros_like(left_ref[g])
            left_ref[g, tall : tall + count, :] = vector_ref[group, at_left, 0:count].T
            right = vector_ref[group, at_right, 0 : hold.shape[2] * -(-width // 128)]
            made = made + dot(left_ref[g, pl.ds(held + tall, tall), :], right, precision=HIGH)
        tiles = -(-width // 128)
        for t in range(tiles):
            wide = min(128, made.shape[1] - 128 * t)
            hold[t, 0:tall, 0:wide] = made[:, 128 * t : 128 * t + wide]
        period = 128 // math.gcd(width, 128)
        stride = period * width // 128

        @pl.when(inside)
        def _():
            for j in range(period):
                begin = offset + (first + j) * width - start + 128 * lead
                row = begin // 128
                shift = begin - row * 128
                size = tall // period
                at_lane = lax.broadcasted_iota(jnp.int32, (size, 128), 1)
                for t in range(tiles):
                    value = hold[t, rows_at(j, size, period), :]
                    value = pltpu.roll(value, shift, 1)
                    where = rows_at(row + t, size, stride)
                    flat[where, :] = flat[where, :] + jnp.where(at_lane >= shift, value, 0.0)
                    where = rows_at(row + t + 1, size, stride)
                    flat[where, :] = flat[where, :] + jnp.where(at_lane < shift, value, 0.0)

    def place_row(offset, value):
        width = value.shape[1]
        begin = offset - start

        @pl.when((begin > -width) & (begin < length))
        def _():
            at = begin + 128 * lead
            row = at // 128
            shift = at - row * 128
            one = lane[0:1]
            for t in range(width // 128):
                tile = pltpu.roll(value[:, 128 * t : 128 * t + 128], shift, 1)
                add_rows(row + t, jnp.where(one >= shift, tile, 0.0))
                add_rows(row + t + 1, jnp.where(one < shift, tile, 0.0))

    place("mlp_out", left_out, 0, 1, tall_out)
    place("head_w", left_head, 2, 3, tall_head)
    place_row(OFFSETS["mlp_out_bias"][0], dw_ref[3:4, 0:DIM])
    place_row(OFFSETS["head_norm"][0], dw_ref[2:3, :])
    place_row(OFFSETS["head_bias"][0], dw_ref[4:5, :])
    place_row(OFFSETS["head_bias"][0] + EXPAND, dw_ref[5:6, 0:256])
    place_row(OFFSETS["mid_norm"][0], norm_ref[0:1, :])
    place_row(OFFSETS["mid_norm"][0] + EXPAND, norm_ref[1:2, :])
    place_row(OFFSETS["dw_norm"][0], dw_ref[1:2, :])
    place_row(OFFSETS["dw_norm"][0] + EXPAND, dw_ref[0:1, :])
    total = flat[lead : lead + rows, :] + late_ref[0:rows] + mid_ref[0:rows]
    out_ref[...] = total
    square = jnp.sum(total * total).reshape(1, 1)
    packet_ref[0:16, :] = stem_ref[...]
    packet_ref[16:24, :] = jnp.where(lane == 0, loss_ref[...], jnp.where(lane == 1, square, 0.0))


def shard_parts(me, length, late, mid, dw_sums, mid_sums, vectors, stem, loss):
    rows = length // 128
    devices = vectors.shape[0]
    part = min(devices, 128)

    def tall(name, unit):
        width = OFFSETS[name][1][1]
        return round_up(-(-length // width) + 1, unit)

    tall_out, tall_head = tall("mlp_out", 8), tall("head_w", 16)
    return pl.pallas_call(
        functools.partial(shard_kernel, length, tall_out, tall_head),
        out_shape=(jax.ShapeDtypeStruct((rows, 128), F32), jax.ShapeDtypeStruct((24, 128), F32)),
        in_specs=[SMEM_SPEC] + [VMEM_SPEC] * 7,
        out_specs=(VMEM_SPEC,) * 2,
        scratch_shapes=[
            pltpu.VMEM((rows + 1024, 128), F32),
            pltpu.VMEM((8, max(tall_out, tall_head), 128), F32),
            pltpu.VMEM((devices // part, MLP + 2 * tall_out, part), F32),
            pltpu.VMEM((devices // part, DIM + 2 * tall_head, part), F32),
        ],
        compiler_params=params_of(16),
        cost_estimate=cost(4),
        name="shard_parts",
    )(me, late, mid, dw_sums, mid_sums, vectors, stem, loss)


def squeeze_lanes():
    table = np.zeros((16 * 48, 16 * 24), np.float32)
    for e in range(16):
        for x in range(24):
            table[e * 48 + x, e * 24 + x] = 1.0
    return table


def slots_of(rel_index):
    last = TOKENS - 1
    corner = lambda i: rel_index[i].reshape(HALF, HALF)
    low_row = jnp.concatenate([corner(last), corner(last - HALF + 1)[:, 1:]], axis=1)
    high_row = jnp.concatenate([corner(HALF - 1), corner(0)[:, 1:]], axis=1)
    return jnp.concatenate([low_row, high_row[1:]], axis=0)


def one_hot(slot_ref, c):
    at = lax.broadcasted_iota(jnp.int32, (256, 2 * WIDE), 1)
    return jnp.where(slot_ref[256 * c : 256 * c + 256, :] == at, 1.0, 0.0).astype(BF16)


def bias_kernel(table_ref, slot_ref, pick_ref, out_ref, held):
    table = table_ref[...].astype(BF16)
    f = jnp.concatenate([dot(table, one_hot(slot_ref, c), NT) for c in range(2 * WIDE // 256)], axis=1)
    for x in range(HALF):
        turned = pltpu.roll(f, (WIDE * 2 - (HALF - 1 - x)) % (WIDE * 2), 1) if x != HALF - 1 else f
        held[16 * x : 16 * x + 16, :] = turned.astype(BF16)
    for part in range(3):
        made = dot(held[:, 768 * part : 768 * part + 768], pick_ref[...])
        for t in range(3):
            for x in range(HALF):
                out_ref[3 * part + t, pl.ds(x, HEADS, stride=HALF), :] = made[
                    16 * x : 16 * x + HEADS, 128 * t : 128 * t + 128
                ]


def build_bias(table, slots, pick):
    return pl.pallas_call(
        bias_kernel,
        out_shape=jax.ShapeDtypeStruct((9, HEADS * HALF, 128), F32),
        in_specs=[VMEM_SPEC] * 3,
        out_specs=VMEM_SPEC,
        scratch_shapes=[pltpu.VMEM((16 * HALF, 2 * WIDE), BF16)],
        compiler_params=params_of(16),
        cost_estimate=cost(8),
        name="bias_build",
    )(table, slots, pick)


def halves_of(v):
    high = v.astype(BF16)
    return high, (v - high.astype(F32)).astype(BF16)


def bias_back_step(grad_ref, slot_ref, pick_ref, out_ref, held):
    for part in range(3):
        rows = jnp.concatenate([grad_ref[3 * part + t] for t in range(3)], axis=1)
        high, rest = halves_of(rows)
        wide = dot(high, pick_ref[...]) + dot(rest, pick_ref[...])
        for t in range(6):
            held[6 * part + t] = wide[:, 128 * t : 128 * t + 128]
    total = jnp.zeros((16, 2 * WIDE), F32)
    for x in range(HALF):
        wide = jnp.concatenate([held[t, pl.ds(x, HEADS, stride=HALF), :] for t in range(18)], axis=1)
        wide = jnp.concatenate([wide, jnp.zeros((4, 2 * WIDE), F32)], axis=0)
        total = total + (pltpu.roll(wide, HALF - 1 - x, 1) if x != HALF - 1 else wide)
    high, rest = halves_of(total)
    result = jnp.zeros((16, 2 * WIDE), F32)
    for c in range(2 * WIDE // 256):
        hot = one_hot(slot_ref, c)
        cols = slice(256 * c, 256 * c + 256)
        result = result + dot(high[:, cols], hot) + dot(rest[:, cols], hot)
    out_ref[...] = result


def sigmoid(v):
    return 1.0 / (1.0 + jnp.exp(-v))


def row8(rows):
    width = rows[0].shape[1]
    return jnp.concatenate(rows + [jnp.zeros((8 - len(rows), width), F32)], axis=0)


def dw_stats(stat, count):
    mean = stat[0:1] / count
    return mean, lax.rsqrt(stat[1:2] / count - mean * mean + EPS)


def valid_places(limit):
    return (limit * limit).astype(F32)


def excite_kernel(
    res_ref, mask_ref, depth_ref, stat_ref, bgram_ref, norm_ref, down_ref, down_b_ref, up_ref, up_b_ref,
    proj_ref, base_ref, short_ref, pre_ref, qkv_ref,
    act_ref, slope_ref, block_ref, skip_ref, normed_ref, project_ref, vec_ref, small_ref, held, total,
):
    limit = limit_of(res_ref)
    count = bgram_ref[64:65, 64:65]
    mean, inverse = dw_stats(stat_ref[...], count)
    gain = norm_ref[0:1] * inverse
    shift = norm_ref[1:2] - mean * gain
    rows = 4 * HALF
    group = pl.program_id(0)

    @pl.when(group == 0)
    def _():
        total[...] = jnp.zeros_like(total)

    def fill(i, sums):
        at = pl.ds(pl.multiple_of(rows * i, 16), rows)
        value, slope = gelu_pair(depth_ref[at, :] * gain + shift)
        inside = jnp.concatenate([mask_ref[at, :]] * CHUNKS, axis=1)
        value = value * inside
        held[pl.ds(pl.multiple_of(group * QUAD + rows * i, 16), rows), :] = value
        act_ref[at, :] = value.astype(BF16)
        slope_ref[at, :] = (slope * inside).astype(BF16)
        for k in range(rows // 8):
            sums = sums + value[8 * k : 8 * k + 8]
        return sums

    total[...] = lax.fori_loop(0, QUAD // rows, fill, total[...])

    @pl.when(group == 3)
    def _():
        excite_rest(
            limit, mean, inverse, total, down_ref, down_b_ref, up_ref, up_b_ref, proj_ref, base_ref, short_ref,
            pre_ref, qkv_ref, block_ref, skip_ref, normed_ref, project_ref, vec_ref, small_ref, held,
        )


def excite_rest(
    limit, mean, inverse, total, down_ref, down_b_ref, up_ref, up_b_ref, proj_ref, base_ref, short_ref, pre_ref,
    qkv_ref, block_ref, skip_ref, normed_ref, project_ref, vec_ref, small_ref, held,
):
    pooled = jnp.sum(total[...], axis=0, keepdims=True) / valid_places(limit)
    before = dot(row8([pooled]), down_ref[...].astype(F32), precision=HIGH)[0:1] + down_b_ref[...]
    gate = sigmoid(before)
    squeeze = before * gate
    excite = sigmoid(
        dot(row8([squeeze]), up_ref[...].astype(F32), precision=HIGH)[0:1] + up_b_ref[...]
    )
    vec_ref[...] = row8([pooled, excite, mean, inverse])
    small_ref[...] = row8([squeeze, gate * (1.0 + before * (1.0 - gate))])

    big = 576
    def section(i, _):
        at = pl.ds(pl.multiple_of(big * i, 16), big)
        scaled = (held[at, :] * excite).astype(BF16)
        block_ref[at, :] = dot(scaled, proj_ref[...]) + dot(base_ref[at, :], short_ref[...])
        return 0

    lax.fori_loop(0, PLACES // big, section, 0)
    part = 96

    def tokens(i, _):
        skipped = jnp.zeros((part, MB_CH), F32)
        normed = jnp.zeros((part, MB_CH), F32)
        for group in range(4):
            block = block_ref[pl.ds(pl.multiple_of(group * QUAD + part * i, 16), part), :]
            skipped = skipped + block
            hat, _ = normalise(block)
            normed = normed + hat
        at = pl.ds(pl.multiple_of(part * i, 16), part)
        skip_ref[at, :] = (0.25 * skipped).astype(BF16)
        low = (0.25 * normed * pre_ref[0:1] + pre_ref[1:2]).astype(BF16)
        normed_ref[at, :] = low
        return 0

    lax.fori_loop(0, TOKENS // part, tokens, 0)
    project_ref[...] = dot(normed_ref[...], qkv_ref[...]).astype(BF16)


def normalise(v):
    centered = v - jnp.mean(v, axis=-1, keepdims=True)
    inverse = lax.rsqrt(jnp.mean(centered * centered, axis=-1, keepdims=True) + EPS)
    return centered * inverse, inverse


def normalise_back(grad_hat, hat, inverse):
    first = jnp.mean(grad_hat, axis=-1, keepdims=True)
    second = jnp.mean(grad_hat * hat, axis=-1, keepdims=True)
    return inverse * (grad_hat - first - hat * second)


def excite_forward(res_ids, mask, depth, stat, bgram, base, p):
    part = lambda width: pl.BlockSpec((QUAD, width), lambda i: (i, 0))
    whole = lambda *shape: pl.BlockSpec(shape, lambda i: (0,) * len(shape))
    return pl.pallas_call(
        excite_kernel,
        grid=(4,),
        out_shape=(
            jax.ShapeDtypeStruct((PLACES, EXPAND), BF16),
            jax.ShapeDtypeStruct((PLACES, EXPAND), BF16),
            jax.ShapeDtypeStruct((PLACES, MB_CH), F32),
            jax.ShapeDtypeStruct((TOKENS, MB_CH), BF16),
            jax.ShapeDtypeStruct((TOKENS, MB_CH), BF16),
            jax.ShapeDtypeStruct((TOKENS, 3 * DIM), BF16),
            jax.ShapeDtypeStruct((8, EXPAND), F32),
            jax.ShapeDtypeStruct((8, SQUEEZE), F32),
        ),
        in_specs=[
            SMEM_SPEC, part(128), part(EXPAND), whole(8, EXPAND), whole(72, 128), whole(2, EXPAND),
            whole(EXPAND, SQUEEZE), whole(1, SQUEEZE), whole(SQUEEZE, EXPAND), whole(1, EXPAND),
            whole(EXPAND, MB_CH), whole(PLACES, 128), whole(128, MB_CH), whole(2, MB_CH), whole(MB_CH, 3 * DIM),
        ],
        out_specs=(
            part(EXPAND), part(EXPAND), whole(PLACES, MB_CH), whole(TOKENS, MB_CH), whole(TOKENS, MB_CH),
            whole(TOKENS, 3 * DIM), whole(8, EXPAND), whole(8, SQUEEZE),
        ),
        scratch_shapes=[pltpu.VMEM((PLACES, EXPAND), F32), pltpu.VMEM((8, EXPAND), F32)],
        compiler_params=params_of(40),
        cost_estimate=cost(18),
        name="excite_forward",
    )(
        res_ids, mask, depth, stat, bgram, p["dw_norm"], p["se_down"], p["se_down_bias"], p["se_up"], p["se_up_bias"],
        p["mb_proj"], base, p["mb_short"], p["pre_norm"], p["qkv"],
    )


SCALE = HEAD_DIM ** (-0.5)
PER = BLOCK // HEAD_DIM
ATT_ROWS = 2 * HALF


def token_valid(limit, shape, axis):
    at = lax.broadcasted_iota(jnp.int32, shape, axis)
    y = at // HALF
    x = at - y * HALF
    return (2 * y < limit) & (2 * x < limit)


def head_lanes(h):
    lane = lax.broadcasted_iota(jnp.int32, (TOKENS, BLOCK), 1)
    return lane // HEAD_DIM == h


def bias_cut(up):
    offset = (HALF - 1 - up) * HALF
    lead = offset % 128
    return offset // 128, (5 if lead <= 64 else 6), lead


def attend_kernel(res_ref, q_ref, k_ref, v_ref, bias_ref, out_ref, p_ref, scores):
    limit = limit_of(res_ref)
    usable = token_valid(limit, (1, TOKENS), 1)

    def head(h, total):
        mine = head_lanes(h)
        q = jnp.where(mine, q_ref[...], jnp.zeros((), BF16))
        scores[...] = dot(q, k_ref[...], NT)
        bias_rows = pl.ds(pl.multiple_of(h * HALF, 8), HALF)
        for i in range(TOKENS // ATT_ROWS):
            at = slice(ATT_ROWS * i, ATT_ROWS * i + ATT_ROWS)
            shifted = []
            for k in range(2):
                tile, tiles, lead = bias_cut(2 * i + k)
                bias = jnp.concatenate([bias_ref[tile + t, bias_rows, :] for t in range(tiles)], axis=1)
                if lead:
                    bias = pltpu.roll(bias, 128 * tiles - lead, 1)
                shifted.append(bias[:, :TOKENS])
            s = scores[at, :] * SCALE + jnp.concatenate(shifted, axis=0)
            s = jnp.where(usable, s, -1e30)
            e = jnp.exp(s - jnp.max(s, axis=-1, keepdims=True))
            weights = e * (1.0 / jnp.sum(e, axis=-1, keepdims=True))
            p_ref[h, at, :] = weights.astype(BF16)
        return jnp.where(mine, dot(p_ref[h], v_ref[...]), total)

    total = lax.fori_loop(0, PER, head, jnp.zeros((TOKENS, BLOCK), F32))
    out_ref[...] = total.astype(BF16)


def attend_forward(res_ids, project, bias):
    part = lambda k: pl.BlockSpec((TOKENS, BLOCK), lambda j: (0, 3 * k + j))
    return pl.pallas_call(
        attend_kernel,
        grid=(HEADS // PER,),
        out_shape=(
            jax.ShapeDtypeStruct((TOKENS, DIM), BF16),
            jax.ShapeDtypeStruct((HEADS, TOKENS, TOKENS), BF16),
        ),
        in_specs=[SMEM_SPEC, part(0), part(1), part(2), pl.BlockSpec((9, PER * HALF, 128), lambda j: (0, j, 0))],
        out_specs=(
            pl.BlockSpec((TOKENS, BLOCK), lambda j: (0, j)),
            pl.BlockSpec((PER, TOKENS, TOKENS), lambda j: (j, 0, 0)),
        ),
        scratch_shapes=[pltpu.VMEM((TOKENS, TOKENS), F32)],
        compiler_params=params_of(20),
        cost_estimate=cost(35),
        name="attend_forward",
    )(res_ids, project, project, project, bias)


def attend_back_kernel(
    q_ref, k_ref, v_ref, o_ref, do_ref, p_ref, slot_ref, pick_ref, dq_ref, dk_ref, dv_ref, dtable_ref,
    scores, low, bias, dbias_ref, held,
):
    first_head = pl.program_id(0) * PER

    def head(h, carry):
        dq, dk, dv = carry
        mine = head_lanes(h)
        grad = jnp.where(mine, do_ref[...], jnp.zeros((), BF16))
        scores[...] = dot(grad, v_ref[...], NT)
        bias[...] = jnp.zeros((HALF, WIDE), F32)
        lane = lax.broadcasted_iota(jnp.int32, (ATT_ROWS, BLOCK), 1)
        for i in range(TOKENS // ATT_ROWS):
            at = slice(ATT_ROWS * i, ATT_ROWS * i + ATT_ROWS)
            both = do_ref[at, :].astype(F32) * o_ref[at, :].astype(F32)
            both = jnp.where(lane // HEAD_DIM == h, both, 0.0)
            delta = jnp.sum(both, axis=-1, keepdims=True)
            ds = p_ref[h, at, :].astype(F32) * (scores[at, :] - delta)
            low[at, :] = (ds * SCALE).astype(BF16)
            for k in range(2):
                tile, tiles, lead = bias_cut(2 * i + k)
                wide = jnp.concatenate(
                    [ds[HALF * k : HALF * k + HALF], jnp.zeros((HALF, 128 * tiles - TOKENS), F32)], axis=1
                )
                if lead:
                    wide = pltpu.roll(wide, lead, 1)
                cols = slice(128 * tile, 128 * (tile + tiles))
                bias[:, cols] = bias[:, cols] + wide
        for t in range(9):
            dbias_ref[t, pl.ds(pl.multiple_of((first_head + h) * HALF, 8), HALF), :] = bias[:, 128 * t : 128 * t + 128]
        dq = jnp.where(mine, dot(low[...], k_ref[...]), dq)
        dk = jnp.where(mine, dot(low[...], q_ref[...], TN), dk)
        dv = jnp.where(mine, dot(p_ref[h], do_ref[...], TN), dv)
        return dq, dk, dv

    zero = jnp.zeros((TOKENS, BLOCK), F32)
    dq, dk, dv = lax.fori_loop(0, PER, head, (zero, zero, zero))
    dq_ref[...] = dq.astype(BF16)
    dk_ref[...] = dk.astype(BF16)
    dv_ref[...] = dv.astype(BF16)

    @pl.when(pl.program_id(0) == HEADS // PER - 1)
    def _():
        bias_back_step(dbias_ref, slot_ref, pick_ref, dtable_ref, held)


def attend_backward(project, blended, grad, weights, slots, pick):
    part = lambda k: pl.BlockSpec((TOKENS, BLOCK), lambda j: (0, 3 * k + j))
    whole = lambda *shape: pl.BlockSpec(shape, lambda j: (0,) * len(shape))
    return pl.pallas_call(
        attend_back_kernel,
        grid=(HEADS // PER,),
        out_shape=(jax.ShapeDtypeStruct((TOKENS, DIM), BF16),) * 3
        + (jax.ShapeDtypeStruct((16, 2 * WIDE), F32),),
        in_specs=[
            part(0), part(1), part(2), part(0), part(0),
            pl.BlockSpec((PER, TOKENS, TOKENS), lambda j: (j, 0, 0)), whole(2 * WIDE, 1), whole(16 * HALF, 32 * HALF),
        ],
        out_specs=(part(0), part(0), part(0), whole(16, 2 * WIDE)),
        scratch_shapes=[
            pltpu.VMEM((TOKENS, TOKENS), F32), pltpu.VMEM((TOKENS, TOKENS), BF16), pltpu.VMEM((HALF, WIDE), F32),
            pltpu.VMEM((9, HEADS * HALF, 128), F32), pltpu.VMEM((18, HEADS * HALF, 128), F32),
        ],
        compiler_params=params_of(56),
        cost_estimate=cost(40),
        name="attend_backward",
    )(project, project, project, blended, grad, weights, slots, pick)


MLP_ROWS = 192


def mlp_kernel(
    share, res_ref, label_ref, skip_ref, blend_ref, short_ref, out_ref, out_b_ref, norm_ref, in_ref, in_b_ref,
    back_ref, back_b_ref, hnorm_ref, head_ref, head_b_ref,
    loss_ref, dblend_ref, dskip_ref, dshort_ref, dout_ref, dout_b_ref, dnorm_ref, din_ref, din_b_ref,
    vec_ref, few_ref,
    section, low, slopes, dpres, grads,
):
    limit = limit_of(res_ref)
    n_valid = (limit // 2 * (limit // 2)).astype(F32)
    steps = TOKENS // MLP_ROWS
    cut = 384

    def valid_rows(i):
        at = lax.broadcasted_iota(jnp.int32, (MLP_ROWS, 1), 0) + MLP_ROWS * i
        y = at // HALF
        x = at - y * HALF
        return jnp.where((2 * y < limit) & (2 * x < limit), 1.0, 0.0)

    def forward(i, carry):
        feature, used = carry
        at = pl.ds(pl.multiple_of(MLP_ROWS * i, 16), MLP_ROWS)
        first = dot(skip_ref[at, :], short_ref[...]) + dot(blend_ref[at, :], out_ref[...]) + out_b_ref[...]
        section[at, :] = first
        hat, _ = normalise(first)
        normed = (hat * norm_ref[0:1] + norm_ref[1:2]).astype(BF16)
        low[at, :] = normed
        inside = valid_rows(i)
        second = first + back_b_ref[...]
        parts = []
        for j in range(MLP // cut):
            cols = slice(cut * j, cut * j + cut)
            value, slope = gelu_pair(dot(normed, in_ref[:, cols]) + in_b_ref[:, cols])
            slopes[at, cols] = slope * inside
            value = value.astype(BF16)
            parts.append(jnp.sum(value.astype(F32) * inside, axis=0, keepdims=True))
            second = second + dot(value, back_ref[cols, :])
        feature = feature + jnp.sum(second * inside, axis=0, keepdims=True)
        return feature, used + jnp.concatenate(parts, axis=1)

    feature, used = lax.fori_loop(
        0, steps, forward, (jnp.zeros((1, DIM), F32), jnp.zeros((1, MLP), F32))
    )
    feature = feature / n_valid
    hat, inverse = normalise(feature)
    normed = (hat * hnorm_ref[0:1] + hnorm_ref[1:2]).astype(BF16)
    normed8 = jnp.concatenate([normed.astype(F32), jnp.zeros((15, DIM), F32)], axis=0).astype(BF16)
    logits = dot(normed8, head_ref[...])[0:1] + head_b_ref[...]
    peak = jnp.max(logits, axis=-1, keepdims=True)
    exps = jnp.exp(logits - peak)
    total = jnp.sum(exps, axis=-1, keepdims=True)
    log_probs = logits - peak - jnp.log(total)
    at_class = lax.broadcasted_iota(jnp.int32, (1, CLASSES), 1)
    goal = jnp.where(at_class == label_ref[0], 1.0 - SMOOTH, 0.0) + SMOOTH / CLASSES
    loss = -jnp.sum(goal * log_probs, axis=-1, keepdims=True)
    loss_ref[...] = jnp.broadcast_to(loss, (8, 128))
    grad = (exps / total - goal) * share
    few_ref[...] = jnp.zeros_like(few_ref)
    few_ref[4:5, :] = grad[:, 0:EXPAND]
    few_ref[5:6, 0 : CLASSES - EXPAND] = grad[:, EXPAND:]
    grad16 = jnp.concatenate([grad, jnp.zeros((15, CLASSES), F32)], axis=0).astype(BF16)
    vec_ref[...] = jnp.zeros_like(vec_ref)
    vec_ref[2:3, 0:DIM] = normed8.astype(F32)[0:1]
    vec_ref[3:4, 0:CLASSES] = grad16.astype(F32)[0:1]
    grad = dot(grad16, head_ref[...], NT)[0:1]
    few_ref[2:3, :] = jnp.concatenate([grad * hat, grad], axis=1)
    grad = normalise_back(grad * hnorm_ref[0:1], hat, inverse) / n_valid
    low_grad = jnp.concatenate([grad, jnp.zeros((15, DIM), F32)], axis=0).astype(BF16)
    vec_ref[0:1, :] = used
    vec_ref[1:2, 0:DIM] = low_grad.astype(F32)[0:1]
    few_ref[3:4, 0:DIM] = grad * n_valid
    dhidden = dot(low_grad, back_ref[...], NT)[0:1]

    def backward(i, carry):
        dnorm0, dnorm1, dbias, dout_b = carry
        at = pl.ds(pl.multiple_of(MLP_ROWS * i, 16), MLP_ROWS)
        dnormed = jnp.zeros((MLP_ROWS, DIM), F32)
        parts = []
        for j in range(MLP // cut):
            cols = slice(cut * j, cut * j + cut)
            dpre = slopes[at, cols] * dhidden[:, cols]
            parts.append(jnp.sum(dpre, axis=0, keepdims=True))
            dpre = dpre.astype(BF16)
            dpres[at, cols] = dpre
            dnormed = dnormed + dot(dpre, in_ref[:, cols], NT)
        hat, inverse = normalise(section[at, :])
        dnorm0 = dnorm0 + jnp.sum(dnormed * hat, axis=0, keepdims=True)
        dnorm1 = dnorm1 + jnp.sum(dnormed, axis=0, keepdims=True)
        dsection = normalise_back(dnormed * norm_ref[0:1], hat, inverse) + valid_rows(i) * grad
        grads[at, :] = dsection.astype(BF16)
        dout_b = dout_b + jnp.sum(dsection, axis=0, keepdims=True)
        dblend_ref[at, :] = dot(grads[at, :], out_ref[...], NT).astype(BF16)
        dskip_ref[at, :] = dot(grads[at, :], short_ref[...], NT)
        return dnorm0, dnorm1, dbias + jnp.concatenate(parts, axis=1), dout_b

    row = jnp.zeros((1, DIM), F32)
    dnorm0, dnorm1, dbias, dout_b = lax.fori_loop(0, steps, backward, (row, row, jnp.zeros((1, MLP), F32), row))
    dnorm_ref[...] = jnp.concatenate([dnorm0, dnorm1], axis=0)
    din_b_ref[...] = dbias
    dout_b_ref[...] = dout_b
    din_ref[...] = dot(low[...], dpres[...], TN)
    dout_ref[...] = dot(blend_ref[...], grads[...], TN)
    dshort_ref[...] = dot(skip_ref[...], grads[...], TN)


def mlp_both(share, res_ids, labels, skipped, blended, p):
    s = jax.ShapeDtypeStruct
    return pl.pallas_call(
        functools.partial(mlp_kernel, share),
        out_shape=(
            s((8, 128), F32), s((TOKENS, DIM), BF16), s((TOKENS, MB_CH), F32), s((MB_CH, DIM), F32),
            s((DIM, DIM), F32), s((1, DIM), F32), s((2, DIM), F32), s((DIM, MLP), F32), s((1, MLP), F32),
            s((8, MLP), F32), s((8, EXPAND), F32),
        ),
        in_specs=[SMEM_SPEC] * 2 + [VMEM_SPEC] * 13,
        out_specs=(VMEM_SPEC,) * 11,
        scratch_shapes=[
            pltpu.VMEM((TOKENS, DIM), F32),
            pltpu.VMEM((TOKENS, DIM), BF16),
            pltpu.VMEM((TOKENS, MLP), F32),
            pltpu.VMEM((TOKENS, MLP), BF16),
            pltpu.VMEM((TOKENS, DIM), BF16),
        ],
        compiler_params=params_of(24),
        cost_estimate=cost(23),
        name="mlp_both",
    )(
        res_ids, labels, skipped, blended, p["at_short"], p["attn_out"], p["out_bias"], p["mlp_norm"], p["mlp_in"],
        p["mlp_in_bias"], p["mlp_out"], p["mlp_out_bias"], p["head_norm"], p["head_w"], p["head_bias"],
    )


def proj_back_kernel(
    res_ref, dq_ref, dk_ref, dv_ref, normed_ref, qkv_ref, dskip_ref, block_ref, pre_ref, act_ref, vec_ref,
    small_ref, proj_ref, short_ref, base_ref, down_ref, up_ref,
    dqkv_ref, dpre_ref, dblock_ref, dproj_ref, dshort_ref, dbase_ref, ddown_ref, ddown_b_ref, dup_ref, dup_b_ref,
    dpool_ref, back,
):
    limit = limit_of(res_ref)
    part = 96
    grad = dot(dq_ref[...], qkv_ref[:, 0:DIM], NT)
    grad = grad + dot(dk_ref[...], qkv_ref[:, DIM : 2 * DIM], NT)
    back[...] = grad + dot(dv_ref[...], qkv_ref[:, 2 * DIM :], NT)

    def tokens(i, carry):
        dpre0, dpre1 = carry
        at = pl.ds(pl.multiple_of(part * i, 16), part)
        grad = back[at, :]
        dskip = 0.25 * dskip_ref[at, :]
        dpre1 = dpre1 + jnp.sum(grad, axis=0, keepdims=True)
        grad = 0.25 * grad
        dhat = grad * pre_ref[0:1]
        for group in range(4):
            places = pl.ds(pl.multiple_of(group * QUAD + part * i, 16), part)
            hat, inverse = normalise(block_ref[places, :])
            dpre0 = dpre0 + jnp.sum(grad * hat, axis=0, keepdims=True)
            dblock = normalise_back(dhat, hat, inverse) + dskip
            dblock_ref[places, :] = dblock.astype(BF16)
        return dpre0, dpre1

    row = jnp.zeros((1, MB_CH), F32)
    dpre0, dpre1 = lax.fori_loop(0, TOKENS // part, tokens, (row, row))
    dpre_ref[...] = jnp.concatenate([dpre0, dpre1], axis=0)
    for k, grad_ref in enumerate((dq_ref, dk_ref, dv_ref)):
        dqkv_ref[:, DIM * k : DIM * k + DIM] = dot(normed_ref[...], grad_ref[...], TN)
    dshort_ref[...] = dot(base_ref[...], dblock_ref[...], TN)[0:STEM_CH]
    dbase_ref[...] = dot(dblock_ref[...], short_ref[...], NT)
    excite = vec_ref[1:2]
    parts = []
    for j in range(CHUNKS):
        cols = slice(BLOCK * j, BLOCK * j + BLOCK)
        act = act_ref[:, cols].astype(F32)
        scaled = (act * excite[:, cols]).astype(BF16)
        dproj_ref[cols, :] = dot(scaled, dblock_ref[...], TN)
        dscaled = dot(dblock_ref[...], proj_ref[cols, :], NT)
        parts.append(jnp.sum(dscaled * act, axis=0, keepdims=True))
    dexcite = jnp.concatenate(parts, axis=1)
    dafter = dexcite * excite * (1.0 - excite)
    dup_b_ref[...] = dafter
    dup_ref[...] = dot(row8([small_ref[0:1]]), row8([dafter]), TN, precision=HIGH)
    dsqueeze = dot(row8([dafter]), up_ref[...].astype(F32), NT, precision=HIGH)[0:1]
    dbefore = dsqueeze * small_ref[1:2]
    ddown_b_ref[...] = dbefore
    ddown_ref[...] = dot(row8([vec_ref[0:1]]), row8([dbefore]), TN, precision=HIGH)
    dpool = dot(row8([dbefore]), down_ref[...].astype(F32), NT, precision=HIGH)
    dpool_ref[...] = dpool / valid_places(limit)


def proj_backward(res_ids, dq, dk, dv, normed, dskip, block, act, vec, small, base, p):
    s = jax.ShapeDtypeStruct
    return pl.pallas_call(
        proj_back_kernel,
        out_shape=(
            s((MB_CH, 3 * DIM), F32), s((2, MB_CH), F32), s((PLACES, MB_CH), BF16), s((EXPAND, MB_CH), F32),
            s((STEM_CH, MB_CH), F32), s((PLACES, 128), F32), s((EXPAND, SQUEEZE), F32), s((1, SQUEEZE), F32),
            s((SQUEEZE, EXPAND), F32), s((1, EXPAND), F32), s((8, EXPAND), F32),
        ),
        in_specs=[SMEM_SPEC] + [VMEM_SPEC] * 16,
        out_specs=(VMEM_SPEC,) * 11,
        scratch_shapes=[pltpu.VMEM((TOKENS, MB_CH), F32)],
        compiler_params=params_of(24),
        cost_estimate=cost(13),
        name="proj_backward",
    )(
        res_ids, dq, dk, dv, normed, p["qkv"], dskip, block, p["pre_norm"], act, vec, small, p["mb_proj"],
        p["mb_short"], base, p["se_down"], p["se_up"],
    )


def excite_back_kernel(dblock_ref, proj_ref, vec_ref, dpool_ref, few_ref, slope_ref, x_ref, out_ref, sum_ref, wide):
    excite, mean, inverse = vec_ref[1:2], vec_ref[2:3], vec_ref[3:4]
    dpool = dpool_ref[0:1]
    rows = 288
    wide[...] = dot(dblock_ref[...], proj_ref[...], NT)

    def fold(v):
        total = v[0:8]
        for k in range(1, rows // 8):
            total = total + v[8 * k : 8 * k + 8]
        return total

    def step(i, sums):
        at = pl.ds(pl.multiple_of(rows * i, 16), rows)
        grad = wide[at, :] * excite + dpool
        grad = grad * slope_ref[at, :].astype(F32)
        out_ref[at, :] = grad.astype(BF16)
        hat = (x_ref[at, :] - mean) * inverse
        return sums[0] + fold(grad), sums[1] + fold(grad * hat)

    sums = lax.fori_loop(0, PLACES // rows, step, (jnp.zeros((8, BLOCK), F32),) * 2)
    sum_ref[...] = few_ref[...] + row8([jnp.sum(s, axis=0, keepdims=True) for s in sums])


def excite_backward(dblock, proj, vec, dpool, few, slope, depth):
    col = lambda rows: pl.BlockSpec((rows, BLOCK), lambda j: (0, j))
    return pl.pallas_call(
        excite_back_kernel,
        grid=(CHUNKS,),
        out_shape=(jax.ShapeDtypeStruct((PLACES, EXPAND), BF16), jax.ShapeDtypeStruct((8, EXPAND), F32)),
        in_specs=[
            pl.BlockSpec((PLACES, MB_CH), lambda j: (0, 0)),
            pl.BlockSpec((BLOCK, MB_CH), lambda j: (j, 0)),
            col(8), col(8), col(8), col(PLACES), col(PLACES),
        ],
        out_specs=(col(PLACES), col(8)),
        scratch_shapes=[pltpu.VMEM((PLACES, BLOCK), F32)],
        compiler_params=params_of(56),
        cost_estimate=cost(12),
        name="excite_backward",
    )(dblock, proj, vec, dpool, few, slope, depth)


def depth_back_kernel(
    mask_ref, du_ref, x_ref, vec_ref, sum_ref, bgram_ref, base_ref, expand_ref, dwn_ref, depth_ref, act_ref, slope_ref,
    out_ref, cross_ref, sums_ref, pad,
):
    count = bgram_ref[64:65, 64:65]
    mean1, inverse1 = bn_stats(bgram_ref[...], expand_ref[...], count)
    mean2, inverse2 = vec_ref[2:3], vec_ref[3:4]
    c1 = sum_ref[0:1] / count
    c2 = sum_ref[1:2] / count
    scale2 = dwn_ref[0:1] * inverse2
    slant = scale2 * inverse2 * c2
    level = scale2 * c1 - slant * mean2
    zero = jnp.zeros((4, 1, HALF, BLOCK), F32)
    pad[:, 0:1] = zero
    pad[:, HALF + 1 : HALF + 2] = zero
    rows = 2 * HALF

    def fill(i, _):
        for group in range(4):
            at = pl.ds(pl.multiple_of(group * QUAD + rows * i, 16), rows)
            grad = scale2 * du_ref[at, :].astype(F32) - mask_ref[at, :] * (level + x_ref[at, :] * slant)
            for k in range(2):
                pad[group, 2 * i + k + 1] = grad[HALF * k : HALF * k + HALF]
        return 0

    lax.fori_loop(0, HALF // 2, fill, 0)

    def weight(dy, dx):
        return depth_ref[8 - 3 * dy - dx : 9 - 3 * dy - dx]

    def fold(v):
        return v[0:8] + v[8:16] + v[16:24]

    def step(k, sums):
        sums = list(sums)
        for py in range(2):
            places = [
                pl.ds(pl.multiple_of((2 * py + px) * QUAD + 2 * HALF * k, 16), 2 * HALF) for px in range(2)
            ]
            low_both, high_both = (act_ref[at, :].astype(F32) for at in places)
            made = [[], []]
            for half in range(2):
                up = 2 * k + half
                cut = slice(HALF * half, HALF * half + HALF)
                sources = [(1, -1), (0, 0), (1, 0)] if py == 0 else [(0, 0), (1, 0), (0, 1)]
                low_act, high_act = low_both[cut], high_both[cut]
                even = odd = None
                for t, (gy, off) in enumerate(sources):
                    left, right = pad[2 * gy, up + 1 + off], pad[2 * gy + 1, up + 1 + off]
                    before, after = shift_down(right), shift_up(left)
                    a = before * weight(t, 0) + left * weight(t, 1) + right * weight(t, 2)
                    b = left * weight(t, 0) + right * weight(t, 1) + after * weight(t, 2)
                    even = a if even is None else even + a
                    odd = b if odd is None else odd + b
                    for s, (a, b) in enumerate(((before, left), (left, right), (right, after))):
                        tap = 3 * (2 - t) + 2 - s
                        sums[tap] = sums[tap] + fold(low_act * a + high_act * b)
                made[0].append(even)
                made[1].append(odd)
            for px in range(2):
                grad = jnp.concatenate(made[px], axis=0) * slope_ref[places[px], :].astype(F32)
                out_ref[places[px], :] = grad.astype(BF16)
        return tuple(sums)

    sums = lax.fori_loop(0, HALF // 2, step, (jnp.zeros((8, BLOCK), F32),) * 9)
    cross_ref[72:88, :] = jnp.concatenate(
        [jnp.sum(s, axis=0, keepdims=True) for s in sums] + [jnp.zeros((7, BLOCK), F32)], axis=0
    )
    cross = dot(base_ref[...], out_ref[...], TN)
    cross_ref[0:72, :] = cross[0:72]
    first = cross[64:65]
    second = (jnp.sum(cross[0:64] * expand_ref[0:64, :].astype(F32), axis=0, keepdims=True) - mean1 * first) * inverse1
    sums_ref[...] = row8([second, first])


def depth_backward(mask, du, depth, vec, sums, bgram, base, expand_w, dw_norm, mb_depth, act, slope):
    col = lambda rows: pl.BlockSpec((rows, BLOCK), lambda j: (0, j))
    whole = lambda rows: pl.BlockSpec((rows, BLOCK), lambda j: (0, 0))
    s = jax.ShapeDtypeStruct
    return pl.pallas_call(
        depth_back_kernel,
        grid=(CHUNKS,),
        out_shape=(s((PLACES, EXPAND), BF16), s((88, EXPAND), F32), s((8, EXPAND), F32)),
        in_specs=[
            whole(PLACES), col(PLACES), col(PLACES), col(8), col(8), whole(72), whole(PLACES), col(128), col(2),
            col(9), col(PLACES), col(PLACES),
        ],
        out_specs=(col(PLACES), col(88), col(8)),
        scratch_shapes=[pltpu.VMEM((4, HALF + 2, HALF, BLOCK), F32)],
        compiler_params=params_of(56),
        cost_estimate=cost(35),
        name="depth_backward",
    )(mask, du, depth, vec, sums, bgram, base, expand_w, dw_norm, mb_depth, act, slope)


def stem_back_kernel(
    mask_ref, patch_ref, slope_ref, dbase_ref, du_ref, sum_ref, bgram_ref, base_ref, expand_ref, mid_ref, spread_ref,
    out_ref, total, rows_ref, hold,
):
    step = pl.program_id(0)

    @pl.when(step == 0)
    def _():
        count = bgram_ref[64:65, 64:65]
        mean, inverse = bn_stats(bgram_ref[...], expand_ref[...], count)
        second, first = sum_ref[0:1] / count, sum_ref[1:2] / count
        scale = mid_ref[0:1] * inverse
        slant = scale * inverse * second
        rows_ref[...] = row8([scale, slant, scale * first - slant * mean])
        total[...] = jnp.zeros_like(total)

    scale, slant, level = (rows_ref[k : k + 1] for k in range(3))
    x = dot(base_ref[...], expand_ref[...])
    inside = jnp.concatenate([mask_ref[...]] * CHUNKS, axis=1)
    grad = (scale * du_ref[...].astype(F32) - inside * (level + x * slant)).astype(BF16)
    grad = dot(grad, expand_ref[...], NT) + dbase_ref[...]
    grad = grad[:, 0:64] * (1.0 / 16.0)
    grad = jnp.concatenate([grad, grad], axis=1)
    grad = jnp.concatenate([grad, grad], axis=1)
    block = patch_ref[...]
    for j in range(4):
        cols = slice(256 * j, 256 * j + 256)
        wide = (slope_ref[:, cols].astype(F32) * grad).astype(BF16)
        total[:, cols] = total[:, cols] + dot(block, wide, TN)

    @pl.when(step == STEM_STEPS - 1)
    def _():
        merged = total[0:96, 0:256]
        for px in range(1, 4):
            merged = merged + total[64 * px : 64 * px + 96, 256 * px : 256 * px + 256]
        result = jnp.zeros((32, STEM_CH), F32)
        for pair in range(2):
            wide = dot(
                spread_ref[pair][0:96].astype(F32), merged[:, 128 * pair : 128 * pair + 128], TN, precision=HIGH
            )
            result = result + wide[0:32, 0:64] + wide[32:64, 64:128]
        ones = merged[27:28]
        ones = ones[:, 0:64] + ones[:, 64:128] + ones[:, 128:192] + ones[:, 192:256]
        at = lax.broadcasted_iota(jnp.int32, (32, STEM_CH), 0)
        out_ref[...] = pairs_together(jnp.where(at == 27, ones, result), hold)


def stem_backward(mask, patches, slope, dbase, du, sums, bgram, base, expand_w, mid_norm, spread):
    part = lambda width: pl.BlockSpec((STEM_BLOCK, width), lambda i: (i, 0))
    whole = lambda *shape: pl.BlockSpec(shape, lambda i: (0,) * len(shape))
    return pl.pallas_call(
        stem_back_kernel,
        grid=(STEM_STEPS,),
        out_shape=jax.ShapeDtypeStruct((16, 128), F32),
        in_specs=[
            part(128), part(TAPS), part(1024), part(128), part(EXPAND), whole(8, EXPAND), whole(72, 128), part(128),
            whole(128, EXPAND), whole(2, EXPAND), whole(8, TAPS, 64),
        ],
        out_specs=whole(16, 128),
        scratch_shapes=[
            pltpu.VMEM((TAPS, 1024), F32), pltpu.VMEM((8, EXPAND), F32), pltpu.VMEM((32, 128), F32),
        ],
        compiler_params=params_of(36),
        cost_estimate=cost(8),
        name="stem_backward",
    )(mask, patches, slope, dbase, du, sums, bgram, base, expand_w, mid_norm, spread)


def expand_finish_kernel(cross_ref, sum_ref, bgram_ref, expand_ref, mid_ref, out_ref, square_ref, flat, hold):
    count = bgram_ref[64:65, 64:65]
    square_of = jnp.concatenate([bgram_ref[...], jnp.zeros((56, 128), F32)], axis=0)
    weights = expand_ref[...].astype(F32)
    product = dot(square_of, weights, precision=HIGH)
    mean = product[64:65] / count
    variance = jnp.sum(weights * product, axis=0, keepdims=True) / count - mean * mean
    inverse = lax.rsqrt(variance + EPS)
    second, first = sum_ref[0:1] / count, sum_ref[1:2] / count
    plain = bgram_ref[0:64, 64:65]
    hat = (product[0:64] - mean * plain) * inverse
    hold[...] = mid_ref[0:1] * inverse * (cross_ref[0:64, :] - first * plain - second * hat)
    flat[...] = jnp.zeros_like(flat)
    for name, source in (("mb_expand", hold), ("mb_depth", cross_ref.at[72:88])):
        offset, (rows, width) = OFFSETS[name]
        put_matrix(flat, lambda r, t: source[r, 128 * t : 128 * t + 128], 0, offset, rows, width)
    out_ref[...] = flat[0:EARLY_ROWS, :]
    total = flat[0:EARLY_ROWS, :]
    square_ref[...] = jnp.broadcast_to(jnp.sum(total * total).reshape(1, 1), (8, 128))


def expand_finish(cross, sums, bgram, expand_w, mid_norm):
    return pl.pallas_call(
        expand_finish_kernel,
        out_shape=(jax.ShapeDtypeStruct((EARLY_ROWS, 128), F32), jax.ShapeDtypeStruct((8, 128), F32)),
        in_specs=[VMEM_SPEC] * 5,
        out_specs=(VMEM_SPEC,) * 2,
        scratch_shapes=[pltpu.VMEM((EARLY_ROWS + 8, 128), F32), pltpu.VMEM((STEM_CH, EXPAND), F32)],
        compiler_params=params_of(10),
        cost_estimate=cost(3),
        name="expand_finish",
    )(cross, sums, bgram, expand_w, mid_norm)


def finish_kernel(
    first_ref, packet_ref, stem_ref, spread_ref, early_ref, early_square_ref, shard_ref,
    out_ref, scalar_ref, big, hold, flat,
):
    weights, own_gain, _ = stem_params(stem_ref, hold)
    spread_weights(spread_ref, weights, big, 2)
    gram = stem_ref[0:96, 0:96]
    mean, square = stem_stats(stem_ref[0:96, :], big[0:96, 0:256])
    inverse = lax.rsqrt(square - mean * mean + EPS)
    count = 4.0 * stem_ref[27:28, 27:28]
    got = pairs_apart(packet_ref[0:16], hold)
    product = dot(gram, big[0:96, 0:256].astype(F32), precision=HIGH)
    cross = jnp.zeros((32, STEM_CH), F32)
    plain = jnp.zeros((32, STEM_CH), F32)
    sums = jnp.broadcast_to(gram[:, 27:28], (96, 128))
    for pair in range(2):
        spread = spread_ref[pair][0:96].astype(F32)
        wide = dot(spread, product[:, 128 * pair : 128 * pair + 128], TN, precision=HIGH)
        cross = cross + wide[0:32, 0:64] + wide[32:64, 64:128]
        wide = dot(spread, sums, TN, precision=HIGH)
        plain = plain + wide[0:32, 0:64] + wide[32:64, 0:64]
    at = lax.broadcasted_iota(jnp.int32, (32, STEM_CH), 0)
    taps = at < 27
    grad = jnp.where(taps, got, 0.0)
    first = got[27:28]
    second = (jnp.sum(grad * weights, axis=0, keepdims=True) - mean * first) * inverse
    hat = (cross - mean * plain) * inverse
    result = own_gain * inverse * (grad - (plain * first + hat * second) / count)
    result = jnp.where(taps, result, jnp.where(at == 27, second, jnp.where(at == 28, first, 0.0)))
    square = packet_ref[16:17, 1:2] + early_square_ref[0:1, 0:1] + jnp.sum(result * result).reshape(1, 1)
    norm = jnp.sqrt(square)
    lane = lax.broadcasted_iota(jnp.int32, (8, 128), 1)
    scale = CLIP / jnp.maximum(norm, CLIP)
    scalar_ref[...] = jnp.where(lane == 0, packet_ref[16:17, 0:1], jnp.where(lane == 1, norm, scale))
    both = pairs_together(result, hold)
    rows = shard_ref.shape[0]
    flat[0:16, :] = early_ref[0:16] + both
    flat[16:EARLY_ROWS, :] = early_ref[16:EARLY_ROWS]
    flat[EARLY_ROWS:, :] = jnp.zeros((flat.shape[0] - EARLY_ROWS, 128), F32)
    begin = jnp.minimum(first_ref[0] * rows, EARLY_ROWS)
    out_ref[...] = shard_ref[...] + flat[pl.ds(begin, rows), :]


def finish(me, packet, stem, spread, early, early_square, shard):
    rows = shard.shape[0]
    return pl.pallas_call(
        finish_kernel,
        out_shape=(jax.ShapeDtypeStruct((rows, 128), F32), jax.ShapeDtypeStruct((8, 128), F32)),
        in_specs=[SMEM_SPEC] + [VMEM_SPEC] * 6,
        out_specs=(VMEM_SPEC,) * 2,
        scratch_shapes=[
            pltpu.VMEM((TAPS, 256), BF16), pltpu.VMEM((32, 128), F32),
            pltpu.VMEM((round_up(EARLY_ROWS + rows, 8), 128), F32),
        ],
        compiler_params=params_of(10),
        cost_estimate=cost(4),
        name="finish",
    )(me, packet, stem, spread, early, early_square, shard)


def levels_of(devices):
    levels = []
    stride = 1
    while stride < devices:
        radix = 2 if stride == 1 or devices // stride == 2 else 4
        levels.append((stride, radix))
        stride *= radix
    return levels


def pairs_of(devices, mask):
    return [(i, i ^ mask) for i in range(devices)]


def add_level(v, moved):
    return v + moved[0] if len(moved) == 1 else (v + moved[0]) + (moved[1] + moved[2])


def send_level(v, devices, level):
    stride, radix = level
    return [lax.ppermute(v, "dp", pairs_of(devices, stride * j)) for j in range(1, radix)]


def exchange(v, devices, levels):
    for level in levels:
        v = add_level(v, send_level(v, devices, level))
    return v


def spread_blocks(blocks, masks, devices, level):
    stride, radix = level
    moved = send_level(blocks, devices, level)
    return jnp.concatenate([blocks] + moved), [m ^ (stride * j) for j in range(radix) for m in masks]


def take(blocks, digit, axis):
    return lax.dynamic_index_in_dim(blocks, digit, axis, keepdims=False)


class Scatter:
    def __init__(self, keep, send, devices, me, low, high):
        self.devices, self.me, self.low, self.high = devices, me, low, high
        self.levels = levels_of(devices)
        self.at = 0
        self.mine, self.parts = [keep], [send]
        self.moved = []

    def launch(self):
        stride, radix = self.levels[self.at]
        top = stride * radix == self.devices
        self.moved = []
        for j, part in zip(range(1, radix), self.parts):
            pairs = pairs_of(self.devices, stride * j)
            if top:
                pairs = [(a, b) for a, b in pairs if self.low <= b // stride < self.high]
            self.moved.append(lax.ppermute(part, "dp", pairs))

    def land(self):
        terms = self.mine + [m.astype(F32) for m in self.moved]
        self.at += 1
        if self.at == len(self.levels):
            total = sum(terms[1:], terms[0])
            self.result = total.reshape(total.shape[-2:])
            return
        if len(terms) > 2:
            terms = [sum(terms[1:], terms[0])]
        stride, radix = self.levels[self.at]
        digit = (self.me // stride) % radix
        span = self.high - self.low
        if stride * radix == self.devices:
            blocks = [t.reshape((span,) + t.shape[-2:]) for t in terms]
            part = lambda d: sum(take(b, jnp.clip(d - self.low, 0, span - 1), 0) for b in blocks)
            mine = jnp.where((digit >= self.low) & (digit < self.high), part(digit), 0.0)
        else:
            blocks = [t.reshape((-1, radix) + t.shape[-2:]) for t in terms]
            part = lambda d: sum(take(b, d, 1) for b in blocks)
            mine = part(digit)
        self.mine = [mine]
        self.parts = [part(digit ^ j).astype(BF16) for j in range(1, radix)]

    def finish(self):
        if not self.moved:
            self.launch()
        self.land()
        while self.at < len(self.levels):
            self.launch()
            self.land()
        return self.result


def tie(*values):
    return lax.optimization_barrier(values)


def on_device(images, res_ids, labels, rel_index, master, first_moment, second_moment, ema_weights):
    devices = lax.axis_size("dp")
    me = lax.axis_index("dp").astype(jnp.int32)
    length = master.shape[0]
    rows = length // 128
    held = round_up(rows, 16)
    images_total = res_ids.shape[0] * devices

    levels = levels_of(devices)
    low_master = lax.optimization_barrier(master.astype(BF16).reshape(rows, 128))
    blocks, masks = spread_blocks(jnp.pad(low_master, ((0, held - rows), (0, 0)))[None], [0], devices, levels[-1])
    stem_part = lax.dynamic_update_slice(
        jnp.zeros((16 + rows, 128), BF16), low_master, (jnp.minimum(me * rows, 16), 0)
    )[:16]
    patches, packet, mask = make_patches(res_ids, images, stem_part)
    packet, blocks = tie(packet, blocks)
    packet = exchange(packet, devices, levels[:-1])
    packet, blocks = tie(packet, blocks)
    for level in levels[-2:0:-1]:
        blocks, masks = spread_blocks(blocks, masks, devices, level)
    packet = exchange(packet, devices, levels[-1:])
    spread = jnp.asarray(spread_taps(), BF16)
    base, stem_slope, bgram = stem_forward(patches, packet, spread)
    stem_packet = packet
    bgram, blocks = tie(bgram, blocks)
    others = lax.ppermute(blocks, "dp", pairs_of(devices, 1))
    bgram = exchange(bgram, devices, levels[:-1])
    bgram, others = tie(bgram, others)
    sent = send_level(bgram, devices, levels[-1])
    p = unpack([blocks, others], me.reshape(1), masks + [m ^ 1 for m in masks], rows, ALL_SHAPES)
    bgram = add_level(bgram, sent)
    depth, act1, slope1, stat = depth_forward(mask, base, p["mb_expand"], bgram, p["mid_norm"], p["mb_depth"])
    stat = exchange(stat, devices, levels)
    slots = slots_of(rel_index)
    slots = jnp.pad(slots, ((0, 1), (0, 1)), constant_values=2 * WIDE - 1).reshape(2 * WIDE, 1)
    pick = squeeze_lanes()
    pick, pick_back = jnp.asarray(pick, BF16), jnp.asarray(pick.T, BF16)
    bias = build_bias(p["rel_table"], slots, pick)

    act2, slope2, block, skipped, normed, project, vec, small = excite_forward(res_ids, mask, depth, stat, bgram, base, p)
    blended, weights = attend_forward(res_ids, project, bias)
    loss, dblend, dskip, g_short, g_out, g_out_b, g_mnorm, g_in, g_in_b, vectors, few = mlp_both(
        1.0 / images_total, res_ids, labels, skipped, blended, p
    )

    core = (me % 2).reshape(1)
    top_radix = levels_of(devices)[-1][1]

    def scattered(grads, begin, end):
        span = devices // top_radix
        low = begin // length // span
        high = (end - 1) // length // span + 1
        keep, send = pack(core, grads, low * span * rows, (high - low) * span, rows, held)
        return Scatter(keep, send, devices, me, low, high)

    middle = scattered(
        {
            "attn_out": g_out, "out_bias": g_out_b, "mlp_norm": g_mnorm, "mlp_in": g_in, "mlp_in_bias": g_in_b,
        },
        OFFSETS["attn_out"][0], OFFSETS["mlp_out"][0],
    )
    dblend, middle.parts = tie(dblend, middle.parts)
    middle.launch()
    vectors = lax.all_gather(vectors, "dp", axis=0, tiled=False)

    dq, dk, dv, g_table = attend_backward(project, blended, dblend, weights, slots, pick_back)
    dq, middle.moved = tie(dq, middle.moved)
    middle.land()
    dq, middle.parts = tie(dq, middle.parts)
    middle.launch()
    g_qkv, g_pre, dblock, g_proj, g_mbshort, dbase, g_down, g_down_b, g_up, g_up_b, dpool = proj_backward(
        res_ids, dq, dk, dv, normed, dskip, block, act2, vec, small, base, p
    )
    late = scattered(
        {
            "mb_short": g_mbshort, "se_down": g_down, "se_down_bias": g_down_b, "se_up": g_up, "se_up_bias": g_up_b,
            "mb_proj": g_proj, "at_short": g_short, "pre_norm": g_pre, "qkv": g_qkv, "rel_table": g_table,
        },
        OFFSETS["mb_short"][0], OFFSETS["mlp_norm"][0],
    )
    dblock, late.parts, middle.moved = tie(dblock, late.parts, middle.moved)
    late.launch()
    middle.land()
    dblock, middle.parts = tie(dblock, middle.parts)
    middle.launch()
    du, sums = excite_backward(dblock, p["mb_proj"], vec, dpool, few, slope2, depth)
    sums, late.moved, middle.moved = tie(sums, late.moved, middle.moved)
    late.land()
    sums, late.parts = tie(sums, late.parts)
    late.launch()
    dw_sums = exchange(sums, devices, levels)
    dw_sums, late.moved = tie(dw_sums, late.moved)
    late.land()
    dw_sums, late.parts = tie(dw_sums, late.parts)
    late.launch()
    du, cross, sums = depth_backward(
        mask, du, depth, vec, dw_sums, bgram, base, p["mb_expand"], p["dw_norm"], p["mb_depth"], act1, slope1
    )
    sums, late.moved = tie(sums, late.moved)
    steps = [(1 << k, 2) for k in range(devices.bit_length() - 1)]
    sent = send_level(cross, devices, steps[0])
    mid_sums = exchange(sums, devices, levels[:-1])
    mid_sums, sent = tie(mid_sums, sent)
    cross = add_level(cross, sent)
    moved = send_level(mid_sums, devices, levels[-1])
    sent = send_level(cross, devices, steps[1])
    mid_sums, sent = tie(add_level(mid_sums, moved), sent)
    cross = add_level(cross, sent)
    mid_sums, cross = tie(mid_sums, cross)
    sent = send_level(cross, devices, steps[2])
    stem = stem_backward(
        mask, patches, stem_slope, dbase, du, mid_sums, bgram, base, p["mb_expand"], p["mid_norm"], spread
    )
    stem, sent, late.moved = tie(stem, sent, late.moved)
    cross = add_level(cross, sent)
    stem, cross = tie(stem, cross)
    sent = send_level(cross, devices, steps[3])
    shard, packet = shard_parts(
        me.reshape(1), length, late.finish(), middle.finish(), dw_sums, mid_sums, vectors, stem, loss
    )
    packet, sent = tie(packet, sent)
    cross = add_level(cross, sent)
    cross, packet = tie(cross, packet)
    cross = exchange(cross, devices, steps[4:])
    packet = exchange(packet, devices, levels)
    early_grad, early_square = expand_finish(cross, mid_sums, bgram, p["mb_expand"], p["mid_norm"])
    shard, scalars = finish(
        me.reshape(1), packet, stem_packet, spread, early_grad, early_square, shard
    )
    loss_sum, grad_norm = scalars[0, 0], scalars[0, 1]
    shard = shard.reshape(length)
    clipped = shard * scalars[0, 2]
    moment_one = BETA_ONE * first_moment + (1.0 - BETA_ONE) * clipped
    moment_two = BETA_TWO * second_moment + (1.0 - BETA_TWO) * clipped * clipped
    update = (
        moment_one
        / (1.0 - BETA_ONE**STEP)
        / (jnp.sqrt(moment_two / (1.0 - BETA_TWO**STEP)) + ADAM_EPS)
    )
    weights_out = master - RATE * (update + DECAY * master)
    averaged = EMA_DECAY * ema_weights + (1.0 - EMA_DECAY) * weights_out
    return (
        loss_sum,
        grad_norm,
        weights_out,
        moment_one,
        moment_two,
        averaged,
        weights_out.astype(BF16),
    )


def solution(mesh):
    in_specs = (
        P("dp", None, None, None),
        P("dp"),
        P("dp"),
        P(),
        P("dp"),
        P("dp"),
        P("dp"),
        P("dp"),
    )
    out_specs = (P(), P(), P("dp"), P("dp"), P("dp"), P("dp"), P("dp"))
    return jax.shard_map(
        on_device, mesh=mesh, in_specs=in_specs, out_specs=out_specs, check_vma=False
    )
```

```python
import functools
import math

import jax
import jax.numpy as jnp
import numpy as np
from jax import lax
from jax.experimental import pallas as pl
from jax.experimental.pallas import tpu as pltpu
from jax.sharding import PartitionSpec as P

STEM_CH = 64
MB_CH = 192
EXPAND = 768
SQUEEZE = 48
DIM = 384
HEADS = 12
HEAD_DIM = 32
MLP = 1536
CLASSES = 1000
CANVAS = 384
SMALL_RES = 224
STEP = 10

EPS = 1e-05
CLIP = 0.05
BETA_ONE = 0.5
BETA_TWO = 0.5
ADAM_EPS = 1e-08
RATE = 0.05
DECAY = 0.05
EMA_DECAY = 0.9
SMOOTH = 0.1

SIDE = CANVAS // 8
SMALL_SIDE = SMALL_RES // 8
HALF = SIDE // 2
QUAD = HALF * HALF
PLACES = SIDE * SIDE
TAPS = 288
BLOCK = 128
CHUNKS = EXPAND // BLOCK
WIDE = 2 * HALF * HALF
TOKENS = QUAD

F32 = jnp.float32
BF16 = jnp.bfloat16
HIGH = lax.Precision.HIGHEST
GELU_A = math.sqrt(2.0 / math.pi)
GELU_B = 0.044715


def layout():
    table_slots = (2 * (CANVAS // 16) - 1) ** 2
    return [
        ("stem_w", (3, 3, 3, STEM_CH)),
        ("stem_norm", (2, STEM_CH)),
        ("mb_short", (STEM_CH, MB_CH)),
        ("mb_expand", (STEM_CH, EXPAND)),
        ("mid_norm", (2, EXPAND)),
        ("mb_depth", (9, EXPAND)),
        ("dw_norm", (2, EXPAND)),
        ("se_down", (EXPAND, SQUEEZE)),
        ("se_down_bias", (SQUEEZE,)),
        ("se_up", (SQUEEZE, EXPAND)),
        ("se_up_bias", (EXPAND,)),
        ("mb_proj", (EXPAND, MB_CH)),
        ("at_short", (MB_CH, DIM)),
        ("pre_norm", (2, MB_CH)),
        ("qkv", (MB_CH, 3 * DIM)),
        ("attn_out", (DIM, DIM)),
        ("out_bias", (DIM,)),
        ("rel_table", (HEADS, table_slots)),
        ("mlp_norm", (2, DIM)),
        ("mlp_in", (DIM, MLP)),
        ("mlp_in_bias", (MLP,)),
        ("mlp_out", (MLP, DIM)),
        ("mlp_out_bias", (DIM,)),
        ("head_norm", (2, DIM)),
        ("head_w", (DIM, CLASSES)),
        ("head_bias", (CLASSES,)),
    ]


def offsets():
    table = {}
    offset = 0
    for name, shape in layout():
        table[name] = (offset, shape)
        offset += math.prod(shape)
    return table


OFFSETS = offsets()
STEM_END = OFFSETS["mb_short"][0]
EARLY_END = OFFSETS["se_down"][0]


def dot(a, b, dims=((1,), (0,)), precision=None):
    return lax.dot_general(a, b, (dims, ((), ())), precision=precision, preferred_element_type=F32)


NT = ((1,), (1,))
TN = ((0,), (0,))


def gelu_pair(u):
    sq = u * u
    t = jnp.tanh(u * (GELU_A + (GELU_A * GELU_B) * sq))
    half = 0.5 + 0.5 * t
    slope = half + (0.5 * u) * (1.0 - t * t) * (GELU_A + (3.0 * GELU_A * GELU_B) * sq)
    return u * half, slope


def gelu(u):
    sq = u * u
    t = jnp.tanh(u * (GELU_A + (GELU_A * GELU_B) * sq))
    return u * (0.5 + 0.5 * t)


def limit_of(res_ref):
    return jnp.where(res_ref[0] == 1, SIDE, SMALL_SIDE)


def group_mask(group, limit, first_row, rows, lanes):
    place = lax.broadcasted_iota(jnp.int32, (rows, lanes), 0) + first_row
    up = place // HALF
    across = place - up * HALF
    y = 2 * up + group // 2
    x = 2 * across + group % 2
    return jnp.where((y < limit) & (x < limit), 1.0, 0.0)


def cost(us):
    return pl.CostEstimate(flops=int(us * 2.0e9), bytes_accessed=1000, transcendentals=0)


def params_of(megabytes):
    return pltpu.CompilerParams(vmem_limit_bytes=megabytes * 1024 * 1024)


SMEM_SPEC = pl.BlockSpec(memory_space=pltpu.SMEM)
VMEM_SPEC = pl.BlockSpec(memory_space=pltpu.VMEM)


def patch_kernel(res_ref, img_ref, stem_ref, patch_ref, packet_ref, mask_ref):
    limit = limit_of(res_ref)
    lane = lax.broadcasted_iota(jnp.int32, (32, CANVAS), 1)
    rem = lane % 8
    row = lax.broadcasted_iota(jnp.int32, (SIDE, CANVAS), 0)
    col = lax.broadcasted_iota(jnp.int32, (SIDE, CANVAS), 1)
    wanted = jnp.where(row < HALF, 2 * row, 2 * (row - HALF) + 1)
    pick = jnp.where(col // 8 == wanted, 1.0, 0.0).astype(BF16)
    sub = lax.broadcasted_iota(jnp.int32, (8, CANVAS), 0)
    tap = lax.broadcasted_iota(jnp.int32, (2 * HALF, TAPS), 1)
    ones_at = (tap % 64 == 27) & (tap < 256)

    def step(i, _):
        bands = [[], [], [], []]
        above = []
        for c in range(3):
            before = img_ref[0, c, pl.ds(pl.multiple_of(jnp.maximum(32 * i - 16, 0), 16), 16), :]
            above.append(jnp.where(i > 0, before.astype(F32)[8:16], 0.0))
            for q in range(2):
                band = img_ref[0, c, pl.ds(pl.multiple_of(32 * i + 16 * q, 16), 16), :].astype(F32)
                bands[2 * q].append(band[0:8])
                bands[2 * q + 1].append(band[8:16])
        made = []
        for q in range(4):
            prev = above if q == 0 else bands[q - 1]
            edge = jnp.zeros((8, CANVAS), F32)
            for c in range(3):
                edge = jnp.where(sub == c, prev[c][7:8], edge)
            rows = jnp.concatenate(bands[q] + [edge], axis=0)
            rolled = pltpu.roll(rows, 8, 1)
            pieces = [jnp.where((rem == 7) & (lane >= 8), rolled, 0.0)]
            pieces += [jnp.where(rem == r, rows, 0.0) for r in range(8)]
            wide = jnp.concatenate(pieces, axis=0).astype(BF16)
            made.append(dot(pick, wide, NT))
        for py in range(2):
            for px in range(2):
                group = 2 * py + px
                two = jnp.concatenate(
                    [made[py][HALF * px : HALF * px + HALF], made[2 + py][HALF * px : HALF * px + HALF]],
                    axis=0,
                )
                inside = group_mask(group, limit, 2 * HALF * i, 2 * HALF, 128)
                mask_ref[pl.ds(pl.multiple_of(group * QUAD + 2 * HALF * i, 16), 2 * HALF), :] = inside
                two = jnp.where(ones_at, 1.0, two) * inside[:, 0:1]
                patch_ref[pl.ds(pl.multiple_of(group * QUAD + 2 * HALF * i, 16), 2 * HALF), :] = (
                    two.astype(BF16)
                )
        return 0

    lax.fori_loop(0, HALF // 2, step, 0, unroll=3)
    patches = patch_ref[...]
    gram = dot(patches, patches, TN)
    total = gram[0:96, 0:96]
    for px in range(1, 4):
        total = total + gram[64 * px : 64 * px + 96, 64 * px : 64 * px + 96]
    packet_ref[0:96, :] = jnp.concatenate([total, jnp.zeros((96, 32), F32)], axis=1)
    packet_ref[96:112, :] = stem_ref[...].astype(F32)


def make_patches(res_ids, images, stem):
    return pl.pallas_call(
        patch_kernel,
        out_shape=(
            jax.ShapeDtypeStruct((PLACES, TAPS), BF16),
            jax.ShapeDtypeStruct((112, 128), F32),
            jax.ShapeDtypeStruct((PLACES, 128), F32),
        ),
        in_specs=[SMEM_SPEC, VMEM_SPEC, VMEM_SPEC],
        out_specs=(VMEM_SPEC,) * 3,
        compiler_params=params_of(16),
        cost_estimate=cost(8),
        name="patches",
    )(res_ids, images, stem)


def spread_taps():
    table = np.zeros((8, TAPS, 64), np.float32)
    for px in range(4):
        for py in range(4):
            pair, half = px * 2 + py // 2, py % 2
            for dy in range(3):
                for dx in range(3):
                    for c in range(3):
                        ry = 2 * py + dy - 1
                        r = 24 + c if ry < 0 else 8 * c + ry
                        k = (2 * px + dx) * 32 + r
                        table[pair, k, half * 32 + (dy * 3 + dx) * 3 + c] = 1.0
    return table


def spread_weights(spread_ref, stem_w, out_ref, pairs=8):
    zero = jnp.zeros((32, STEM_CH), F32)
    double = jnp.concatenate(
        [jnp.concatenate([stem_w, zero], axis=1), jnp.concatenate([zero, stem_w], axis=1)], axis=0
    ).astype(BF16)
    for pair in range(pairs):
        out_ref[:, 128 * pair : 128 * pair + 128] = dot(spread_ref[pair], double).astype(BF16)


def stem_stats(gram, first_phases):
    weights = first_phases.astype(F32)
    product = dot(gram[:, :96], weights, precision=HIGH)
    second = jnp.sum(weights * product, axis=0, keepdims=True)
    first = product[27:28]
    count = 4.0 * gram[27:28, 27:28]
    both = jnp.concatenate([first, second, jnp.zeros((6, 256), F32)], axis=0)
    folded = both[:, 0:64] + both[:, 64:128] + both[:, 128:192] + both[:, 192:256]
    return folded[0:1] / count, folded[1:2] / count


def pairs_apart(rows, hold):
    hold[pl.ds(0, 16, stride=2), :] = rows
    hold[pl.ds(1, 16, stride=2), :] = pltpu.roll(rows, 64, 1)
    return hold[0:32, 0:64]


def pairs_together(rows, hold):
    hold[0:32, 0:64] = rows
    lane = lax.broadcasted_iota(jnp.int32, (16, 128), 1)
    return jnp.where(
        lane < 64, hold[pl.ds(0, 16, stride=2), :], pltpu.roll(hold[pl.ds(1, 16, stride=2), :], 64, 1)
    )


def stem_params(packet_ref, hold):
    rows = pairs_apart(packet_ref[96:112, :], hold)
    at = lax.broadcasted_iota(jnp.int32, (32, STEM_CH), 0)
    return jnp.where(at < 27, rows, 0.0), rows[27:28], rows[28:29]


STEM_STEPS = 3
STEM_BLOCK = PLACES // STEM_STEPS


def stem_kernel(patch_ref, packet_ref, spread_ref, base_ref, slope_ref, bgram_ref, big, hold, norm):
    @pl.when(pl.program_id(0) == 0)
    def _():
        weights, gain, shift = stem_params(packet_ref, hold)
        spread_weights(spread_ref, weights, big)
        mean, square = stem_stats(packet_ref[0:96, :], big[0:96, 0:256])
        gain = gain * lax.rsqrt(square - mean * mean + EPS)
        shift = shift - mean * gain
        norm[0:1, :] = jnp.concatenate([gain] * 4, axis=1)
        norm[1:2, :] = jnp.concatenate([shift] * 4, axis=1)
        bgram_ref[...] = jnp.zeros_like(bgram_ref)

    gain, shift = norm[0:1, :], norm[1:2, :]
    lane = lax.broadcasted_iota(jnp.int32, (STEM_BLOCK, 128), 1)
    block = patch_ref[...]
    pooled = jnp.zeros((STEM_BLOCK, 128), F32)
    for j in range(4):
        u = dot(block, big[:, 256 * j : 256 * j + 256]) * gain + shift
        value, slope = gelu_pair(u)
        slope_ref[:, 256 * j : 256 * j + 256] = slope.astype(BF16)
        pooled = pooled + value[:, 0:128] + value[:, 128:256]
    pooled = (pooled + pltpu.roll(pooled, 64, 1)) * (1.0 / 16.0)
    ones = block[:, 0:128].astype(F32)
    ones = pltpu.roll(ones, 64 - 27, 1)
    pooled = jnp.where(lane < 64, pooled, jnp.where(lane == 64, ones, 0.0)).astype(BF16)
    base_ref[...] = pooled
    masked = (pooled.astype(F32) * pooled[:, 64:65].astype(F32)).astype(BF16)
    bgram_ref[...] = bgram_ref[...] + dot(masked, pooled, TN)[0:72]


def stem_forward(patches, packet, spread):
    part = lambda width: pl.BlockSpec((STEM_BLOCK, width), lambda i: (i, 0))
    whole = lambda shape: pl.BlockSpec(shape, lambda i: (0,) * len(shape))
    return pl.pallas_call(
        stem_kernel,
        grid=(STEM_STEPS,),
        out_shape=(
            jax.ShapeDtypeStruct((PLACES, 128), BF16),
            jax.ShapeDtypeStruct((PLACES, 1024), BF16),
            jax.ShapeDtypeStruct((72, 128), F32),
        ),
        in_specs=[part(TAPS), whole((112, 128)), whole((8, TAPS, 64))],
        out_specs=(part(128), part(1024), whole((72, 128))),
        scratch_shapes=[
            pltpu.VMEM((TAPS, 1024), BF16), pltpu.VMEM((40, 128), F32), pltpu.VMEM((8, 256), F32),
        ],
        compiler_params=params_of(28),
        cost_estimate=cost(10),
        name="stem_forward",
    )(patches, packet, spread)


def taps_row(load, weight, py):
    sources = [(1, -1), (0, 0), (1, 0)] if py == 0 else [(0, 0), (1, 0), (0, 1)]
    rows = [[load(2 * gy + px, off) for px in range(2)] for gy, off in sources]

    def column(px, dx):
        total = rows[0][px] * weight(0, dx)
        total = total + rows[1][px] * weight(1, dx)
        return total + rows[2][px] * weight(2, dx)

    even = column(0, 1) + column(1, 2) + shift_down(column(1, 0))
    odd = column(1, 1) + column(0, 0) + shift_up(column(0, 2))
    return even, odd


def shift_down(v):
    at = lax.broadcasted_iota(jnp.int32, v.shape, 0)
    return jnp.where(at == 0, 0.0, pltpu.roll(v, 1, 0))


def shift_up(v):
    at = lax.broadcasted_iota(jnp.int32, v.shape, 0)
    return jnp.where(at == HALF - 1, 0.0, pltpu.roll(v, HALF - 1, 0))


def bn_stats(bgram, expand_w, count):
    weights = expand_w.astype(F32)
    square_of = jnp.concatenate([bgram, jnp.zeros((56, 128), F32)], axis=0)
    product = dot(square_of, weights, precision=HIGH)
    mean = product[64:65] / count
    second = jnp.sum(weights * product, axis=0, keepdims=True) / count
    return mean, lax.rsqrt(second - mean * mean + EPS)


def depth_kernel(mask_ref, base_ref, expand_ref, bgram_ref, norm_ref, depth_ref, out_ref, act_ref, slope_ref, stat_ref, pad, wide):
    count = bgram_ref[64:65, 64:65]
    mean, inverse = bn_stats(bgram_ref[...], expand_ref[...], count)
    gain = norm_ref[0:1] * inverse
    shift = norm_ref[1:2] - mean * gain
    zero = jnp.zeros((4, 1, HALF, BLOCK), F32)
    pad[:, 0:1] = zero
    pad[:, HALF + 1 : HALF + 2] = zero
    wide[...] = dot(base_ref[...], expand_ref[...])
    rows = 8 * HALF
    for group in range(4):

        def fill(i, _, group=group):
            first = pl.multiple_of(group * QUAD + rows * i, 16)
            at = pl.ds(first, rows)
            x = wide[at, :]
            inside = mask_ref[at, :]
            value, slope = gelu_pair(x * gain + shift)
            value = value * inside
            act_ref[at, :] = value.astype(BF16)
            slope_ref[at, :] = (slope * inside).astype(BF16)
            for k in range(8):
                pad[group, 8 * i + k + 1] = value[HALF * k : HALF * k + HALF]
            return 0

        lax.fori_loop(0, QUAD // rows, fill, 0)

    def weight(dy, dx):
        return depth_ref[3 * dy + dx : 3 * dy + dx + 1]

    def fold(v):
        return v[0:8] + v[8:16] + v[16:24]

    def step(up, sums):
        first, second = sums
        for py in range(2):
            made = taps_row(lambda g, off: pad[g, up + 1 + off], weight, py)
            for px in range(2):
                at = pl.ds(pl.multiple_of((2 * py + px) * QUAD + HALF * up, 8), HALF)
                x = made[px] * mask_ref[at, :]
                out_ref[at, :] = x
                first = first + fold(x)
                second = second + fold(x * x)
        return first, second

    sums = lax.fori_loop(0, HALF, step, (jnp.zeros((8, BLOCK), F32),) * 2, unroll=4)
    rows_out = [jnp.sum(s, axis=0, keepdims=True) for s in sums]
    stat_ref[...] = jnp.concatenate(rows_out + [jnp.zeros((6, BLOCK), F32)], axis=0)


def depth_forward(mask, base, expand_w, bgram, mid_norm, mb_depth):
    col = lambda rows: pl.BlockSpec((rows, BLOCK), lambda j: (0, j))
    whole = lambda rows: pl.BlockSpec((rows, BLOCK), lambda j: (0, 0))
    return pl.pallas_call(
        depth_kernel,
        grid=(CHUNKS,),
        out_shape=(
            jax.ShapeDtypeStruct((PLACES, EXPAND), F32),
            jax.ShapeDtypeStruct((PLACES, EXPAND), BF16),
            jax.ShapeDtypeStruct((PLACES, EXPAND), BF16),
            jax.ShapeDtypeStruct((8, EXPAND), F32),
        ),
        in_specs=[whole(PLACES), whole(PLACES), col(128), whole(72), col(2), col(9)],
        out_specs=(col(PLACES),) * 3 + (col(8),),
        scratch_shapes=[pltpu.VMEM((4, HALF + 2, HALF, BLOCK), F32), pltpu.VMEM((PLACES, BLOCK), F32)],
        compiler_params=params_of(56),
        cost_estimate=cost(25),
        name="depth_forward",
    )(mask, base, expand_w, bgram, mid_norm, mb_depth)


EARLY_ROWS = 576
STEM_ROWS = 15


def runs_of(offset, rows, width):
    period = min(128 // math.gcd(width, 128), rows)
    stride = period * width // 128 if rows > period else 1
    for j in range(period):
        start = offset + j * width
        yield j, period, start // 128, start % 128, -(-(rows - j) // period), stride


def rows_at(first, count, stride):
    return pl.ds(first, count) if stride == 1 or count == 1 else pl.ds(first, count, stride=stride)


def chunks_of(count, size=128):
    for begin in range(0, count, size):
        yield begin, min(size, count - begin)


def round_up(n, m):
    return -(-n // m) * m


def take_matrix(flat, out_ref, hold, offset, rows, width):
    direct = True
    for j, period, first, shift, count, stride in runs_of(offset, rows, width):
        direct = period == 1
        for t in range(-(-width // 128)):
            wide = min(128, width - 128 * t)
            for begin, size in chunks_of(count):
                at = first + t + begin * stride
                value = flat[rows_at(at, size, stride), :]
                if shift:
                    if shift + wide > 128:
                        lane = lax.broadcasted_iota(jnp.int32, (size, 128), 1)
                        value = jnp.where(lane >= shift, value, flat[rows_at(at + 1, size, stride), :])
                    value = pltpu.roll(value, 128 - shift, 1)
                if direct:
                    out_ref[begin : begin + size, 128 * t : 128 * t + wide] = value[:, :wide].astype(out_ref.dtype)
                elif count == 1:
                    out_ref[j : j + 1, 128 * t : 128 * t + wide] = value[:, :wide].astype(out_ref.dtype)
                else:
                    hold[t, rows_at(j + begin * period, size, period), :] = value
    if not direct and count > 1:
        for t in range(-(-width // 128)):
            wide = min(128, width - 128 * t)
            out_ref[0:rows, 128 * t : 128 * t + wide] = hold[t, 0:rows, 0:wide].astype(out_ref.dtype)


def put_matrix(flat, value_of, base, offset, rows, width):
    for j, period, first, shift, count, stride in runs_of(offset, rows, width):
        tiles = -(-width // 128)
        for begin, size in chunks_of(count):
            before = None
            lane = lax.broadcasted_iota(jnp.int32, (size, 128), 1)
            picked = rows_at(j + begin * period, size, period)
            at = first - base + begin * stride
            for t in range(tiles):
                value = value_of(picked, t)
                if shift:
                    value = pltpu.roll(value, shift, 1)
                    mixed = jnp.where(lane >= shift, value, 0.0 if before is None else before)
                else:
                    mixed = value
                before = value
                where = rows_at(at + t, size, stride)
                full = 0 < t < tiles - 1 or (shift == 0 and width % 128 == 0)
                flat[where, :] = mixed if full else flat[where, :] + mixed
            if shift:
                where = rows_at(at + tiles, size, stride)
                flat[where, :] = flat[where, :] + jnp.where(lane < shift, before, 0.0)


def unpack_kernel(names, shapes, pieces, shard_rows, me_ref, masks_ref, *refs):
    blocks, outs, (flat, hold) = refs[:pieces], refs[pieces:-2], refs[-2:]
    base = 0
    for block in blocks:

        def place(k, _, block=block, base=base):
            where = pl.ds((masks_ref[base + k] ^ me_ref[0]) * shard_rows, shard_rows)
            flat[where, :] = block[k].astype(F32)[:shard_rows]
            return 0

        lax.fori_loop(0, block.shape[0], place, 0)
        base += block.shape[0]
    for name, shape, out in zip(names, shapes, outs):
        offset, own = OFFSETS[name]
        width = own[-1]
        rows = math.prod(own) // width
        if shape[0][0] > rows or shape[0][1] > width:
            out[...] = jnp.zeros_like(out)
        take_matrix(flat, out, hold, offset, rows, width)


def unpack(blocks, me, masks, shard_rows, shapes):
    names = tuple(shapes)
    kinds = tuple(shapes[n] for n in names)
    total = sum(b.shape[0] for b in blocks) * shard_rows + 136
    made = pl.pallas_call(
        functools.partial(unpack_kernel, names, kinds, len(blocks), shard_rows),
        out_shape=tuple(jax.ShapeDtypeStruct(*k) for k in kinds),
        in_specs=[SMEM_SPEC] * 2 + [VMEM_SPEC] * len(blocks),
        out_specs=(VMEM_SPEC,) * len(names),
        scratch_shapes=[pltpu.VMEM((total, 128), F32), pltpu.VMEM((8, EXPAND + 16, 128), F32)],
        compiler_params=params_of(60),
        cost_estimate=cost(6),
        name="unpack",
    )(me, jnp.asarray(masks, jnp.int32), *blocks)
    return dict(zip(names, made))


EARLY_SHAPES = {
    "mb_short": ((128, MB_CH), BF16), "mb_expand": ((128, EXPAND), BF16), "mid_norm": ((2, EXPAND), F32),
    "mb_depth": ((9, EXPAND), F32), "dw_norm": ((2, EXPAND), F32),
}
LATE_SHAPES = {
    "se_down": ((EXPAND, SQUEEZE), BF16), "se_down_bias": ((1, SQUEEZE), F32), "se_up": ((SQUEEZE, EXPAND), BF16),
    "se_up_bias": ((1, EXPAND), F32), "mb_proj": ((EXPAND, MB_CH), BF16), "at_short": ((MB_CH, DIM), BF16),
    "pre_norm": ((2, MB_CH), F32), "qkv": ((MB_CH, 3 * DIM), BF16), "attn_out": ((DIM, DIM), BF16),
    "out_bias": ((1, DIM), F32), "rel_table": ((16, 2 * WIDE), F32), "mlp_norm": ((2, DIM), F32),
    "mlp_in": ((DIM, MLP), BF16), "mlp_in_bias": ((1, MLP), F32), "mlp_out": ((MLP, DIM), BF16),
    "mlp_out_bias": ((1, DIM), F32), "head_norm": ((2, DIM), F32), "head_w": ((DIM, CLASSES), BF16),
    "head_bias": ((1, CLASSES), F32),
}


ALL_SHAPES = EARLY_SHAPES | LATE_SHAPES


def pack_kernel(names, base, shards, shard_rows, core_ref, *refs):
    grads, (keep_ref, send_ref), (flat, hold) = refs[: len(names)], refs[len(names) : -2], refs[-2:]
    rows_all = flat.shape[0]
    step = 384

    def clear(i, _):
        flat[pl.ds(pl.multiple_of(i * step, 8), step), :] = jnp.zeros((step, 128), F32)
        return 0

    lax.fori_loop(0, rows_all // step, clear, 0)
    for name, grad in zip(names, grads):
        offset, own = OFFSETS[name]
        width = own[-1]
        rows = math.prod(own) // width
        tiles = -(-width // 128)
        read = lambda r, t: grad[r, 128 * t : 128 * t + 128]
        if grad.shape[1] < 128 * tiles:
            hold[tiles - 1, 0:rows, :] = jnp.zeros((rows, 128), F32)
            for t in range(tiles):
                wide = min(128, width - 128 * t)
                hold[t, 0:rows, 0:wide] = grad[0:rows, 128 * t : 128 * t + wide]
            read = lambda r, t: hold[t, r, :]
        put_matrix(flat, read, base, offset, rows, width)

    def share(k, _):
        block = flat[pl.ds(k * shard_rows, shard_rows), :]
        ours = k % 2 == core_ref[0]

        @pl.when(ours)
        def _():
            keep_ref[k // 2, 0:shard_rows] = block

        @pl.when(jnp.logical_not(ours))
        def _():
            send_ref[k // 2, 0:shard_rows] = block

        return 0

    lax.fori_loop(0, shards, share, 0)


def pack(core, grads, base, shards, shard_rows, held_rows):
    names = tuple(grads)
    total = -(-(shards * shard_rows + 8) // 384) * 384
    out = jax.ShapeDtypeStruct((shards // 2, held_rows, 128), F32)
    return pl.pallas_call(
        functools.partial(pack_kernel, names, base, shards, shard_rows),
        out_shape=(out, out),
        in_specs=[SMEM_SPEC] + [VMEM_SPEC] * len(names),
        out_specs=(VMEM_SPEC,) * 2,
        scratch_shapes=[pltpu.VMEM((total, 128), F32), pltpu.VMEM((2, EXPAND + 16, 128), F32)],
        compiler_params=params_of(32),
        cost_estimate=cost(6),
        name="pack",
    )(core, *grads.values())


def shard_kernel(
    length, tall_out, tall_head, first_ref, late_ref, mid_ref, dw_ref, norm_ref, vector_ref, stem_ref, loss_ref,
    out_ref, packet_ref, flat, hold, left_out, left_head,
):
    rows = length // 128
    lead = 16
    flat[...] = jnp.zeros_like(flat)
    start = first_ref[0] * length
    lane = lax.broadcasted_iota(jnp.int32, (8, 128), 1)

    def add_rows(first, value):
        flat[pl.ds(first, value.shape[0]), :] = flat[pl.ds(first, value.shape[0]), :] + value

    devices = vector_ref.shape[0]
    part = min(devices, 128)

    def place(name, left_ref, at_left, at_right, tall):
        offset, (count, width) = OFFSETS[name]
        first = (start - offset + 2**20 * width) // width - 2**20
        inside = (first > -tall) & (first < count)
        held = jnp.where(inside, first, -tall)
        made = jnp.zeros((tall, 128 * -(-width // 128)), F32)
        for g in range(devices // part):
            group = slice(g * part, g * part + part)
            left_ref[g] = jnp.zeros_like(left_ref[g])
            left_ref[g, tall : tall + count, :] = vector_ref[group, at_left, 0:count].T
            right = vector_ref[group, at_right, 0 : hold.shape[2] * -(-width // 128)]
            made = made + dot(left_ref[g, pl.ds(held + tall, tall), :], right, precision=HIGH)
        tiles = -(-width // 128)
        for t in range(tiles):
            wide = min(128, made.shape[1] - 128 * t)
            hold[t, 0:tall, 0:wide] = made[:, 128 * t : 128 * t + wide]
        period = 128 // math.gcd(width, 128)
        stride = period * width // 128

        @pl.when(inside)
        def _():
            for j in range(period):
                begin = offset + (first + j) * width - start + 128 * lead
                row = begin // 128
                shift = begin - row * 128
                size = tall // period
                at_lane = lax.broadcasted_iota(jnp.int32, (size, 128), 1)
                for t in range(tiles):
                    value = hold[t, rows_at(j, size, period), :]
                    value = pltpu.roll(value, shift, 1)
                    where = rows_at(row + t, size, stride)
                    flat[where, :] = flat[where, :] + jnp.where(at_lane >= shift, value, 0.0)
                    where = rows_at(row + t + 1, size, stride)
                    flat[where, :] = flat[where, :] + jnp.where(at_lane < shift, value, 0.0)

    def place_row(offset, value):
        width = value.shape[1]
        begin = offset - start

        @pl.when((begin > -width) & (begin < length))
        def _():
            at = begin + 128 * lead
            row = at // 128
            shift = at - row * 128
            one = lane[0:1]
            for t in range(width // 128):
                tile = pltpu.roll(value[:, 128 * t : 128 * t + 128], shift, 1)
                add_rows(row + t, jnp.where(one >= shift, tile, 0.0))
                add_rows(row + t + 1, jnp.where(one < shift, tile, 0.0))

    place("mlp_out", left_out, 0, 1, tall_out)
    place("head_w", left_head, 2, 3, tall_head)
    place_row(OFFSETS["mlp_out_bias"][0], dw_ref[3:4, 0:DIM])
    place_row(OFFSETS["head_norm"][0], dw_ref[2:3, :])
    place_row(OFFSETS["head_bias"][0], dw_ref[4:5, :])
    place_row(OFFSETS["head_bias"][0] + EXPAND, dw_ref[5:6, 0:256])
    place_row(OFFSETS["mid_norm"][0], norm_ref[0:1, :])
    place_row(OFFSETS["mid_norm"][0] + EXPAND, norm_ref[1:2, :])
    place_row(OFFSETS["dw_norm"][0], dw_ref[1:2, :])
    place_row(OFFSETS["dw_norm"][0] + EXPAND, dw_ref[0:1, :])
    total = flat[lead : lead + rows, :] + late_ref[0:rows] + mid_ref[0:rows]
    out_ref[...] = total
    square = jnp.sum(total * total).reshape(1, 1)
    packet_ref[0:16, :] = stem_ref[...]
    packet_ref[16:24, :] = jnp.where(lane == 0, loss_ref[...], jnp.where(lane == 1, square, 0.0))


def shard_parts(me, length, late, mid, dw_sums, mid_sums, vectors, stem, loss):
    rows = length // 128
    devices = vectors.shape[0]
    part = min(devices, 128)

    def tall(name, unit):
        width = OFFSETS[name][1][1]
        return round_up(-(-length // width) + 1, unit)

    tall_out, tall_head = tall("mlp_out", 8), tall("head_w", 16)
    return pl.pallas_call(
        functools.partial(shard_kernel, length, tall_out, tall_head),
        out_shape=(jax.ShapeDtypeStruct((rows, 128), F32), jax.ShapeDtypeStruct((24, 128), F32)),
        in_specs=[SMEM_SPEC] + [VMEM_SPEC] * 7,
        out_specs=(VMEM_SPEC,) * 2,
        scratch_shapes=[
            pltpu.VMEM((rows + 1024, 128), F32),
            pltpu.VMEM((8, max(tall_out, tall_head) + 16, 128), F32),
            pltpu.VMEM((devices // part, MLP + 2 * tall_out, part), F32),
            pltpu.VMEM((devices // part, DIM + 2 * tall_head, part), F32),
        ],
        compiler_params=params_of(16),
        cost_estimate=cost(4),
        name="shard_parts",
    )(me, late, mid, dw_sums, mid_sums, vectors, stem, loss)


def squeeze_lanes():
    table = np.zeros((16 * 48, 16 * 24), np.float32)
    for e in range(16):
        for x in range(24):
            table[e * 48 + x, e * 24 + x] = 1.0
    return table


def slots_of(rel_index):
    last = TOKENS - 1
    corner = lambda i: rel_index[i].reshape(HALF, HALF)
    low_row = jnp.concatenate([corner(last), corner(last - HALF + 1)[:, 1:]], axis=1)
    high_row = jnp.concatenate([corner(HALF - 1), corner(0)[:, 1:]], axis=1)
    return jnp.concatenate([low_row, high_row[1:]], axis=0)


def one_hot(slot_ref, c):
    at = lax.broadcasted_iota(jnp.int32, (256, 2 * WIDE), 1)
    return jnp.where(slot_ref[256 * c : 256 * c + 256, :] == at, 1.0, 0.0).astype(BF16)


def bias_kernel(table_ref, slot_ref, pick_ref, out_ref, held):
    table = table_ref[...].astype(BF16)
    f = jnp.concatenate([dot(table, one_hot(slot_ref, c), NT) for c in range(2 * WIDE // 256)], axis=1)
    for x in range(HALF):
        turned = pltpu.roll(f, (WIDE * 2 - (HALF - 1 - x)) % (WIDE * 2), 1) if x != HALF - 1 else f
        held[16 * x : 16 * x + 16, :] = turned.astype(BF16)
    for part in range(3):
        made = dot(held[:, 768 * part : 768 * part + 768], pick_ref[...])
        for t in range(3):
            for x in range(HALF):
                out_ref[3 * part + t, pl.ds(x, HEADS, stride=HALF), :] = made[
                    16 * x : 16 * x + HEADS, 128 * t : 128 * t + 128
                ]


def build_bias(table, slots, pick):
    return pl.pallas_call(
        bias_kernel,
        out_shape=jax.ShapeDtypeStruct((9, HEADS * HALF + HALF, 128), F32),
        in_specs=[VMEM_SPEC] * 3,
        out_specs=VMEM_SPEC,
        scratch_shapes=[pltpu.VMEM((16 * HALF, 2 * WIDE), BF16)],
        compiler_params=params_of(16),
        cost_estimate=cost(8),
        name="bias_build",
    )(table, slots, pick)


def halves_of(v):
    high = v.astype(BF16)
    return high, (v - high.astype(F32)).astype(BF16)


def bias_back_step(grad_ref, slot_ref, pick_ref, out_ref, held):
    for part in range(3):
        rows = jnp.concatenate([grad_ref[3 * part + t] for t in range(3)], axis=1)
        high, rest = halves_of(rows)
        wide = dot(high, pick_ref[...]) + dot(rest, pick_ref[...])
        for t in range(6):
                held[6 * part + t, 0 : HEADS * HALF, :] = wide[:, 128 * t : 128 * t + 128]
    total = jnp.zeros((16, 2 * WIDE), F32)
    for x in range(HALF):
        wide = jnp.concatenate([held[t, pl.ds(x, HEADS, stride=HALF), :] for t in range(18)], axis=1)
        wide = jnp.concatenate([wide, jnp.zeros((4, 2 * WIDE), F32)], axis=0)
        total = total + (pltpu.roll(wide, HALF - 1 - x, 1) if x != HALF - 1 else wide)
    high, rest = halves_of(total)
    result = jnp.zeros((16, 2 * WIDE), F32)
    for c in range(2 * WIDE // 256):
        hot = one_hot(slot_ref, c)
        cols = slice(256 * c, 256 * c + 256)
        result = result + dot(high[:, cols], hot) + dot(rest[:, cols], hot)
    out_ref[...] = result


def sigmoid(v):
    return 1.0 / (1.0 + jnp.exp(-v))


def row8(rows):
    width = rows[0].shape[1]
    return jnp.concatenate(rows + [jnp.zeros((8 - len(rows), width), F32)], axis=0)


def dw_stats(stat, count):
    mean = stat[0:1] / count
    return mean, lax.rsqrt(stat[1:2] / count - mean * mean + EPS)


def valid_places(limit):
    return (limit * limit).astype(F32)


def excite_kernel(
    res_ref, mask_ref, depth_ref, stat_ref, bgram_ref, norm_ref, down_ref, down_b_ref, up_ref, up_b_ref,
    proj_ref, base_ref, short_ref, pre_ref, qkv_ref,
    act_ref, slope_ref, block_ref, skip_ref, normed_ref, project_ref, vec_ref, small_ref, held, total,
):
    limit = limit_of(res_ref)
    count = bgram_ref[64:65, 64:65]
    mean, inverse = dw_stats(stat_ref[...], count)
    gain = norm_ref[0:1] * inverse
    shift = norm_ref[1:2] - mean * gain
    rows = 4 * HALF
    group = pl.program_id(0)

    @pl.when(group == 0)
    def _():
        total[...] = jnp.zeros_like(total)

    def fill(i, sums):
        at = pl.ds(pl.multiple_of(rows * i, 16), rows)
        value, slope = gelu_pair(depth_ref[at, :] * gain + shift)
        inside = jnp.concatenate([mask_ref[at, :]] * CHUNKS, axis=1)
        value = value * inside
        held[pl.ds(pl.multiple_of(group * QUAD + rows * i, 16), rows), :] = value
        act_ref[at, :] = value.astype(BF16)
        slope_ref[at, :] = (slope * inside).astype(BF16)
        for k in range(rows // 8):
            sums = sums + value[8 * k : 8 * k + 8]
        return sums

    total[...] = lax.fori_loop(0, QUAD // rows, fill, total[...])

    @pl.when(group == 3)
    def _():
        excite_rest(
            limit, mean, inverse, total, down_ref, down_b_ref, up_ref, up_b_ref, proj_ref, base_ref, short_ref,
            pre_ref, qkv_ref, block_ref, skip_ref, normed_ref, project_ref, vec_ref, small_ref, held,
        )


def excite_rest(
    limit, mean, inverse, total, down_ref, down_b_ref, up_ref, up_b_ref, proj_ref, base_ref, short_ref, pre_ref,
    qkv_ref, block_ref, skip_ref, normed_ref, project_ref, vec_ref, small_ref, held,
):
    pooled = jnp.sum(total[...], axis=0, keepdims=True) / valid_places(limit)
    before = dot(row8([pooled]), down_ref[...].astype(F32), precision=HIGH)[0:1] + down_b_ref[...]
    gate = sigmoid(before)
    squeeze = before * gate
    excite = sigmoid(
        dot(row8([squeeze]), up_ref[...].astype(F32), precision=HIGH)[0:1] + up_b_ref[...]
    )
    vec_ref[...] = row8([pooled, excite, mean, inverse])
    small_ref[...] = row8([squeeze, gate * (1.0 + before * (1.0 - gate))])

    big = 576
    def section(i, _):
        at = pl.ds(pl.multiple_of(big * i, 16), big)
        scaled = (held[at, :] * excite).astype(BF16)
        block_ref[at, :] = dot(scaled, proj_ref[...]) + dot(base_ref[at, :], short_ref[...])
        return 0

    lax.fori_loop(0, PLACES // big, section, 0)
    part = 96

    def tokens(i, _):
        skipped = jnp.zeros((part, MB_CH), F32)
        normed = jnp.zeros((part, MB_CH), F32)
        for group in range(4):
            block = block_ref[pl.ds(pl.multiple_of(group * QUAD + part * i, 16), part), :]
            skipped = skipped + block
            hat, _ = normalise(block)
            normed = normed + hat
        at = pl.ds(pl.multiple_of(part * i, 16), part)
        skip_ref[at, :] = (0.25 * skipped).astype(BF16)
        low = (0.25 * normed * pre_ref[0:1] + pre_ref[1:2]).astype(BF16)
        normed_ref[at, :] = low
        return 0

    lax.fori_loop(0, TOKENS // part, tokens, 0)
    project_ref[...] = dot(normed_ref[...], qkv_ref[...]).astype(BF16)


def normalise(v):
    centered = v - jnp.mean(v, axis=-1, keepdims=True)
    inverse = lax.rsqrt(jnp.mean(centered * centered, axis=-1, keepdims=True) + EPS)
    return centered * inverse, inverse


def normalise_back(grad_hat, hat, inverse):
    first = jnp.mean(grad_hat, axis=-1, keepdims=True)
    second = jnp.mean(grad_hat * hat, axis=-1, keepdims=True)
    return inverse * (grad_hat - first - hat * second)


def excite_forward(res_ids, mask, depth, stat, bgram, base, p):
    part = lambda width: pl.BlockSpec((QUAD, width), lambda i: (i, 0))
    whole = lambda *shape: pl.BlockSpec(shape, lambda i: (0,) * len(shape))
    return pl.pallas_call(
        excite_kernel,
        grid=(4,),
        out_shape=(
            jax.ShapeDtypeStruct((PLACES, EXPAND), BF16),
            jax.ShapeDtypeStruct((PLACES, EXPAND), BF16),
            jax.ShapeDtypeStruct((PLACES, MB_CH), F32),
            jax.ShapeDtypeStruct((TOKENS, MB_CH), BF16),
            jax.ShapeDtypeStruct((TOKENS, MB_CH), BF16),
            jax.ShapeDtypeStruct((TOKENS, 3 * DIM), BF16),
            jax.ShapeDtypeStruct((8, EXPAND), F32),
            jax.ShapeDtypeStruct((8, SQUEEZE), F32),
        ),
        in_specs=[
            SMEM_SPEC, part(128), part(EXPAND), whole(8, EXPAND), whole(72, 128), whole(2, EXPAND),
            whole(EXPAND, SQUEEZE), whole(1, SQUEEZE), whole(SQUEEZE, EXPAND), whole(1, EXPAND),
            whole(EXPAND, MB_CH), whole(PLACES, 128), whole(128, MB_CH), whole(2, MB_CH), whole(MB_CH, 3 * DIM),
        ],
        out_specs=(
            part(EXPAND), part(EXPAND), whole(PLACES, MB_CH), whole(TOKENS, MB_CH), whole(TOKENS, MB_CH),
            whole(TOKENS, 3 * DIM), whole(8, EXPAND), whole(8, SQUEEZE),
        ),
        scratch_shapes=[pltpu.VMEM((PLACES, EXPAND), F32), pltpu.VMEM((8, EXPAND), F32)],
        compiler_params=params_of(40),
        cost_estimate=cost(18),
        name="excite_forward",
    )(
        res_ids, mask, depth, stat, bgram, p["dw_norm"], p["se_down"], p["se_down_bias"], p["se_up"], p["se_up_bias"],
        p["mb_proj"], base, p["mb_short"], p["pre_norm"], p["qkv"],
    )


SCALE = HEAD_DIM ** (-0.5)
PER = BLOCK // HEAD_DIM
ATT_ROWS = 2 * HALF


def token_valid(limit, shape, axis):
    at = lax.broadcasted_iota(jnp.int32, shape, axis)
    y = at // HALF
    x = at - y * HALF
    return (2 * y < limit) & (2 * x < limit)


def head_lanes(h):
    lane = lax.broadcasted_iota(jnp.int32, (TOKENS, BLOCK), 1)
    return lane // HEAD_DIM == h


def bias_cut(up):
    offset = (HALF - 1 - up) * HALF
    lead = offset % 128
    return offset // 128, (5 if lead <= 64 else 6), lead


def attend_kernel(res_ref, q_ref, k_ref, v_ref, bias_ref, out_ref, p_ref, scores):
    limit = limit_of(res_ref)
    usable = token_valid(limit, (1, TOKENS), 1)

    def head(h, total):
        mine = head_lanes(h)
        q = jnp.where(mine, q_ref[...], jnp.zeros((), BF16))
        scores[h % 2] = dot(q, k_ref[...], NT)
        bias_rows = pl.ds(pl.multiple_of(h * HALF, 8), HALF)
        for i in range(TOKENS // ATT_ROWS):
            at = slice(ATT_ROWS * i, ATT_ROWS * i + ATT_ROWS)
            shifted = []
            for k in range(2):
                tile, tiles, lead = bias_cut(2 * i + k)
                bias = jnp.concatenate([bias_ref[tile + t, bias_rows, :] for t in range(tiles)], axis=1)
                if lead:
                    bias = pltpu.roll(bias, 128 * tiles - lead, 1)
                shifted.append(bias[:, :TOKENS])
            s = scores[h % 2, at, :] * SCALE + jnp.concatenate(shifted, axis=0)
            s = jnp.where(usable, s, -1e30)
            e = jnp.exp(s - jnp.max(s, axis=-1, keepdims=True))
            weights = e * (1.0 / jnp.sum(e, axis=-1, keepdims=True))
            p_ref[h, at, :] = weights.astype(BF16)
        return jnp.where(mine, dot(p_ref[h], v_ref[...]), total)

    total = lax.fori_loop(0, PER, head, jnp.zeros((TOKENS, BLOCK), F32), unroll=2)
    out_ref[...] = total.astype(BF16)


def attend_forward(res_ids, project, bias):
    part = lambda k: pl.BlockSpec((TOKENS, BLOCK), lambda j: (0, 3 * k + j))
    return pl.pallas_call(
        attend_kernel,
        grid=(HEADS // PER,),
        out_shape=(
            jax.ShapeDtypeStruct((TOKENS, DIM), BF16),
            jax.ShapeDtypeStruct((HEADS, TOKENS, TOKENS), BF16),
        ),
        in_specs=[SMEM_SPEC, part(0), part(1), part(2), pl.BlockSpec((9, PER * HALF, 128), lambda j: (0, j, 0))],
        out_specs=(
            pl.BlockSpec((TOKENS, BLOCK), lambda j: (0, j)),
            pl.BlockSpec((PER, TOKENS, TOKENS), lambda j: (j, 0, 0)),
        ),
        scratch_shapes=[pltpu.VMEM((2, TOKENS, TOKENS), F32)],
        compiler_params=params_of(20),
        cost_estimate=cost(35),
        name="attend_forward",
    )(res_ids, project, project, project, bias)


def attend_back_kernel(
    q_ref, k_ref, v_ref, o_ref, do_ref, p_ref, slot_ref, pick_ref, dq_ref, dk_ref, dv_ref, dtable_ref,
    scores, low, bias, dbias_ref, held, turned, sums,
):
    first_head = pl.program_id(0) * PER

    turned[0] = q_ref[...].astype(F32).T.astype(BF16)
    turned[1] = do_ref[...].astype(F32).T.astype(BF16)

    def head(h, dq):
        mine = head_lanes(h)
        grad = jnp.where(mine, do_ref[...], jnp.zeros((), BF16))
        scores[...] = dot(grad, v_ref[...], NT)
        bias[...] = jnp.zeros((HALF, WIDE), F32)
        lane = lax.broadcasted_iota(jnp.int32, (ATT_ROWS, BLOCK), 1)
        for i in range(TOKENS // ATT_ROWS):
            at = slice(ATT_ROWS * i, ATT_ROWS * i + ATT_ROWS)
            both = do_ref[at, :].astype(F32) * o_ref[at, :].astype(F32)
            both = jnp.where(lane // HEAD_DIM == h, both, 0.0)
            delta = jnp.sum(both, axis=-1, keepdims=True)
            ds = p_ref[h, at, :].astype(F32) * (scores[at, :] - delta)
            low[at, :] = (ds * SCALE).astype(BF16)
            for k in range(2):
                tile, tiles, lead = bias_cut(2 * i + k)
                wide = jnp.concatenate(
                    [ds[HALF * k : HALF * k + HALF], jnp.zeros((HALF, 128 * tiles - TOKENS), F32)], axis=1
                )
                if lead:
                    wide = pltpu.roll(wide, lead, 1)
                cols = slice(128 * tile, 128 * (tile + tiles))
                bias[:, cols] = bias[:, cols] + wide
        for t in range(9):
            dbias_ref[t, pl.ds(pl.multiple_of((first_head + h) * HALF, 8), HALF), :] = bias[:, 128 * t : 128 * t + 128]
        dq = jnp.where(mine, dot(low[...], k_ref[...]), dq)
        own = pl.ds(pl.multiple_of(h * HEAD_DIM, HEAD_DIM), HEAD_DIM)
        sums[0, own, :] = dot(turned[0, own, :], low[...])
        sums[1, own, :] = dot(turned[1, own, :], p_ref[h])
        return dq

    dq = lax.fori_loop(0, PER, head, jnp.zeros((TOKENS, BLOCK), F32))
    dq_ref[...] = dq.astype(BF16)
    dk_ref[...] = sums[0].T.astype(BF16)
    dv_ref[...] = sums[1].T.astype(BF16)

    @pl.when(pl.program_id(0) == HEADS // PER - 1)
    def _():
        bias_back_step(dbias_ref, slot_ref, pick_ref, dtable_ref, held)


def attend_backward(project, blended, grad, weights, slots, pick):
    part = lambda k: pl.BlockSpec((TOKENS, BLOCK), lambda j: (0, 3 * k + j))
    whole = lambda *shape: pl.BlockSpec(shape, lambda j: (0,) * len(shape))
    return pl.pallas_call(
        attend_back_kernel,
        grid=(HEADS // PER,),
        out_shape=(jax.ShapeDtypeStruct((TOKENS, DIM), BF16),) * 3
        + (jax.ShapeDtypeStruct((16, 2 * WIDE), F32),),
        in_specs=[
            part(0), part(1), part(2), part(0), part(0),
            pl.BlockSpec((PER, TOKENS, TOKENS), lambda j: (j, 0, 0)), whole(2 * WIDE, 1), whole(16 * HALF, 32 * HALF),
        ],
        out_specs=(part(0), part(0), part(0), whole(16, 2 * WIDE)),
        scratch_shapes=[
            pltpu.VMEM((TOKENS, TOKENS), F32), pltpu.VMEM((TOKENS, TOKENS), BF16), pltpu.VMEM((HALF, WIDE), F32),
            pltpu.VMEM((9, HEADS * HALF, 128), F32), pltpu.VMEM((18, HEADS * HALF + HALF, 128), F32),
            pltpu.VMEM((2, BLOCK, TOKENS), BF16), pltpu.VMEM((2, BLOCK, TOKENS), F32),
        ],
        compiler_params=params_of(56),
        cost_estimate=cost(40),
        name="attend_backward",
    )(project, project, project, blended, grad, weights, slots, pick)


MLP_ROWS = 192


def mlp_kernel(
    share, res_ref, label_ref, skip_ref, blend_ref, short_ref, out_ref, out_b_ref, norm_ref, in_ref, in_b_ref,
    back_ref, back_b_ref, hnorm_ref, head_ref, head_b_ref,
    loss_ref, dblend_ref, dskip_ref, dshort_ref, dout_ref, dout_b_ref, dnorm_ref, din_ref, din_b_ref,
    vec_ref, few_ref,
    section, low, slopes, dpres, grads,
):
    limit = limit_of(res_ref)
    n_valid = (limit // 2 * (limit // 2)).astype(F32)
    steps = TOKENS // MLP_ROWS
    cut = 384

    def valid_rows(i):
        at = lax.broadcasted_iota(jnp.int32, (MLP_ROWS, 1), 0) + MLP_ROWS * i
        y = at // HALF
        x = at - y * HALF
        return jnp.where((2 * y < limit) & (2 * x < limit), 1.0, 0.0)

    def forward(i, carry):
        feature, used = carry
        at = pl.ds(pl.multiple_of(MLP_ROWS * i, 16), MLP_ROWS)
        first = dot(skip_ref[at, :], short_ref[...]) + dot(blend_ref[at, :], out_ref[...]) + out_b_ref[...]
        section[at, :] = first
        hat, _ = normalise(first)
        normed = (hat * norm_ref[0:1] + norm_ref[1:2]).astype(BF16)
        low[at, :] = normed
        inside = valid_rows(i)
        second = first + back_b_ref[...]
        parts = []
        for j in range(MLP // cut):
            cols = slice(cut * j, cut * j + cut)
            value, slope = gelu_pair(dot(normed, in_ref[:, cols]) + in_b_ref[:, cols])
            slopes[at, cols] = slope * inside
            value = value.astype(BF16)
            parts.append(jnp.sum(value.astype(F32) * inside, axis=0, keepdims=True))
            second = second + dot(value, back_ref[cols, :])
        feature = feature + jnp.sum(second * inside, axis=0, keepdims=True)
        return feature, used + jnp.concatenate(parts, axis=1)

    feature, used = lax.fori_loop(
        0, steps, forward, (jnp.zeros((1, DIM), F32), jnp.zeros((1, MLP), F32))
    )
    feature = feature / n_valid
    hat, inverse = normalise(feature)
    normed = (hat * hnorm_ref[0:1] + hnorm_ref[1:2]).astype(BF16)
    normed8 = jnp.concatenate([normed.astype(F32), jnp.zeros((15, DIM), F32)], axis=0).astype(BF16)
    logits = dot(normed8, head_ref[...])[0:1] + head_b_ref[...]
    peak = jnp.max(logits, axis=-1, keepdims=True)
    exps = jnp.exp(logits - peak)
    total = jnp.sum(exps, axis=-1, keepdims=True)
    log_probs = logits - peak - jnp.log(total)
    at_class = lax.broadcasted_iota(jnp.int32, (1, CLASSES), 1)
    goal = jnp.where(at_class == label_ref[0], 1.0 - SMOOTH, 0.0) + SMOOTH / CLASSES
    loss = -jnp.sum(goal * log_probs, axis=-1, keepdims=True)
    loss_ref[...] = jnp.broadcast_to(loss, (8, 128))
    grad = (exps / total - goal) * share
    few_ref[...] = jnp.zeros_like(few_ref)
    few_ref[4:5, :] = grad[:, 0:EXPAND]
    few_ref[5:6, 0 : CLASSES - EXPAND] = grad[:, EXPAND:]
    grad16 = jnp.concatenate([grad, jnp.zeros((15, CLASSES), F32)], axis=0).astype(BF16)
    vec_ref[...] = jnp.zeros_like(vec_ref)
    vec_ref[2:3, 0:DIM] = normed8.astype(F32)[0:1]
    vec_ref[3:4, 0:CLASSES] = grad16.astype(F32)[0:1]
    grad = dot(grad16, head_ref[...], NT)[0:1]
    few_ref[2:3, :] = jnp.concatenate([grad * hat, grad], axis=1)
    grad = normalise_back(grad * hnorm_ref[0:1], hat, inverse) / n_valid
    low_grad = jnp.concatenate([grad, jnp.zeros((15, DIM), F32)], axis=0).astype(BF16)
    vec_ref[0:1, :] = used
    vec_ref[1:2, 0:DIM] = low_grad.astype(F32)[0:1]
    few_ref[3:4, 0:DIM] = grad * n_valid
    dhidden = dot(low_grad, back_ref[...], NT)[0:1]

    def backward(i, carry):
        dnorm0, dnorm1, dbias, dout_b = carry
        at = pl.ds(pl.multiple_of(MLP_ROWS * i, 16), MLP_ROWS)
        dnormed = jnp.zeros((MLP_ROWS, DIM), F32)
        parts = []
        for j in range(MLP // cut):
            cols = slice(cut * j, cut * j + cut)
            dpre = slopes[at, cols] * dhidden[:, cols]
            parts.append(jnp.sum(dpre, axis=0, keepdims=True))
            dpre = dpre.astype(BF16)
            dpres[at, cols] = dpre
            dnormed = dnormed + dot(dpre, in_ref[:, cols], NT)
        hat, inverse = normalise(section[at, :])
        dnorm0 = dnorm0 + jnp.sum(dnormed * hat, axis=0, keepdims=True)
        dnorm1 = dnorm1 + jnp.sum(dnormed, axis=0, keepdims=True)
        dsection = normalise_back(dnormed * norm_ref[0:1], hat, inverse) + valid_rows(i) * grad
        grads[at, :] = dsection.astype(BF16)
        dout_b = dout_b + jnp.sum(dsection, axis=0, keepdims=True)
        dblend_ref[at, :] = dot(grads[at, :], out_ref[...], NT).astype(BF16)
        dskip_ref[at, :] = dot(grads[at, :], short_ref[...], NT)
        return dnorm0, dnorm1, dbias + jnp.concatenate(parts, axis=1), dout_b

    row = jnp.zeros((1, DIM), F32)
    dnorm0, dnorm1, dbias, dout_b = lax.fori_loop(0, steps, backward, (row, row, jnp.zeros((1, MLP), F32), row))
    dnorm_ref[...] = jnp.concatenate([dnorm0, dnorm1], axis=0)
    din_b_ref[...] = dbias
    dout_b_ref[...] = dout_b
    din_ref[...] = dot(low[...], dpres[...], TN)
    dout_ref[...] = dot(blend_ref[...], grads[...], TN)
    dshort_ref[...] = dot(skip_ref[...], grads[...], TN)


def mlp_both(share, res_ids, labels, skipped, blended, p):
    s = jax.ShapeDtypeStruct
    return pl.pallas_call(
        functools.partial(mlp_kernel, share),
        out_shape=(
            s((8, 128), F32), s((TOKENS, DIM), BF16), s((TOKENS, MB_CH), F32), s((MB_CH, DIM), F32),
            s((DIM, DIM), F32), s((1, DIM), F32), s((2, DIM), F32), s((DIM, MLP), F32), s((1, MLP), F32),
            s((8, MLP), F32), s((8, EXPAND), F32),
        ),
        in_specs=[SMEM_SPEC] * 2 + [VMEM_SPEC] * 13,
        out_specs=(VMEM_SPEC,) * 11,
        scratch_shapes=[
            pltpu.VMEM((TOKENS, DIM), F32),
            pltpu.VMEM((TOKENS, DIM), BF16),
            pltpu.VMEM((TOKENS, MLP), F32),
            pltpu.VMEM((TOKENS, MLP), BF16),
            pltpu.VMEM((TOKENS, DIM), BF16),
        ],
        compiler_params=params_of(24),
        cost_estimate=cost(23),
        name="mlp_both",
    )(
        res_ids, labels, skipped, blended, p["at_short"], p["attn_out"], p["out_bias"], p["mlp_norm"], p["mlp_in"],
        p["mlp_in_bias"], p["mlp_out"], p["mlp_out_bias"], p["head_norm"], p["head_w"], p["head_bias"],
    )


def proj_back_kernel(
    res_ref, dq_ref, dk_ref, dv_ref, normed_ref, qkv_ref, dskip_ref, block_ref, pre_ref, act_ref, vec_ref,
    small_ref, proj_ref, short_ref, base_ref, down_ref, up_ref,
    dqkv_ref, dpre_ref, dblock_ref, dproj_ref, dshort_ref, dbase_ref, ddown_ref, ddown_b_ref, dup_ref, dup_b_ref,
    dpool_ref, back,
):
    limit = limit_of(res_ref)
    part = 96
    grad = dot(dq_ref[...], qkv_ref[:, 0:DIM], NT)
    grad = grad + dot(dk_ref[...], qkv_ref[:, DIM : 2 * DIM], NT)
    back[...] = grad + dot(dv_ref[...], qkv_ref[:, 2 * DIM :], NT)

    def tokens(i, carry):
        dpre0, dpre1 = carry
        at = pl.ds(pl.multiple_of(part * i, 16), part)
        grad = back[at, :]
        dskip = 0.25 * dskip_ref[at, :]
        dpre1 = dpre1 + jnp.sum(grad, axis=0, keepdims=True)
        grad = 0.25 * grad
        dhat = grad * pre_ref[0:1]
        for group in range(4):
            places = pl.ds(pl.multiple_of(group * QUAD + part * i, 16), part)
            hat, inverse = normalise(block_ref[places, :])
            dpre0 = dpre0 + jnp.sum(grad * hat, axis=0, keepdims=True)
            dblock = normalise_back(dhat, hat, inverse) + dskip
            dblock_ref[places, :] = dblock.astype(BF16)
        return dpre0, dpre1

    row = jnp.zeros((1, MB_CH), F32)
    dpre0, dpre1 = lax.fori_loop(0, TOKENS // part, tokens, (row, row))
    dpre_ref[...] = jnp.concatenate([dpre0, dpre1], axis=0)
    for k, grad_ref in enumerate((dq_ref, dk_ref, dv_ref)):
        dqkv_ref[:, DIM * k : DIM * k + DIM] = dot(normed_ref[...], grad_ref[...], TN)
    dshort_ref[...] = dot(base_ref[...], dblock_ref[...], TN)[0:STEM_CH]
    dbase_ref[...] = dot(dblock_ref[...], short_ref[...], NT)
    excite = vec_ref[1:2]
    parts = []
    for j in range(CHUNKS):
        cols = slice(BLOCK * j, BLOCK * j + BLOCK)
        act = act_ref[:, cols].astype(F32)
        scaled = (act * excite[:, cols]).astype(BF16)
        dproj_ref[cols, :] = dot(scaled, dblock_ref[...], TN)
        dscaled = dot(dblock_ref[...], proj_ref[cols, :], NT)
        parts.append(jnp.sum(dscaled * act, axis=0, keepdims=True))
    dexcite = jnp.concatenate(parts, axis=1)
    dafter = dexcite * excite * (1.0 - excite)
    dup_b_ref[...] = dafter
    dup_ref[...] = dot(row8([small_ref[0:1]]), row8([dafter]), TN, precision=HIGH)
    dsqueeze = dot(row8([dafter]), up_ref[...].astype(F32), NT, precision=HIGH)[0:1]
    dbefore = dsqueeze * small_ref[1:2]
    ddown_b_ref[...] = dbefore
    ddown_ref[...] = dot(row8([vec_ref[0:1]]), row8([dbefore]), TN, precision=HIGH)
    dpool = dot(row8([dbefore]), down_ref[...].astype(F32), NT, precision=HIGH)
    dpool_ref[...] = dpool / valid_places(limit)


def proj_backward(res_ids, dq, dk, dv, normed, dskip, block, act, vec, small, base, p):
    s = jax.ShapeDtypeStruct
    return pl.pallas_call(
        proj_back_kernel,
        out_shape=(
            s((MB_CH, 3 * DIM), F32), s((2, MB_CH), F32), s((PLACES, MB_CH), BF16), s((EXPAND, MB_CH), F32),
            s((STEM_CH, MB_CH), F32), s((PLACES, 128), F32), s((EXPAND, SQUEEZE), F32), s((1, SQUEEZE), F32),
            s((SQUEEZE, EXPAND), F32), s((1, EXPAND), F32), s((8, EXPAND), F32),
        ),
        in_specs=[SMEM_SPEC] + [VMEM_SPEC] * 16,
        out_specs=(VMEM_SPEC,) * 11,
        scratch_shapes=[pltpu.VMEM((TOKENS, MB_CH), F32)],
        compiler_params=params_of(24),
        cost_estimate=cost(13),
        name="proj_backward",
    )(
        res_ids, dq, dk, dv, normed, p["qkv"], dskip, block, p["pre_norm"], act, vec, small, p["mb_proj"],
        p["mb_short"], base, p["se_down"], p["se_up"],
    )


def excite_back_kernel(dblock_ref, proj_ref, vec_ref, dpool_ref, few_ref, slope_ref, x_ref, out_ref, sum_ref, wide):
    excite, mean, inverse = vec_ref[1:2], vec_ref[2:3], vec_ref[3:4]
    dpool = dpool_ref[0:1]
    rows = 288
    wide[...] = dot(dblock_ref[...], proj_ref[...], NT)

    def fold(v):
        total = v[0:8]
        for k in range(1, rows // 8):
            total = total + v[8 * k : 8 * k + 8]
        return total

    def step(i, sums):
        at = pl.ds(pl.multiple_of(rows * i, 16), rows)
        grad = wide[at, :] * excite + dpool
        grad = grad * slope_ref[at, :].astype(F32)
        out_ref[at, :] = grad.astype(BF16)
        hat = (x_ref[at, :] - mean) * inverse
        return sums[0] + fold(grad), sums[1] + fold(grad * hat)

    sums = lax.fori_loop(0, PLACES // rows, step, (jnp.zeros((8, BLOCK), F32),) * 2)
    sum_ref[...] = few_ref[...] + row8([jnp.sum(s, axis=0, keepdims=True) for s in sums])


def excite_backward(dblock, proj, vec, dpool, few, slope, depth):
    col = lambda rows: pl.BlockSpec((rows, BLOCK), lambda j: (0, j))
    return pl.pallas_call(
        excite_back_kernel,
        grid=(CHUNKS,),
        out_shape=(jax.ShapeDtypeStruct((PLACES, EXPAND), BF16), jax.ShapeDtypeStruct((8, EXPAND), F32)),
        in_specs=[
            pl.BlockSpec((PLACES, MB_CH), lambda j: (0, 0)),
            pl.BlockSpec((BLOCK, MB_CH), lambda j: (j, 0)),
            col(8), col(8), col(8), col(PLACES), col(PLACES),
        ],
        out_specs=(col(PLACES), col(8)),
        scratch_shapes=[pltpu.VMEM((PLACES, BLOCK), F32)],
        compiler_params=params_of(56),
        cost_estimate=cost(12),
        name="excite_backward",
    )(dblock, proj, vec, dpool, few, slope, depth)


def depth_back_kernel(
    mask_ref, du_ref, x_ref, vec_ref, sum_ref, bgram_ref, base_ref, expand_ref, dwn_ref, depth_ref, act_ref, slope_ref,
    out_ref, cross_ref, sums_ref, pad,
):
    count = bgram_ref[64:65, 64:65]
    mean1, inverse1 = bn_stats(bgram_ref[...], expand_ref[...], count)
    mean2, inverse2 = vec_ref[2:3], vec_ref[3:4]
    c1 = sum_ref[0:1] / count
    c2 = sum_ref[1:2] / count
    scale2 = dwn_ref[0:1] * inverse2
    slant = scale2 * inverse2 * c2
    level = scale2 * c1 - slant * mean2
    zero = jnp.zeros((4, 1, HALF, BLOCK), F32)
    pad[:, 0:1] = zero
    pad[:, HALF + 1 : HALF + 2] = zero
    rows = 2 * HALF

    def fill(i, _):
        for group in range(4):
            at = pl.ds(pl.multiple_of(group * QUAD + rows * i, 16), rows)
            grad = scale2 * du_ref[at, :].astype(F32) - mask_ref[at, :] * (level + x_ref[at, :] * slant)
            for k in range(2):
                pad[group, 2 * i + k + 1] = grad[HALF * k : HALF * k + HALF]
        return 0

    lax.fori_loop(0, HALF // 2, fill, 0)

    def weight(dy, dx):
        return depth_ref[8 - 3 * dy - dx : 9 - 3 * dy - dx]

    def fold(v):
        return v[0:8] + v[8:16] + v[16:24]

    def step(k, sums):
        sums = list(sums)
        for py in range(2):
            places = [
                pl.ds(pl.multiple_of((2 * py + px) * QUAD + 2 * HALF * k, 16), 2 * HALF) for px in range(2)
            ]
            low_both, high_both = (act_ref[at, :].astype(F32) for at in places)
            made = [[], []]
            for half in range(2):
                up = 2 * k + half
                cut = slice(HALF * half, HALF * half + HALF)
                sources = [(1, -1), (0, 0), (1, 0)] if py == 0 else [(0, 0), (1, 0), (0, 1)]
                low_act, high_act = low_both[cut], high_both[cut]
                even = odd = None
                for t, (gy, off) in enumerate(sources):
                    left, right = pad[2 * gy, up + 1 + off], pad[2 * gy + 1, up + 1 + off]
                    before, after = shift_down(right), shift_up(left)
                    a = before * weight(t, 0) + left * weight(t, 1) + right * weight(t, 2)
                    b = left * weight(t, 0) + right * weight(t, 1) + after * weight(t, 2)
                    even = a if even is None else even + a
                    odd = b if odd is None else odd + b
                    for s, (a, b) in enumerate(((before, left), (left, right), (right, after))):
                        tap = 3 * (2 - t) + 2 - s
                        sums[tap] = sums[tap] + fold(low_act * a + high_act * b)
                made[0].append(even)
                made[1].append(odd)
            for px in range(2):
                grad = jnp.concatenate(made[px], axis=0) * slope_ref[places[px], :].astype(F32)
                out_ref[places[px], :] = grad.astype(BF16)
        return tuple(sums)

    sums = lax.fori_loop(0, HALF // 2, step, (jnp.zeros((8, BLOCK), F32),) * 9)
    cross_ref[72:88, :] = jnp.concatenate(
        [jnp.sum(s, axis=0, keepdims=True) for s in sums] + [jnp.zeros((7, BLOCK), F32)], axis=0
    )
    cross = dot(base_ref[...], out_ref[...], TN)
    cross_ref[0:72, :] = cross[0:72]
    first = cross[64:65]
    second = (jnp.sum(cross[0:64] * expand_ref[0:64, :].astype(F32), axis=0, keepdims=True) - mean1 * first) * inverse1
    sums_ref[...] = row8([second, first])


def depth_backward(mask, du, depth, vec, sums, bgram, base, expand_w, dw_norm, mb_depth, act, slope):
    col = lambda rows: pl.BlockSpec((rows, BLOCK), lambda j: (0, j))
    whole = lambda rows: pl.BlockSpec((rows, BLOCK), lambda j: (0, 0))
    s = jax.ShapeDtypeStruct
    return pl.pallas_call(
        depth_back_kernel,
        grid=(CHUNKS,),
        out_shape=(s((PLACES, EXPAND), BF16), s((88, EXPAND), F32), s((8, EXPAND), F32)),
        in_specs=[
            whole(PLACES), col(PLACES), col(PLACES), col(8), col(8), whole(72), whole(PLACES), col(128), col(2),
            col(9), col(PLACES), col(PLACES),
        ],
        out_specs=(col(PLACES), col(88), col(8)),
        scratch_shapes=[pltpu.VMEM((4, HALF + 2, HALF, BLOCK), F32)],
        compiler_params=params_of(56),
        cost_estimate=cost(35),
        name="depth_backward",
    )(mask, du, depth, vec, sums, bgram, base, expand_w, dw_norm, mb_depth, act, slope)


def stem_back_kernel(
    mask_ref, patch_ref, slope_ref, dbase_ref, du_ref, sum_ref, bgram_ref, base_ref, expand_ref, mid_ref, spread_ref,
    out_ref, total, rows_ref, hold,
):
    step = pl.program_id(0)

    @pl.when(step == 0)
    def _():
        count = bgram_ref[64:65, 64:65]
        mean, inverse = bn_stats(bgram_ref[...], expand_ref[...], count)
        second, first = sum_ref[0:1] / count, sum_ref[1:2] / count
        scale = mid_ref[0:1] * inverse
        slant = scale * inverse * second
        rows_ref[...] = row8([scale, slant, scale * first - slant * mean])
        total[...] = jnp.zeros_like(total)

    scale, slant, level = (rows_ref[k : k + 1] for k in range(3))
    x = dot(base_ref[...], expand_ref[...])
    inside = jnp.concatenate([mask_ref[...]] * CHUNKS, axis=1)
    grad = (scale * du_ref[...].astype(F32) - inside * (level + x * slant)).astype(BF16)
    grad = dot(grad, expand_ref[...], NT) + dbase_ref[...]
    grad = grad[:, 0:64] * (1.0 / 16.0)
    grad = jnp.concatenate([grad, grad], axis=1)
    grad = jnp.concatenate([grad, grad], axis=1)
    block = patch_ref[...]
    for j in range(4):
        cols = slice(256 * j, 256 * j + 256)
        wide = (slope_ref[:, cols].astype(F32) * grad).astype(BF16)
        total[:, cols] = total[:, cols] + dot(block, wide, TN)

    @pl.when(step == STEM_STEPS - 1)
    def _():
        merged = total[0:96, 0:256]
        for px in range(1, 4):
            merged = merged + total[64 * px : 64 * px + 96, 256 * px : 256 * px + 256]
        result = jnp.zeros((32, STEM_CH), F32)
        for pair in range(2):
            wide = dot(
                spread_ref[pair][0:96].astype(F32), merged[:, 128 * pair : 128 * pair + 128], TN, precision=HIGH
            )
            result = result + wide[0:32, 0:64] + wide[32:64, 64:128]
        ones = merged[27:28]
        ones = ones[:, 0:64] + ones[:, 64:128] + ones[:, 128:192] + ones[:, 192:256]
        at = lax.broadcasted_iota(jnp.int32, (32, STEM_CH), 0)
        out_ref[...] = pairs_together(jnp.where(at == 27, ones, result), hold)


def stem_backward(mask, patches, slope, dbase, du, sums, bgram, base, expand_w, mid_norm, spread):
    part = lambda width: pl.BlockSpec((STEM_BLOCK, width), lambda i: (i, 0))
    whole = lambda *shape: pl.BlockSpec(shape, lambda i: (0,) * len(shape))
    return pl.pallas_call(
        stem_back_kernel,
        grid=(STEM_STEPS,),
        out_shape=jax.ShapeDtypeStruct((16, 128), F32),
        in_specs=[
            part(128), part(TAPS), part(1024), part(128), part(EXPAND), whole(8, EXPAND), whole(72, 128), part(128),
            whole(128, EXPAND), whole(2, EXPAND), whole(8, TAPS, 64),
        ],
        out_specs=whole(16, 128),
        scratch_shapes=[
            pltpu.VMEM((TAPS, 1024), F32), pltpu.VMEM((8, EXPAND), F32), pltpu.VMEM((40, 128), F32),
        ],
        compiler_params=params_of(60),
        cost_estimate=cost(8),
        name="stem_backward",
    )(mask, patches, slope, dbase, du, sums, bgram, base, expand_w, mid_norm, spread)


def expand_finish_kernel(cross_ref, sum_ref, bgram_ref, expand_ref, mid_ref, out_ref, square_ref, flat, hold):
    count = bgram_ref[64:65, 64:65]
    square_of = jnp.concatenate([bgram_ref[...], jnp.zeros((56, 128), F32)], axis=0)
    weights = expand_ref[...].astype(F32)
    product = dot(square_of, weights, precision=HIGH)
    mean = product[64:65] / count
    variance = jnp.sum(weights * product, axis=0, keepdims=True) / count - mean * mean
    inverse = lax.rsqrt(variance + EPS)
    second, first = sum_ref[0:1] / count, sum_ref[1:2] / count
    plain = bgram_ref[0:64, 64:65]
    hat = (product[0:64] - mean * plain) * inverse
    hold[...] = mid_ref[0:1] * inverse * (cross_ref[0:64, :] - first * plain - second * hat)
    flat[...] = jnp.zeros_like(flat)
    for name, source in (("mb_expand", hold), ("mb_depth", cross_ref.at[72:88])):
        offset, (rows, width) = OFFSETS[name]
        put_matrix(flat, lambda r, t: source[r, 128 * t : 128 * t + 128], 0, offset, rows, width)
    out_ref[...] = flat[0:EARLY_ROWS, :]
    total = flat[0:EARLY_ROWS, :]
    square_ref[...] = jnp.broadcast_to(jnp.sum(total * total).reshape(1, 1), (8, 128))


def expand_finish(cross, sums, bgram, expand_w, mid_norm):
    return pl.pallas_call(
        expand_finish_kernel,
        out_shape=(jax.ShapeDtypeStruct((EARLY_ROWS, 128), F32), jax.ShapeDtypeStruct((8, 128), F32)),
        in_specs=[VMEM_SPEC] * 5,
        out_specs=(VMEM_SPEC,) * 2,
        scratch_shapes=[pltpu.VMEM((EARLY_ROWS + 8, 128), F32), pltpu.VMEM((STEM_CH, EXPAND), F32)],
        compiler_params=params_of(10),
        cost_estimate=cost(3),
        name="expand_finish",
    )(cross, sums, bgram, expand_w, mid_norm)


def finish_kernel(
    first_ref, packet_ref, stem_ref, spread_ref, early_ref, early_square_ref, shard_ref,
    out_ref, scalar_ref, big, hold, flat,
):
    weights, own_gain, _ = stem_params(stem_ref, hold)
    spread_weights(spread_ref, weights, big, 2)
    gram = stem_ref[0:96, 0:96]
    mean, square = stem_stats(stem_ref[0:96, :], big[0:96, 0:256])
    inverse = lax.rsqrt(square - mean * mean + EPS)
    count = 4.0 * stem_ref[27:28, 27:28]
    got = pairs_apart(packet_ref[0:16], hold)
    product = dot(gram, big[0:96, 0:256].astype(F32), precision=HIGH)
    cross = jnp.zeros((32, STEM_CH), F32)
    plain = jnp.zeros((32, STEM_CH), F32)
    sums = jnp.broadcast_to(gram[:, 27:28], (96, 128))
    for pair in range(2):
        spread = spread_ref[pair][0:96].astype(F32)
        wide = dot(spread, product[:, 128 * pair : 128 * pair + 128], TN, precision=HIGH)
        cross = cross + wide[0:32, 0:64] + wide[32:64, 64:128]
        wide = dot(spread, sums, TN, precision=HIGH)
        plain = plain + wide[0:32, 0:64] + wide[32:64, 0:64]
    at = lax.broadcasted_iota(jnp.int32, (32, STEM_CH), 0)
    taps = at < 27
    grad = jnp.where(taps, got, 0.0)
    first = got[27:28]
    second = (jnp.sum(grad * weights, axis=0, keepdims=True) - mean * first) * inverse
    hat = (cross - mean * plain) * inverse
    result = own_gain * inverse * (grad - (plain * first + hat * second) / count)
    result = jnp.where(taps, result, jnp.where(at == 27, second, jnp.where(at == 28, first, 0.0)))
    square = packet_ref[16:17, 1:2] + early_square_ref[0:1, 0:1] + jnp.sum(result * result).reshape(1, 1)
    norm = jnp.sqrt(square)
    lane = lax.broadcasted_iota(jnp.int32, (8, 128), 1)
    scale = CLIP / jnp.maximum(norm, CLIP)
    scalar_ref[...] = jnp.where(lane == 0, packet_ref[16:17, 0:1], jnp.where(lane == 1, norm, scale))
    both = pairs_together(result, hold)
    rows = shard_ref.shape[0]
    flat[0:16, :] = early_ref[0:16] + both
    flat[16:EARLY_ROWS, :] = early_ref[16:EARLY_ROWS]
    flat[EARLY_ROWS:, :] = jnp.zeros((flat.shape[0] - EARLY_ROWS, 128), F32)
    begin = jnp.minimum(first_ref[0] * rows, EARLY_ROWS)
    out_ref[...] = shard_ref[...] + flat[pl.ds(begin, rows), :]


def finish(me, packet, stem, spread, early, early_square, shard):
    rows = shard.shape[0]
    return pl.pallas_call(
        finish_kernel,
        out_shape=(jax.ShapeDtypeStruct((rows, 128), F32), jax.ShapeDtypeStruct((8, 128), F32)),
        in_specs=[SMEM_SPEC] + [VMEM_SPEC] * 6,
        out_specs=(VMEM_SPEC,) * 2,
        scratch_shapes=[
            pltpu.VMEM((TAPS, 256), BF16), pltpu.VMEM((40, 128), F32),
            pltpu.VMEM((round_up(EARLY_ROWS + rows, 8), 128), F32),
        ],
        compiler_params=params_of(10),
        cost_estimate=cost(4),
        name="finish",
    )(me, packet, stem, spread, early, early_square, shard)


def levels_of(devices):
    levels = []
    stride = 1
    while stride < devices:
        radix = 2 if stride == 1 or devices // stride == 2 else 4
        levels.append((stride, radix))
        stride *= radix
    return levels


def pairs_of(devices, mask):
    return [(i, i ^ mask) for i in range(devices)]


def add_level(v, moved):
    return v + moved[0] if len(moved) == 1 else (v + moved[0]) + (moved[1] + moved[2])


def send_level(v, devices, level):
    stride, radix = level
    return [lax.ppermute(v, "dp", pairs_of(devices, stride * j)) for j in range(1, radix)]


def exchange(v, devices, levels):
    for level in levels:
        v = add_level(v, send_level(v, devices, level))
    return v


def spread_blocks(blocks, masks, devices, level):
    stride, radix = level
    moved = send_level(blocks, devices, level)
    return jnp.concatenate([blocks] + moved), [m ^ (stride * j) for j in range(radix) for m in masks]


def take(blocks, digit, axis):
    return lax.dynamic_index_in_dim(blocks, digit, axis, keepdims=False)


class Scatter:
    def __init__(self, keep, send, devices, me, low, high):
        self.devices, self.me, self.low, self.high = devices, me, low, high
        self.levels = levels_of(devices)
        self.at = 0
        self.mine, self.parts = [keep], [send]
        self.moved = []

    def launch(self):
        stride, radix = self.levels[self.at]
        top = stride * radix == self.devices
        self.moved = []
        for j, part in zip(range(1, radix), self.parts):
            pairs = pairs_of(self.devices, stride * j)
            if top:
                pairs = [(a, b) for a, b in pairs if self.low <= b // stride < self.high]
            self.moved.append(lax.ppermute(part, "dp", pairs))

    def land(self):
        terms = self.mine + [m.astype(F32) for m in self.moved]
        self.at += 1
        if self.at == len(self.levels):
            total = sum(terms[1:], terms[0])
            self.result = total.reshape(total.shape[-2:])
            return
        if len(terms) > 2:
            terms = [sum(terms[1:], terms[0])]
        stride, radix = self.levels[self.at]
        digit = (self.me // stride) % radix
        span = self.high - self.low
        if stride * radix == self.devices:
            blocks = [t.reshape((span,) + t.shape[-2:]) for t in terms]
            part = lambda d: sum(take(b, jnp.clip(d - self.low, 0, span - 1), 0) for b in blocks)
            mine = jnp.where((digit >= self.low) & (digit < self.high), part(digit), 0.0)
        else:
            blocks = [t.reshape((-1, radix) + t.shape[-2:]) for t in terms]
            part = lambda d: sum(take(b, d, 1) for b in blocks)
            mine = part(digit)
        self.mine = [mine]
        self.parts = [part(digit ^ j).astype(BF16) for j in range(1, radix)]

    def finish(self):
        if not self.moved:
            self.launch()
        self.land()
        while self.at < len(self.levels):
            self.launch()
            self.land()
        return self.result


def tie(*values):
    return lax.optimization_barrier(values)


def on_device(images, res_ids, labels, rel_index, master, first_moment, second_moment, ema_weights):
    devices = lax.axis_size("dp")
    me = lax.axis_index("dp").astype(jnp.int32)
    length = master.shape[0]
    rows = length // 128
    held = round_up(rows, 16)
    images_total = res_ids.shape[0] * devices

    levels = levels_of(devices)
    low_master = lax.optimization_barrier(master.astype(BF16).reshape(rows, 128))
    blocks, masks = spread_blocks(jnp.pad(low_master, ((0, held - rows), (0, 0)))[None], [0], devices, levels[-1])
    stem_part = lax.dynamic_update_slice(
        jnp.zeros((16 + rows, 128), BF16), low_master, (jnp.minimum(me * rows, 16), 0)
    )[:16]
    patches, packet, mask = make_patches(res_ids, images, stem_part)
    packet, blocks = tie(packet, blocks)
    packet = exchange(packet, devices, levels[:-1])
    packet, blocks = tie(packet, blocks)
    for level in levels[-2:0:-1]:
        blocks, masks = spread_blocks(blocks, masks, devices, level)
    packet = exchange(packet, devices, levels[-1:])
    spread = jnp.asarray(spread_taps(), BF16)
    base, stem_slope, bgram = stem_forward(patches, packet, spread)
    stem_packet = packet
    bgram, blocks = tie(bgram, blocks)
    others = lax.ppermute(blocks, "dp", pairs_of(devices, 1))
    bgram = exchange(bgram, devices, levels[:-1])
    bgram, others = tie(bgram, others)
    sent = send_level(bgram, devices, levels[-1])
    p = unpack([blocks, others], me.reshape(1), masks + [m ^ 1 for m in masks], rows, ALL_SHAPES)
    bgram = add_level(bgram, sent)
    depth, act1, slope1, stat = depth_forward(mask, base, p["mb_expand"], bgram, p["mid_norm"], p["mb_depth"])
    stat = exchange(stat, devices, levels)
    slots = slots_of(rel_index)
    slots = jnp.pad(slots, ((0, 1), (0, 1)), constant_values=2 * WIDE - 1).reshape(2 * WIDE, 1)
    pick = squeeze_lanes()
    pick, pick_back = jnp.asarray(pick, BF16), jnp.asarray(pick.T, BF16)
    bias = build_bias(p["rel_table"], slots, pick)

    act2, slope2, block, skipped, normed, project, vec, small = excite_forward(res_ids, mask, depth, stat, bgram, base, p)
    blended, weights = attend_forward(res_ids, project, bias)
    loss, dblend, dskip, g_short, g_out, g_out_b, g_mnorm, g_in, g_in_b, vectors, few = mlp_both(
        1.0 / images_total, res_ids, labels, skipped, blended, p
    )

    core = (me % 2).reshape(1)
    top_radix = levels_of(devices)[-1][1]

    def scattered(grads, begin, end):
        span = devices // top_radix
        low = begin // length // span
        high = (end - 1) // length // span + 1
        keep, send = pack(core, grads, low * span * rows, (high - low) * span, rows, held)
        return Scatter(keep, send, devices, me, low, high)

    middle = scattered(
        {
            "attn_out": g_out, "out_bias": g_out_b, "mlp_norm": g_mnorm, "mlp_in": g_in, "mlp_in_bias": g_in_b,
        },
        OFFSETS["attn_out"][0], OFFSETS["mlp_out"][0],
    )
    dblend, middle.parts = tie(dblend, middle.parts)
    middle.launch()
    vectors = lax.all_gather(vectors, "dp", axis=0, tiled=False)

    dq, dk, dv, g_table = attend_backward(project, blended, dblend, weights, slots, pick_back)
    dq, middle.moved = tie(dq, middle.moved)
    middle.land()
    dq, middle.parts = tie(dq, middle.parts)
    middle.launch()
    g_qkv, g_pre, dblock, g_proj, g_mbshort, dbase, g_down, g_down_b, g_up, g_up_b, dpool = proj_backward(
        res_ids, dq, dk, dv, normed, dskip, block, act2, vec, small, base, p
    )
    late = scattered(
        {
            "mb_short": g_mbshort, "se_down": g_down, "se_down_bias": g_down_b, "se_up": g_up, "se_up_bias": g_up_b,
            "mb_proj": g_proj, "at_short": g_short, "pre_norm": g_pre, "qkv": g_qkv, "rel_table": g_table,
        },
        OFFSETS["mb_short"][0], OFFSETS["mlp_norm"][0],
    )
    dblock, late.parts, middle.moved = tie(dblock, late.parts, middle.moved)
    late.launch()
    middle.land()
    dblock, middle.parts = tie(dblock, middle.parts)
    middle.launch()
    du, sums = excite_backward(dblock, p["mb_proj"], vec, dpool, few, slope2, depth)
    sums, late.moved, middle.moved = tie(sums, late.moved, middle.moved)
    late.land()
    sums, late.parts = tie(sums, late.parts)
    late.launch()
    dw_sums = exchange(sums, devices, levels)
    dw_sums, late.moved = tie(dw_sums, late.moved)
    late.land()
    dw_sums, late.parts = tie(dw_sums, late.parts)
    late.launch()
    du, cross, sums = depth_backward(
        mask, du, depth, vec, dw_sums, bgram, base, p["mb_expand"], p["dw_norm"], p["mb_depth"], act1, slope1
    )
    sums, late.moved = tie(sums, late.moved)
    steps = [(1 << k, 2) for k in range(devices.bit_length() - 1)]
    sent = send_level(cross, devices, steps[0])
    mid_sums = exchange(sums, devices, levels[:-1])
    mid_sums, sent = tie(mid_sums, sent)
    cross = add_level(cross, sent)
    moved = send_level(mid_sums, devices, levels[-1])
    sent = send_level(cross, devices, steps[1])
    mid_sums, sent = tie(add_level(mid_sums, moved), sent)
    cross = add_level(cross, sent)
    mid_sums, cross = tie(mid_sums, cross)
    sent = send_level(cross, devices, steps[2])
    stem = stem_backward(
        mask, patches, stem_slope, dbase, du, mid_sums, bgram, base, p["mb_expand"], p["mid_norm"], spread
    )
    stem, sent, late.moved = tie(stem, sent, late.moved)
    cross = add_level(cross, sent)
    stem, cross = tie(stem, cross)
    sent = send_level(cross, devices, steps[3])
    shard, packet = shard_parts(
        me.reshape(1), length, late.finish(), middle.finish(), dw_sums, mid_sums, vectors, stem, loss
    )
    packet, sent = tie(packet, sent)
    cross = add_level(cross, sent)
    cross, packet = tie(cross, packet)
    cross = exchange(cross, devices, steps[4:])
    packet = exchange(packet, devices, levels)
    early_grad, early_square = expand_finish(cross, mid_sums, bgram, p["mb_expand"], p["mid_norm"])
    shard, scalars = finish(
        me.reshape(1), packet, stem_packet, spread, early_grad, early_square, shard
    )
    loss_sum, grad_norm = scalars[0, 0], scalars[0, 1]
    shard = shard.reshape(length)
    clipped = shard * scalars[0, 2]
    moment_one = BETA_ONE * first_moment + (1.0 - BETA_ONE) * clipped
    moment_two = BETA_TWO * second_moment + (1.0 - BETA_TWO) * clipped * clipped
    update = (
        moment_one
        / (1.0 - BETA_ONE**STEP)
        / (jnp.sqrt(moment_two / (1.0 - BETA_TWO**STEP)) + ADAM_EPS)
    )
    weights_out = master - RATE * (update + DECAY * master)
    averaged = EMA_DECAY * ema_weights + (1.0 - EMA_DECAY) * weights_out
    return (
        loss_sum,
        grad_norm,
        weights_out,
        moment_one,
        moment_two,
        averaged,
        weights_out.astype(BF16),
    )


def solution(mesh):
    in_specs = (
        P("dp", None, None, None),
        P("dp"),
        P("dp"),
        P(),
        P("dp"),
        P("dp"),
        P("dp"),
        P("dp"),
    )
    out_specs = (P(), P(), P("dp"), P("dp"), P("dp"), P("dp"), P("dp"))
    return jax.shard_map(
        on_device, mesh=mesh, in_specs=in_specs, out_specs=out_specs, check_vma=False
    )
```

```python
import functools
import math

import jax
import jax.numpy as jnp
import numpy as np
from jax import lax
from jax.experimental import pallas as pl
from jax.experimental.pallas import tpu as pltpu
from jax.sharding import PartitionSpec as P

STEM_CH = 64
MB_CH = 192
EXPAND = 768
SQUEEZE = 48
DIM = 384
HEADS = 12
HEAD_DIM = 32
MLP = 1536
CLASSES = 1000
CANVAS = 384
SMALL_RES = 224
STEP = 10

EPS = 1e-05
CLIP = 0.05
BETA_ONE = 0.5
BETA_TWO = 0.5
ADAM_EPS = 1e-08
RATE = 0.05
DECAY = 0.05
EMA_DECAY = 0.9
SMOOTH = 0.1

SIDE = CANVAS // 8
SMALL_SIDE = SMALL_RES // 8
HALF = SIDE // 2
QUAD = HALF * HALF
PLACES = SIDE * SIDE
TAPS = 288
BLOCK = 128
CHUNKS = EXPAND // BLOCK
WIDE = 2 * HALF * HALF
TOKENS = QUAD

F32 = jnp.float32
BF16 = jnp.bfloat16
HIGH = lax.Precision.HIGHEST
GELU_A = math.sqrt(2.0 / math.pi)
GELU_B = 0.044715


def layout():
    table_slots = (2 * (CANVAS // 16) - 1) ** 2
    return [
        ("stem_w", (3, 3, 3, STEM_CH)),
        ("stem_norm", (2, STEM_CH)),
        ("mb_short", (STEM_CH, MB_CH)),
        ("mb_expand", (STEM_CH, EXPAND)),
        ("mid_norm", (2, EXPAND)),
        ("mb_depth", (9, EXPAND)),
        ("dw_norm", (2, EXPAND)),
        ("se_down", (EXPAND, SQUEEZE)),
        ("se_down_bias", (SQUEEZE,)),
        ("se_up", (SQUEEZE, EXPAND)),
        ("se_up_bias", (EXPAND,)),
        ("mb_proj", (EXPAND, MB_CH)),
        ("at_short", (MB_CH, DIM)),
        ("pre_norm", (2, MB_CH)),
        ("qkv", (MB_CH, 3 * DIM)),
        ("attn_out", (DIM, DIM)),
        ("out_bias", (DIM,)),
        ("rel_table", (HEADS, table_slots)),
        ("mlp_norm", (2, DIM)),
        ("mlp_in", (DIM, MLP)),
        ("mlp_in_bias", (MLP,)),
        ("mlp_out", (MLP, DIM)),
        ("mlp_out_bias", (DIM,)),
        ("head_norm", (2, DIM)),
        ("head_w", (DIM, CLASSES)),
        ("head_bias", (CLASSES,)),
    ]


def offsets():
    table = {}
    offset = 0
    for name, shape in layout():
        table[name] = (offset, shape)
        offset += math.prod(shape)
    return table


OFFSETS = offsets()
STEM_END = OFFSETS["mb_short"][0]
EARLY_END = OFFSETS["se_down"][0]


def dot(a, b, dims=((1,), (0,)), precision=None):
    return lax.dot_general(a, b, (dims, ((), ())), precision=precision, preferred_element_type=F32)


NT = ((1,), (1,))
TN = ((0,), (0,))


def gelu_pair(u):
    sq = u * u
    t = jnp.tanh(u * (GELU_A + (GELU_A * GELU_B) * sq))
    half = 0.5 + 0.5 * t
    slope = half + (0.5 * u) * (1.0 - t * t) * (GELU_A + (3.0 * GELU_A * GELU_B) * sq)
    return u * half, slope


def gelu(u):
    sq = u * u
    t = jnp.tanh(u * (GELU_A + (GELU_A * GELU_B) * sq))
    return u * (0.5 + 0.5 * t)


def limit_of(res_ref):
    return jnp.where(res_ref[0] == 1, SIDE, SMALL_SIDE)


def group_mask(group, limit, first_row, rows, lanes):
    place = lax.broadcasted_iota(jnp.int32, (rows, lanes), 0) + first_row
    up = place // HALF
    across = place - up * HALF
    y = 2 * up + group // 2
    x = 2 * across + group % 2
    return jnp.where((y < limit) & (x < limit), 1.0, 0.0)


def cost(us):
    return pl.CostEstimate(flops=int(us * 2.0e9), bytes_accessed=1000, transcendentals=0)


def params_of(megabytes):
    return pltpu.CompilerParams(vmem_limit_bytes=megabytes * 1024 * 1024)


SMEM_SPEC = pl.BlockSpec(memory_space=pltpu.SMEM)
VMEM_SPEC = pl.BlockSpec(memory_space=pltpu.VMEM)


def patch_kernel(res_ref, img_ref, stem_ref, patch_ref, packet_ref, mask_ref):
    limit = limit_of(res_ref)
    lane = lax.broadcasted_iota(jnp.int32, (32, CANVAS), 1)
    rem = lane % 8
    row = lax.broadcasted_iota(jnp.int32, (SIDE, CANVAS), 0)
    col = lax.broadcasted_iota(jnp.int32, (SIDE, CANVAS), 1)
    wanted = jnp.where(row < HALF, 2 * row, 2 * (row - HALF) + 1)
    pick = jnp.where(col // 8 == wanted, 1.0, 0.0).astype(BF16)
    sub = lax.broadcasted_iota(jnp.int32, (8, CANVAS), 0)
    tap = lax.broadcasted_iota(jnp.int32, (2 * HALF, TAPS), 1)
    ones_at = (tap % 64 == 27) & (tap < 256)

    def step(i, _):
        bands = [[], [], [], []]
        above = []
        for c in range(3):
            before = img_ref[0, c, pl.ds(pl.multiple_of(jnp.maximum(32 * i - 16, 0), 16), 16), :]
            above.append(jnp.where(i > 0, before.astype(F32)[8:16], 0.0))
            for q in range(2):
                band = img_ref[0, c, pl.ds(pl.multiple_of(32 * i + 16 * q, 16), 16), :].astype(F32)
                bands[2 * q].append(band[0:8])
                bands[2 * q + 1].append(band[8:16])
        made = []
        for q in range(4):
            prev = above if q == 0 else bands[q - 1]
            edge = jnp.zeros((8, CANVAS), F32)
            for c in range(3):
                edge = jnp.where(sub == c, prev[c][7:8], edge)
            rows = jnp.concatenate(bands[q] + [edge], axis=0)
            rolled = pltpu.roll(rows, 8, 1)
            pieces = [jnp.where((rem == 7) & (lane >= 8), rolled, 0.0)]
            pieces += [jnp.where(rem == r, rows, 0.0) for r in range(8)]
            wide = jnp.concatenate(pieces, axis=0).astype(BF16)
            made.append(dot(pick, wide, NT))
        for py in range(2):
            for px in range(2):
                group = 2 * py + px
                two = jnp.concatenate(
                    [made[py][HALF * px : HALF * px + HALF], made[2 + py][HALF * px : HALF * px + HALF]],
                    axis=0,
                )
                inside = group_mask(group, limit, 2 * HALF * i, 2 * HALF, 128)
                mask_ref[pl.ds(pl.multiple_of(group * QUAD + 2 * HALF * i, 16), 2 * HALF), :] = inside
                two = jnp.where(ones_at, 1.0, two) * inside[:, 0:1]
                patch_ref[pl.ds(pl.multiple_of(group * QUAD + 2 * HALF * i, 16), 2 * HALF), :] = (
                    two.astype(BF16)
                )
        return 0

    lax.fori_loop(0, HALF // 2, step, 0, unroll=3)
    patches = patch_ref[...]
    gram = dot(patches, patches, TN)
    total = gram[0:96, 0:96]
    for px in range(1, 4):
        total = total + gram[64 * px : 64 * px + 96, 64 * px : 64 * px + 96]
    packet_ref[0:96, :] = jnp.concatenate([total, jnp.zeros((96, 32), F32)], axis=1)
    packet_ref[96:112, :] = stem_ref[...].astype(F32)


def make_patches(res_ids, images, stem):
    return pl.pallas_call(
        patch_kernel,
        out_shape=(
            jax.ShapeDtypeStruct((PLACES, TAPS), BF16),
            jax.ShapeDtypeStruct((112, 128), F32),
            jax.ShapeDtypeStruct((PLACES, 128), F32),
        ),
        in_specs=[SMEM_SPEC, VMEM_SPEC, VMEM_SPEC],
        out_specs=(VMEM_SPEC,) * 3,
        compiler_params=params_of(16),
        cost_estimate=cost(8),
        name="patches",
    )(res_ids, images, stem)


def spread_taps():
    table = np.zeros((8, TAPS, 64), np.float32)
    for px in range(4):
        for py in range(4):
            pair, half = px * 2 + py // 2, py % 2
            for dy in range(3):
                for dx in range(3):
                    for c in range(3):
                        ry = 2 * py + dy - 1
                        r = 24 + c if ry < 0 else 8 * c + ry
                        k = (2 * px + dx) * 32 + r
                        table[pair, k, half * 32 + (dy * 3 + dx) * 3 + c] = 1.0
    return table


def spread_weights(spread_ref, stem_w, out_ref, pairs=8):
    zero = jnp.zeros((32, STEM_CH), F32)
    double = jnp.concatenate(
        [jnp.concatenate([stem_w, zero], axis=1), jnp.concatenate([zero, stem_w], axis=1)], axis=0
    ).astype(BF16)
    for pair in range(pairs):
        out_ref[:, 128 * pair : 128 * pair + 128] = dot(spread_ref[pair], double).astype(BF16)


def stem_stats(gram, first_phases):
    weights = first_phases.astype(F32)
    product = dot(gram[:, :96], weights, precision=HIGH)
    second = jnp.sum(weights * product, axis=0, keepdims=True)
    first = product[27:28]
    count = 4.0 * gram[27:28, 27:28]
    both = jnp.concatenate([first, second, jnp.zeros((6, 256), F32)], axis=0)
    folded = both[:, 0:64] + both[:, 64:128] + both[:, 128:192] + both[:, 192:256]
    return folded[0:1] / count, folded[1:2] / count


def pairs_apart(rows, hold):
    hold[pl.ds(0, 16, stride=2), :] = rows
    hold[pl.ds(1, 16, stride=2), :] = pltpu.roll(rows, 64, 1)
    return hold[0:32, 0:64]


def pairs_together(rows, hold):
    hold[0:32, 0:64] = rows
    lane = lax.broadcasted_iota(jnp.int32, (16, 128), 1)
    return jnp.where(
        lane < 64, hold[pl.ds(0, 16, stride=2), :], pltpu.roll(hold[pl.ds(1, 16, stride=2), :], 64, 1)
    )


def stem_params(packet_ref, hold):
    rows = pairs_apart(packet_ref[96:112, :], hold)
    at = lax.broadcasted_iota(jnp.int32, (32, STEM_CH), 0)
    return jnp.where(at < 27, rows, 0.0), rows[27:28], rows[28:29]


STEM_STEPS = 3
STEM_BLOCK = PLACES // STEM_STEPS


def stem_kernel(patch_ref, packet_ref, spread_ref, base_ref, slope_ref, bgram_ref, big, hold, norm):
    @pl.when(pl.program_id(0) == 0)
    def _():
        weights, gain, shift = stem_params(packet_ref, hold)
        spread_weights(spread_ref, weights, big)
        mean, square = stem_stats(packet_ref[0:96, :], big[0:96, 0:256])
        gain = gain * lax.rsqrt(square - mean * mean + EPS)
        shift = shift - mean * gain
        norm[0:1, :] = jnp.concatenate([gain] * 4, axis=1)
        norm[1:2, :] = jnp.concatenate([shift] * 4, axis=1)
        bgram_ref[...] = jnp.zeros_like(bgram_ref)

    gain, shift = norm[0:1, :], norm[1:2, :]
    lane = lax.broadcasted_iota(jnp.int32, (STEM_BLOCK, 128), 1)
    block = patch_ref[...]
    pooled = jnp.zeros((STEM_BLOCK, 128), F32)
    for j in range(4):
        u = dot(block, big[:, 256 * j : 256 * j + 256]) * gain + shift
        value, slope = gelu_pair(u)
        slope_ref[:, 256 * j : 256 * j + 256] = slope.astype(BF16)
        pooled = pooled + value[:, 0:128] + value[:, 128:256]
    pooled = (pooled + pltpu.roll(pooled, 64, 1)) * (1.0 / 16.0)
    ones = block[:, 0:128].astype(F32)
    ones = pltpu.roll(ones, 64 - 27, 1)
    pooled = jnp.where(lane < 64, pooled, jnp.where(lane == 64, ones, 0.0)).astype(BF16)
    base_ref[...] = pooled
    masked = (pooled.astype(F32) * pooled[:, 64:65].astype(F32)).astype(BF16)
    bgram_ref[...] = bgram_ref[...] + dot(masked, pooled, TN)[0:72]


def stem_forward(patches, packet, spread):
    part = lambda width: pl.BlockSpec((STEM_BLOCK, width), lambda i: (i, 0))
    whole = lambda shape: pl.BlockSpec(shape, lambda i: (0,) * len(shape))
    return pl.pallas_call(
        stem_kernel,
        grid=(STEM_STEPS,),
        out_shape=(
            jax.ShapeDtypeStruct((PLACES, 128), BF16),
            jax.ShapeDtypeStruct((PLACES, 1024), BF16),
            jax.ShapeDtypeStruct((72, 128), F32),
        ),
        in_specs=[part(TAPS), whole((112, 128)), whole((8, TAPS, 64))],
        out_specs=(part(128), part(1024), whole((72, 128))),
        scratch_shapes=[
            pltpu.VMEM((TAPS, 1024), BF16), pltpu.VMEM((40, 128), F32), pltpu.VMEM((8, 256), F32),
        ],
        compiler_params=params_of(28),
        cost_estimate=cost(10),
        name="stem_forward",
    )(patches, packet, spread)


def taps_row(load, weight, py):
    sources = [(1, -1), (0, 0), (1, 0)] if py == 0 else [(0, 0), (1, 0), (0, 1)]
    rows = [[load(2 * gy + px, off) for px in range(2)] for gy, off in sources]

    def column(px, dx):
        total = rows[0][px] * weight(0, dx)
        total = total + rows[1][px] * weight(1, dx)
        return total + rows[2][px] * weight(2, dx)

    even = column(0, 1) + column(1, 2) + shift_down(column(1, 0))
    odd = column(1, 1) + column(0, 0) + shift_up(column(0, 2))
    return even, odd


def shift_down(v):
    at = lax.broadcasted_iota(jnp.int32, v.shape, 0)
    return jnp.where(at == 0, 0.0, pltpu.roll(v, 1, 0))


def shift_up(v):
    at = lax.broadcasted_iota(jnp.int32, v.shape, 0)
    return jnp.where(at == HALF - 1, 0.0, pltpu.roll(v, HALF - 1, 0))


def bn_stats(bgram, expand_w, count):
    weights = expand_w.astype(F32)
    square_of = jnp.concatenate([bgram, jnp.zeros((56, 128), F32)], axis=0)
    product = dot(square_of, weights, precision=HIGH)
    mean = product[64:65] / count
    second = jnp.sum(weights * product, axis=0, keepdims=True) / count
    return mean, lax.rsqrt(second - mean * mean + EPS)


def depth_kernel(mask_ref, base_ref, expand_ref, bgram_ref, norm_ref, depth_ref, out_ref, act_ref, slope_ref, stat_ref, pad, wide):
    count = bgram_ref[64:65, 64:65]
    mean, inverse = bn_stats(bgram_ref[...], expand_ref[...], count)
    gain = norm_ref[0:1] * inverse
    shift = norm_ref[1:2] - mean * gain
    zero = jnp.zeros((4, 1, HALF, BLOCK), F32)
    pad[:, 0:1] = zero
    pad[:, HALF + 1 : HALF + 2] = zero
    wide[...] = dot(base_ref[...], expand_ref[...])
    rows = 8 * HALF
    for group in range(4):

        def fill(i, _, group=group):
            first = pl.multiple_of(group * QUAD + rows * i, 16)
            at = pl.ds(first, rows)
            x = wide[at, :]
            inside = mask_ref[at, :]
            value, slope = gelu_pair(x * gain + shift)
            value = value * inside
            act_ref[at, :] = value.astype(BF16)
            slope_ref[at, :] = (slope * inside).astype(BF16)
            for k in range(8):
                pad[group, 8 * i + k + 1] = value[HALF * k : HALF * k + HALF]
            return 0

        lax.fori_loop(0, QUAD // rows, fill, 0)

    def weight(dy, dx):
        return depth_ref[3 * dy + dx : 3 * dy + dx + 1]

    def fold(v):
        return v[0:8] + v[8:16] + v[16:24]

    def step(up, sums):
        first, second = sums
        for py in range(2):
            made = taps_row(lambda g, off: pad[g, up + 1 + off], weight, py)
            for px in range(2):
                at = pl.ds(pl.multiple_of((2 * py + px) * QUAD + HALF * up, 8), HALF)
                x = made[px] * mask_ref[at, :]
                out_ref[at, :] = x
                first = first + fold(x)
                second = second + fold(x * x)
        return first, second

    sums = lax.fori_loop(0, HALF, step, (jnp.zeros((8, BLOCK), F32),) * 2, unroll=4)
    rows_out = [jnp.sum(s, axis=0, keepdims=True) for s in sums]
    stat_ref[...] = jnp.concatenate(rows_out + [jnp.zeros((6, BLOCK), F32)], axis=0)


def depth_forward(mask, base, expand_w, bgram, mid_norm, mb_depth):
    col = lambda rows: pl.BlockSpec((rows, BLOCK), lambda j: (0, j))
    whole = lambda rows: pl.BlockSpec((rows, BLOCK), lambda j: (0, 0))
    return pl.pallas_call(
        depth_kernel,
        grid=(CHUNKS,),
        out_shape=(
            jax.ShapeDtypeStruct((PLACES, EXPAND), F32),
            jax.ShapeDtypeStruct((PLACES, EXPAND), BF16),
            jax.ShapeDtypeStruct((PLACES, EXPAND), BF16),
            jax.ShapeDtypeStruct((8, EXPAND), F32),
        ),
        in_specs=[whole(PLACES), whole(PLACES), col(128), whole(72), col(2), col(9)],
        out_specs=(col(PLACES),) * 3 + (col(8),),
        scratch_shapes=[pltpu.VMEM((4, HALF + 2, HALF, BLOCK), F32), pltpu.VMEM((PLACES, BLOCK), F32)],
        compiler_params=params_of(56),
        cost_estimate=cost(25),
        name="depth_forward",
    )(mask, base, expand_w, bgram, mid_norm, mb_depth)


EARLY_ROWS = 576
STEM_ROWS = 15


def runs_of(offset, rows, width):
    period = min(128 // math.gcd(width, 128), rows)
    stride = period * width // 128 if rows > period else 1
    for j in range(period):
        start = offset + j * width
        yield j, period, start // 128, start % 128, -(-(rows - j) // period), stride


def rows_at(first, count, stride):
    return pl.ds(first, count) if stride == 1 or count == 1 else pl.ds(first, count, stride=stride)


def chunks_of(count, size=128):
    for begin in range(0, count, size):
        yield begin, min(size, count - begin)


def round_up(n, m):
    return -(-n // m) * m


def take_matrix(flat, out_ref, hold, offset, rows, width):
    direct = True
    for j, period, first, shift, count, stride in runs_of(offset, rows, width):
        direct = period == 1
        for t in range(-(-width // 128)):
            wide = min(128, width - 128 * t)
            for begin, size in chunks_of(count):
                at = first + t + begin * stride
                value = flat[rows_at(at, size, stride), :]
                if shift:
                    if shift + wide > 128:
                        lane = lax.broadcasted_iota(jnp.int32, (size, 128), 1)
                        value = jnp.where(lane >= shift, value, flat[rows_at(at + 1, size, stride), :])
                    value = pltpu.roll(value, 128 - shift, 1)
                if direct:
                    out_ref[begin : begin + size, 128 * t : 128 * t + wide] = value[:, :wide].astype(out_ref.dtype)
                elif count == 1:
                    out_ref[j : j + 1, 128 * t : 128 * t + wide] = value[:, :wide].astype(out_ref.dtype)
                else:
                    hold[t, rows_at(j + begin * period, size, period), :] = value
    if not direct and count > 1:
        for t in range(-(-width // 128)):
            wide = min(128, width - 128 * t)
            out_ref[0:rows, 128 * t : 128 * t + wide] = hold[t, 0:rows, 0:wide].astype(out_ref.dtype)


def put_matrix(flat, value_of, base, offset, rows, width):
    for j, period, first, shift, count, stride in runs_of(offset, rows, width):
        tiles = -(-width // 128)
        for begin, size in chunks_of(count):
            before = None
            lane = lax.broadcasted_iota(jnp.int32, (size, 128), 1)
            picked = rows_at(j + begin * period, size, period)
            at = first - base + begin * stride
            for t in range(tiles):
                value = value_of(picked, t)
                if shift:
                    value = pltpu.roll(value, shift, 1)
                    mixed = jnp.where(lane >= shift, value, 0.0 if before is None else before)
                else:
                    mixed = value
                before = value
                where = rows_at(at + t, size, stride)
                full = 0 < t < tiles - 1 or (shift == 0 and width % 128 == 0)
                flat[where, :] = mixed if full else flat[where, :] + mixed
            if shift:
                where = rows_at(at + tiles, size, stride)
                flat[where, :] = flat[where, :] + jnp.where(lane < shift, before, 0.0)


def unpack_kernel(names, shapes, pieces, shard_rows, me_ref, masks_ref, *refs):
    blocks, outs, (flat, hold) = refs[:pieces], refs[pieces:-2], refs[-2:]
    base = 0
    for block in blocks:

        def place(k, _, block=block, base=base):
            where = pl.ds((masks_ref[base + k] ^ me_ref[0]) * shard_rows, shard_rows)
            flat[where, :] = block[k].astype(F32)[:shard_rows]
            return 0

        lax.fori_loop(0, block.shape[0], place, 0)
        base += block.shape[0]
    for name, shape, out in zip(names, shapes, outs):
        offset, own = OFFSETS[name]
        width = own[-1]
        rows = math.prod(own) // width
        if shape[0][0] > rows or shape[0][1] > width:
            out[...] = jnp.zeros_like(out)
        take_matrix(flat, out, hold, offset, rows, width)


def unpack(blocks, me, masks, shard_rows, shapes):
    names = tuple(shapes)
    kinds = tuple(shapes[n] for n in names)
    total = sum(b.shape[0] for b in blocks) * shard_rows + 136
    made = pl.pallas_call(
        functools.partial(unpack_kernel, names, kinds, len(blocks), shard_rows),
        out_shape=tuple(jax.ShapeDtypeStruct(*k) for k in kinds),
        in_specs=[SMEM_SPEC] * 2 + [VMEM_SPEC] * len(blocks),
        out_specs=(VMEM_SPEC,) * len(names),
        scratch_shapes=[pltpu.VMEM((total, 128), F32), pltpu.VMEM((8, EXPAND + 16, 128), F32)],
        compiler_params=params_of(60),
        cost_estimate=cost(6),
        name="unpack",
    )(me, jnp.asarray(masks, jnp.int32), *blocks)
    return dict(zip(names, made))


EARLY_SHAPES = {
    "mb_short": ((128, MB_CH), BF16), "mb_expand": ((128, EXPAND), BF16), "mid_norm": ((2, EXPAND), F32),
    "mb_depth": ((9, EXPAND), F32), "dw_norm": ((2, EXPAND), F32),
}
LATE_SHAPES = {
    "se_down": ((EXPAND, SQUEEZE), BF16), "se_down_bias": ((1, SQUEEZE), F32), "se_up": ((SQUEEZE, EXPAND), BF16),
    "se_up_bias": ((1, EXPAND), F32), "mb_proj": ((EXPAND, MB_CH), BF16), "at_short": ((MB_CH, DIM), BF16),
    "pre_norm": ((2, MB_CH), F32), "qkv": ((MB_CH, 3 * DIM), BF16), "attn_out": ((DIM, DIM), BF16),
    "out_bias": ((1, DIM), F32), "rel_table": ((16, 2 * WIDE), F32), "mlp_norm": ((2, DIM), F32),
    "mlp_in": ((DIM, MLP), BF16), "mlp_in_bias": ((1, MLP), F32), "mlp_out": ((MLP, DIM), BF16),
    "mlp_out_bias": ((1, DIM), F32), "head_norm": ((2, DIM), F32), "head_w": ((DIM, CLASSES), BF16),
    "head_bias": ((1, CLASSES), F32),
}


ALL_SHAPES = EARLY_SHAPES | LATE_SHAPES


def pack_kernel(names, base, shards, shard_rows, core_ref, *refs):
    grads, (keep_ref, send_ref), (flat, hold) = refs[: len(names)], refs[len(names) : -2], refs[-2:]
    rows_all = flat.shape[0]
    step = 384

    def clear(i, _):
        flat[pl.ds(pl.multiple_of(i * step, 8), step), :] = jnp.zeros((step, 128), F32)
        return 0

    lax.fori_loop(0, rows_all // step, clear, 0)
    for name, grad in zip(names, grads):
        offset, own = OFFSETS[name]
        width = own[-1]
        rows = math.prod(own) // width
        tiles = -(-width // 128)
        read = lambda r, t: grad[r, 128 * t : 128 * t + 128]
        if grad.shape[1] < 128 * tiles:
            hold[tiles - 1, 0:rows, :] = jnp.zeros((rows, 128), F32)
            for t in range(tiles):
                wide = min(128, width - 128 * t)
                hold[t, 0:rows, 0:wide] = grad[0:rows, 128 * t : 128 * t + wide]
            read = lambda r, t: hold[t, r, :]
        put_matrix(flat, read, base, offset, rows, width)

    def share(k, _):
        block = flat[pl.ds(k * shard_rows, shard_rows), :]
        ours = k % 2 == core_ref[0]

        @pl.when(ours)
        def _():
            keep_ref[k // 2, 0:shard_rows] = block

        @pl.when(jnp.logical_not(ours))
        def _():
            send_ref[k // 2, 0:shard_rows] = block

        return 0

    lax.fori_loop(0, shards, share, 0)


def pack(core, grads, base, shards, shard_rows, held_rows):
    names = tuple(grads)
    total = -(-(shards * shard_rows + 8) // 384) * 384
    out = jax.ShapeDtypeStruct((shards // 2, held_rows, 128), F32)
    return pl.pallas_call(
        functools.partial(pack_kernel, names, base, shards, shard_rows),
        out_shape=(out, out),
        in_specs=[SMEM_SPEC] + [VMEM_SPEC] * len(names),
        out_specs=(VMEM_SPEC,) * 2,
        scratch_shapes=[pltpu.VMEM((total, 128), F32), pltpu.VMEM((2, EXPAND + 16, 128), F32)],
        compiler_params=params_of(32),
        cost_estimate=cost(6),
        name="pack",
    )(core, *grads.values())


def shard_kernel(
    length, tall_out, tall_head, first_ref, late_ref, mid_ref, dw_ref, norm_ref, vector_ref, stem_ref, loss_ref,
    out_ref, packet_ref, flat, hold, left_out, left_head,
):
    rows = length // 128
    lead = 16
    flat[...] = jnp.zeros_like(flat)
    start = first_ref[0] * length
    lane = lax.broadcasted_iota(jnp.int32, (8, 128), 1)

    def add_rows(first, value):
        flat[pl.ds(first, value.shape[0]), :] = flat[pl.ds(first, value.shape[0]), :] + value

    devices = vector_ref.shape[0]
    part = min(devices, 128)

    def place(name, left_ref, at_left, at_right, tall):
        offset, (count, width) = OFFSETS[name]
        first = (start - offset + 2**20 * width) // width - 2**20
        inside = (first > -tall) & (first < count)
        held = jnp.where(inside, first, -tall)
        made = jnp.zeros((tall, 128 * -(-width // 128)), F32)
        for g in range(devices // part):
            group = slice(g * part, g * part + part)
            left_ref[g] = jnp.zeros_like(left_ref[g])
            left_ref[g, tall : tall + count, :] = vector_ref[group, at_left, 0:count].T
            right = vector_ref[group, at_right, 0 : hold.shape[2] * -(-width // 128)]
            made = made + dot(left_ref[g, pl.ds(held + tall, tall), :], right, precision=HIGH)
        tiles = -(-width // 128)
        for t in range(tiles):
            wide = min(128, made.shape[1] - 128 * t)
            hold[t, 0:tall, 0:wide] = made[:, 128 * t : 128 * t + wide]
        period = 128 // math.gcd(width, 128)
        stride = period * width // 128

        @pl.when(inside)
        def _():
            for j in range(period):
                begin = offset + (first + j) * width - start + 128 * lead
                row = begin // 128
                shift = begin - row * 128
                size = tall // period
                at_lane = lax.broadcasted_iota(jnp.int32, (size, 128), 1)
                for t in range(tiles):
                    value = hold[t, rows_at(j, size, period), :]
                    value = pltpu.roll(value, shift, 1)
                    where = rows_at(row + t, size, stride)
                    flat[where, :] = flat[where, :] + jnp.where(at_lane >= shift, value, 0.0)
                    where = rows_at(row + t + 1, size, stride)
                    flat[where, :] = flat[where, :] + jnp.where(at_lane < shift, value, 0.0)

    def place_row(offset, value):
        width = value.shape[1]
        begin = offset - start

        @pl.when((begin > -width) & (begin < length))
        def _():
            at = begin + 128 * lead
            row = at // 128
            shift = at - row * 128
            one = lane[0:1]
            for t in range(width // 128):
                tile = pltpu.roll(value[:, 128 * t : 128 * t + 128], shift, 1)
                add_rows(row + t, jnp.where(one >= shift, tile, 0.0))
                add_rows(row + t + 1, jnp.where(one < shift, tile, 0.0))

    place("mlp_out", left_out, 0, 1, tall_out)
    place("head_w", left_head, 2, 3, tall_head)
    place_row(OFFSETS["mlp_out_bias"][0], dw_ref[3:4, 0:DIM])
    place_row(OFFSETS["head_norm"][0], dw_ref[2:3, :])
    place_row(OFFSETS["head_bias"][0], dw_ref[4:5, :])
    place_row(OFFSETS["head_bias"][0] + EXPAND, dw_ref[5:6, 0:256])
    place_row(OFFSETS["mid_norm"][0], norm_ref[0:1, :])
    place_row(OFFSETS["mid_norm"][0] + EXPAND, norm_ref[1:2, :])
    place_row(OFFSETS["dw_norm"][0], dw_ref[1:2, :])
    place_row(OFFSETS["dw_norm"][0] + EXPAND, dw_ref[0:1, :])
    total = flat[lead : lead + rows, :] + late_ref[0:rows] + mid_ref[0:rows]
    out_ref[...] = total
    square = jnp.sum(total * total).reshape(1, 1)
    packet_ref[0:16, :] = stem_ref[...]
    packet_ref[16:24, :] = jnp.where(lane == 0, loss_ref[...], jnp.where(lane == 1, square, 0.0))


def shard_parts(me, length, late, mid, dw_sums, mid_sums, vectors, stem, loss):
    rows = length // 128
    devices = vectors.shape[0]
    part = min(devices, 128)

    def tall(name, unit):
        width = OFFSETS[name][1][1]
        return round_up(-(-length // width) + 1, unit)

    tall_out, tall_head = tall("mlp_out", 8), tall("head_w", 16)
    return pl.pallas_call(
        functools.partial(shard_kernel, length, tall_out, tall_head),
        out_shape=(jax.ShapeDtypeStruct((rows, 128), F32), jax.ShapeDtypeStruct((24, 128), F32)),
        in_specs=[SMEM_SPEC] + [VMEM_SPEC] * 7,
        out_specs=(VMEM_SPEC,) * 2,
        scratch_shapes=[
            pltpu.VMEM((rows + 1024, 128), F32),
            pltpu.VMEM((8, max(tall_out, tall_head) + 16, 128), F32),
            pltpu.VMEM((devices // part, MLP + 2 * tall_out, part), F32),
            pltpu.VMEM((devices // part, DIM + 2 * tall_head, part), F32),
        ],
        compiler_params=params_of(16),
        cost_estimate=cost(4),
        name="shard_parts",
    )(me, late, mid, dw_sums, mid_sums, vectors, stem, loss)


def squeeze_lanes():
    table = np.zeros((16 * 48, 16 * 24), np.float32)
    for e in range(16):
        for x in range(24):
            table[e * 48 + x, e * 24 + x] = 1.0
    return table


def slots_of(rel_index):
    last = TOKENS - 1
    corner = lambda i: rel_index[i].reshape(HALF, HALF)
    low_row = jnp.concatenate([corner(last), corner(last - HALF + 1)[:, 1:]], axis=1)
    high_row = jnp.concatenate([corner(HALF - 1), corner(0)[:, 1:]], axis=1)
    return jnp.concatenate([low_row, high_row[1:]], axis=0)


def one_hot(slot_ref, c):
    at = lax.broadcasted_iota(jnp.int32, (256, 2 * WIDE), 1)
    return jnp.where(slot_ref[256 * c : 256 * c + 256, :] == at, 1.0, 0.0).astype(BF16)


def bias_kernel(table_ref, slot_ref, pick_ref, out_ref, held):
    table = table_ref[...].astype(BF16)
    f = jnp.concatenate([dot(table, one_hot(slot_ref, c), NT) for c in range(2 * WIDE // 256)], axis=1)
    for x in range(HALF):
        turned = pltpu.roll(f, (WIDE * 2 - (HALF - 1 - x)) % (WIDE * 2), 1) if x != HALF - 1 else f
        held[16 * x : 16 * x + 16, :] = turned.astype(BF16)
    for part in range(3):
        made = dot(held[:, 768 * part : 768 * part + 768], pick_ref[...])
        for t in range(3):
            for x in range(HALF):
                out_ref[3 * part + t, pl.ds(x, HEADS, stride=HALF), :] = made[
                    16 * x : 16 * x + HEADS, 128 * t : 128 * t + 128
                ]


def build_bias(table, slots, pick):
    return pl.pallas_call(
        bias_kernel,
        out_shape=jax.ShapeDtypeStruct((9, HEADS * HALF + HALF, 128), F32),
        in_specs=[VMEM_SPEC] * 3,
        out_specs=VMEM_SPEC,
        scratch_shapes=[pltpu.VMEM((16 * HALF, 2 * WIDE), BF16)],
        compiler_params=params_of(16),
        cost_estimate=cost(8),
        name="bias_build",
    )(table, slots, pick)


def halves_of(v):
    high = v.astype(BF16)
    return high, (v - high.astype(F32)).astype(BF16)


def bias_back_step(grad_ref, slot_ref, pick_ref, out_ref, held):
    for part in range(3):
        rows = jnp.concatenate([grad_ref[3 * part + t] for t in range(3)], axis=1)
        high, rest = halves_of(rows)
        wide = dot(high, pick_ref[...]) + dot(rest, pick_ref[...])
        for t in range(6):
                held[6 * part + t, 0 : HEADS * HALF, :] = wide[:, 128 * t : 128 * t + 128]
    total = jnp.zeros((16, 2 * WIDE), F32)
    for x in range(HALF):
        wide = jnp.concatenate([held[t, pl.ds(x, HEADS, stride=HALF), :] for t in range(18)], axis=1)
        wide = jnp.concatenate([wide, jnp.zeros((4, 2 * WIDE), F32)], axis=0)
        total = total + (pltpu.roll(wide, HALF - 1 - x, 1) if x != HALF - 1 else wide)
    high, rest = halves_of(total)
    result = jnp.zeros((16, 2 * WIDE), F32)
    for c in range(2 * WIDE // 256):
        hot = one_hot(slot_ref, c)
        cols = slice(256 * c, 256 * c + 256)
        result = result + dot(high[:, cols], hot) + dot(rest[:, cols], hot)
    out_ref[...] = result


def sigmoid(v):
    return 1.0 / (1.0 + jnp.exp(-v))


def row8(rows):
    width = rows[0].shape[1]
    return jnp.concatenate(rows + [jnp.zeros((8 - len(rows), width), F32)], axis=0)


def dw_stats(stat, count):
    mean = stat[0:1] / count
    return mean, lax.rsqrt(stat[1:2] / count - mean * mean + EPS)


def valid_places(limit):
    return (limit * limit).astype(F32)


def excite_kernel(
    res_ref, mask_ref, depth_ref, stat_ref, bgram_ref, norm_ref, down_ref, down_b_ref, up_ref, up_b_ref,
    proj_ref, base_ref, short_ref, pre_ref, qkv_ref,
    act_ref, slope_ref, block_ref, skip_ref, normed_ref, project_ref, vec_ref, small_ref, held, total,
):
    limit = limit_of(res_ref)
    count = bgram_ref[64:65, 64:65]
    mean, inverse = dw_stats(stat_ref[...], count)
    gain = norm_ref[0:1] * inverse
    shift = norm_ref[1:2] - mean * gain
    rows = 4 * HALF
    group = pl.program_id(0)

    @pl.when(group == 0)
    def _():
        total[...] = jnp.zeros_like(total)

    def fill(i, sums):
        at = pl.ds(pl.multiple_of(rows * i, 16), rows)
        value, slope = gelu_pair(depth_ref[at, :] * gain + shift)
        inside = jnp.concatenate([mask_ref[at, :]] * CHUNKS, axis=1)
        value = value * inside
        held[pl.ds(pl.multiple_of(group * QUAD + rows * i, 16), rows), :] = value
        act_ref[at, :] = value.astype(BF16)
        slope_ref[at, :] = (slope * inside).astype(BF16)
        for k in range(rows // 8):
            sums = sums + value[8 * k : 8 * k + 8]
        return sums

    total[...] = lax.fori_loop(0, QUAD // rows, fill, total[...])

    @pl.when(group == 3)
    def _():
        excite_rest(
            limit, mean, inverse, total, down_ref, down_b_ref, up_ref, up_b_ref, proj_ref, base_ref, short_ref,
            pre_ref, qkv_ref, block_ref, skip_ref, normed_ref, project_ref, vec_ref, small_ref, held,
        )


def excite_rest(
    limit, mean, inverse, total, down_ref, down_b_ref, up_ref, up_b_ref, proj_ref, base_ref, short_ref, pre_ref,
    qkv_ref, block_ref, skip_ref, normed_ref, project_ref, vec_ref, small_ref, held,
):
    pooled = jnp.sum(total[...], axis=0, keepdims=True) / valid_places(limit)
    before = dot(row8([pooled]), down_ref[...].astype(F32), precision=HIGH)[0:1] + down_b_ref[...]
    gate = sigmoid(before)
    squeeze = before * gate
    excite = sigmoid(
        dot(row8([squeeze]), up_ref[...].astype(F32), precision=HIGH)[0:1] + up_b_ref[...]
    )
    vec_ref[...] = row8([pooled, excite, mean, inverse])
    small_ref[...] = row8([squeeze, gate * (1.0 + before * (1.0 - gate))])

    big = 576
    def section(i, _):
        at = pl.ds(pl.multiple_of(big * i, 16), big)
        scaled = (held[at, :] * excite).astype(BF16)
        block_ref[at, :] = dot(scaled, proj_ref[...]) + dot(base_ref[at, :], short_ref[...])
        return 0

    lax.fori_loop(0, PLACES // big, section, 0)
    part = 96

    def tokens(i, _):
        skipped = jnp.zeros((part, MB_CH), F32)
        normed = jnp.zeros((part, MB_CH), F32)
        for group in range(4):
            block = block_ref[pl.ds(pl.multiple_of(group * QUAD + part * i, 16), part), :]
            skipped = skipped + block
            hat, _ = normalise(block)
            normed = normed + hat
        at = pl.ds(pl.multiple_of(part * i, 16), part)
        skip_ref[at, :] = (0.25 * skipped).astype(BF16)
        low = (0.25 * normed * pre_ref[0:1] + pre_ref[1:2]).astype(BF16)
        normed_ref[at, :] = low
        return 0

    lax.fori_loop(0, TOKENS // part, tokens, 0)
    project_ref[...] = dot(normed_ref[...], qkv_ref[...]).astype(BF16)


def normalise(v):
    centered = v - jnp.mean(v, axis=-1, keepdims=True)
    inverse = lax.rsqrt(jnp.mean(centered * centered, axis=-1, keepdims=True) + EPS)
    return centered * inverse, inverse


def normalise_back(grad_hat, hat, inverse):
    first = jnp.mean(grad_hat, axis=-1, keepdims=True)
    second = jnp.mean(grad_hat * hat, axis=-1, keepdims=True)
    return inverse * (grad_hat - first - hat * second)


def excite_forward(res_ids, mask, depth, stat, bgram, base, p):
    part = lambda width: pl.BlockSpec((QUAD, width), lambda i: (i, 0))
    whole = lambda *shape: pl.BlockSpec(shape, lambda i: (0,) * len(shape))
    return pl.pallas_call(
        excite_kernel,
        grid=(4,),
        out_shape=(
            jax.ShapeDtypeStruct((PLACES, EXPAND), BF16),
            jax.ShapeDtypeStruct((PLACES, EXPAND), BF16),
            jax.ShapeDtypeStruct((PLACES, MB_CH), F32),
            jax.ShapeDtypeStruct((TOKENS, MB_CH), BF16),
            jax.ShapeDtypeStruct((TOKENS, MB_CH), BF16),
            jax.ShapeDtypeStruct((TOKENS, 3 * DIM), BF16),
            jax.ShapeDtypeStruct((8, EXPAND), F32),
            jax.ShapeDtypeStruct((8, SQUEEZE), F32),
        ),
        in_specs=[
            SMEM_SPEC, part(128), part(EXPAND), whole(8, EXPAND), whole(72, 128), whole(2, EXPAND),
            whole(EXPAND, SQUEEZE), whole(1, SQUEEZE), whole(SQUEEZE, EXPAND), whole(1, EXPAND),
            whole(EXPAND, MB_CH), whole(PLACES, 128), whole(128, MB_CH), whole(2, MB_CH), whole(MB_CH, 3 * DIM),
        ],
        out_specs=(
            part(EXPAND), part(EXPAND), whole(PLACES, MB_CH), whole(TOKENS, MB_CH), whole(TOKENS, MB_CH),
            whole(TOKENS, 3 * DIM), whole(8, EXPAND), whole(8, SQUEEZE),
        ),
        scratch_shapes=[pltpu.VMEM((PLACES, EXPAND), F32), pltpu.VMEM((8, EXPAND), F32)],
        compiler_params=params_of(40),
        cost_estimate=cost(18),
        name="excite_forward",
    )(
        res_ids, mask, depth, stat, bgram, p["dw_norm"], p["se_down"], p["se_down_bias"], p["se_up"], p["se_up_bias"],
        p["mb_proj"], base, p["mb_short"], p["pre_norm"], p["qkv"],
    )


SCALE = HEAD_DIM ** (-0.5)
PER = BLOCK // HEAD_DIM
ATT_ROWS = 2 * HALF


def token_valid(limit, shape, axis):
    at = lax.broadcasted_iota(jnp.int32, shape, axis)
    y = at // HALF
    x = at - y * HALF
    return (2 * y < limit) & (2 * x < limit)


def head_lanes(h):
    lane = lax.broadcasted_iota(jnp.int32, (TOKENS, BLOCK), 1)
    return lane // HEAD_DIM == h


def bias_cut(up):
    offset = (HALF - 1 - up) * HALF
    lead = offset % 128
    return offset // 128, (5 if lead <= 64 else 6), lead


def attend_kernel(res_ref, q_ref, k_ref, v_ref, bias_ref, out_ref, p_ref, scores):
    limit = limit_of(res_ref)
    usable = token_valid(limit, (1, TOKENS), 1)

    def head(h, total):
        mine = head_lanes(h)
        q = jnp.where(mine, q_ref[...], jnp.zeros((), BF16))
        scores[h % 2] = dot(q, k_ref[...], NT)
        bias_rows = pl.ds(pl.multiple_of(h * HALF, 8), HALF)
        for i in range(TOKENS // ATT_ROWS):
            at = slice(ATT_ROWS * i, ATT_ROWS * i + ATT_ROWS)
            shifted = []
            for k in range(2):
                tile, tiles, lead = bias_cut(2 * i + k)
                bias = jnp.concatenate([bias_ref[tile + t, bias_rows, :] for t in range(tiles)], axis=1)
                if lead:
                    bias = pltpu.roll(bias, 128 * tiles - lead, 1)
                shifted.append(bias[:, :TOKENS])
            s = scores[h % 2, at, :] * SCALE + jnp.concatenate(shifted, axis=0)
            s = jnp.where(usable, s, -1e30)
            e = jnp.exp(s - jnp.max(s, axis=-1, keepdims=True))
            weights = e * (1.0 / jnp.sum(e, axis=-1, keepdims=True))
            p_ref[h, at, :] = weights.astype(BF16)
        return jnp.where(mine, dot(p_ref[h], v_ref[...]), total)

    total = lax.fori_loop(0, PER, head, jnp.zeros((TOKENS, BLOCK), F32), unroll=2)
    out_ref[...] = total.astype(BF16)


def attend_forward(res_ids, project, bias):
    part = lambda k: pl.BlockSpec((TOKENS, BLOCK), lambda j: (0, 3 * k + j))
    return pl.pallas_call(
        attend_kernel,
        grid=(HEADS // PER,),
        out_shape=(
            jax.ShapeDtypeStruct((TOKENS, DIM), BF16),
            jax.ShapeDtypeStruct((HEADS, TOKENS, TOKENS), BF16),
        ),
        in_specs=[SMEM_SPEC, part(0), part(1), part(2), pl.BlockSpec((9, PER * HALF, 128), lambda j: (0, j, 0))],
        out_specs=(
            pl.BlockSpec((TOKENS, BLOCK), lambda j: (0, j)),
            pl.BlockSpec((PER, TOKENS, TOKENS), lambda j: (j, 0, 0)),
        ),
        scratch_shapes=[pltpu.VMEM((2, TOKENS, TOKENS), F32)],
        compiler_params=params_of(20),
        cost_estimate=cost(35),
        name="attend_forward",
    )(res_ids, project, project, project, bias)


def attend_back_kernel(
    q_ref, k_ref, v_ref, o_ref, do_ref, p_ref, slot_ref, pick_ref, dq_ref, dk_ref, dv_ref, dtable_ref,
    scores, low, bias, dbias_ref, held, turned, sums,
):
    first_head = pl.program_id(0) * PER

    turned[0] = q_ref[...].astype(F32).T.astype(BF16)
    turned[1] = do_ref[...].astype(F32).T.astype(BF16)

    def head(h, dq):
        mine = head_lanes(h)
        grad = jnp.where(mine, do_ref[...], jnp.zeros((), BF16))
        scores[...] = dot(grad, v_ref[...], NT)
        bias[...] = jnp.zeros((HALF, WIDE), F32)
        lane = lax.broadcasted_iota(jnp.int32, (ATT_ROWS, BLOCK), 1)
        for i in range(TOKENS // ATT_ROWS):
            at = slice(ATT_ROWS * i, ATT_ROWS * i + ATT_ROWS)
            both = do_ref[at, :].astype(F32) * o_ref[at, :].astype(F32)
            both = jnp.where(lane // HEAD_DIM == h, both, 0.0)
            delta = jnp.sum(both, axis=-1, keepdims=True)
            ds = p_ref[h, at, :].astype(F32) * (scores[at, :] - delta)
            low[at, :] = (ds * SCALE).astype(BF16)
            for k in range(2):
                tile, tiles, lead = bias_cut(2 * i + k)
                wide = jnp.concatenate(
                    [ds[HALF * k : HALF * k + HALF], jnp.zeros((HALF, 128 * tiles - TOKENS), F32)], axis=1
                )
                if lead:
                    wide = pltpu.roll(wide, lead, 1)
                cols = slice(128 * tile, 128 * (tile + tiles))
                bias[:, cols] = bias[:, cols] + wide
        for t in range(9):
            dbias_ref[t, pl.ds(pl.multiple_of((first_head + h) * HALF, 8), HALF), :] = bias[:, 128 * t : 128 * t + 128]
        dq = jnp.where(mine, dot(low[...], k_ref[...]), dq)
        own = pl.ds(pl.multiple_of(h * HEAD_DIM, HEAD_DIM), HEAD_DIM)
        sums[0, own, :] = dot(turned[0, own, :], low[...])
        sums[1, own, :] = dot(turned[1, own, :], p_ref[h])
        return dq

    dq = lax.fori_loop(0, PER, head, jnp.zeros((TOKENS, BLOCK), F32))
    dq_ref[...] = dq.astype(BF16)
    dk_ref[...] = sums[0].T.astype(BF16)
    dv_ref[...] = sums[1].T.astype(BF16)

    @pl.when(pl.program_id(0) == HEADS // PER - 1)
    def _():
        bias_back_step(dbias_ref, slot_ref, pick_ref, dtable_ref, held)


def attend_backward(project, blended, grad, weights, slots, pick):
    part = lambda k: pl.BlockSpec((TOKENS, BLOCK), lambda j: (0, 3 * k + j))
    whole = lambda *shape: pl.BlockSpec(shape, lambda j: (0,) * len(shape))
    return pl.pallas_call(
        attend_back_kernel,
        grid=(HEADS // PER,),
        out_shape=(jax.ShapeDtypeStruct((TOKENS, DIM), BF16),) * 3
        + (jax.ShapeDtypeStruct((16, 2 * WIDE), F32),),
        in_specs=[
            part(0), part(1), part(2), part(0), part(0),
            pl.BlockSpec((PER, TOKENS, TOKENS), lambda j: (j, 0, 0)), whole(2 * WIDE, 1), whole(16 * HALF, 32 * HALF),
        ],
        out_specs=(part(0), part(0), part(0), whole(16, 2 * WIDE)),
        scratch_shapes=[
            pltpu.VMEM((TOKENS, TOKENS), F32), pltpu.VMEM((TOKENS, TOKENS), BF16), pltpu.VMEM((HALF, WIDE), F32),
            pltpu.VMEM((9, HEADS * HALF, 128), F32), pltpu.VMEM((18, HEADS * HALF + HALF, 128), F32),
            pltpu.VMEM((2, BLOCK, TOKENS), BF16), pltpu.VMEM((2, BLOCK, TOKENS), F32),
        ],
        compiler_params=params_of(50),
        cost_estimate=cost(40),
        name="attend_backward",
    )(project, project, project, blended, grad, weights, slots, pick)


MLP_ROWS = 192


def mlp_kernel(
    share, res_ref, label_ref, skip_ref, blend_ref, short_ref, out_ref, out_b_ref, norm_ref, in_ref, in_b_ref,
    back_ref, back_b_ref, hnorm_ref, head_ref, head_b_ref,
    loss_ref, dblend_ref, dskip_ref, dshort_ref, dout_ref, dout_b_ref, dnorm_ref, din_ref, din_b_ref,
    vec_ref, few_ref,
    section, low, slopes, dpres, grads,
):
    limit = limit_of(res_ref)
    n_valid = (limit // 2 * (limit // 2)).astype(F32)
    steps = TOKENS // MLP_ROWS
    cut = 384

    def valid_rows(i):
        at = lax.broadcasted_iota(jnp.int32, (MLP_ROWS, 1), 0) + MLP_ROWS * i
        y = at // HALF
        x = at - y * HALF
        return jnp.where((2 * y < limit) & (2 * x < limit), 1.0, 0.0)

    def forward(i, carry):
        feature, used = carry
        at = pl.ds(pl.multiple_of(MLP_ROWS * i, 16), MLP_ROWS)
        first = dot(skip_ref[at, :], short_ref[...]) + dot(blend_ref[at, :], out_ref[...]) + out_b_ref[...]
        section[at, :] = first
        hat, _ = normalise(first)
        normed = (hat * norm_ref[0:1] + norm_ref[1:2]).astype(BF16)
        low[at, :] = normed
        inside = valid_rows(i)
        second = first + back_b_ref[...]
        parts = []
        for j in range(MLP // cut):
            cols = slice(cut * j, cut * j + cut)
            value, slope = gelu_pair(dot(normed, in_ref[:, cols]) + in_b_ref[:, cols])
            slopes[at, cols] = slope * inside
            value = value.astype(BF16)
            parts.append(jnp.sum(value.astype(F32) * inside, axis=0, keepdims=True))
            second = second + dot(value, back_ref[cols, :])
        feature = feature + jnp.sum(second * inside, axis=0, keepdims=True)
        return feature, used + jnp.concatenate(parts, axis=1)

    feature, used = lax.fori_loop(
        0, steps, forward, (jnp.zeros((1, DIM), F32), jnp.zeros((1, MLP), F32))
    )
    feature = feature / n_valid
    hat, inverse = normalise(feature)
    normed = (hat * hnorm_ref[0:1] + hnorm_ref[1:2]).astype(BF16)
    normed8 = jnp.concatenate([normed.astype(F32), jnp.zeros((15, DIM), F32)], axis=0).astype(BF16)
    logits = dot(normed8, head_ref[...])[0:1] + head_b_ref[...]
    peak = jnp.max(logits, axis=-1, keepdims=True)
    exps = jnp.exp(logits - peak)
    total = jnp.sum(exps, axis=-1, keepdims=True)
    log_probs = logits - peak - jnp.log(total)
    at_class = lax.broadcasted_iota(jnp.int32, (1, CLASSES), 1)
    goal = jnp.where(at_class == label_ref[0], 1.0 - SMOOTH, 0.0) + SMOOTH / CLASSES
    loss = -jnp.sum(goal * log_probs, axis=-1, keepdims=True)
    loss_ref[...] = jnp.broadcast_to(loss, (8, 128))
    grad = (exps / total - goal) * share
    few_ref[...] = jnp.zeros_like(few_ref)
    few_ref[4:5, :] = grad[:, 0:EXPAND]
    few_ref[5:6, 0 : CLASSES - EXPAND] = grad[:, EXPAND:]
    grad16 = jnp.concatenate([grad, jnp.zeros((15, CLASSES), F32)], axis=0).astype(BF16)
    vec_ref[...] = jnp.zeros_like(vec_ref)
    vec_ref[2:3, 0:DIM] = normed8.astype(F32)[0:1]
    vec_ref[3:4, 0:CLASSES] = grad16.astype(F32)[0:1]
    grad = dot(grad16, head_ref[...], NT)[0:1]
    few_ref[2:3, :] = jnp.concatenate([grad * hat, grad], axis=1)
    grad = normalise_back(grad * hnorm_ref[0:1], hat, inverse) / n_valid
    low_grad = jnp.concatenate([grad, jnp.zeros((15, DIM), F32)], axis=0).astype(BF16)
    vec_ref[0:1, :] = used
    vec_ref[1:2, 0:DIM] = low_grad.astype(F32)[0:1]
    few_ref[3:4, 0:DIM] = grad * n_valid
    dhidden = dot(low_grad, back_ref[...], NT)[0:1]

    def backward(i, carry):
        dnorm0, dnorm1, dbias, dout_b = carry
        at = pl.ds(pl.multiple_of(MLP_ROWS * i, 16), MLP_ROWS)
        dnormed = jnp.zeros((MLP_ROWS, DIM), F32)
        parts = []
        for j in range(MLP // cut):
            cols = slice(cut * j, cut * j + cut)
            dpre = slopes[at, cols] * dhidden[:, cols]
            parts.append(jnp.sum(dpre, axis=0, keepdims=True))
            dpre = dpre.astype(BF16)
            dpres[at, cols] = dpre
            dnormed = dnormed + dot(dpre, in_ref[:, cols], NT)
        hat, inverse = normalise(section[at, :])
        dnorm0 = dnorm0 + jnp.sum(dnormed * hat, axis=0, keepdims=True)
        dnorm1 = dnorm1 + jnp.sum(dnormed, axis=0, keepdims=True)
        dsection = normalise_back(dnormed * norm_ref[0:1], hat, inverse) + valid_rows(i) * grad
        grads[at, :] = dsection.astype(BF16)
        dout_b = dout_b + jnp.sum(dsection, axis=0, keepdims=True)
        dblend_ref[at, :] = dot(grads[at, :], out_ref[...], NT).astype(BF16)
        dskip_ref[at, :] = dot(grads[at, :], short_ref[...], NT)
        return dnorm0, dnorm1, dbias + jnp.concatenate(parts, axis=1), dout_b

    row = jnp.zeros((1, DIM), F32)
    dnorm0, dnorm1, dbias, dout_b = lax.fori_loop(0, steps, backward, (row, row, jnp.zeros((1, MLP), F32), row))
    dnorm_ref[...] = jnp.concatenate([dnorm0, dnorm1], axis=0)
    din_b_ref[...] = dbias
    dout_b_ref[...] = dout_b
    din_ref[...] = dot(low[...], dpres[...], TN)
    dout_ref[...] = dot(blend_ref[...], grads[...], TN)
    dshort_ref[...] = dot(skip_ref[...], grads[...], TN)


def mlp_both(share, res_ids, labels, skipped, blended, p):
    s = jax.ShapeDtypeStruct
    return pl.pallas_call(
        functools.partial(mlp_kernel, share),
        out_shape=(
            s((8, 128), F32), s((TOKENS, DIM), BF16), s((TOKENS, MB_CH), F32), s((MB_CH, DIM), F32),
            s((DIM, DIM), F32), s((1, DIM), F32), s((2, DIM), F32), s((DIM, MLP), F32), s((1, MLP), F32),
            s((8, MLP), F32), s((8, EXPAND), F32),
        ),
        in_specs=[SMEM_SPEC] * 2 + [VMEM_SPEC] * 13,
        out_specs=(VMEM_SPEC,) * 11,
        scratch_shapes=[
            pltpu.VMEM((TOKENS, DIM), F32),
            pltpu.VMEM((TOKENS, DIM), BF16),
            pltpu.VMEM((TOKENS, MLP), F32),
            pltpu.VMEM((TOKENS, MLP), BF16),
            pltpu.VMEM((TOKENS, DIM), BF16),
        ],
        compiler_params=params_of(24),
        cost_estimate=cost(23),
        name="mlp_both",
    )(
        res_ids, labels, skipped, blended, p["at_short"], p["attn_out"], p["out_bias"], p["mlp_norm"], p["mlp_in"],
        p["mlp_in_bias"], p["mlp_out"], p["mlp_out_bias"], p["head_norm"], p["head_w"], p["head_bias"],
    )


def proj_back_kernel(
    res_ref, dq_ref, dk_ref, dv_ref, normed_ref, qkv_ref, dskip_ref, block_ref, pre_ref, act_ref, vec_ref,
    small_ref, proj_ref, short_ref, base_ref, down_ref, up_ref,
    dqkv_ref, dpre_ref, dblock_ref, dproj_ref, dshort_ref, dbase_ref, ddown_ref, ddown_b_ref, dup_ref, dup_b_ref,
    dpool_ref, back,
):
    limit = limit_of(res_ref)
    part = 96
    grad = dot(dq_ref[...], qkv_ref[:, 0:DIM], NT)
    grad = grad + dot(dk_ref[...], qkv_ref[:, DIM : 2 * DIM], NT)
    back[...] = grad + dot(dv_ref[...], qkv_ref[:, 2 * DIM :], NT)

    def tokens(i, carry):
        dpre0, dpre1 = carry
        at = pl.ds(pl.multiple_of(part * i, 16), part)
        grad = back[at, :]
        dskip = 0.25 * dskip_ref[at, :]
        dpre1 = dpre1 + jnp.sum(grad, axis=0, keepdims=True)
        grad = 0.25 * grad
        dhat = grad * pre_ref[0:1]
        for group in range(4):
            places = pl.ds(pl.multiple_of(group * QUAD + part * i, 16), part)
            hat, inverse = normalise(block_ref[places, :])
            dpre0 = dpre0 + jnp.sum(grad * hat, axis=0, keepdims=True)
            dblock = normalise_back(dhat, hat, inverse) + dskip
            dblock_ref[places, :] = dblock.astype(BF16)
        return dpre0, dpre1

    row = jnp.zeros((1, MB_CH), F32)
    dpre0, dpre1 = lax.fori_loop(0, TOKENS // part, tokens, (row, row))
    dpre_ref[...] = jnp.concatenate([dpre0, dpre1], axis=0)
    for k, grad_ref in enumerate((dq_ref, dk_ref, dv_ref)):
        dqkv_ref[:, DIM * k : DIM * k + DIM] = dot(normed_ref[...], grad_ref[...], TN)
    dshort_ref[...] = dot(base_ref[...], dblock_ref[...], TN)[0:STEM_CH]
    dbase_ref[...] = dot(dblock_ref[...], short_ref[...], NT)
    excite = vec_ref[1:2]
    parts = []
    for j in range(CHUNKS):
        cols = slice(BLOCK * j, BLOCK * j + BLOCK)
        act = act_ref[:, cols].astype(F32)
        scaled = (act * excite[:, cols]).astype(BF16)
        dproj_ref[cols, :] = dot(scaled, dblock_ref[...], TN)
        dscaled = dot(dblock_ref[...], proj_ref[cols, :], NT)
        parts.append(jnp.sum(dscaled * act, axis=0, keepdims=True))
    dexcite = jnp.concatenate(parts, axis=1)
    dafter = dexcite * excite * (1.0 - excite)
    dup_b_ref[...] = dafter
    dup_ref[...] = dot(row8([small_ref[0:1]]), row8([dafter]), TN, precision=HIGH)
    dsqueeze = dot(row8([dafter]), up_ref[...].astype(F32), NT, precision=HIGH)[0:1]
    dbefore = dsqueeze * small_ref[1:2]
    ddown_b_ref[...] = dbefore
    ddown_ref[...] = dot(row8([vec_ref[0:1]]), row8([dbefore]), TN, precision=HIGH)
    dpool = dot(row8([dbefore]), down_ref[...].astype(F32), NT, precision=HIGH)
    dpool_ref[...] = dpool / valid_places(limit)


def proj_backward(res_ids, dq, dk, dv, normed, dskip, block, act, vec, small, base, p):
    s = jax.ShapeDtypeStruct
    return pl.pallas_call(
        proj_back_kernel,
        out_shape=(
            s((MB_CH, 3 * DIM), F32), s((2, MB_CH), F32), s((PLACES, MB_CH), BF16), s((EXPAND, MB_CH), F32),
            s((STEM_CH, MB_CH), F32), s((PLACES, 128), F32), s((EXPAND, SQUEEZE), F32), s((1, SQUEEZE), F32),
            s((SQUEEZE, EXPAND), F32), s((1, EXPAND), F32), s((8, EXPAND), F32),
        ),
        in_specs=[SMEM_SPEC] + [VMEM_SPEC] * 16,
        out_specs=(VMEM_SPEC,) * 11,
        scratch_shapes=[pltpu.VMEM((TOKENS, MB_CH), F32)],
        compiler_params=params_of(24),
        cost_estimate=cost(13),
        name="proj_backward",
    )(
        res_ids, dq, dk, dv, normed, p["qkv"], dskip, block, p["pre_norm"], act, vec, small, p["mb_proj"],
        p["mb_short"], base, p["se_down"], p["se_up"],
    )


def excite_back_kernel(dblock_ref, proj_ref, vec_ref, dpool_ref, few_ref, slope_ref, x_ref, out_ref, sum_ref, wide):
    excite, mean, inverse = vec_ref[1:2], vec_ref[2:3], vec_ref[3:4]
    dpool = dpool_ref[0:1]
    rows = 288
    wide[...] = dot(dblock_ref[...], proj_ref[...], NT)

    def fold(v):
        total = v[0:8]
        for k in range(1, rows // 8):
            total = total + v[8 * k : 8 * k + 8]
        return total

    def step(i, sums):
        at = pl.ds(pl.multiple_of(rows * i, 16), rows)
        grad = wide[at, :] * excite + dpool
        grad = grad * slope_ref[at, :].astype(F32)
        out_ref[at, :] = grad.astype(BF16)
        hat = (x_ref[at, :] - mean) * inverse
        return sums[0] + fold(grad), sums[1] + fold(grad * hat)

    sums = lax.fori_loop(0, PLACES // rows, step, (jnp.zeros((8, BLOCK), F32),) * 2)
    sum_ref[...] = few_ref[...] + row8([jnp.sum(s, axis=0, keepdims=True) for s in sums])


def excite_backward(dblock, proj, vec, dpool, few, slope, depth):
    col = lambda rows: pl.BlockSpec((rows, BLOCK), lambda j: (0, j))
    return pl.pallas_call(
        excite_back_kernel,
        grid=(CHUNKS,),
        out_shape=(jax.ShapeDtypeStruct((PLACES, EXPAND), BF16), jax.ShapeDtypeStruct((8, EXPAND), F32)),
        in_specs=[
            pl.BlockSpec((PLACES, MB_CH), lambda j: (0, 0)),
            pl.BlockSpec((BLOCK, MB_CH), lambda j: (j, 0)),
            col(8), col(8), col(8), col(PLACES), col(PLACES),
        ],
        out_specs=(col(PLACES), col(8)),
        scratch_shapes=[pltpu.VMEM((PLACES, BLOCK), F32)],
        compiler_params=params_of(56),
        cost_estimate=cost(12),
        name="excite_backward",
    )(dblock, proj, vec, dpool, few, slope, depth)


def depth_back_kernel(
    mask_ref, du_ref, x_ref, vec_ref, sum_ref, bgram_ref, base_ref, expand_ref, dwn_ref, depth_ref, act_ref, slope_ref,
    out_ref, cross_ref, sums_ref, pad,
):
    count = bgram_ref[64:65, 64:65]
    mean1, inverse1 = bn_stats(bgram_ref[...], expand_ref[...], count)
    mean2, inverse2 = vec_ref[2:3], vec_ref[3:4]
    c1 = sum_ref[0:1] / count
    c2 = sum_ref[1:2] / count
    scale2 = dwn_ref[0:1] * inverse2
    slant = scale2 * inverse2 * c2
    level = scale2 * c1 - slant * mean2
    zero = jnp.zeros((4, 1, HALF, BLOCK), F32)
    pad[:, 0:1] = zero
    pad[:, HALF + 1 : HALF + 2] = zero
    rows = 2 * HALF

    def fill(i, _):
        for group in range(4):
            at = pl.ds(pl.multiple_of(group * QUAD + rows * i, 16), rows)
            grad = scale2 * du_ref[at, :].astype(F32) - mask_ref[at, :] * (level + x_ref[at, :] * slant)
            for k in range(2):
                pad[group, 2 * i + k + 1] = grad[HALF * k : HALF * k + HALF]
        return 0

    lax.fori_loop(0, HALF // 2, fill, 0)

    def weight(dy, dx):
        return depth_ref[8 - 3 * dy - dx : 9 - 3 * dy - dx]

    def fold(v):
        return v[0:8] + v[8:16] + v[16:24]

    def step(k, sums):
        sums = list(sums)
        for py in range(2):
            places = [
                pl.ds(pl.multiple_of((2 * py + px) * QUAD + 2 * HALF * k, 16), 2 * HALF) for px in range(2)
            ]
            low_both, high_both = (act_ref[at, :].astype(F32) for at in places)
            made = [[], []]
            for half in range(2):
                up = 2 * k + half
                cut = slice(HALF * half, HALF * half + HALF)
                sources = [(1, -1), (0, 0), (1, 0)] if py == 0 else [(0, 0), (1, 0), (0, 1)]
                low_act, high_act = low_both[cut], high_both[cut]
                even = odd = None
                for t, (gy, off) in enumerate(sources):
                    left, right = pad[2 * gy, up + 1 + off], pad[2 * gy + 1, up + 1 + off]
                    before, after = shift_down(right), shift_up(left)
                    a = before * weight(t, 0) + left * weight(t, 1) + right * weight(t, 2)
                    b = left * weight(t, 0) + right * weight(t, 1) + after * weight(t, 2)
                    even = a if even is None else even + a
                    odd = b if odd is None else odd + b
                    for s, (a, b) in enumerate(((before, left), (left, right), (right, after))):
                        tap = 3 * (2 - t) + 2 - s
                        sums[tap] = sums[tap] + fold(low_act * a + high_act * b)
                made[0].append(even)
                made[1].append(odd)
            for px in range(2):
                grad = jnp.concatenate(made[px], axis=0) * slope_ref[places[px], :].astype(F32)
                out_ref[places[px], :] = grad.astype(BF16)
        return tuple(sums)

    sums = lax.fori_loop(0, HALF // 2, step, (jnp.zeros((8, BLOCK), F32),) * 9)
    cross_ref[72:88, :] = jnp.concatenate(
        [jnp.sum(s, axis=0, keepdims=True) for s in sums] + [jnp.zeros((7, BLOCK), F32)], axis=0
    )
    cross = dot(base_ref[...], out_ref[...], TN)
    cross_ref[0:72, :] = cross[0:72]
    first = cross[64:65]
    second = (jnp.sum(cross[0:64] * expand_ref[0:64, :].astype(F32), axis=0, keepdims=True) - mean1 * first) * inverse1
    sums_ref[...] = row8([second, first])


def depth_backward(mask, du, depth, vec, sums, bgram, base, expand_w, dw_norm, mb_depth, act, slope):
    col = lambda rows: pl.BlockSpec((rows, BLOCK), lambda j: (0, j))
    whole = lambda rows: pl.BlockSpec((rows, BLOCK), lambda j: (0, 0))
    s = jax.ShapeDtypeStruct
    return pl.pallas_call(
        depth_back_kernel,
        grid=(CHUNKS,),
        out_shape=(s((PLACES, EXPAND), BF16), s((88, EXPAND), F32), s((8, EXPAND), F32)),
        in_specs=[
            whole(PLACES), col(PLACES), col(PLACES), col(8), col(8), whole(72), whole(PLACES), col(128), col(2),
            col(9), col(PLACES), col(PLACES),
        ],
        out_specs=(col(PLACES), col(88), col(8)),
        scratch_shapes=[pltpu.VMEM((4, HALF + 2, HALF, BLOCK), F32)],
        compiler_params=params_of(56),
        cost_estimate=cost(35),
        name="depth_backward",
    )(mask, du, depth, vec, sums, bgram, base, expand_w, dw_norm, mb_depth, act, slope)


def stem_back_kernel(
    mask_ref, patch_ref, slope_ref, dbase_ref, du_ref, sum_ref, bgram_ref, base_ref, expand_ref, mid_ref, spread_ref,
    out_ref, total, rows_ref, hold,
):
    step = pl.program_id(0)

    @pl.when(step == 0)
    def _():
        count = bgram_ref[64:65, 64:65]
        mean, inverse = bn_stats(bgram_ref[...], expand_ref[...], count)
        second, first = sum_ref[0:1] / count, sum_ref[1:2] / count
        scale = mid_ref[0:1] * inverse
        slant = scale * inverse * second
        rows_ref[...] = row8([scale, slant, scale * first - slant * mean])
        total[...] = jnp.zeros_like(total)

    scale, slant, level = (rows_ref[k : k + 1] for k in range(3))
    x = dot(base_ref[...], expand_ref[...])
    inside = jnp.concatenate([mask_ref[...]] * CHUNKS, axis=1)
    grad = (scale * du_ref[...].astype(F32) - inside * (level + x * slant)).astype(BF16)
    grad = dot(grad, expand_ref[...], NT) + dbase_ref[...]
    grad = grad[:, 0:64] * (1.0 / 16.0)
    grad = jnp.concatenate([grad, grad], axis=1)
    grad = jnp.concatenate([grad, grad], axis=1)
    block = patch_ref[...]
    for j in range(4):
        cols = slice(256 * j, 256 * j + 256)
        wide = (slope_ref[:, cols].astype(F32) * grad).astype(BF16)
        total[:, cols] = total[:, cols] + dot(block, wide, TN)

    @pl.when(step == STEM_STEPS - 1)
    def _():
        merged = total[0:96, 0:256]
        for px in range(1, 4):
            merged = merged + total[64 * px : 64 * px + 96, 256 * px : 256 * px + 256]
        result = jnp.zeros((32, STEM_CH), F32)
        for pair in range(2):
            wide = dot(
                spread_ref[pair][0:96].astype(F32), merged[:, 128 * pair : 128 * pair + 128], TN, precision=HIGH
            )
            result = result + wide[0:32, 0:64] + wide[32:64, 64:128]
        ones = merged[27:28]
        ones = ones[:, 0:64] + ones[:, 64:128] + ones[:, 128:192] + ones[:, 192:256]
        at = lax.broadcasted_iota(jnp.int32, (32, STEM_CH), 0)
        out_ref[...] = pairs_together(jnp.where(at == 27, ones, result), hold)


def stem_backward(mask, patches, slope, dbase, du, sums, bgram, base, expand_w, mid_norm, spread):
    part = lambda width: pl.BlockSpec((STEM_BLOCK, width), lambda i: (i, 0))
    whole = lambda *shape: pl.BlockSpec(shape, lambda i: (0,) * len(shape))
    return pl.pallas_call(
        stem_back_kernel,
        grid=(STEM_STEPS,),
        out_shape=jax.ShapeDtypeStruct((16, 128), F32),
        in_specs=[
            part(128), part(TAPS), part(1024), part(128), part(EXPAND), whole(8, EXPAND), whole(72, 128), part(128),
            whole(128, EXPAND), whole(2, EXPAND), whole(8, TAPS, 64),
        ],
        out_specs=whole(16, 128),
        scratch_shapes=[
            pltpu.VMEM((TAPS, 1024), F32), pltpu.VMEM((8, EXPAND), F32), pltpu.VMEM((40, 128), F32),
        ],
        compiler_params=params_of(60),
        cost_estimate=cost(8),
        name="stem_backward",
    )(mask, patches, slope, dbase, du, sums, bgram, base, expand_w, mid_norm, spread)


def expand_finish_kernel(cross_ref, sum_ref, bgram_ref, expand_ref, mid_ref, out_ref, square_ref, flat, hold):
    count = bgram_ref[64:65, 64:65]
    square_of = jnp.concatenate([bgram_ref[...], jnp.zeros((56, 128), F32)], axis=0)
    weights = expand_ref[...].astype(F32)
    product = dot(square_of, weights, precision=HIGH)
    mean = product[64:65] / count
    variance = jnp.sum(weights * product, axis=0, keepdims=True) / count - mean * mean
    inverse = lax.rsqrt(variance + EPS)
    second, first = sum_ref[0:1] / count, sum_ref[1:2] / count
    plain = bgram_ref[0:64, 64:65]
    hat = (product[0:64] - mean * plain) * inverse
    hold[...] = mid_ref[0:1] * inverse * (cross_ref[0:64, :] - first * plain - second * hat)
    flat[...] = jnp.zeros_like(flat)
    for name, source in (("mb_expand", hold), ("mb_depth", cross_ref.at[72:88])):
        offset, (rows, width) = OFFSETS[name]
        put_matrix(flat, lambda r, t: source[r, 128 * t : 128 * t + 128], 0, offset, rows, width)
    out_ref[...] = flat[0:EARLY_ROWS, :]
    total = flat[0:EARLY_ROWS, :]
    square_ref[...] = jnp.broadcast_to(jnp.sum(total * total).reshape(1, 1), (8, 128))


def expand_finish(cross, sums, bgram, expand_w, mid_norm):
    return pl.pallas_call(
        expand_finish_kernel,
        out_shape=(jax.ShapeDtypeStruct((EARLY_ROWS, 128), F32), jax.ShapeDtypeStruct((8, 128), F32)),
        in_specs=[VMEM_SPEC] * 5,
        out_specs=(VMEM_SPEC,) * 2,
        scratch_shapes=[pltpu.VMEM((EARLY_ROWS + 8, 128), F32), pltpu.VMEM((STEM_CH, EXPAND), F32)],
        compiler_params=params_of(10),
        cost_estimate=cost(3),
        name="expand_finish",
    )(cross, sums, bgram, expand_w, mid_norm)


def finish_kernel(
    first_ref, packet_ref, stem_ref, spread_ref, early_ref, early_square_ref, shard_ref,
    out_ref, scalar_ref, big, hold, flat,
):
    weights, own_gain, _ = stem_params(stem_ref, hold)
    spread_weights(spread_ref, weights, big, 2)
    gram = stem_ref[0:96, 0:96]
    mean, square = stem_stats(stem_ref[0:96, :], big[0:96, 0:256])
    inverse = lax.rsqrt(square - mean * mean + EPS)
    count = 4.0 * stem_ref[27:28, 27:28]
    got = pairs_apart(packet_ref[0:16], hold)
    product = dot(gram, big[0:96, 0:256].astype(F32), precision=HIGH)
    cross = jnp.zeros((32, STEM_CH), F32)
    plain = jnp.zeros((32, STEM_CH), F32)
    sums = jnp.broadcast_to(gram[:, 27:28], (96, 128))
    for pair in range(2):
        spread = spread_ref[pair][0:96].astype(F32)
        wide = dot(spread, product[:, 128 * pair : 128 * pair + 128], TN, precision=HIGH)
        cross = cross + wide[0:32, 0:64] + wide[32:64, 64:128]
        wide = dot(spread, sums, TN, precision=HIGH)
        plain = plain + wide[0:32, 0:64] + wide[32:64, 0:64]
    at = lax.broadcasted_iota(jnp.int32, (32, STEM_CH), 0)
    taps = at < 27
    grad = jnp.where(taps, got, 0.0)
    first = got[27:28]
    second = (jnp.sum(grad * weights, axis=0, keepdims=True) - mean * first) * inverse
    hat = (cross - mean * plain) * inverse
    result = own_gain * inverse * (grad - (plain * first + hat * second) / count)
    result = jnp.where(taps, result, jnp.where(at == 27, second, jnp.where(at == 28, first, 0.0)))
    square = packet_ref[16:17, 1:2] + early_square_ref[0:1, 0:1] + jnp.sum(result * result).reshape(1, 1)
    norm = jnp.sqrt(square)
    lane = lax.broadcasted_iota(jnp.int32, (8, 128), 1)
    scale = CLIP / jnp.maximum(norm, CLIP)
    scalar_ref[...] = jnp.where(lane == 0, packet_ref[16:17, 0:1], jnp.where(lane == 1, norm, scale))
    both = pairs_together(result, hold)
    rows = shard_ref.shape[0]
    flat[0:16, :] = early_ref[0:16] + both
    flat[16:EARLY_ROWS, :] = early_ref[16:EARLY_ROWS]
    flat[EARLY_ROWS:, :] = jnp.zeros((flat.shape[0] - EARLY_ROWS, 128), F32)
    begin = jnp.minimum(first_ref[0] * rows, EARLY_ROWS)
    out_ref[...] = shard_ref[...] + flat[pl.ds(begin, rows), :]


def finish(me, packet, stem, spread, early, early_square, shard):
    rows = shard.shape[0]
    return pl.pallas_call(
        finish_kernel,
        out_shape=(jax.ShapeDtypeStruct((rows, 128), F32), jax.ShapeDtypeStruct((8, 128), F32)),
        in_specs=[SMEM_SPEC] + [VMEM_SPEC] * 6,
        out_specs=(VMEM_SPEC,) * 2,
        scratch_shapes=[
            pltpu.VMEM((TAPS, 256), BF16), pltpu.VMEM((40, 128), F32),
            pltpu.VMEM((round_up(EARLY_ROWS + rows, 8), 128), F32),
        ],
        compiler_params=params_of(10),
        cost_estimate=cost(4),
        name="finish",
    )(me, packet, stem, spread, early, early_square, shard)


def levels_of(devices):
    levels = []
    stride = 1
    while stride < devices:
        radix = 2 if stride == 1 or devices // stride == 2 else 4
        levels.append((stride, radix))
        stride *= radix
    return levels


def pairs_of(devices, mask):
    return [(i, i ^ mask) for i in range(devices)]


def add_level(v, moved):
    return v + moved[0] if len(moved) == 1 else (v + moved[0]) + (moved[1] + moved[2])


def send_level(v, devices, level):
    stride, radix = level
    return [lax.ppermute(v, "dp", pairs_of(devices, stride * j)) for j in range(1, radix)]


def exchange(v, devices, levels):
    for level in levels:
        v = add_level(v, send_level(v, devices, level))
    return v


def spread_blocks(blocks, masks, devices, level):
    stride, radix = level
    moved = send_level(blocks, devices, level)
    return jnp.concatenate([blocks] + moved), [m ^ (stride * j) for j in range(radix) for m in masks]


def take(blocks, digit, axis):
    return lax.dynamic_index_in_dim(blocks, digit, axis, keepdims=False)


class Scatter:
    def __init__(self, keep, send, devices, me, low, high):
        self.devices, self.me, self.low, self.high = devices, me, low, high
        self.levels = levels_of(devices)
        self.at = 0
        self.mine, self.parts = [keep], [send]
        self.moved = []

    def launch(self):
        stride, radix = self.levels[self.at]
        top = stride * radix == self.devices
        self.moved = []
        for j, part in zip(range(1, radix), self.parts):
            pairs = pairs_of(self.devices, stride * j)
            if top:
                pairs = [(a, b) for a, b in pairs if self.low <= b // stride < self.high]
            self.moved.append(lax.ppermute(part, "dp", pairs))

    def land(self):
        terms = self.mine + [m.astype(F32) for m in self.moved]
        self.at += 1
        if self.at == len(self.levels):
            total = sum(terms[1:], terms[0])
            self.result = total.reshape(total.shape[-2:])
            return
        if len(terms) > 2:
            terms = [sum(terms[1:], terms[0])]
        stride, radix = self.levels[self.at]
        digit = (self.me // stride) % radix
        span = self.high - self.low
        if stride * radix == self.devices:
            blocks = [t.reshape((span,) + t.shape[-2:]) for t in terms]
            part = lambda d: sum(take(b, jnp.clip(d - self.low, 0, span - 1), 0) for b in blocks)
            mine = jnp.where((digit >= self.low) & (digit < self.high), part(digit), 0.0)
        else:
            blocks = [t.reshape((-1, radix) + t.shape[-2:]) for t in terms]
            part = lambda d: sum(take(b, d, 1) for b in blocks)
            mine = part(digit)
        self.mine = [mine]
        self.parts = [part(digit ^ j).astype(BF16) for j in range(1, radix)]

    def finish(self):
        if not self.moved:
            self.launch()
        self.land()
        while self.at < len(self.levels):
            self.launch()
            self.land()
        return self.result


def tie(*values):
    return lax.optimization_barrier(values)


def on_device(images, res_ids, labels, rel_index, master, first_moment, second_moment, ema_weights):
    devices = lax.axis_size("dp")
    me = lax.axis_index("dp").astype(jnp.int32)
    length = master.shape[0]
    rows = length // 128
    held = round_up(rows, 16)
    images_total = res_ids.shape[0] * devices

    levels = levels_of(devices)
    low_master = lax.optimization_barrier(master.astype(BF16).reshape(rows, 128))
    blocks, masks = spread_blocks(jnp.pad(low_master, ((0, held - rows), (0, 0)))[None], [0], devices, levels[-1])
    stem_part = lax.dynamic_update_slice(
        jnp.zeros((16 + rows, 128), BF16), low_master, (jnp.minimum(me * rows, 16), 0)
    )[:16]
    patches, packet, mask = make_patches(res_ids, images, stem_part)
    packet, blocks = tie(packet, blocks)
    packet = exchange(packet, devices, levels[:-1])
    packet, blocks = tie(packet, blocks)
    for level in levels[-2:0:-1]:
        blocks, masks = spread_blocks(blocks, masks, devices, level)
    packet = exchange(packet, devices, levels[-1:])
    spread = jnp.asarray(spread_taps(), BF16)
    base, stem_slope, bgram = stem_forward(patches, packet, spread)
    stem_packet = packet
    bgram, blocks = tie(bgram, blocks)
    others = lax.ppermute(blocks, "dp", pairs_of(devices, 1))
    bgram = exchange(bgram, devices, levels[:-1])
    bgram, others = tie(bgram, others)
    sent = send_level(bgram, devices, levels[-1])
    p = unpack([blocks, others], me.reshape(1), masks + [m ^ 1 for m in masks], rows, ALL_SHAPES)
    bgram = add_level(bgram, sent)
    depth, act1, slope1, stat = depth_forward(mask, base, p["mb_expand"], bgram, p["mid_norm"], p["mb_depth"])
    stat = exchange(stat, devices, levels)
    slots = slots_of(rel_index)
    slots = jnp.pad(slots, ((0, 1), (0, 1)), constant_values=2 * WIDE - 1).reshape(2 * WIDE, 1)
    pick = squeeze_lanes()
    pick, pick_back = jnp.asarray(pick, BF16), jnp.asarray(pick.T, BF16)
    bias = build_bias(p["rel_table"], slots, pick)

    act2, slope2, block, skipped, normed, project, vec, small = excite_forward(res_ids, mask, depth, stat, bgram, base, p)
    blended, weights = attend_forward(res_ids, project, bias)
    loss, dblend, dskip, g_short, g_out, g_out_b, g_mnorm, g_in, g_in_b, vectors, few = mlp_both(
        1.0 / images_total, res_ids, labels, skipped, blended, p
    )

    core = (me % 2).reshape(1)
    top_radix = levels_of(devices)[-1][1]

    def scattered(grads, begin, end):
        span = devices // top_radix
        low = begin // length // span
        high = (end - 1) // length // span + 1
        keep, send = pack(core, grads, low * span * rows, (high - low) * span, rows, held)
        return Scatter(keep, send, devices, me, low, high)

    middle = scattered(
        {
            "attn_out": g_out, "out_bias": g_out_b, "mlp_norm": g_mnorm, "mlp_in": g_in, "mlp_in_bias": g_in_b,
        },
        OFFSETS["attn_out"][0], OFFSETS["mlp_out"][0],
    )
    dblend, middle.parts = tie(dblend, middle.parts)
    middle.launch()
    vectors = lax.all_gather(vectors, "dp", axis=0, tiled=False)

    dq, dk, dv, g_table = attend_backward(project, blended, dblend, weights, slots, pick_back)
    dq, middle.moved = tie(dq, middle.moved)
    middle.land()
    dq, middle.parts = tie(dq, middle.parts)
    middle.launch()
    g_qkv, g_pre, dblock, g_proj, g_mbshort, dbase, g_down, g_down_b, g_up, g_up_b, dpool = proj_backward(
        res_ids, dq, dk, dv, normed, dskip, block, act2, vec, small, base, p
    )
    late = scattered(
        {
            "mb_short": g_mbshort, "se_down": g_down, "se_down_bias": g_down_b, "se_up": g_up, "se_up_bias": g_up_b,
            "mb_proj": g_proj, "at_short": g_short, "pre_norm": g_pre, "qkv": g_qkv, "rel_table": g_table,
        },
        OFFSETS["mb_short"][0], OFFSETS["mlp_norm"][0],
    )
    dblock, late.parts, middle.moved = tie(dblock, late.parts, middle.moved)
    late.launch()
    middle.land()
    dblock, middle.parts = tie(dblock, middle.parts)
    middle.launch()
    du, sums = excite_backward(dblock, p["mb_proj"], vec, dpool, few, slope2, depth)
    sums, late.moved, middle.moved = tie(sums, late.moved, middle.moved)
    late.land()
    sums, late.parts = tie(sums, late.parts)
    late.launch()
    dw_sums = exchange(sums, devices, levels)
    dw_sums, late.moved = tie(dw_sums, late.moved)
    late.land()
    dw_sums, late.parts = tie(dw_sums, late.parts)
    late.launch()
    du, cross, sums = depth_backward(
        mask, du, depth, vec, dw_sums, bgram, base, p["mb_expand"], p["dw_norm"], p["mb_depth"], act1, slope1
    )
    sums, late.moved = tie(sums, late.moved)
    steps = [(1 << k, 2) for k in range(devices.bit_length() - 1)]
    sent = send_level(cross, devices, steps[0])
    mid_sums = exchange(sums, devices, levels[:-1])
    mid_sums, sent = tie(mid_sums, sent)
    cross = add_level(cross, sent)
    moved = send_level(mid_sums, devices, levels[-1])
    sent = send_level(cross, devices, steps[1])
    mid_sums, sent = tie(add_level(mid_sums, moved), sent)
    cross = add_level(cross, sent)
    mid_sums, cross = tie(mid_sums, cross)
    sent = send_level(cross, devices, steps[2])
    stem = stem_backward(
        mask, patches, stem_slope, dbase, du, mid_sums, bgram, base, p["mb_expand"], p["mid_norm"], spread
    )
    stem, sent, late.moved = tie(stem, sent, late.moved)
    cross = add_level(cross, sent)
    stem, cross = tie(stem, cross)
    sent = send_level(cross, devices, steps[3])
    shard, packet = shard_parts(
        me.reshape(1), length, late.finish(), middle.finish(), dw_sums, mid_sums, vectors, stem, loss
    )
    packet, sent = tie(packet, sent)
    cross = add_level(cross, sent)
    cross, packet = tie(cross, packet)
    cross = exchange(cross, devices, steps[4:])
    packet = exchange(packet, devices, levels)
    early_grad, early_square = expand_finish(cross, mid_sums, bgram, p["mb_expand"], p["mid_norm"])
    shard, scalars = finish(
        me.reshape(1), packet, stem_packet, spread, early_grad, early_square, shard
    )
    loss_sum, grad_norm = scalars[0, 0], scalars[0, 1]
    shard = shard.reshape(length)
    clipped = shard * scalars[0, 2]
    moment_one = BETA_ONE * first_moment + (1.0 - BETA_ONE) * clipped
    moment_two = BETA_TWO * second_moment + (1.0 - BETA_TWO) * clipped * clipped
    update = (
        moment_one
        / (1.0 - BETA_ONE**STEP)
        / (jnp.sqrt(moment_two / (1.0 - BETA_TWO**STEP)) + ADAM_EPS)
    )
    weights_out = master - RATE * (update + DECAY * master)
    averaged = EMA_DECAY * ema_weights + (1.0 - EMA_DECAY) * weights_out
    return (
        loss_sum,
        grad_norm,
        weights_out,
        moment_one,
        moment_two,
        averaged,
        weights_out.astype(BF16),
    )


def solution(mesh):
    in_specs = (
        P("dp", None, None, None),
        P("dp"),
        P("dp"),
        P(),
        P("dp"),
        P("dp"),
        P("dp"),
        P("dp"),
    )
    out_specs = (P(), P(), P("dp"), P("dp"), P("dp"), P("dp"), P("dp"))
    return jax.shard_map(
        on_device, mesh=mesh, in_specs=in_specs, out_specs=out_specs, check_vma=False
    )
```

```python
import functools
import math

import jax
import jax.numpy as jnp
import numpy as np
from jax import lax
from jax.experimental import pallas as pl
from jax.experimental.pallas import tpu as pltpu
from jax.sharding import PartitionSpec as P

STEM_CH = 64
MB_CH = 192
EXPAND = 768
SQUEEZE = 48
DIM = 384
HEADS = 12
HEAD_DIM = 32
MLP = 1536
CLASSES = 1000
CANVAS = 384
SMALL_RES = 224
STEP = 10

EPS = 1e-05
CLIP = 0.05
BETA_ONE = 0.5
BETA_TWO = 0.5
ADAM_EPS = 1e-08
RATE = 0.05
DECAY = 0.05
EMA_DECAY = 0.9
SMOOTH = 0.1

SIDE = CANVAS // 8
SMALL_SIDE = SMALL_RES // 8
HALF = SIDE // 2
QUAD = HALF * HALF
PLACES = SIDE * SIDE
TAPS = 288
BLOCK = 128
CHUNKS = EXPAND // BLOCK
WIDE = 2 * HALF * HALF
TOKENS = QUAD

F32 = jnp.float32
BF16 = jnp.bfloat16
HIGH = lax.Precision.HIGHEST
GELU_A = math.sqrt(2.0 / math.pi)
GELU_B = 0.044715


def layout():
    table_slots = (2 * (CANVAS // 16) - 1) ** 2
    return [
        ("stem_w", (3, 3, 3, STEM_CH)),
        ("stem_norm", (2, STEM_CH)),
        ("mb_short", (STEM_CH, MB_CH)),
        ("mb_expand", (STEM_CH, EXPAND)),
        ("mid_norm", (2, EXPAND)),
        ("mb_depth", (9, EXPAND)),
        ("dw_norm", (2, EXPAND)),
        ("se_down", (EXPAND, SQUEEZE)),
        ("se_down_bias", (SQUEEZE,)),
        ("se_up", (SQUEEZE, EXPAND)),
        ("se_up_bias", (EXPAND,)),
        ("mb_proj", (EXPAND, MB_CH)),
        ("at_short", (MB_CH, DIM)),
        ("pre_norm", (2, MB_CH)),
        ("qkv", (MB_CH, 3 * DIM)),
        ("attn_out", (DIM, DIM)),
        ("out_bias", (DIM,)),
        ("rel_table", (HEADS, table_slots)),
        ("mlp_norm", (2, DIM)),
        ("mlp_in", (DIM, MLP)),
        ("mlp_in_bias", (MLP,)),
        ("mlp_out", (MLP, DIM)),
        ("mlp_out_bias", (DIM,)),
        ("head_norm", (2, DIM)),
        ("head_w", (DIM, CLASSES)),
        ("head_bias", (CLASSES,)),
    ]


def offsets():
    table = {}
    offset = 0
    for name, shape in layout():
        table[name] = (offset, shape)
        offset += math.prod(shape)
    return table


OFFSETS = offsets()
STEM_END = OFFSETS["mb_short"][0]
EARLY_END = OFFSETS["se_down"][0]


def dot(a, b, dims=((1,), (0,)), precision=None):
    return lax.dot_general(a, b, (dims, ((), ())), precision=precision, preferred_element_type=F32)


NT = ((1,), (1,))
TN = ((0,), (0,))


def gelu_pair(u):
    sq = u * u
    t = jnp.tanh(u * (GELU_A + (GELU_A * GELU_B) * sq))
    half = 0.5 + 0.5 * t
    slope = half + (0.5 * u) * (1.0 - t * t) * (GELU_A + (3.0 * GELU_A * GELU_B) * sq)
    return u * half, slope


def gelu(u):
    sq = u * u
    t = jnp.tanh(u * (GELU_A + (GELU_A * GELU_B) * sq))
    return u * (0.5 + 0.5 * t)


def limit_of(res_ref):
    return jnp.where(res_ref[0] == 1, SIDE, SMALL_SIDE)


def group_mask(group, limit, first_row, rows, lanes):
    place = lax.broadcasted_iota(jnp.int32, (rows, lanes), 0) + first_row
    up = place // HALF
    across = place - up * HALF
    y = 2 * up + group // 2
    x = 2 * across + group % 2
    return jnp.where((y < limit) & (x < limit), 1.0, 0.0)


def cost(us):
    return pl.CostEstimate(flops=int(us * 2.0e9), bytes_accessed=1000, transcendentals=0)


def params_of(megabytes):
    return pltpu.CompilerParams(vmem_limit_bytes=megabytes * 1024 * 1024)


SMEM_SPEC = pl.BlockSpec(memory_space=pltpu.SMEM)
VMEM_SPEC = pl.BlockSpec(memory_space=pltpu.VMEM)


def patch_kernel(res_ref, img_ref, stem_ref, patch_ref, packet_ref, mask_ref):
    limit = limit_of(res_ref)
    lane = lax.broadcasted_iota(jnp.int32, (32, CANVAS), 1)
    rem = lane % 8
    row = lax.broadcasted_iota(jnp.int32, (SIDE, CANVAS), 0)
    col = lax.broadcasted_iota(jnp.int32, (SIDE, CANVAS), 1)
    wanted = jnp.where(row < HALF, 2 * row, 2 * (row - HALF) + 1)
    pick = jnp.where(col // 8 == wanted, 1.0, 0.0).astype(BF16)
    sub = lax.broadcasted_iota(jnp.int32, (8, CANVAS), 0)
    tap = lax.broadcasted_iota(jnp.int32, (2 * HALF, TAPS), 1)
    ones_at = (tap % 64 == 27) & (tap < 256)

    def step(i, _):
        bands = [[], [], [], []]
        above = []
        for c in range(3):
            before = img_ref[0, c, pl.ds(pl.multiple_of(jnp.maximum(32 * i - 16, 0), 16), 16), :]
            above.append(jnp.where(i > 0, before.astype(F32)[8:16], 0.0))
            for q in range(2):
                band = img_ref[0, c, pl.ds(pl.multiple_of(32 * i + 16 * q, 16), 16), :].astype(F32)
                bands[2 * q].append(band[0:8])
                bands[2 * q + 1].append(band[8:16])
        made = []
        for q in range(4):
            prev = above if q == 0 else bands[q - 1]
            edge = jnp.zeros((8, CANVAS), F32)
            for c in range(3):
                edge = jnp.where(sub == c, prev[c][7:8], edge)
            rows = jnp.concatenate(bands[q] + [edge], axis=0)
            rolled = pltpu.roll(rows, 8, 1)
            pieces = [jnp.where((rem == 7) & (lane >= 8), rolled, 0.0)]
            pieces += [jnp.where(rem == r, rows, 0.0) for r in range(8)]
            wide = jnp.concatenate(pieces, axis=0).astype(BF16)
            made.append(dot(pick, wide, NT))
        for py in range(2):
            for px in range(2):
                group = 2 * py + px
                two = jnp.concatenate(
                    [made[py][HALF * px : HALF * px + HALF], made[2 + py][HALF * px : HALF * px + HALF]],
                    axis=0,
                )
                inside = group_mask(group, limit, 2 * HALF * i, 2 * HALF, 128)
                mask_ref[pl.ds(pl.multiple_of(group * QUAD + 2 * HALF * i, 16), 2 * HALF), :] = inside
                two = jnp.where(ones_at, 1.0, two) * inside[:, 0:1]
                patch_ref[pl.ds(pl.multiple_of(group * QUAD + 2 * HALF * i, 16), 2 * HALF), :] = (
                    two.astype(BF16)
                )
        return 0

    lax.fori_loop(0, HALF // 2, step, 0, unroll=3)
    patches = patch_ref[...]
    gram = dot(patches, patches, TN)
    total = gram[0:96, 0:96]
    for px in range(1, 4):
        total = total + gram[64 * px : 64 * px + 96, 64 * px : 64 * px + 96]
    packet_ref[0:96, :] = jnp.concatenate([total, jnp.zeros((96, 32), F32)], axis=1)
    packet_ref[96:112, :] = stem_ref[...].astype(F32)


def make_patches(res_ids, images, stem):
    return pl.pallas_call(
        patch_kernel,
        out_shape=(
            jax.ShapeDtypeStruct((PLACES, TAPS), BF16),
            jax.ShapeDtypeStruct((112, 128), F32),
            jax.ShapeDtypeStruct((PLACES, 128), F32),
        ),
        in_specs=[SMEM_SPEC, VMEM_SPEC, VMEM_SPEC],
        out_specs=(VMEM_SPEC,) * 3,
        compiler_params=params_of(16),
        cost_estimate=cost(8),
        name="patches",
    )(res_ids, images, stem)


def spread_taps():
    table = np.zeros((8, TAPS, 64), np.float32)
    for px in range(4):
        for py in range(4):
            pair, half = px * 2 + py // 2, py % 2
            for dy in range(3):
                for dx in range(3):
                    for c in range(3):
                        ry = 2 * py + dy - 1
                        r = 24 + c if ry < 0 else 8 * c + ry
                        k = (2 * px + dx) * 32 + r
                        table[pair, k, half * 32 + (dy * 3 + dx) * 3 + c] = 1.0
    return table


def spread_weights(spread_ref, stem_w, out_ref, pairs=8):
    zero = jnp.zeros((32, STEM_CH), F32)
    double = jnp.concatenate(
        [jnp.concatenate([stem_w, zero], axis=1), jnp.concatenate([zero, stem_w], axis=1)], axis=0
    ).astype(BF16)
    for pair in range(pairs):
        out_ref[:, 128 * pair : 128 * pair + 128] = dot(spread_ref[pair], double).astype(BF16)


def stem_stats(gram, first_phases):
    weights = first_phases.astype(F32)
    product = dot(gram[:, :96], weights, precision=HIGH)
    second = jnp.sum(weights * product, axis=0, keepdims=True)
    first = product[27:28]
    count = 4.0 * gram[27:28, 27:28]
    both = jnp.concatenate([first, second, jnp.zeros((6, 256), F32)], axis=0)
    folded = both[:, 0:64] + both[:, 64:128] + both[:, 128:192] + both[:, 192:256]
    return folded[0:1] / count, folded[1:2] / count


def pairs_apart(rows, hold):
    hold[pl.ds(0, 16, stride=2), :] = rows
    hold[pl.ds(1, 16, stride=2), :] = pltpu.roll(rows, 64, 1)
    return hold[0:32, 0:64]


def pairs_together(rows, hold):
    hold[0:32, 0:64] = rows
    lane = lax.broadcasted_iota(jnp.int32, (16, 128), 1)
    return jnp.where(
        lane < 64, hold[pl.ds(0, 16, stride=2), :], pltpu.roll(hold[pl.ds(1, 16, stride=2), :], 64, 1)
    )


def stem_params(packet_ref, hold):
    rows = pairs_apart(packet_ref[96:112, :], hold)
    at = lax.broadcasted_iota(jnp.int32, (32, STEM_CH), 0)
    return jnp.where(at < 27, rows, 0.0), rows[27:28], rows[28:29]


STEM_STEPS = 3
STEM_BLOCK = PLACES // STEM_STEPS


def stem_kernel(patch_ref, packet_ref, spread_ref, base_ref, slope_ref, bgram_ref, big, hold, norm):
    @pl.when(pl.program_id(0) == 0)
    def _():
        weights, gain, shift = stem_params(packet_ref, hold)
        spread_weights(spread_ref, weights, big)
        mean, square = stem_stats(packet_ref[0:96, :], big[0:96, 0:256])
        gain = gain * lax.rsqrt(square - mean * mean + EPS)
        shift = shift - mean * gain
        norm[0:1, :] = jnp.concatenate([gain] * 4, axis=1)
        norm[1:2, :] = jnp.concatenate([shift] * 4, axis=1)
        bgram_ref[...] = jnp.zeros_like(bgram_ref)

    gain, shift = norm[0:1, :], norm[1:2, :]
    lane = lax.broadcasted_iota(jnp.int32, (STEM_BLOCK, 128), 1)
    block = patch_ref[...]
    pooled = jnp.zeros((STEM_BLOCK, 128), F32)
    for j in range(4):
        u = dot(block, big[:, 256 * j : 256 * j + 256]) * gain + shift
        value, slope = gelu_pair(u)
        slope_ref[:, 256 * j : 256 * j + 256] = slope.astype(BF16)
        pooled = pooled + value[:, 0:128] + value[:, 128:256]
    pooled = (pooled + pltpu.roll(pooled, 64, 1)) * (1.0 / 16.0)
    ones = block[:, 0:128].astype(F32)
    ones = pltpu.roll(ones, 64 - 27, 1)
    pooled = jnp.where(lane < 64, pooled, jnp.where(lane == 64, ones, 0.0)).astype(BF16)
    base_ref[...] = pooled
    masked = (pooled.astype(F32) * pooled[:, 64:65].astype(F32)).astype(BF16)
    bgram_ref[...] = bgram_ref[...] + dot(masked, pooled, TN)[0:72]


def stem_forward(patches, packet, spread):
    part = lambda width: pl.BlockSpec((STEM_BLOCK, width), lambda i: (i, 0))
    whole = lambda shape: pl.BlockSpec(shape, lambda i: (0,) * len(shape))
    return pl.pallas_call(
        stem_kernel,
        grid=(STEM_STEPS,),
        out_shape=(
            jax.ShapeDtypeStruct((PLACES, 128), BF16),
            jax.ShapeDtypeStruct((PLACES, 1024), BF16),
            jax.ShapeDtypeStruct((72, 128), F32),
        ),
        in_specs=[part(TAPS), whole((112, 128)), whole((8, TAPS, 64))],
        out_specs=(part(128), part(1024), whole((72, 128))),
        scratch_shapes=[
            pltpu.VMEM((TAPS, 1024), BF16), pltpu.VMEM((40, 128), F32), pltpu.VMEM((8, 256), F32),
        ],
        compiler_params=params_of(28),
        cost_estimate=cost(10),
        name="stem_forward",
    )(patches, packet, spread)


def taps_row(load, weight, py):
    sources = [(1, -1), (0, 0), (1, 0)] if py == 0 else [(0, 0), (1, 0), (0, 1)]
    rows = [[load(2 * gy + px, off) for px in range(2)] for gy, off in sources]

    def column(px, dx):
        total = rows[0][px] * weight(0, dx)
        total = total + rows[1][px] * weight(1, dx)
        return total + rows[2][px] * weight(2, dx)

    even = column(0, 1) + column(1, 2) + shift_down(column(1, 0))
    odd = column(1, 1) + column(0, 0) + shift_up(column(0, 2))
    return even, odd


def shift_down(v):
    at = lax.broadcasted_iota(jnp.int32, v.shape, 0)
    return jnp.where(at == 0, 0.0, pltpu.roll(v, 1, 0))


def shift_up(v):
    at = lax.broadcasted_iota(jnp.int32, v.shape, 0)
    return jnp.where(at == HALF - 1, 0.0, pltpu.roll(v, HALF - 1, 0))


def bn_stats(bgram, expand_w, count):
    weights = expand_w.astype(F32)
    square_of = jnp.concatenate([bgram, jnp.zeros((56, 128), F32)], axis=0)
    product = dot(square_of, weights, precision=HIGH)
    mean = product[64:65] / count
    second = jnp.sum(weights * product, axis=0, keepdims=True) / count
    return mean, lax.rsqrt(second - mean * mean + EPS)


def depth_kernel(mask_ref, base_ref, expand_ref, bgram_ref, norm_ref, depth_ref, out_ref, act_ref, slope_ref, stat_ref, pad, wide):
    count = bgram_ref[64:65, 64:65]
    mean, inverse = bn_stats(bgram_ref[...], expand_ref[...], count)
    gain = norm_ref[0:1] * inverse
    shift = norm_ref[1:2] - mean * gain
    zero = jnp.zeros((4, 1, HALF, BLOCK), F32)
    pad[:, 0:1] = zero
    pad[:, HALF + 1 : HALF + 2] = zero
    wide[...] = dot(base_ref[...], expand_ref[...])
    rows = 8 * HALF
    for group in range(4):

        def fill(i, _, group=group):
            first = pl.multiple_of(group * QUAD + rows * i, 16)
            at = pl.ds(first, rows)
            x = wide[at, :]
            inside = mask_ref[at, :]
            value, slope = gelu_pair(x * gain + shift)
            value = value * inside
            act_ref[at, :] = value.astype(BF16)
            slope_ref[at, :] = (slope * inside).astype(BF16)
            for k in range(8):
                pad[group, 8 * i + k + 1] = value[HALF * k : HALF * k + HALF]
            return 0

        lax.fori_loop(0, QUAD // rows, fill, 0)

    def weight(dy, dx):
        return depth_ref[3 * dy + dx : 3 * dy + dx + 1]

    def fold(v):
        return v[0:8] + v[8:16] + v[16:24]

    def step(up, sums):
        first, second = sums
        for py in range(2):
            made = taps_row(lambda g, off: pad[g, up + 1 + off], weight, py)
            for px in range(2):
                at = pl.ds(pl.multiple_of((2 * py + px) * QUAD + HALF * up, 8), HALF)
                x = made[px] * mask_ref[at, :]
                out_ref[at, :] = x
                first = first + fold(x)
                second = second + fold(x * x)
        return first, second

    sums = lax.fori_loop(0, HALF, step, (jnp.zeros((8, BLOCK), F32),) * 2, unroll=4)
    rows_out = [jnp.sum(s, axis=0, keepdims=True) for s in sums]
    stat_ref[...] = jnp.concatenate(rows_out + [jnp.zeros((6, BLOCK), F32)], axis=0)


def depth_forward(mask, base, expand_w, bgram, mid_norm, mb_depth):
    col = lambda rows: pl.BlockSpec((rows, BLOCK), lambda j: (0, j))
    whole = lambda rows: pl.BlockSpec((rows, BLOCK), lambda j: (0, 0))
    return pl.pallas_call(
        depth_kernel,
        grid=(CHUNKS,),
        out_shape=(
            jax.ShapeDtypeStruct((PLACES, EXPAND), F32),
            jax.ShapeDtypeStruct((PLACES, EXPAND), BF16),
            jax.ShapeDtypeStruct((PLACES, EXPAND), BF16),
            jax.ShapeDtypeStruct((8, EXPAND), F32),
        ),
        in_specs=[whole(PLACES), whole(PLACES), col(128), whole(72), col(2), col(9)],
        out_specs=(col(PLACES),) * 3 + (col(8),),
        scratch_shapes=[pltpu.VMEM((4, HALF + 2, HALF, BLOCK), F32), pltpu.VMEM((PLACES, BLOCK), F32)],
        compiler_params=params_of(56),
        cost_estimate=cost(25),
        name="depth_forward",
    )(mask, base, expand_w, bgram, mid_norm, mb_depth)


EARLY_ROWS = 576
STEM_ROWS = 15


def runs_of(offset, rows, width):
    period = min(128 // math.gcd(width, 128), rows)
    stride = period * width // 128 if rows > period else 1
    for j in range(period):
        start = offset + j * width
        yield j, period, start // 128, start % 128, -(-(rows - j) // period), stride


def rows_at(first, count, stride):
    return pl.ds(first, count) if stride == 1 or count == 1 else pl.ds(first, count, stride=stride)


def chunks_of(count, size=128):
    for begin in range(0, count, size):
        yield begin, min(size, count - begin)


def round_up(n, m):
    return -(-n // m) * m


def take_matrix(flat, out_ref, hold, offset, rows, width):
    direct = True
    for j, period, first, shift, count, stride in runs_of(offset, rows, width):
        direct = period == 1
        for t in range(-(-width // 128)):
            wide = min(128, width - 128 * t)
            for begin, size in chunks_of(count):
                at = first + t + begin * stride
                value = flat[rows_at(at, size, stride), :]
                if shift:
                    if shift + wide > 128:
                        lane = lax.broadcasted_iota(jnp.int32, (size, 128), 1)
                        value = jnp.where(lane >= shift, value, flat[rows_at(at + 1, size, stride), :])
                    value = pltpu.roll(value, 128 - shift, 1)
                if direct:
                    out_ref[begin : begin + size, 128 * t : 128 * t + wide] = value[:, :wide].astype(out_ref.dtype)
                elif count == 1:
                    out_ref[j : j + 1, 128 * t : 128 * t + wide] = value[:, :wide].astype(out_ref.dtype)
                else:
                    hold[t, rows_at(j + begin * period, size, period), :] = value
    if not direct and count > 1:
        for t in range(-(-width // 128)):
            wide = min(128, width - 128 * t)
            out_ref[0:rows, 128 * t : 128 * t + wide] = hold[t, 0:rows, 0:wide].astype(out_ref.dtype)


def put_matrix(flat, value_of, base, offset, rows, width):
    for j, period, first, shift, count, stride in runs_of(offset, rows, width):
        tiles = -(-width // 128)
        for begin, size in chunks_of(count):
            before = None
            lane = lax.broadcasted_iota(jnp.int32, (size, 128), 1)
            picked = rows_at(j + begin * period, size, period)
            at = first - base + begin * stride
            for t in range(tiles):
                value = value_of(picked, t)
                if shift:
                    value = pltpu.roll(value, shift, 1)
                    mixed = jnp.where(lane >= shift, value, 0.0 if before is None else before)
                else:
                    mixed = value
                before = value
                where = rows_at(at + t, size, stride)
                full = 0 < t < tiles - 1 or (shift == 0 and width % 128 == 0)
                flat[where, :] = mixed if full else flat[where, :] + mixed
            if shift:
                where = rows_at(at + tiles, size, stride)
                flat[where, :] = flat[where, :] + jnp.where(lane < shift, before, 0.0)


def unpack_kernel(names, shapes, pieces, shard_rows, me_ref, masks_ref, *refs):
    blocks, outs, (flat, hold) = refs[:pieces], refs[pieces:-2], refs[-2:]
    base = 0
    for block in blocks:

        def place(k, _, block=block, base=base):
            where = pl.ds((masks_ref[base + k] ^ me_ref[0]) * shard_rows, shard_rows)
            flat[where, :] = block[k].astype(F32)[:shard_rows]
            return 0

        lax.fori_loop(0, block.shape[0], place, 0)
        base += block.shape[0]
    for name, shape, out in zip(names, shapes, outs):
        offset, own = OFFSETS[name]
        width = own[-1]
        rows = math.prod(own) // width
        if shape[0][0] > rows or shape[0][1] > width:
            out[...] = jnp.zeros_like(out)
        take_matrix(flat, out, hold, offset, rows, width)


def unpack(blocks, me, masks, shard_rows, shapes):
    names = tuple(shapes)
    kinds = tuple(shapes[n] for n in names)
    total = sum(b.shape[0] for b in blocks) * shard_rows + 136
    made = pl.pallas_call(
        functools.partial(unpack_kernel, names, kinds, len(blocks), shard_rows),
        out_shape=tuple(jax.ShapeDtypeStruct(*k) for k in kinds),
        in_specs=[SMEM_SPEC] * 2 + [VMEM_SPEC] * len(blocks),
        out_specs=(VMEM_SPEC,) * len(names),
        scratch_shapes=[pltpu.VMEM((total, 128), F32), pltpu.VMEM((8, EXPAND + 16, 128), F32)],
        compiler_params=params_of(60),
        cost_estimate=cost(6),
        name="unpack",
    )(me, jnp.asarray(masks, jnp.int32), *blocks)
    return dict(zip(names, made))


EARLY_SHAPES = {
    "mb_short": ((128, MB_CH), BF16), "mb_expand": ((128, EXPAND), BF16), "mid_norm": ((2, EXPAND), F32),
    "mb_depth": ((9, EXPAND), F32), "dw_norm": ((2, EXPAND), F32),
}
LATE_SHAPES = {
    "se_down": ((EXPAND, SQUEEZE), BF16), "se_down_bias": ((1, SQUEEZE), F32), "se_up": ((SQUEEZE, EXPAND), BF16),
    "se_up_bias": ((1, EXPAND), F32), "mb_proj": ((EXPAND, MB_CH), BF16), "at_short": ((MB_CH, DIM), BF16),
    "pre_norm": ((2, MB_CH), F32), "qkv": ((MB_CH, 3 * DIM), BF16), "attn_out": ((DIM, DIM), BF16),
    "out_bias": ((1, DIM), F32), "rel_table": ((16, 2 * WIDE), F32), "mlp_norm": ((2, DIM), F32),
    "mlp_in": ((DIM, MLP), BF16), "mlp_in_bias": ((1, MLP), F32), "mlp_out": ((MLP, DIM), BF16),
    "mlp_out_bias": ((1, DIM), F32), "head_norm": ((2, DIM), F32), "head_w": ((DIM, CLASSES), BF16),
    "head_bias": ((1, CLASSES), F32),
}


ALL_SHAPES = EARLY_SHAPES | LATE_SHAPES


def pack_kernel(names, base, shards, shard_rows, core_ref, *refs):
    grads, (keep_ref, send_ref), (flat, hold) = refs[: len(names)], refs[len(names) : -2], refs[-2:]
    rows_all = flat.shape[0]
    step = 384

    def clear(i, _):
        flat[pl.ds(pl.multiple_of(i * step, 8), step), :] = jnp.zeros((step, 128), F32)
        return 0

    lax.fori_loop(0, rows_all // step, clear, 0)
    for name, grad in zip(names, grads):
        offset, own = OFFSETS[name]
        width = own[-1]
        rows = math.prod(own) // width
        tiles = -(-width // 128)
        read = lambda r, t: grad[r, 128 * t : 128 * t + 128]
        if grad.shape[1] < 128 * tiles:
            hold[tiles - 1, 0:rows, :] = jnp.zeros((rows, 128), F32)
            for t in range(tiles):
                wide = min(128, width - 128 * t)
                hold[t, 0:rows, 0:wide] = grad[0:rows, 128 * t : 128 * t + wide]
            read = lambda r, t: hold[t, r, :]
        put_matrix(flat, read, base, offset, rows, width)

    def share(k, _):
        block = flat[pl.ds(k * shard_rows, shard_rows), :]
        ours = k % 2 == core_ref[0]

        @pl.when(ours)
        def _():
            keep_ref[k // 2, 0:shard_rows] = block

        @pl.when(jnp.logical_not(ours))
        def _():
            send_ref[k // 2, 0:shard_rows] = block

        return 0

    lax.fori_loop(0, shards, share, 0)


def pack(core, grads, base, shards, shard_rows, held_rows):
    names = tuple(grads)
    total = -(-(shards * shard_rows + 8) // 384) * 384
    out = jax.ShapeDtypeStruct((shards // 2, held_rows, 128), F32)
    return pl.pallas_call(
        functools.partial(pack_kernel, names, base, shards, shard_rows),
        out_shape=(out, out),
        in_specs=[SMEM_SPEC] + [VMEM_SPEC] * len(names),
        out_specs=(VMEM_SPEC,) * 2,
        scratch_shapes=[pltpu.VMEM((total, 128), F32), pltpu.VMEM((2, EXPAND + 16, 128), F32)],
        compiler_params=params_of(32),
        cost_estimate=cost(6),
        name="pack",
    )(core, *grads.values())


def shard_kernel(
    length, tall_out, tall_head, first_ref, late_ref, mid_ref, dw_ref, norm_ref, vector_ref, stem_ref, loss_ref,
    out_ref, packet_ref, flat, hold, left_out, left_head,
):
    rows = length // 128
    lead = 16
    flat[...] = jnp.zeros_like(flat)
    start = first_ref[0] * length
    lane = lax.broadcasted_iota(jnp.int32, (8, 128), 1)

    def add_rows(first, value):
        flat[pl.ds(first, value.shape[0]), :] = flat[pl.ds(first, value.shape[0]), :] + value

    devices = vector_ref.shape[0]
    part = min(devices, 128)

    def place(name, left_ref, at_left, at_right, tall):
        offset, (count, width) = OFFSETS[name]
        first = (start - offset + 2**20 * width) // width - 2**20
        inside = (first > -tall) & (first < count)
        held = jnp.where(inside, first, -tall)
        made = jnp.zeros((tall, 128 * -(-width // 128)), F32)
        for g in range(devices // part):
            group = slice(g * part, g * part + part)
            left_ref[g] = jnp.zeros_like(left_ref[g])
            left_ref[g, tall : tall + count, :] = vector_ref[group, at_left, 0:count].T
            right = vector_ref[group, at_right, 0 : hold.shape[2] * -(-width // 128)]
            made = made + dot(left_ref[g, pl.ds(held + tall, tall), :], right, precision=HIGH)
        tiles = -(-width // 128)
        for t in range(tiles):
            wide = min(128, made.shape[1] - 128 * t)
            hold[t, 0:tall, 0:wide] = made[:, 128 * t : 128 * t + wide]
        period = 128 // math.gcd(width, 128)
        stride = period * width // 128

        @pl.when(inside)
        def _():
            for j in range(period):
                begin = offset + (first + j) * width - start + 128 * lead
                row = begin // 128
                shift = begin - row * 128
                size = tall // period
                at_lane = lax.broadcasted_iota(jnp.int32, (size, 128), 1)
                for t in range(tiles):
                    value = hold[t, rows_at(j, size, period), :]
                    value = pltpu.roll(value, shift, 1)
                    where = rows_at(row + t, size, stride)
                    flat[where, :] = flat[where, :] + jnp.where(at_lane >= shift, value, 0.0)
                    where = rows_at(row + t + 1, size, stride)
                    flat[where, :] = flat[where, :] + jnp.where(at_lane < shift, value, 0.0)

    def place_row(offset, value):
        width = value.shape[1]
        begin = offset - start

        @pl.when((begin > -width) & (begin < length))
        def _():
            at = begin + 128 * lead
            row = at // 128
            shift = at - row * 128
            one = lane[0:1]
            for t in range(width // 128):
                tile = pltpu.roll(value[:, 128 * t : 128 * t + 128], shift, 1)
                add_rows(row + t, jnp.where(one >= shift, tile, 0.0))
                add_rows(row + t + 1, jnp.where(one < shift, tile, 0.0))

    place("mlp_out", left_out, 0, 1, tall_out)
    place("head_w", left_head, 2, 3, tall_head)
    place_row(OFFSETS["mlp_out_bias"][0], dw_ref[3:4, 0:DIM])
    place_row(OFFSETS["head_norm"][0], dw_ref[2:3, :])
    place_row(OFFSETS["head_bias"][0], dw_ref[4:5, :])
    place_row(OFFSETS["head_bias"][0] + EXPAND, dw_ref[5:6, 0:256])
    place_row(OFFSETS["mid_norm"][0], norm_ref[0:1, :])
    place_row(OFFSETS["mid_norm"][0] + EXPAND, norm_ref[1:2, :])
    place_row(OFFSETS["dw_norm"][0], dw_ref[1:2, :])
    place_row(OFFSETS["dw_norm"][0] + EXPAND, dw_ref[0:1, :])
    total = flat[lead : lead + rows, :] + late_ref[0:rows] + mid_ref[0:rows]
    out_ref[...] = total
    square = jnp.sum(total * total).reshape(1, 1)
    packet_ref[0:16, :] = stem_ref[...]
    packet_ref[16:24, :] = jnp.where(lane == 0, loss_ref[...], jnp.where(lane == 1, square, 0.0))


def shard_parts(me, length, late, mid, dw_sums, mid_sums, vectors, stem, loss):
    rows = length // 128
    devices = vectors.shape[0]
    part = min(devices, 128)

    def tall(name, unit):
        width = OFFSETS[name][1][1]
        return round_up(-(-length // width) + 1, unit)

    tall_out, tall_head = tall("mlp_out", 8), tall("head_w", 16)
    return pl.pallas_call(
        functools.partial(shard_kernel, length, tall_out, tall_head),
        out_shape=(jax.ShapeDtypeStruct((rows, 128), F32), jax.ShapeDtypeStruct((24, 128), F32)),
        in_specs=[SMEM_SPEC] + [VMEM_SPEC] * 7,
        out_specs=(VMEM_SPEC,) * 2,
        scratch_shapes=[
            pltpu.VMEM((rows + 1024, 128), F32),
            pltpu.VMEM((8, max(tall_out, tall_head) + 16, 128), F32),
            pltpu.VMEM((devices // part, MLP + 2 * tall_out, part), F32),
            pltpu.VMEM((devices // part, DIM + 2 * tall_head, part), F32),
        ],
        compiler_params=params_of(16),
        cost_estimate=cost(4),
        name="shard_parts",
    )(me, late, mid, dw_sums, mid_sums, vectors, stem, loss)


def squeeze_lanes():
    table = np.zeros((16 * 48, 16 * 24), np.float32)
    for e in range(16):
        for x in range(24):
            table[e * 48 + x, e * 24 + x] = 1.0
    return table


def slots_of(rel_index):
    last = TOKENS - 1
    corner = lambda i: rel_index[i].reshape(HALF, HALF)
    low_row = jnp.concatenate([corner(last), corner(last - HALF + 1)[:, 1:]], axis=1)
    high_row = jnp.concatenate([corner(HALF - 1), corner(0)[:, 1:]], axis=1)
    return jnp.concatenate([low_row, high_row[1:]], axis=0)


def one_hot(slot_ref, c):
    at = lax.broadcasted_iota(jnp.int32, (256, 2 * WIDE), 1)
    return jnp.where(slot_ref[256 * c : 256 * c + 256, :] == at, 1.0, 0.0).astype(BF16)


def bias_kernel(table_ref, slot_ref, pick_ref, out_ref, held):
    table = table_ref[...].astype(BF16)
    f = jnp.concatenate([dot(table, one_hot(slot_ref, c), NT) for c in range(2 * WIDE // 256)], axis=1)
    for x in range(HALF):
        turned = pltpu.roll(f, (WIDE * 2 - (HALF - 1 - x)) % (WIDE * 2), 1) if x != HALF - 1 else f
        held[16 * x : 16 * x + 16, :] = turned.astype(BF16)
    for part in range(3):
        made = dot(held[:, 768 * part : 768 * part + 768], pick_ref[...])
        for t in range(3):
            for x in range(HALF):
                out_ref[3 * part + t, pl.ds(x, HEADS, stride=HALF), :] = made[
                    16 * x : 16 * x + HEADS, 128 * t : 128 * t + 128
                ]


def build_bias(table, slots, pick):
    return pl.pallas_call(
        bias_kernel,
        out_shape=jax.ShapeDtypeStruct((9, HEADS * HALF + HALF, 128), F32),
        in_specs=[VMEM_SPEC] * 3,
        out_specs=VMEM_SPEC,
        scratch_shapes=[pltpu.VMEM((16 * HALF, 2 * WIDE), BF16)],
        compiler_params=params_of(16),
        cost_estimate=cost(8),
        name="bias_build",
    )(table, slots, pick)


def halves_of(v):
    high = v.astype(BF16)
    return high, (v - high.astype(F32)).astype(BF16)


def bias_back_step(grad_ref, slot_ref, pick_ref, out_ref, held):
    for part in range(3):
        rows = jnp.concatenate([grad_ref[3 * part + t] for t in range(3)], axis=1)
        high, rest = halves_of(rows)
        wide = dot(high, pick_ref[...]) + dot(rest, pick_ref[...])
        for t in range(6):
                held[6 * part + t, 0 : HEADS * HALF, :] = wide[:, 128 * t : 128 * t + 128]
    total = jnp.zeros((16, 2 * WIDE), F32)
    for x in range(HALF):
        wide = jnp.concatenate([held[t, pl.ds(x, HEADS, stride=HALF), :] for t in range(18)], axis=1)
        wide = jnp.concatenate([wide, jnp.zeros((4, 2 * WIDE), F32)], axis=0)
        total = total + (pltpu.roll(wide, HALF - 1 - x, 1) if x != HALF - 1 else wide)
    high, rest = halves_of(total)
    result = jnp.zeros((16, 2 * WIDE), F32)
    for c in range(2 * WIDE // 256):
        hot = one_hot(slot_ref, c)
        cols = slice(256 * c, 256 * c + 256)
        result = result + dot(high[:, cols], hot) + dot(rest[:, cols], hot)
    out_ref[...] = result


def sigmoid(v):
    return 1.0 / (1.0 + jnp.exp(-v))


def row8(rows):
    width = rows[0].shape[1]
    return jnp.concatenate(rows + [jnp.zeros((8 - len(rows), width), F32)], axis=0)


def dw_stats(stat, count):
    mean = stat[0:1] / count
    return mean, lax.rsqrt(stat[1:2] / count - mean * mean + EPS)


def valid_places(limit):
    return (limit * limit).astype(F32)


def excite_kernel(
    res_ref, mask_ref, depth_ref, stat_ref, bgram_ref, norm_ref, down_ref, down_b_ref, up_ref, up_b_ref,
    proj_ref, base_ref, short_ref, pre_ref, qkv_ref,
    act_ref, slope_ref, block_ref, skip_ref, normed_ref, project_ref, vec_ref, small_ref, held, total,
):
    limit = limit_of(res_ref)
    count = bgram_ref[64:65, 64:65]
    mean, inverse = dw_stats(stat_ref[...], count)
    gain = norm_ref[0:1] * inverse
    shift = norm_ref[1:2] - mean * gain
    rows = 4 * HALF
    group = pl.program_id(0)

    @pl.when(group == 0)
    def _():
        total[...] = jnp.zeros_like(total)

    def fill(i, sums):
        at = pl.ds(pl.multiple_of(rows * i, 16), rows)
        value, slope = gelu_pair(depth_ref[at, :] * gain + shift)
        inside = jnp.concatenate([mask_ref[at, :]] * CHUNKS, axis=1)
        value = value * inside
        held[pl.ds(pl.multiple_of(group * QUAD + rows * i, 16), rows), :] = value
        act_ref[at, :] = value.astype(BF16)
        slope_ref[at, :] = (slope * inside).astype(BF16)
        for k in range(rows // 8):
            sums = sums + value[8 * k : 8 * k + 8]
        return sums

    total[...] = lax.fori_loop(0, QUAD // rows, fill, total[...])

    @pl.when(group == 3)
    def _():
        excite_rest(
            limit, mean, inverse, total, down_ref, down_b_ref, up_ref, up_b_ref, proj_ref, base_ref, short_ref,
            pre_ref, qkv_ref, block_ref, skip_ref, normed_ref, project_ref, vec_ref, small_ref, held,
        )


def excite_rest(
    limit, mean, inverse, total, down_ref, down_b_ref, up_ref, up_b_ref, proj_ref, base_ref, short_ref, pre_ref,
    qkv_ref, block_ref, skip_ref, normed_ref, project_ref, vec_ref, small_ref, held,
):
    pooled = jnp.sum(total[...], axis=0, keepdims=True) / valid_places(limit)
    before = dot(row8([pooled]), down_ref[...].astype(F32), precision=HIGH)[0:1] + down_b_ref[...]
    gate = sigmoid(before)
    squeeze = before * gate
    excite = sigmoid(
        dot(row8([squeeze]), up_ref[...].astype(F32), precision=HIGH)[0:1] + up_b_ref[...]
    )
    vec_ref[...] = row8([pooled, excite, mean, inverse])
    small_ref[...] = row8([squeeze, gate * (1.0 + before * (1.0 - gate))])

    big = 576
    def section(i, _):
        at = pl.ds(pl.multiple_of(big * i, 16), big)
        scaled = (held[at, :] * excite).astype(BF16)
        block_ref[at, :] = dot(scaled, proj_ref[...]) + dot(base_ref[at, :], short_ref[...])
        return 0

    lax.fori_loop(0, PLACES // big, section, 0)
    part = 96

    def tokens(i, _):
        skipped = jnp.zeros((part, MB_CH), F32)
        normed = jnp.zeros((part, MB_CH), F32)
        for group in range(4):
            block = block_ref[pl.ds(pl.multiple_of(group * QUAD + part * i, 16), part), :]
            skipped = skipped + block
            hat, _ = normalise(block)
            normed = normed + hat
        at = pl.ds(pl.multiple_of(part * i, 16), part)
        skip_ref[at, :] = (0.25 * skipped).astype(BF16)
        low = (0.25 * normed * pre_ref[0:1] + pre_ref[1:2]).astype(BF16)
        normed_ref[at, :] = low
        return 0

    lax.fori_loop(0, TOKENS // part, tokens, 0)
    project_ref[...] = dot(normed_ref[...], qkv_ref[...]).astype(BF16)


def normalise(v):
    centered = v - jnp.mean(v, axis=-1, keepdims=True)
    inverse = lax.rsqrt(jnp.mean(centered * centered, axis=-1, keepdims=True) + EPS)
    return centered * inverse, inverse


def normalise_back(grad_hat, hat, inverse):
    first = jnp.mean(grad_hat, axis=-1, keepdims=True)
    second = jnp.mean(grad_hat * hat, axis=-1, keepdims=True)
    return inverse * (grad_hat - first - hat * second)


def excite_forward(res_ids, mask, depth, stat, bgram, base, p):
    part = lambda width: pl.BlockSpec((QUAD, width), lambda i: (i, 0))
    whole = lambda *shape: pl.BlockSpec(shape, lambda i: (0,) * len(shape))
    return pl.pallas_call(
        excite_kernel,
        grid=(4,),
        out_shape=(
            jax.ShapeDtypeStruct((PLACES, EXPAND), BF16),
            jax.ShapeDtypeStruct((PLACES, EXPAND), BF16),
            jax.ShapeDtypeStruct((PLACES, MB_CH), F32),
            jax.ShapeDtypeStruct((TOKENS, MB_CH), BF16),
            jax.ShapeDtypeStruct((TOKENS, MB_CH), BF16),
            jax.ShapeDtypeStruct((TOKENS, 3 * DIM), BF16),
            jax.ShapeDtypeStruct((8, EXPAND), F32),
            jax.ShapeDtypeStruct((8, SQUEEZE), F32),
        ),
        in_specs=[
            SMEM_SPEC, part(128), part(EXPAND), whole(8, EXPAND), whole(72, 128), whole(2, EXPAND),
            whole(EXPAND, SQUEEZE), whole(1, SQUEEZE), whole(SQUEEZE, EXPAND), whole(1, EXPAND),
            whole(EXPAND, MB_CH), whole(PLACES, 128), whole(128, MB_CH), whole(2, MB_CH), whole(MB_CH, 3 * DIM),
        ],
        out_specs=(
            part(EXPAND), part(EXPAND), whole(PLACES, MB_CH), whole(TOKENS, MB_CH), whole(TOKENS, MB_CH),
            whole(TOKENS, 3 * DIM), whole(8, EXPAND), whole(8, SQUEEZE),
        ),
        scratch_shapes=[pltpu.VMEM((PLACES, EXPAND), F32), pltpu.VMEM((8, EXPAND), F32)],
        compiler_params=params_of(40),
        cost_estimate=cost(18),
        name="excite_forward",
    )(
        res_ids, mask, depth, stat, bgram, p["dw_norm"], p["se_down"], p["se_down_bias"], p["se_up"], p["se_up_bias"],
        p["mb_proj"], base, p["mb_short"], p["pre_norm"], p["qkv"],
    )


SCALE = HEAD_DIM ** (-0.5)
PER = BLOCK // HEAD_DIM
ATT_ROWS = 2 * HALF


def token_valid(limit, shape, axis):
    at = lax.broadcasted_iota(jnp.int32, shape, axis)
    y = at // HALF
    x = at - y * HALF
    return (2 * y < limit) & (2 * x < limit)


def head_lanes(h):
    lane = lax.broadcasted_iota(jnp.int32, (TOKENS, BLOCK), 1)
    return lane // HEAD_DIM == h


def bias_cut(up):
    offset = (HALF - 1 - up) * HALF
    lead = offset % 128
    return offset // 128, (5 if lead <= 64 else 6), lead


def attend_kernel(res_ref, q_ref, k_ref, v_ref, bias_ref, out_ref, p_ref, scores):
    limit = limit_of(res_ref)
    usable = token_valid(limit, (1, TOKENS), 1)

    def head(h, total):
        mine = head_lanes(h)
        q = jnp.where(mine, q_ref[...], jnp.zeros((), BF16))
        scores[h % 2] = dot(q, k_ref[...], NT)
        bias_rows = pl.ds(pl.multiple_of(h * HALF, 8), HALF)
        for i in range(TOKENS // ATT_ROWS):
            at = slice(ATT_ROWS * i, ATT_ROWS * i + ATT_ROWS)
            shifted = []
            for k in range(2):
                tile, tiles, lead = bias_cut(2 * i + k)
                bias = jnp.concatenate([bias_ref[tile + t, bias_rows, :] for t in range(tiles)], axis=1)
                if lead:
                    bias = pltpu.roll(bias, 128 * tiles - lead, 1)
                shifted.append(bias[:, :TOKENS])
            s = scores[h % 2, at, :] * SCALE + jnp.concatenate(shifted, axis=0)
            s = jnp.where(usable, s, -1e30)
            e = jnp.exp(s - jnp.max(s, axis=-1, keepdims=True))
            weights = e * (1.0 / jnp.sum(e, axis=-1, keepdims=True))
            p_ref[h, at, :] = weights.astype(BF16)
        return jnp.where(mine, dot(p_ref[h], v_ref[...]), total)

    total = lax.fori_loop(0, PER, head, jnp.zeros((TOKENS, BLOCK), F32), unroll=2)
    out_ref[...] = total.astype(BF16)


def attend_forward(res_ids, project, bias):
    part = lambda k: pl.BlockSpec((TOKENS, BLOCK), lambda j: (0, 3 * k + j))
    return pl.pallas_call(
        attend_kernel,
        grid=(HEADS // PER,),
        out_shape=(
            jax.ShapeDtypeStruct((TOKENS, DIM), BF16),
            jax.ShapeDtypeStruct((HEADS, TOKENS, TOKENS), BF16),
        ),
        in_specs=[SMEM_SPEC, part(0), part(1), part(2), pl.BlockSpec((9, PER * HALF, 128), lambda j: (0, j, 0))],
        out_specs=(
            pl.BlockSpec((TOKENS, BLOCK), lambda j: (0, j)),
            pl.BlockSpec((PER, TOKENS, TOKENS), lambda j: (j, 0, 0)),
        ),
        scratch_shapes=[pltpu.VMEM((2, TOKENS, TOKENS), F32)],
        compiler_params=params_of(56),
        cost_estimate=cost(35),
        name="attend_forward",
    )(res_ids, project, project, project, bias)


def attend_back_kernel(
    q_ref, k_ref, v_ref, o_ref, do_ref, p_ref, slot_ref, pick_ref, dq_ref, dk_ref, dv_ref, dtable_ref,
    scores, low, bias, dbias_ref, held, turned, sums,
):
    first_head = pl.program_id(0) * PER

    turned[0] = q_ref[...].astype(F32).T.astype(BF16)
    turned[1] = do_ref[...].astype(F32).T.astype(BF16)

    def head(h, dq):
        mine = head_lanes(h)
        grad = jnp.where(mine, do_ref[...], jnp.zeros((), BF16))
        scores[...] = dot(grad, v_ref[...], NT)
        bias[...] = jnp.zeros((HALF, WIDE), F32)
        lane = lax.broadcasted_iota(jnp.int32, (ATT_ROWS, BLOCK), 1)
        for i in range(TOKENS // ATT_ROWS):
            at = slice(ATT_ROWS * i, ATT_ROWS * i + ATT_ROWS)
            both = do_ref[at, :].astype(F32) * o_ref[at, :].astype(F32)
            both = jnp.where(lane // HEAD_DIM == h, both, 0.0)
            delta = jnp.sum(both, axis=-1, keepdims=True)
            ds = p_ref[h, at, :].astype(F32) * (scores[at, :] - delta)
            low[at, :] = (ds * SCALE).astype(BF16)
            for k in range(2):
                tile, tiles, lead = bias_cut(2 * i + k)
                wide = jnp.concatenate(
                    [ds[HALF * k : HALF * k + HALF], jnp.zeros((HALF, 128 * tiles - TOKENS), F32)], axis=1
                )
                if lead:
                    wide = pltpu.roll(wide, lead, 1)
                cols = slice(128 * tile, 128 * (tile + tiles))
                bias[:, cols] = bias[:, cols] + wide
        for t in range(9):
            dbias_ref[t, pl.ds(pl.multiple_of((first_head + h) * HALF, 8), HALF), :] = bias[:, 128 * t : 128 * t + 128]
        dq = jnp.where(mine, dot(low[...], k_ref[...]), dq)
        own = pl.ds(pl.multiple_of(h * HEAD_DIM, HEAD_DIM), HEAD_DIM)
        sums[0, own, :] = dot(turned[0, own, :], low[...])
        sums[1, own, :] = dot(turned[1, own, :], p_ref[h])
        return dq

    dq = lax.fori_loop(0, PER, head, jnp.zeros((TOKENS, BLOCK), F32))
    dq_ref[...] = dq.astype(BF16)
    dk_ref[...] = sums[0].T.astype(BF16)
    dv_ref[...] = sums[1].T.astype(BF16)

    @pl.when(pl.program_id(0) == HEADS // PER - 1)
    def _():
        bias_back_step(dbias_ref, slot_ref, pick_ref, dtable_ref, held)


def attend_backward(project, blended, grad, weights, slots, pick):
    part = lambda k: pl.BlockSpec((TOKENS, BLOCK), lambda j: (0, 3 * k + j))
    whole = lambda *shape: pl.BlockSpec(shape, lambda j: (0,) * len(shape))
    return pl.pallas_call(
        attend_back_kernel,
        grid=(HEADS // PER,),
        out_shape=(jax.ShapeDtypeStruct((TOKENS, DIM), BF16),) * 3
        + (jax.ShapeDtypeStruct((16, 2 * WIDE), F32),),
        in_specs=[
            part(0), part(1), part(2), part(0), part(0),
            pl.BlockSpec((PER, TOKENS, TOKENS), lambda j: (j, 0, 0)), whole(2 * WIDE, 1), whole(16 * HALF, 32 * HALF),
        ],
        out_specs=(part(0), part(0), part(0), whole(16, 2 * WIDE)),
        scratch_shapes=[
            pltpu.VMEM((TOKENS, TOKENS), F32), pltpu.VMEM((TOKENS, TOKENS), BF16), pltpu.VMEM((HALF, WIDE), F32),
            pltpu.VMEM((9, HEADS * HALF, 128), F32), pltpu.VMEM((18, HEADS * HALF + HALF, 128), F32),
            pltpu.VMEM((2, BLOCK, TOKENS), BF16), pltpu.VMEM((2, BLOCK, TOKENS), F32),
        ],
        compiler_params=params_of(50),
        cost_estimate=cost(40),
        name="attend_backward",
    )(project, project, project, blended, grad, weights, slots, pick)


MLP_ROWS = 192


def mlp_kernel(
    share, res_ref, label_ref, skip_ref, blend_ref, short_ref, out_ref, out_b_ref, norm_ref, in_ref, in_b_ref,
    back_ref, back_b_ref, hnorm_ref, head_ref, head_b_ref,
    loss_ref, dblend_ref, dskip_ref, dshort_ref, dout_ref, dout_b_ref, dnorm_ref, din_ref, din_b_ref,
    vec_ref, few_ref,
    section, low, slopes, dpres, grads,
):
    limit = limit_of(res_ref)
    n_valid = (limit // 2 * (limit // 2)).astype(F32)
    steps = TOKENS // MLP_ROWS
    cut = 384

    def valid_rows(i):
        at = lax.broadcasted_iota(jnp.int32, (MLP_ROWS, 1), 0) + MLP_ROWS * i
        y = at // HALF
        x = at - y * HALF
        return jnp.where((2 * y < limit) & (2 * x < limit), 1.0, 0.0)

    def forward(i, carry):
        feature, used = carry
        at = pl.ds(pl.multiple_of(MLP_ROWS * i, 16), MLP_ROWS)
        first = dot(skip_ref[at, :], short_ref[...]) + dot(blend_ref[at, :], out_ref[...]) + out_b_ref[...]
        section[at, :] = first
        hat, _ = normalise(first)
        normed = (hat * norm_ref[0:1] + norm_ref[1:2]).astype(BF16)
        low[at, :] = normed
        inside = valid_rows(i)
        second = first + back_b_ref[...]
        parts = []
        for j in range(MLP // cut):
            cols = slice(cut * j, cut * j + cut)
            value, slope = gelu_pair(dot(normed, in_ref[:, cols]) + in_b_ref[:, cols])
            slopes[at, cols] = slope * inside
            value = value.astype(BF16)
            parts.append(jnp.sum(value.astype(F32) * inside, axis=0, keepdims=True))
            second = second + dot(value, back_ref[cols, :])
        feature = feature + jnp.sum(second * inside, axis=0, keepdims=True)
        return feature, used + jnp.concatenate(parts, axis=1)

    feature, used = lax.fori_loop(
        0, steps, forward, (jnp.zeros((1, DIM), F32), jnp.zeros((1, MLP), F32))
    )
    feature = feature / n_valid
    hat, inverse = normalise(feature)
    normed = (hat * hnorm_ref[0:1] + hnorm_ref[1:2]).astype(BF16)
    normed8 = jnp.concatenate([normed.astype(F32), jnp.zeros((15, DIM), F32)], axis=0).astype(BF16)
    logits = dot(normed8, head_ref[...])[0:1] + head_b_ref[...]
    peak = jnp.max(logits, axis=-1, keepdims=True)
    exps = jnp.exp(logits - peak)
    total = jnp.sum(exps, axis=-1, keepdims=True)
    log_probs = logits - peak - jnp.log(total)
    at_class = lax.broadcasted_iota(jnp.int32, (1, CLASSES), 1)
    goal = jnp.where(at_class == label_ref[0], 1.0 - SMOOTH, 0.0) + SMOOTH / CLASSES
    loss = -jnp.sum(goal * log_probs, axis=-1, keepdims=True)
    loss_ref[...] = jnp.broadcast_to(loss, (8, 128))
    grad = (exps / total - goal) * share
    few_ref[...] = jnp.zeros_like(few_ref)
    few_ref[4:5, :] = grad[:, 0:EXPAND]
    few_ref[5:6, 0 : CLASSES - EXPAND] = grad[:, EXPAND:]
    grad16 = jnp.concatenate([grad, jnp.zeros((15, CLASSES), F32)], axis=0).astype(BF16)
    vec_ref[...] = jnp.zeros_like(vec_ref)
    vec_ref[2:3, 0:DIM] = normed8.astype(F32)[0:1]
    vec_ref[3:4, 0:CLASSES] = grad16.astype(F32)[0:1]
    grad = dot(grad16, head_ref[...], NT)[0:1]
    few_ref[2:3, :] = jnp.concatenate([grad * hat, grad], axis=1)
    grad = normalise_back(grad * hnorm_ref[0:1], hat, inverse) / n_valid
    low_grad = jnp.concatenate([grad, jnp.zeros((15, DIM), F32)], axis=0).astype(BF16)
    vec_ref[0:1, :] = used
    vec_ref[1:2, 0:DIM] = low_grad.astype(F32)[0:1]
    few_ref[3:4, 0:DIM] = grad * n_valid
    dhidden = dot(low_grad, back_ref[...], NT)[0:1]

    def backward(i, carry):
        dnorm0, dnorm1, dbias, dout_b = carry
        at = pl.ds(pl.multiple_of(MLP_ROWS * i, 16), MLP_ROWS)
        dnormed = jnp.zeros((MLP_ROWS, DIM), F32)
        parts = []
        for j in range(MLP // cut):
            cols = slice(cut * j, cut * j + cut)
            dpre = slopes[at, cols] * dhidden[:, cols]
            parts.append(jnp.sum(dpre, axis=0, keepdims=True))
            dpre = dpre.astype(BF16)
            dpres[at, cols] = dpre
            dnormed = dnormed + dot(dpre, in_ref[:, cols], NT)
        hat, inverse = normalise(section[at, :])
        dnorm0 = dnorm0 + jnp.sum(dnormed * hat, axis=0, keepdims=True)
        dnorm1 = dnorm1 + jnp.sum(dnormed, axis=0, keepdims=True)
        dsection = normalise_back(dnormed * norm_ref[0:1], hat, inverse) + valid_rows(i) * grad
        grads[at, :] = dsection.astype(BF16)
        dout_b = dout_b + jnp.sum(dsection, axis=0, keepdims=True)
        dblend_ref[at, :] = dot(grads[at, :], out_ref[...], NT).astype(BF16)
        dskip_ref[at, :] = dot(grads[at, :], short_ref[...], NT)
        return dnorm0, dnorm1, dbias + jnp.concatenate(parts, axis=1), dout_b

    row = jnp.zeros((1, DIM), F32)
    dnorm0, dnorm1, dbias, dout_b = lax.fori_loop(0, steps, backward, (row, row, jnp.zeros((1, MLP), F32), row))
    dnorm_ref[...] = jnp.concatenate([dnorm0, dnorm1], axis=0)
    din_b_ref[...] = dbias
    dout_b_ref[...] = dout_b
    din_ref[...] = dot(low[...], dpres[...], TN)
    dout_ref[...] = dot(blend_ref[...], grads[...], TN)
    dshort_ref[...] = dot(skip_ref[...], grads[...], TN)


def mlp_both(share, res_ids, labels, skipped, blended, p):
    s = jax.ShapeDtypeStruct
    return pl.pallas_call(
        functools.partial(mlp_kernel, share),
        out_shape=(
            s((8, 128), F32), s((TOKENS, DIM), BF16), s((TOKENS, MB_CH), F32), s((MB_CH, DIM), F32),
            s((DIM, DIM), F32), s((1, DIM), F32), s((2, DIM), F32), s((DIM, MLP), F32), s((1, MLP), F32),
            s((8, MLP), F32), s((8, EXPAND), F32),
        ),
        in_specs=[SMEM_SPEC] * 2 + [VMEM_SPEC] * 13,
        out_specs=(VMEM_SPEC,) * 11,
        scratch_shapes=[
            pltpu.VMEM((TOKENS, DIM), F32),
            pltpu.VMEM((TOKENS, DIM), BF16),
            pltpu.VMEM((TOKENS, MLP), F32),
            pltpu.VMEM((TOKENS, MLP), BF16),
            pltpu.VMEM((TOKENS, DIM), BF16),
        ],
        compiler_params=params_of(24),
        cost_estimate=cost(23),
        name="mlp_both",
    )(
        res_ids, labels, skipped, blended, p["at_short"], p["attn_out"], p["out_bias"], p["mlp_norm"], p["mlp_in"],
        p["mlp_in_bias"], p["mlp_out"], p["mlp_out_bias"], p["head_norm"], p["head_w"], p["head_bias"],
    )


def proj_back_kernel(
    res_ref, dq_ref, dk_ref, dv_ref, normed_ref, qkv_ref, dskip_ref, block_ref, pre_ref, act_ref, vec_ref,
    small_ref, proj_ref, short_ref, base_ref, down_ref, up_ref,
    dqkv_ref, dpre_ref, dblock_ref, dproj_ref, dshort_ref, dbase_ref, ddown_ref, ddown_b_ref, dup_ref, dup_b_ref,
    dpool_ref, back,
):
    limit = limit_of(res_ref)
    part = 96
    grad = dot(dq_ref[...], qkv_ref[:, 0:DIM], NT)
    grad = grad + dot(dk_ref[...], qkv_ref[:, DIM : 2 * DIM], NT)
    back[...] = grad + dot(dv_ref[...], qkv_ref[:, 2 * DIM :], NT)

    def tokens(i, carry):
        dpre0, dpre1 = carry
        at = pl.ds(pl.multiple_of(part * i, 16), part)
        grad = back[at, :]
        dskip = 0.25 * dskip_ref[at, :]
        dpre1 = dpre1 + jnp.sum(grad, axis=0, keepdims=True)
        grad = 0.25 * grad
        dhat = grad * pre_ref[0:1]
        for group in range(4):
            places = pl.ds(pl.multiple_of(group * QUAD + part * i, 16), part)
            hat, inverse = normalise(block_ref[places, :])
            dpre0 = dpre0 + jnp.sum(grad * hat, axis=0, keepdims=True)
            dblock = normalise_back(dhat, hat, inverse) + dskip
            dblock_ref[places, :] = dblock.astype(BF16)
        return dpre0, dpre1

    row = jnp.zeros((1, MB_CH), F32)
    dpre0, dpre1 = lax.fori_loop(0, TOKENS // part, tokens, (row, row))
    dpre_ref[...] = jnp.concatenate([dpre0, dpre1], axis=0)
    for k, grad_ref in enumerate((dq_ref, dk_ref, dv_ref)):
        dqkv_ref[:, DIM * k : DIM * k + DIM] = dot(normed_ref[...], grad_ref[...], TN)
    dshort_ref[...] = dot(base_ref[...], dblock_ref[...], TN)[0:STEM_CH]
    dbase_ref[...] = dot(dblock_ref[...], short_ref[...], NT)
    excite = vec_ref[1:2]
    parts = []
    for j in range(CHUNKS):
        cols = slice(BLOCK * j, BLOCK * j + BLOCK)
        act = act_ref[:, cols].astype(F32)
        scaled = (act * excite[:, cols]).astype(BF16)
        dproj_ref[cols, :] = dot(scaled, dblock_ref[...], TN)
        dscaled = dot(dblock_ref[...], proj_ref[cols, :], NT)
        parts.append(jnp.sum(dscaled * act, axis=0, keepdims=True))
    dexcite = jnp.concatenate(parts, axis=1)
    dafter = dexcite * excite * (1.0 - excite)
    dup_b_ref[...] = dafter
    dup_ref[...] = dot(row8([small_ref[0:1]]), row8([dafter]), TN, precision=HIGH)
    dsqueeze = dot(row8([dafter]), up_ref[...].astype(F32), NT, precision=HIGH)[0:1]
    dbefore = dsqueeze * small_ref[1:2]
    ddown_b_ref[...] = dbefore
    ddown_ref[...] = dot(row8([vec_ref[0:1]]), row8([dbefore]), TN, precision=HIGH)
    dpool = dot(row8([dbefore]), down_ref[...].astype(F32), NT, precision=HIGH)
    dpool_ref[...] = dpool / valid_places(limit)


def proj_backward(res_ids, dq, dk, dv, normed, dskip, block, act, vec, small, base, p):
    s = jax.ShapeDtypeStruct
    return pl.pallas_call(
        proj_back_kernel,
        out_shape=(
            s((MB_CH, 3 * DIM), F32), s((2, MB_CH), F32), s((PLACES, MB_CH), BF16), s((EXPAND, MB_CH), F32),
            s((STEM_CH, MB_CH), F32), s((PLACES, 128), F32), s((EXPAND, SQUEEZE), F32), s((1, SQUEEZE), F32),
            s((SQUEEZE, EXPAND), F32), s((1, EXPAND), F32), s((8, EXPAND), F32),
        ),
        in_specs=[SMEM_SPEC] + [VMEM_SPEC] * 16,
        out_specs=(VMEM_SPEC,) * 11,
        scratch_shapes=[pltpu.VMEM((TOKENS, MB_CH), F32)],
        compiler_params=params_of(24),
        cost_estimate=cost(13),
        name="proj_backward",
    )(
        res_ids, dq, dk, dv, normed, p["qkv"], dskip, block, p["pre_norm"], act, vec, small, p["mb_proj"],
        p["mb_short"], base, p["se_down"], p["se_up"],
    )


def excite_back_kernel(dblock_ref, proj_ref, vec_ref, dpool_ref, few_ref, slope_ref, x_ref, out_ref, sum_ref, wide):
    excite, mean, inverse = vec_ref[1:2], vec_ref[2:3], vec_ref[3:4]
    dpool = dpool_ref[0:1]
    rows = 288
    wide[...] = dot(dblock_ref[...], proj_ref[...], NT)

    def fold(v):
        total = v[0:8]
        for k in range(1, rows // 8):
            total = total + v[8 * k : 8 * k + 8]
        return total

    def step(i, sums):
        at = pl.ds(pl.multiple_of(rows * i, 16), rows)
        grad = wide[at, :] * excite + dpool
        grad = grad * slope_ref[at, :].astype(F32)
        out_ref[at, :] = grad.astype(BF16)
        hat = (x_ref[at, :] - mean) * inverse
        return sums[0] + fold(grad), sums[1] + fold(grad * hat)

    sums = lax.fori_loop(0, PLACES // rows, step, (jnp.zeros((8, BLOCK), F32),) * 2)
    sum_ref[...] = few_ref[...] + row8([jnp.sum(s, axis=0, keepdims=True) for s in sums])


def excite_backward(dblock, proj, vec, dpool, few, slope, depth):
    col = lambda rows: pl.BlockSpec((rows, BLOCK), lambda j: (0, j))
    return pl.pallas_call(
        excite_back_kernel,
        grid=(CHUNKS,),
        out_shape=(jax.ShapeDtypeStruct((PLACES, EXPAND), BF16), jax.ShapeDtypeStruct((8, EXPAND), F32)),
        in_specs=[
            pl.BlockSpec((PLACES, MB_CH), lambda j: (0, 0)),
            pl.BlockSpec((BLOCK, MB_CH), lambda j: (j, 0)),
            col(8), col(8), col(8), col(PLACES), col(PLACES),
        ],
        out_specs=(col(PLACES), col(8)),
        scratch_shapes=[pltpu.VMEM((PLACES, BLOCK), F32)],
        compiler_params=params_of(56),
        cost_estimate=cost(12),
        name="excite_backward",
    )(dblock, proj, vec, dpool, few, slope, depth)


def depth_back_kernel(
    mask_ref, du_ref, x_ref, vec_ref, sum_ref, bgram_ref, base_ref, expand_ref, dwn_ref, depth_ref, act_ref, slope_ref,
    out_ref, cross_ref, sums_ref, pad,
):
    count = bgram_ref[64:65, 64:65]
    mean1, inverse1 = bn_stats(bgram_ref[...], expand_ref[...], count)
    mean2, inverse2 = vec_ref[2:3], vec_ref[3:4]
    c1 = sum_ref[0:1] / count
    c2 = sum_ref[1:2] / count
    scale2 = dwn_ref[0:1] * inverse2
    slant = scale2 * inverse2 * c2
    level = scale2 * c1 - slant * mean2
    zero = jnp.zeros((4, 1, HALF, BLOCK), F32)
    pad[:, 0:1] = zero
    pad[:, HALF + 1 : HALF + 2] = zero
    rows = 2 * HALF

    def fill(i, _):
        for group in range(4):
            at = pl.ds(pl.multiple_of(group * QUAD + rows * i, 16), rows)
            grad = scale2 * du_ref[at, :].astype(F32) - mask_ref[at, :] * (level + x_ref[at, :] * slant)
            for k in range(2):
                pad[group, 2 * i + k + 1] = grad[HALF * k : HALF * k + HALF]
        return 0

    lax.fori_loop(0, HALF // 2, fill, 0)

    def weight(dy, dx):
        return depth_ref[8 - 3 * dy - dx : 9 - 3 * dy - dx]

    def fold(v):
        return v[0:8] + v[8:16] + v[16:24]

    def step(k, sums):
        sums = list(sums)
        for py in range(2):
            places = [
                pl.ds(pl.multiple_of((2 * py + px) * QUAD + 2 * HALF * k, 16), 2 * HALF) for px in range(2)
            ]
            low_both, high_both = (act_ref[at, :].astype(F32) for at in places)
            made = [[], []]
            for half in range(2):
                up = 2 * k + half
                cut = slice(HALF * half, HALF * half + HALF)
                sources = [(1, -1), (0, 0), (1, 0)] if py == 0 else [(0, 0), (1, 0), (0, 1)]
                low_act, high_act = low_both[cut], high_both[cut]
                even = odd = None
                for t, (gy, off) in enumerate(sources):
                    left, right = pad[2 * gy, up + 1 + off], pad[2 * gy + 1, up + 1 + off]
                    before, after = shift_down(right), shift_up(left)
                    a = before * weight(t, 0) + left * weight(t, 1) + right * weight(t, 2)
                    b = left * weight(t, 0) + right * weight(t, 1) + after * weight(t, 2)
                    even = a if even is None else even + a
                    odd = b if odd is None else odd + b
                    for s, (a, b) in enumerate(((before, left), (left, right), (right, after))):
                        tap = 3 * (2 - t) + 2 - s
                        sums[tap] = sums[tap] + fold(low_act * a + high_act * b)
                made[0].append(even)
                made[1].append(odd)
            for px in range(2):
                grad = jnp.concatenate(made[px], axis=0) * slope_ref[places[px], :].astype(F32)
                out_ref[places[px], :] = grad.astype(BF16)
        return tuple(sums)

    sums = lax.fori_loop(0, HALF // 2, step, (jnp.zeros((8, BLOCK), F32),) * 9)
    cross_ref[72:88, :] = jnp.concatenate(
        [jnp.sum(s, axis=0, keepdims=True) for s in sums] + [jnp.zeros((7, BLOCK), F32)], axis=0
    )
    cross = dot(base_ref[...], out_ref[...], TN)
    cross_ref[0:72, :] = cross[0:72]
    first = cross[64:65]
    second = (jnp.sum(cross[0:64] * expand_ref[0:64, :].astype(F32), axis=0, keepdims=True) - mean1 * first) * inverse1
    sums_ref[...] = row8([second, first])


def depth_backward(mask, du, depth, vec, sums, bgram, base, expand_w, dw_norm, mb_depth, act, slope):
    col = lambda rows: pl.BlockSpec((rows, BLOCK), lambda j: (0, j))
    whole = lambda rows: pl.BlockSpec((rows, BLOCK), lambda j: (0, 0))
    s = jax.ShapeDtypeStruct
    return pl.pallas_call(
        depth_back_kernel,
        grid=(CHUNKS,),
        out_shape=(s((PLACES, EXPAND), BF16), s((88, EXPAND), F32), s((8, EXPAND), F32)),
        in_specs=[
            whole(PLACES), col(PLACES), col(PLACES), col(8), col(8), whole(72), whole(PLACES), col(128), col(2),
            col(9), col(PLACES), col(PLACES),
        ],
        out_specs=(col(PLACES), col(88), col(8)),
        scratch_shapes=[pltpu.VMEM((4, HALF + 2, HALF, BLOCK), F32)],
        compiler_params=params_of(56),
        cost_estimate=cost(35),
        name="depth_backward",
    )(mask, du, depth, vec, sums, bgram, base, expand_w, dw_norm, mb_depth, act, slope)


def stem_back_kernel(
    mask_ref, patch_ref, slope_ref, dbase_ref, du_ref, sum_ref, bgram_ref, base_ref, expand_ref, mid_ref, spread_ref,
    out_ref, total, rows_ref, hold,
):
    step = pl.program_id(0)

    @pl.when(step == 0)
    def _():
        count = bgram_ref[64:65, 64:65]
        mean, inverse = bn_stats(bgram_ref[...], expand_ref[...], count)
        second, first = sum_ref[0:1] / count, sum_ref[1:2] / count
        scale = mid_ref[0:1] * inverse
        slant = scale * inverse * second
        rows_ref[...] = row8([scale, slant, scale * first - slant * mean])
        total[...] = jnp.zeros_like(total)

    scale, slant, level = (rows_ref[k : k + 1] for k in range(3))
    x = dot(base_ref[...], expand_ref[...])
    inside = jnp.concatenate([mask_ref[...]] * CHUNKS, axis=1)
    grad = (scale * du_ref[...].astype(F32) - inside * (level + x * slant)).astype(BF16)
    grad = dot(grad, expand_ref[...], NT) + dbase_ref[...]
    grad = grad[:, 0:64] * (1.0 / 16.0)
    grad = jnp.concatenate([grad, grad], axis=1)
    grad = jnp.concatenate([grad, grad], axis=1)
    block = patch_ref[...]
    for j in range(4):
        cols = slice(256 * j, 256 * j + 256)
        wide = (slope_ref[:, cols].astype(F32) * grad).astype(BF16)
        total[:, cols] = total[:, cols] + dot(block, wide, TN)

    @pl.when(step == STEM_STEPS - 1)
    def _():
        merged = total[0:96, 0:256]
        for px in range(1, 4):
            merged = merged + total[64 * px : 64 * px + 96, 256 * px : 256 * px + 256]
        result = jnp.zeros((32, STEM_CH), F32)
        for pair in range(2):
            wide = dot(
                spread_ref[pair][0:96].astype(F32), merged[:, 128 * pair : 128 * pair + 128], TN, precision=HIGH
            )
            result = result + wide[0:32, 0:64] + wide[32:64, 64:128]
        ones = merged[27:28]
        ones = ones[:, 0:64] + ones[:, 64:128] + ones[:, 128:192] + ones[:, 192:256]
        at = lax.broadcasted_iota(jnp.int32, (32, STEM_CH), 0)
        out_ref[...] = pairs_together(jnp.where(at == 27, ones, result), hold)


def stem_backward(mask, patches, slope, dbase, du, sums, bgram, base, expand_w, mid_norm, spread):
    part = lambda width: pl.BlockSpec((STEM_BLOCK, width), lambda i: (i, 0))
    whole = lambda *shape: pl.BlockSpec(shape, lambda i: (0,) * len(shape))
    return pl.pallas_call(
        stem_back_kernel,
        grid=(STEM_STEPS,),
        out_shape=jax.ShapeDtypeStruct((16, 128), F32),
        in_specs=[
            part(128), part(TAPS), part(1024), part(128), part(EXPAND), whole(8, EXPAND), whole(72, 128), part(128),
            whole(128, EXPAND), whole(2, EXPAND), whole(8, TAPS, 64),
        ],
        out_specs=whole(16, 128),
        scratch_shapes=[
            pltpu.VMEM((TAPS, 1024), F32), pltpu.VMEM((8, EXPAND), F32), pltpu.VMEM((40, 128), F32),
        ],
        compiler_params=params_of(60),
        cost_estimate=cost(8),
        name="stem_backward",
    )(mask, patches, slope, dbase, du, sums, bgram, base, expand_w, mid_norm, spread)


def expand_finish_kernel(cross_ref, sum_ref, bgram_ref, expand_ref, mid_ref, out_ref, square_ref, flat, hold):
    count = bgram_ref[64:65, 64:65]
    square_of = jnp.concatenate([bgram_ref[...], jnp.zeros((56, 128), F32)], axis=0)
    weights = expand_ref[...].astype(F32)
    product = dot(square_of, weights, precision=HIGH)
    mean = product[64:65] / count
    variance = jnp.sum(weights * product, axis=0, keepdims=True) / count - mean * mean
    inverse = lax.rsqrt(variance + EPS)
    second, first = sum_ref[0:1] / count, sum_ref[1:2] / count
    plain = bgram_ref[0:64, 64:65]
    hat = (product[0:64] - mean * plain) * inverse
    hold[...] = mid_ref[0:1] * inverse * (cross_ref[0:64, :] - first * plain - second * hat)
    flat[...] = jnp.zeros_like(flat)
    for name, source in (("mb_expand", hold), ("mb_depth", cross_ref.at[72:88])):
        offset, (rows, width) = OFFSETS[name]
        put_matrix(flat, lambda r, t: source[r, 128 * t : 128 * t + 128], 0, offset, rows, width)
    out_ref[...] = flat[0:EARLY_ROWS, :]
    total = flat[0:EARLY_ROWS, :]
    square_ref[...] = jnp.broadcast_to(jnp.sum(total * total).reshape(1, 1), (8, 128))


def expand_finish(cross, sums, bgram, expand_w, mid_norm):
    return pl.pallas_call(
        expand_finish_kernel,
        out_shape=(jax.ShapeDtypeStruct((EARLY_ROWS, 128), F32), jax.ShapeDtypeStruct((8, 128), F32)),
        in_specs=[VMEM_SPEC] * 5,
        out_specs=(VMEM_SPEC,) * 2,
        scratch_shapes=[pltpu.VMEM((EARLY_ROWS + 8, 128), F32), pltpu.VMEM((STEM_CH, EXPAND), F32)],
        compiler_params=params_of(10),
        cost_estimate=cost(3),
        name="expand_finish",
    )(cross, sums, bgram, expand_w, mid_norm)


def finish_kernel(
    first_ref, packet_ref, stem_ref, spread_ref, early_ref, early_square_ref, shard_ref,
    out_ref, scalar_ref, big, hold, flat,
):
    weights, own_gain, _ = stem_params(stem_ref, hold)
    spread_weights(spread_ref, weights, big, 2)
    gram = stem_ref[0:96, 0:96]
    mean, square = stem_stats(stem_ref[0:96, :], big[0:96, 0:256])
    inverse = lax.rsqrt(square - mean * mean + EPS)
    count = 4.0 * stem_ref[27:28, 27:28]
    got = pairs_apart(packet_ref[0:16], hold)
    product = dot(gram, big[0:96, 0:256].astype(F32), precision=HIGH)
    cross = jnp.zeros((32, STEM_CH), F32)
    plain = jnp.zeros((32, STEM_CH), F32)
    sums = jnp.broadcast_to(gram[:, 27:28], (96, 128))
    for pair in range(2):
        spread = spread_ref[pair][0:96].astype(F32)
        wide = dot(spread, product[:, 128 * pair : 128 * pair + 128], TN, precision=HIGH)
        cross = cross + wide[0:32, 0:64] + wide[32:64, 64:128]
        wide = dot(spread, sums, TN, precision=HIGH)
        plain = plain + wide[0:32, 0:64] + wide[32:64, 0:64]
    at = lax.broadcasted_iota(jnp.int32, (32, STEM_CH), 0)
    taps = at < 27
    grad = jnp.where(taps, got, 0.0)
    first = got[27:28]
    second = (jnp.sum(grad * weights, axis=0, keepdims=True) - mean * first) * inverse
    hat = (cross - mean * plain) * inverse
    result = own_gain * inverse * (grad - (plain * first + hat * second) / count)
    result = jnp.where(taps, result, jnp.where(at == 27, second, jnp.where(at == 28, first, 0.0)))
    square = packet_ref[16:17, 1:2] + early_square_ref[0:1, 0:1] + jnp.sum(result * result).reshape(1, 1)
    norm = jnp.sqrt(square)
    lane = lax.broadcasted_iota(jnp.int32, (8, 128), 1)
    scale = CLIP / jnp.maximum(norm, CLIP)
    scalar_ref[...] = jnp.where(lane == 0, packet_ref[16:17, 0:1], jnp.where(lane == 1, norm, scale))
    both = pairs_together(result, hold)
    rows = shard_ref.shape[0]
    flat[0:16, :] = early_ref[0:16] + both
    flat[16:EARLY_ROWS, :] = early_ref[16:EARLY_ROWS]
    flat[EARLY_ROWS:, :] = jnp.zeros((flat.shape[0] - EARLY_ROWS, 128), F32)
    begin = jnp.minimum(first_ref[0] * rows, EARLY_ROWS)
    out_ref[...] = shard_ref[...] + flat[pl.ds(begin, rows), :]


def finish(me, packet, stem, spread, early, early_square, shard):
    rows = shard.shape[0]
    return pl.pallas_call(
        finish_kernel,
        out_shape=(jax.ShapeDtypeStruct((rows, 128), F32), jax.ShapeDtypeStruct((8, 128), F32)),
        in_specs=[SMEM_SPEC] + [VMEM_SPEC] * 6,
        out_specs=(VMEM_SPEC,) * 2,
        scratch_shapes=[
            pltpu.VMEM((TAPS, 256), BF16), pltpu.VMEM((40, 128), F32),
            pltpu.VMEM((round_up(EARLY_ROWS + rows, 8), 128), F32),
        ],
        compiler_params=params_of(10),
        cost_estimate=cost(4),
        name="finish",
    )(me, packet, stem, spread, early, early_square, shard)


def levels_of(devices):
    levels = []
    stride = 1
    while stride < devices:
        radix = 2 if stride == 1 or devices // stride == 2 else 4
        levels.append((stride, radix))
        stride *= radix
    return levels


def pairs_of(devices, mask):
    return [(i, i ^ mask) for i in range(devices)]


def add_level(v, moved):
    return v + moved[0] if len(moved) == 1 else (v + moved[0]) + (moved[1] + moved[2])


def send_level(v, devices, level):
    stride, radix = level
    return [lax.ppermute(v, "dp", pairs_of(devices, stride * j)) for j in range(1, radix)]


def exchange(v, devices, levels):
    for level in levels:
        v = add_level(v, send_level(v, devices, level))
    return v


def spread_blocks(blocks, masks, devices, level):
    stride, radix = level
    moved = send_level(blocks, devices, level)
    return jnp.concatenate([blocks] + moved), [m ^ (stride * j) for j in range(radix) for m in masks]


def take(blocks, digit, axis):
    return lax.dynamic_index_in_dim(blocks, digit, axis, keepdims=False)


class Scatter:
    def __init__(self, keep, send, devices, me, low, high):
        self.devices, self.me, self.low, self.high = devices, me, low, high
        self.levels = levels_of(devices)
        self.at = 0
        self.mine, self.parts = [keep], [send]
        self.moved = []

    def launch(self):
        stride, radix = self.levels[self.at]
        top = stride * radix == self.devices
        self.moved = []
        for j, part in zip(range(1, radix), self.parts):
            pairs = pairs_of(self.devices, stride * j)
            if top:
                pairs = [(a, b) for a, b in pairs if self.low <= b // stride < self.high]
            self.moved.append(lax.ppermute(part, "dp", pairs))

    def land(self):
        terms = self.mine + [m.astype(F32) for m in self.moved]
        self.at += 1
        if self.at == len(self.levels):
            total = sum(terms[1:], terms[0])
            self.result = total.reshape(total.shape[-2:])
            return
        if len(terms) > 2:
            terms = [sum(terms[1:], terms[0])]
        stride, radix = self.levels[self.at]
        digit = (self.me // stride) % radix
        span = self.high - self.low
        if stride * radix == self.devices:
            blocks = [t.reshape((span,) + t.shape[-2:]) for t in terms]
            part = lambda d: sum(take(b, jnp.clip(d - self.low, 0, span - 1), 0) for b in blocks)
            mine = jnp.where((digit >= self.low) & (digit < self.high), part(digit), 0.0)
        else:
            blocks = [t.reshape((-1, radix) + t.shape[-2:]) for t in terms]
            part = lambda d: sum(take(b, d, 1) for b in blocks)
            mine = part(digit)
        self.mine = [mine]
        self.parts = [part(digit ^ j).astype(BF16) for j in range(1, radix)]

    def finish(self):
        if not self.moved:
            self.launch()
        self.land()
        while self.at < len(self.levels):
            self.launch()
            self.land()
        return self.result


def tie(*values):
    return lax.optimization_barrier(values)


def on_device(images, res_ids, labels, rel_index, master, first_moment, second_moment, ema_weights):
    devices = lax.axis_size("dp")
    me = lax.axis_index("dp").astype(jnp.int32)
    length = master.shape[0]
    rows = length // 128
    held = round_up(rows, 16)
    images_total = res_ids.shape[0] * devices

    levels = levels_of(devices)
    low_master = lax.optimization_barrier(master.astype(BF16).reshape(rows, 128))
    blocks, masks = spread_blocks(jnp.pad(low_master, ((0, held - rows), (0, 0)))[None], [0], devices, levels[-1])
    stem_part = lax.dynamic_update_slice(
        jnp.zeros((16 + rows, 128), BF16), low_master, (jnp.minimum(me * rows, 16), 0)
    )[:16]
    patches, packet, mask = make_patches(res_ids, images, stem_part)
    packet, blocks = tie(packet, blocks)
    packet = exchange(packet, devices, levels[:-1])
    packet, blocks = tie(packet, blocks)
    for level in levels[-2:0:-1]:
        blocks, masks = spread_blocks(blocks, masks, devices, level)
    packet = exchange(packet, devices, levels[-1:])
    spread = jnp.asarray(spread_taps(), BF16)
    base, stem_slope, bgram = stem_forward(patches, packet, spread)
    stem_packet = packet
    bgram, blocks = tie(bgram, blocks)
    others = lax.ppermute(blocks, "dp", pairs_of(devices, 1))
    bgram = exchange(bgram, devices, levels[:-1])
    bgram, others = tie(bgram, others)
    sent = send_level(bgram, devices, levels[-1])
    p = unpack([blocks, others], me.reshape(1), masks + [m ^ 1 for m in masks], rows, ALL_SHAPES)
    bgram = add_level(bgram, sent)
    depth, act1, slope1, stat = depth_forward(mask, base, p["mb_expand"], bgram, p["mid_norm"], p["mb_depth"])
    stat = exchange(stat, devices, levels)
    slots = slots_of(rel_index)
    slots = jnp.pad(slots, ((0, 1), (0, 1)), constant_values=2 * WIDE - 1).reshape(2 * WIDE, 1)
    pick = squeeze_lanes()
    pick, pick_back = jnp.asarray(pick, BF16), jnp.asarray(pick.T, BF16)
    bias = build_bias(p["rel_table"], slots, pick)

    act2, slope2, block, skipped, normed, project, vec, small = excite_forward(res_ids, mask, depth, stat, bgram, base, p)
    blended, weights = attend_forward(res_ids, project, bias)
    loss, dblend, dskip, g_short, g_out, g_out_b, g_mnorm, g_in, g_in_b, vectors, few = mlp_both(
        1.0 / images_total, res_ids, labels, skipped, blended, p
    )

    core = (me % 2).reshape(1)
    top_radix = levels_of(devices)[-1][1]

    def scattered(grads, begin, end):
        span = devices // top_radix
        low = begin // length // span
        high = (end - 1) // length // span + 1
        keep, send = pack(core, grads, low * span * rows, (high - low) * span, rows, held)
        return Scatter(keep, send, devices, me, low, high)

    middle = scattered(
        {
            "attn_out": g_out, "out_bias": g_out_b, "mlp_norm": g_mnorm, "mlp_in": g_in, "mlp_in_bias": g_in_b,
        },
        OFFSETS["attn_out"][0], OFFSETS["mlp_out"][0],
    )
    dblend, middle.parts = tie(dblend, middle.parts)
    middle.launch()
    vectors = lax.all_gather(vectors, "dp", axis=0, tiled=False)

    dq, dk, dv, g_table = attend_backward(project, blended, dblend, weights, slots, pick_back)
    dq, middle.moved = tie(dq, middle.moved)
    middle.land()
    dq, middle.parts = tie(dq, middle.parts)
    middle.launch()
    g_qkv, g_pre, dblock, g_proj, g_mbshort, dbase, g_down, g_down_b, g_up, g_up_b, dpool = proj_backward(
        res_ids, dq, dk, dv, normed, dskip, block, act2, vec, small, base, p
    )
    late = scattered(
        {
            "mb_short": g_mbshort, "se_down": g_down, "se_down_bias": g_down_b, "se_up": g_up, "se_up_bias": g_up_b,
            "mb_proj": g_proj, "at_short": g_short, "pre_norm": g_pre, "qkv": g_qkv, "rel_table": g_table,
        },
        OFFSETS["mb_short"][0], OFFSETS["mlp_norm"][0],
    )
    dblock, late.parts, middle.moved = tie(dblock, late.parts, middle.moved)
    late.launch()
    middle.land()
    dblock, middle.parts = tie(dblock, middle.parts)
    middle.launch()
    du, sums = excite_backward(dblock, p["mb_proj"], vec, dpool, few, slope2, depth)
    sums, late.moved, middle.moved = tie(sums, late.moved, middle.moved)
    late.land()
    sums, late.parts = tie(sums, late.parts)
    late.launch()
    dw_sums = exchange(sums, devices, levels)
    dw_sums, late.moved = tie(dw_sums, late.moved)
    late.land()
    dw_sums, late.parts = tie(dw_sums, late.parts)
    late.launch()
    du, cross, sums = depth_backward(
        mask, du, depth, vec, dw_sums, bgram, base, p["mb_expand"], p["dw_norm"], p["mb_depth"], act1, slope1
    )
    sums, late.moved = tie(sums, late.moved)
    steps = [(1 << k, 2) for k in range(devices.bit_length() - 1)]
    sent = send_level(cross, devices, steps[0])
    mid_sums = exchange(sums, devices, levels[:-1])
    mid_sums, sent = tie(mid_sums, sent)
    cross = add_level(cross, sent)
    moved = send_level(mid_sums, devices, levels[-1])
    sent = send_level(cross, devices, steps[1])
    mid_sums, sent = tie(add_level(mid_sums, moved), sent)
    cross = add_level(cross, sent)
    mid_sums, cross = tie(mid_sums, cross)
    sent = send_level(cross, devices, steps[2])
    stem = stem_backward(
        mask, patches, stem_slope, dbase, du, mid_sums, bgram, base, p["mb_expand"], p["mid_norm"], spread
    )
    stem, sent, late.moved = tie(stem, sent, late.moved)
    cross = add_level(cross, sent)
    stem, cross = tie(stem, cross)
    sent = send_level(cross, devices, steps[3])
    shard, packet = shard_parts(
        me.reshape(1), length, late.finish(), middle.finish(), dw_sums, mid_sums, vectors, stem, loss
    )
    packet, sent = tie(packet, sent)
    cross = add_level(cross, sent)
    cross, packet = tie(cross, packet)
    cross = exchange(cross, devices, steps[4:])
    packet = exchange(packet, devices, levels)
    early_grad, early_square = expand_finish(cross, mid_sums, bgram, p["mb_expand"], p["mid_norm"])
    shard, scalars = finish(
        me.reshape(1), packet, stem_packet, spread, early_grad, early_square, shard
    )
    loss_sum, grad_norm = scalars[0, 0], scalars[0, 1]
    shard = shard.reshape(length)
    clipped = shard * scalars[0, 2]
    moment_one = BETA_ONE * first_moment + (1.0 - BETA_ONE) * clipped
    moment_two = BETA_TWO * second_moment + (1.0 - BETA_TWO) * clipped * clipped
    update = (
        moment_one
        / (1.0 - BETA_ONE**STEP)
        / (jnp.sqrt(moment_two / (1.0 - BETA_TWO**STEP)) + ADAM_EPS)
    )
    weights_out = master - RATE * (update + DECAY * master)
    averaged = EMA_DECAY * ema_weights + (1.0 - EMA_DECAY) * weights_out
    return (
        loss_sum,
        grad_norm,
        weights_out,
        moment_one,
        moment_two,
        averaged,
        weights_out.astype(BF16),
    )


def solution(mesh):
    in_specs = (
        P("dp", None, None, None),
        P("dp"),
        P("dp"),
        P(),
        P("dp"),
        P("dp"),
        P("dp"),
        P("dp"),
    )
    out_specs = (P(), P(), P("dp"), P("dp"), P("dp"), P("dp"), P("dp"))
    return jax.shard_map(
        on_device, mesh=mesh, in_specs=in_specs, out_specs=out_specs, check_vma=False
    )
```
